32 devices in a mesh: img: 4 (over x, core), pix: 8 (over z, y).
Axes of the slice: x: 2, y: 2, z: 4, core: 2. Of those that a mesh axis runs over, the one named last changes fastest.
Arguments:
- rgb_pixels: bfloat16 [16, 3, 50176], P('img', None, 'pix'), may hold values from -6 to 6
- keep_mask: int32 [16, 50176], P('img', 'pix'), may hold values 0 or 1
- latent_array: bfloat16 [512, 1024], P('pix'), may hold values from -6 to 6
- gain_input: float32 [261], replicated, may hold values from 0.5 to 1.5
- gain_latent: float32 [1024], replicated, may hold values from 0.5 to 1.5
- w_query: bfloat16 [1024, 1024], P('pix'), may hold values from -0.1875 to 0.1875
- w_key: bfloat16 [261, 1024], P(None, 'pix'), may hold values from -0.375 to 0.375
- w_value: bfloat16 [261, 1024], P(None, 'pix'), may hold values from -0.375 to 0.375
- w_cross_out: bfloat16 [1024, 1024], P('pix'), may hold values from -0.75 to 0.75
- gain_mlp_one: float32 [1024], replicated, may hold values from 0.5 to 1.5
- w_up_one: bfloat16 [1024, 1024], P(None, 'pix'), may hold values from -0.1875 to 0.1875
- w_down_one: bfloat16 [1024, 1024], P('pix'), may hold values from -0.1875 to 0.1875
- gain_self: float32 [1024], replicated, may hold values from 0.5 to 1.5
- w_self_query: bfloat16 [1024, 1024], P('pix'), may hold values from -0.1875 to 0.1875
- w_self_key: bfloat16 [1024, 1024], P('pix'), may hold values from -0.1875 to 0.1875
- w_self_value: bfloat16 [1024, 1024], P('pix'), may hold values from -0.1875 to 0.1875
- w_self_out: bfloat16 [1024, 1024], P('pix'), may hold values from -1 to 1
- gain_mlp_two: float32 [1024], replicated, may hold values from 0.5 to 1.5
- w_up_two: bfloat16 [1024, 1024], P(None, 'pix'), may hold values from -0.1875 to 0.1875
- w_down_two: bfloat16 [1024, 1024], P('pix'), may hold values from -0.1875 to 0.1875
- cotangent: bfloat16 [16, 512, 1024], P('img', 'pix'), may hold values from -6 to 6
Outputs:
- latent_out: bfloat16 [16, 512, 1024], P('img', 'pix')
- grad_pixels: float32 [16, 3, 50176], P('img', None, 'pix')
- grad_latent_array: float32 [512, 1024], P('pix')
- grad_gain_input: float32 [261], replicated
- grad_gain_latent: float32 [1024], replicated
- grad_w_query: float32 [1024, 1024], P('pix')
- grad_w_key: float32 [261, 1024], P(None, 'pix')
- grad_w_value: float32 [261, 1024], P(None, 'pix')
- grad_w_cross_out: float32 [1024, 1024], P('pix')
- grad_gain_mlp_one: float32 [1024], replicated
- grad_w_up_one: float32 [1024, 1024], P(None, 'pix')
- grad_w_down_one: float32 [1024, 1024], P('pix')
- grad_gain_self: float32 [1024], replicated
- grad_w_self_query: float32 [1024, 1024], P('pix')
- grad_w_self_key: float32 [1024, 1024], P('pix')
- grad_w_self_value: float32 [1024, 1024], P('pix')
- grad_w_self_out: float32 [1024, 1024], P('pix')
- grad_gain_mlp_two: float32 [1024], replicated
- grad_w_up_two: float32 [1024, 1024], P(None, 'pix')
- grad_w_down_two: float32 [1024, 1024], P('pix')
The draws below stay inside these ranges and needn't reach their ends.
All inputs are finite; a program needn't handle non-finite values. No bound on the sum of `keep_mask` on one device may be relied on, other than what follows from the above.
Results may differ from the reference program's by a relative error of at most 0.033.
Values may be sent and summed in bfloat16 or wider, within the bound.
A program may use at most 448 MiB of HBM per device.

```python
import jax
import jax.numpy as jnp
from jax import lax

D = 1024
HEADS = 8
HEAD_DIM = 128
FF = 1024
LAT = 512
BANDS = 64
SIDE = 224
P_SIZE = 50176
C = 261
IMAGES = 16


def place_ends(result, rng, smallest, top_value):
    shape = result.shape
    spot = [jax.random.randint(jax.random.fold_in(rng, axis), (), 0, shape[axis]) for axis in range(len(shape))]
    result = result.at[tuple(spot)].set(smallest)
    longest = shape.index(max(shape))
    spot[longest] = (spot[longest] + 1) % shape[longest]
    return result.at[tuple(spot)].set(top_value)


def shard_levels(own_key, shape, pieces, low, high):
    loudness, own = 1.0, jax.random.fold_in(own_key, 6)
    for axis_at, shards_of in pieces:
        draws = jnp.exp(jax.random.uniform(jax.random.fold_in(own, axis_at), (shards_of,), jnp.float32, low / len(pieces), high / len(pieces)))
        loudness = loudness * jnp.repeat(draws, shape[axis_at] // shards_of).reshape([-1 if axis == axis_at else 1 for axis in range(len(shape))])
    return loudness


def noise(rng, extent, scale, limit, pieces=(), dtype=jnp.bfloat16):
    drawn = scale * jax.random.normal(rng, extent, jnp.float32)
    if pieces:
        drawn = drawn * shard_levels(rng, extent, pieces, -0.22, 0.18)
    return jnp.clip(drawn, -limit, limit).astype(dtype)


def setup_inputs(seed: int = 0) -> dict:
    seeds = jax.random.split(jax.random.key(seed), 22)
    rgb_pixels = noise(seeds[0], (IMAGES, 3, P_SIZE), 1.0, 6.0, ((0, 4), (2, 8)))
    keep_mask = place_ends((jax.random.randint(seeds[1], (IMAGES, P_SIZE), 0, 4) < 3).astype(jnp.int32), jax.random.fold_in(seeds[1], 1), 0, 1)
    latent_array = noise(seeds[2], (LAT, D), 1.0, 6.0, ((0, 8),))
    gain_input = jnp.clip(1.0 + 0.1 * jax.random.normal(seeds[3], (C,), jnp.float32), 0.5, 1.5)
    gain_latent = jnp.clip(1.0 + 0.1 * jax.random.normal(seeds[4], (D,), jnp.float32), 0.5, 1.5)
    w_query = noise(seeds[5], (D, D), D ** -0.5, 0.1875, ((0, 8),))
    w_key = noise(seeds[6], (C, D), C ** -0.5, 0.375, ((1, 8),))
    w_value = noise(seeds[7], (C, D), C ** -0.5, 0.375, ((1, 8),))
    w_cross_out = noise(seeds[8], (D, D), (D // 16) ** -0.5, 0.75, ((0, 8),))
    gain_mlp_one = jnp.clip(1.0 + 0.1 * jax.random.normal(seeds[9], (D,), jnp.float32), 0.5, 1.5)
    w_up_one = noise(seeds[10], (D, FF), D ** -0.5, 0.1875, ((1, 8),))
    w_down_one = noise(seeds[11], (FF, D), FF ** -0.5, 0.1875, ((0, 8),))
    gain_self = jnp.clip(1.0 + 0.1 * jax.random.normal(seeds[12], (D,), jnp.float32), 0.5, 1.5)
    w_self_query = noise(seeds[13], (D, D), D ** -0.5, 0.1875, ((0, 8),))
    w_self_key = noise(seeds[14], (D, D), D ** -0.5, 0.1875, ((0, 8),))
    w_self_value = noise(seeds[15], (D, D), D ** -0.5, 0.1875, ((0, 8),))
    w_self_out = noise(seeds[16], (D, D), (D // 32) ** -0.5, 1.0, ((0, 8),))
    gain_mlp_two = jnp.clip(1.0 + 0.1 * jax.random.normal(seeds[17], (D,), jnp.float32), 0.5, 1.5)
    w_up_two = noise(seeds[18], (D, FF), D ** -0.5, 0.1875, ((1, 8),))
    w_down_two = noise(seeds[19], (FF, D), FF ** -0.5, 0.1875, ((0, 8),))
    cotangent = noise(seeds[20], (IMAGES, LAT, D), 1.0, 6.0, ((0, 4), (1, 8)))
    return dict(rgb_pixels=rgb_pixels, keep_mask=keep_mask, latent_array=latent_array, gain_input=gain_input, gain_latent=gain_latent, w_query=w_query, w_key=w_key, w_value=w_value, w_cross_out=w_cross_out, gain_mlp_one=gain_mlp_one, w_up_one=w_up_one, w_down_one=w_down_one, gain_self=gain_self, w_self_query=w_self_query, w_self_key=w_self_key, w_self_value=w_self_value, w_self_out=w_self_out, gain_mlp_two=gain_mlp_two, w_up_two=w_up_two, w_down_two=w_down_two, cotangent=cotangent)


eps = 1e-05

@jax.custom_vjp
def low(v):
    return lax.optimization_barrier(v.astype(jnp.bfloat16)).astype(jnp.float32)

@jax.custom_vjp
def low_back(v):
    return v

def low_keep(v):
    return (low(v), None)

def low_pass(kept, grad):
    return (grad,)

def back_keep(v):
    return (v, None)

def back_low(kept, grad):
    return (low(grad),)
low.defvjp(low_keep, low_pass)
low_back.defvjp(back_keep, back_low)

def layer_norm(rows, gain):
    average = lax.optimization_barrier(jnp.mean(rows, axis=-1, keepdims=True))
    centred = rows - average
    spread = lax.optimization_barrier(jnp.mean(centred * centred, axis=-1, keepdims=True))
    return centred * lax.rsqrt(spread + eps) * gain

def matmul(left, right):
    return jnp.dot(left, right, precision=lax.Precision.HIGHEST, preferred_element_type=jnp.float32)

def fourier_rows(position, image_side, band_count):
    row_pos = (position // image_side).astype(jnp.float32) * (2.0 / (image_side - 1)) - 1.0
    col_pos = (position % image_side).astype(jnp.float32) * (2.0 / (image_side - 1)) - 1.0
    band_steps = lax.iota(jnp.int32, band_count).astype(jnp.float32)
    frequency = 1.0 + band_steps * ((image_side / 2.0 - 1.0) / (band_count - 1))
    row_angle = jnp.pi * row_pos[:, None] * frequency[None, :]
    col_angle = jnp.pi * col_pos[:, None] * frequency[None, :]
    return jnp.concatenate([row_pos[:, None], col_pos[:, None], jnp.sin(row_angle), jnp.sin(col_angle), jnp.cos(row_angle), jnp.cos(col_angle)], axis=1)

def feed_forward(resid, gain, up_mat, down_mat):
    normed = low(layer_norm(resid, gain))
    hidden = low(jax.nn.gelu(low_back(matmul(normed, up_mat))))
    return low_back(matmul(hidden, down_mat))

def self_attention(normed, self_query, self_key, self_value):
    count = normed.shape[0]
    head_queries = low_back(low(matmul(normed, self_query))).reshape(count, HEADS, HEAD_DIM)
    head_keys = low_back(low(matmul(normed, self_key))).reshape(count, HEADS, HEAD_DIM)
    head_values = low_back(low(matmul(normed, self_value))).reshape(count, HEADS, HEAD_DIM)
    scores = jnp.einsum('qhd,khd->hqk', head_queries, head_keys, precision=lax.Precision.HIGHEST, preferred_element_type=jnp.float32)
    scores = low_back(scores * HEAD_DIM ** (-0.5))
    shifted = jnp.exp(scores - lax.optimization_barrier(jnp.max(scores, axis=-1, keepdims=True)))
    probs = shifted / lax.optimization_barrier(jnp.sum(shifted, axis=-1, keepdims=True))
    mixed = jnp.einsum('hqk,khd->qhd', low(probs), head_values, precision=lax.Precision.HIGHEST, preferred_element_type=jnp.float32)
    return low_back(low(mixed.reshape(count, D)))

def reference(rgb_pixels, keep_mask, latent_array, gain_input, gain_latent, w_query, w_key, w_value, w_cross_out, gain_mlp_one, w_up_one, w_down_one, gain_self, w_self_query, w_self_key, w_self_value, w_self_out, gain_mlp_two, w_up_two, w_down_two, cotangent):
    features = fourier_rows(lax.iota(jnp.int32, P_SIZE), SIDE, BANDS)
    allowed = keep_mask.astype(jnp.float32)
    width_scale = D ** (-0.5)
    members = (rgb_pixels, latent_array, gain_input, gain_latent, w_query, w_key, w_value, w_cross_out, gain_mlp_one, w_up_one, w_down_one, gain_self, w_self_query, w_self_key, w_self_value, w_self_out, gain_mlp_two, w_up_two, w_down_two)
    params = tuple((member.astype(jnp.float32) for member in members))

    def forward(pixels, latents, gain_in, gain_lat, query_mat, key_mat, value_mat, cross_out, gain_one, up_one, down_one, gain_attn, self_query, self_key, self_value, self_out, gain_two, up_two, down_two):
        latent_normed = low(layer_norm(latents, gain_lat))
        queries = low_back(low(matmul(latent_normed, query_mat)))

        def one_image(image_pixels, image_mask):
            inputs = jnp.concatenate([image_pixels.T, features], axis=1)
            normed = low(layer_norm(inputs, gain_in))
            keys = low_back(low(matmul(normed, key_mat)))
            values = low_back(low(matmul(normed, value_mat)))
            scores = low_back(matmul(queries, keys.T) * width_scale)
            shifted = jnp.exp(scores - lax.optimization_barrier(jnp.max(scores, axis=1, keepdims=True))) * image_mask[None, :]
            probs = shifted / lax.optimization_barrier(jnp.sum(shifted, axis=1, keepdims=True))
            attended = low_back(low(matmul(low(probs), values)))
            resid_one = latents + low_back(matmul(attended, cross_out))
            resid_two = resid_one + feed_forward(resid_one, gain_one, up_one, down_one)
            normed_two = low(layer_norm(resid_two, gain_attn))
            mixed = self_attention(normed_two, self_query, self_key, self_value)
            resid_three = resid_two + low_back(matmul(mixed, self_out))
            return resid_three + feed_forward(resid_three, gain_two, up_two, down_two)

        def step(carry, slices):
            return (carry, jax.checkpoint(one_image)(slices[0], slices[1]))
        _, outputs = lax.scan(step, jnp.zeros((), jnp.float32), (pixels, allowed))
        return outputs
    outputs, pullback = jax.vjp(forward, *params)
    grads = pullback(cotangent.astype(jnp.float32))
    return (outputs.astype(jnp.bfloat16), grads[0], grads[1], grads[2], grads[3], grads[4], grads[5], grads[6], grads[7], grads[8], grads[9], grads[10], grads[11], grads[12], grads[13], grads[14], grads[15], grads[16], grads[17], grads[18])
```

```python
import functools

import jax
import jax.numpy as jnp
from jax import lax
from jax.experimental import pallas as pl
from jax.experimental.pallas import tpu as pltpu
from jax.sharding import PartitionSpec as P

HEADS = 8
HEAD_DIM = 128
BANDS = 64
SIDE = 224
CHANNELS = 256
LOG2E = 1.4426950408889634

eps = 1e-05
f32 = jnp.float32
bf16 = jnp.bfloat16


def exact(left, right):
    return jnp.dot(left, right, precision=lax.Precision.HIGHEST, preferred_element_type=f32)


def mm(left, right):
    return jnp.dot(left, right, preferred_element_type=f32)


def mm_nt(left, right):
    return lax.dot_general(left, right, (((1,), (1,)), ((), ())), preferred_element_type=f32)


def mm_tn(left, right):
    return lax.dot_general(left, right, (((0,), (0,)), ((), ())), preferred_element_type=f32)


def layer_norm(rows, gain):
    average = jnp.mean(rows, axis=-1, keepdims=True)
    centred = rows - average
    spread = jnp.mean(centred * centred, axis=-1, keepdims=True)
    return centred * lax.rsqrt(spread + eps) * gain


def angles(index):
    place = index.astype(f32) * (2.0 / (SIDE - 1)) - 1.0
    steps = lax.iota(jnp.int32, BANDS).astype(f32)
    frequency = 1.0 + steps * ((SIDE / 2.0 - 1.0) / (BANDS - 1))
    angle = jnp.pi * place[:, None] * frequency[None, :]
    return place[:, None], jnp.sin(angle), jnp.cos(angle)


def pixel_tile(pixels):
    return 896 if pixels % 896 == 0 else pixels


def score_kernel(x_ref, xt_ref, at_ref, u_ref, m_ref, acc, top):
    step = pl.program_id(1)

    @pl.when(step == 0)
    def _():
        acc[...] = jnp.zeros_like(acc)
        top[...] = jnp.full_like(top, -jnp.inf)

    scores = mm(x_ref[...], at_ref[...])
    old = top[0:1, :]
    new = jnp.maximum(old, jnp.max(scores, axis=0, keepdims=True))
    weights = jnp.exp2(scores - new).astype(bf16)
    acc[...] = acc[...] * jnp.exp2(old - new) + mm(xt_ref[0], weights)
    top[...] = jnp.broadcast_to(new, top.shape)

    @pl.when(step == pl.num_programs(1) - 1)
    def _():
        u_ref[0] = acc[...]
        m_ref[0] = top[...]


def score_pass(x, xt, at):
    images, rows, pixels = xt.shape
    tile = pixel_tile(pixels)
    steps = pixels // tile
    latents = at.shape[1]
    return pl.pallas_call(
        score_kernel,
        grid=(images, steps),
        in_specs=[
            pl.BlockSpec((tile, CHANNELS), lambda i, t: (i * steps + t, 0)),
            pl.BlockSpec((1, rows, tile), lambda i, t: (i, 0, t)),
            pl.BlockSpec((CHANNELS, latents), lambda i, t: (0, 0)),
        ],
        out_specs=[
            pl.BlockSpec((1, rows, latents), lambda i, t: (i, 0, 0)),
            pl.BlockSpec((1, 8, latents), lambda i, t: (i, 0, 0)),
        ],
        out_shape=[
            jax.ShapeDtypeStruct((images, rows, latents), f32),
            jax.ShapeDtypeStruct((images, 8, latents), f32),
        ],
        scratch_shapes=[pltpu.VMEM((rows, latents), f32), pltpu.VMEM((8, latents), f32)],
        compiler_params=pltpu.CompilerParams(vmem_limit_bytes=40 * 2**20),
        cost_estimate=pl.CostEstimate(
            flops=4 * images * pixels * CHANNELS * latents,
            bytes_accessed=4 * images * pixels * CHANNELS,
            transcendentals=images * pixels * latents,
        ),
    )(x, xt, at)


def grad_kernel(x_ref, xt_ref, at_ref, bt_ref, a_ref, b_ref, stat_ref, t_ref, out_ref):
    first = (pl.program_id(0) == 0) & (pl.program_id(1) == 0)

    @pl.when(first)
    def _():
        t_ref[...] = jnp.zeros_like(t_ref)

    x = x_ref[...]
    scores = mm(x, at_ref[...])
    grad_p = mm(x, bt_ref[0])
    probs = jnp.exp2(scores - stat_ref[0, 0:1, :])
    grad_s = (probs * (grad_p - stat_ref[0, 1:2, :])).astype(bf16)
    probs = probs.astype(bf16)
    t_ref[...] += mm(xt_ref[0], grad_s)
    back = mm(grad_s, a_ref[...]) + mm(probs, b_ref[0])
    along = jnp.sum(back * x.astype(f32), axis=1, keepdims=True)
    half = back[:, CHANNELS - 128 :]
    lane = lax.broadcasted_iota(jnp.int32, half.shape, 1)
    half = jnp.where(lane == 120, along, half)
    out_ref[0] = half.T[120:128, :]


def grad_pass(x, xt, at, bt, a, b, stat):
    images, rows, pixels = xt.shape
    tile = pixel_tile(pixels)
    steps = pixels // tile
    latents = at.shape[1]
    return pl.pallas_call(
        grad_kernel,
        grid=(images, steps),
        in_specs=[
            pl.BlockSpec((tile, CHANNELS), lambda i, t: (i * steps + t, 0)),
            pl.BlockSpec((1, rows, tile), lambda i, t: (i, 0, t)),
            pl.BlockSpec((CHANNELS, latents), lambda i, t: (0, 0)),
            pl.BlockSpec((1, CHANNELS, latents), lambda i, t: (i, 0, 0)),
            pl.BlockSpec((latents, CHANNELS), lambda i, t: (0, 0)),
            pl.BlockSpec((1, latents, CHANNELS), lambda i, t: (i, 0, 0)),
            pl.BlockSpec((1, 8, latents), lambda i, t: (i, 0, 0)),
        ],
        out_specs=[
            pl.BlockSpec((rows, latents), lambda i, t: (0, 0)),
            pl.BlockSpec((1, 8, tile), lambda i, t: (i, 0, t)),
        ],
        out_shape=[
            jax.ShapeDtypeStruct((rows, latents), f32),
            jax.ShapeDtypeStruct((images, 8, pixels), f32),
        ],
        compiler_params=pltpu.CompilerParams(vmem_limit_bytes=40 * 2**20),
        cost_estimate=pl.CostEstimate(
            flops=10 * images * pixels * CHANNELS * latents,
            bytes_accessed=4 * images * pixels * CHANNELS,
            transcendentals=images * pixels * latents,
        ),
    )(x, xt, at, bt, a, b, stat)


MESH = pl.DeviceIdType.MESH
DMA = pltpu.SemaphoreType.DMA


def ring_place(count):
    me = lax.axis_index("pix")
    return jnp.where(me % 2 == 0, me // 2, count - 1 - me // 2)


def ring_device(place, count):
    place = lax.rem(place + 2 * count, count)
    return jnp.where(place < count // 2, 2 * place, 2 * (count - 1 - place) + 1)


def greet(devices):
    barrier = pltpu.get_barrier_semaphore()
    for device in devices:
        pl.semaphore_signal(barrier, inc=1, device_id=device, device_id_type=MESH)
    pl.semaphore_wait(barrier, len(devices))


def gather_kernel(count, shapes, *refs):
    number = len(shapes)
    sources, fulls = refs[:number], refs[number : 2 * number]
    local_sem, send_sem, recv_sem, hand_send, hand_recv = refs[2 * number :]
    group, me = lax.axis_index("img"), lax.axis_index("pix")
    core = lax.rem(group, 2)
    place = ring_place(count)
    sides = ((group, ring_device(place + 1, count)), (group, ring_device(place - 1, count)))
    other = (group + 1 - 2 * core, me)
    greet(sides + (other,))
    own = [
        pltpu.make_async_copy(sources[a], fulls[a].at[:, me], local_sem.at[a])
        for a in range(number)
    ]
    for copy in own:
        copy.start()
    first = [sum(shape[0] for shape in shapes[:a]) for a in range(number)]

    def spot(a, k, stage, way, source):
        wide = shapes[a][2] // 4
        columns = pl.ds(pl.multiple_of((core * 2 + way) * wide, 128), wide)
        if source:
            return sources[a].at[k, :, columns]
        origin = ring_device(place - stage if way == 0 else place + stage, count)
        return fulls[a].at[k, origin, :, columns]

    def hop(a, k, stage, way):
        return pltpu.make_async_remote_copy(
            spot(a, k, stage, way, stage == 0),
            spot(a, k, stage, way, False),
            send_sem.at[stage, way, first[a] + k],
            recv_sem.at[stage, way, first[a] + k],
            device_id=sides[way],
            device_id_type=MESH,
        )

    def hand(a, k, stage, way):
        part = spot(a, k, stage, way, False)
        return pltpu.make_async_remote_copy(
            part,
            part,
            hand_send.at[stage - 1, way, first[a] + k],
            hand_recv.at[stage - 1, way, first[a] + k],
            device_id=other,
            device_id_type=MESH,
        )

    for stage in range(count):
        for a in range(number):

            @pl.loop(0, shapes[a][0])
            def _(k):
                for way in range(2):
                    if stage > 0:
                        hop(a, k, stage - 1, way).wait_recv()
                    if stage < count - 1:
                        hop(a, k, stage, way).start()
                    if stage > 0:
                        hand(a, k, stage, way).start()

    for copy in own:
        copy.wait()
    for stage in range(count):
        for a in range(number):

            @pl.loop(0, shapes[a][0])
            def _(k):
                for way in range(2):
                    if stage < count - 1:
                        hop(a, k, stage, way).wait_send()
                    if stage > 0:
                        hand(a, k, stage, way).wait()


def ring_gather(arrays, collective_id):
    count = lax.axis_size("pix")
    shapes = [array.shape for array in arrays]
    total = sum(shape[0] for shape in shapes)
    anywhere = pl.BlockSpec(memory_space=pl.ANY)
    return pl.pallas_call(
        functools.partial(gather_kernel, count, shapes),
        out_shape=[
            jax.ShapeDtypeStruct((shape[0], count) + shape[1:], array.dtype)
            for shape, array in zip(shapes, arrays)
        ],
        in_specs=[anywhere] * len(arrays),
        out_specs=[anywhere] * len(arrays),
        scratch_shapes=[DMA((len(arrays),))] + [DMA((count - 1, 2, total))] * 4,
        compiler_params=pltpu.CompilerParams(collective_id=collective_id, has_side_effects=True),
    )(*arrays)


def reduce_kernel(
    count,
    teams,
    xs_ref,
    gs_ref,
    out_ref,
    xv,
    gv,
    first,
    held,
    across,
    done,
    load_sem,
    pair_send,
    pair_recv,
    send_sem,
    recv_sem,
    cross_send,
    cross_recv,
    out_sem,
    hand_send,
    hand_recv,
):
    number, rows, width = gs_ref.shape
    kinds = xs_ref.shape[0]
    depth = xs_ref.shape[3]
    half, wide = width // 2, width // 4
    group, me = lax.axis_index("img"), lax.axis_index("pix")
    core, team = lax.rem(group, 2), group // 2
    place = ring_place(count)
    sides = ((group, ring_device(place + 1, count)), (group, ring_device(place - 1, count)))
    other = (group + 1 - 2 * core, me)
    partners = [(lax.rem(team + d, teams) * 2 + core, me) for d in range(1, teams)]
    greet(sides + (other,) + tuple(partners))

    mine = pl.ds(pl.multiple_of(core * rows, 16), rows)

    def load_x(j):
        return pltpu.make_async_copy(xs_ref.at[j], xv.at[j, :, mine], load_sem.at[0, j])

    def load_g(k):
        part = gs_ref.at[k, :, pl.ds(pl.multiple_of(core * half, 128), half)]
        return pltpu.make_async_copy(part, gv.at[k, mine], load_sem.at[1, k])

    def pair_x(j):
        return pltpu.make_async_remote_copy(
            xs_ref.at[j],
            xv.at[j, :, mine],
            pair_send.at[0, j],
            pair_recv.at[0, j],
            device_id=other,
            device_id_type=MESH,
        )

    def pair_g(k):
        part = gs_ref.at[k, :, pl.ds(pl.multiple_of((1 - core) * half, 128), half)]
        return pltpu.make_async_remote_copy(
            part,
            gv.at[k, mine],
            pair_send.at[1, k],
            pair_recv.at[1, k],
            device_id=other,
            device_id_type=MESH,
        )

    for j in range(number):
        if j < kinds:
            load_x(j).start()
            pair_x(j).start()
        load_g(j).start()
        pair_g(j).start()

    def part(k, owner, way):
        j = jnp.maximum(k - (number - kinds), 0)
        return mm_tn(xv[j, owner], gv[k, :, way * wide : (way + 1) * wide])

    def hop(k, stage, way):
        source = first.at[k, way] if stage == 0 else held.at[k, way, stage - 1]
        return pltpu.make_async_remote_copy(
            source,
            held.at[k, way, stage],
            send_sem.at[stage, way, k],
            recv_sem.at[stage, way, k],
            device_id=sides[way],
            device_id_type=MESH,
        )

    def cross(k, way, d):
        return pltpu.make_async_remote_copy(
            across.at[team, k, way],
            across.at[team, k, way],
            cross_send.at[d, way, k],
            cross_recv.at[d, way, k],
            device_id=partners[d],
            device_id_type=MESH,
        )

    for stage in range(count):

        @pl.loop(0, number)
        def _(k):
            if stage == 0:
                j = jnp.maximum(k - (number - kinds), 0)

                @pl.when((k == 0) | (k > number - kinds))
                def _():
                    load_x(j).wait()
                    pair_x(j).wait_recv()

                load_g(k).wait()
                pair_g(k).wait_recv()
            for way in range(2):
                step = stage + 1
                owner = ring_device(place - step if way == 0 else place + step, count)
                total = part(k, owner, way)
                if stage == 0:
                    first[k, way] = total.astype(bf16)
                    hop(k, 0, way).start()
                else:
                    hop(k, stage - 1, way).wait_recv()
                    total = total + held[k, way, stage - 1].astype(f32)
                    if stage < count - 1:
                        held[k, way, stage - 1] = total.astype(bf16)
                        hop(k, stage, way).start()
                    else:
                        across[team, k, way] = total.astype(bf16)
                        for d in range(teams - 1):
                            cross(k, way, d).start()

    def finish(k):
        columns = pl.ds(pl.multiple_of(core * half, 128), half)
        return pltpu.make_async_copy(done.at[k], out_ref.at[k, :, columns], out_sem.at[k])

    def hand(k):
        columns = pl.ds(pl.multiple_of(core * half, 128), half)
        return pltpu.make_async_remote_copy(
            done.at[k],
            out_ref.at[k, :, columns],
            hand_send.at[k],
            hand_recv.at[k],
            device_id=other,
            device_id_type=MESH,
        )

    @pl.loop(0, number)
    def _(k):
        for way in range(2):
            for d in range(teams - 1):
                cross(k, way, d).wait_recv()
            total = across[0, k, way].astype(f32)
            for t in range(1, teams):
                total = total + across[t, k, way].astype(f32)
            done[k, :, way * wide : (way + 1) * wide] = total
        finish(k).start()
        hand(k).start()

    @pl.loop(0, number)
    def _(k):
        finish(k).wait()
        hand(k).wait()
        pair_g(k).wait_send()
        for way in range(2):
            for stage in range(count - 1):
                hop(k, stage, way).wait_send()
            for d in range(teams - 1):
                cross(k, way, d).wait_send()

    @pl.loop(0, kinds)
    def _(j):
        pair_x(j).wait_send()


def ring_reduce(xs, gs, collective_id):
    count = lax.axis_size("pix")
    teams = lax.axis_size("img") // 2
    kinds, rows, columns = xs.shape
    number, _, width = gs.shape
    depth = columns // count
    xs = jnp.swapaxes(xs.reshape(kinds, rows, count, depth), 1, 2)
    anywhere = pl.BlockSpec(memory_space=pl.ANY)
    chunk = (depth, width // 4)
    return pl.pallas_call(
        functools.partial(reduce_kernel, count, teams),
        out_shape=jax.ShapeDtypeStruct((number, depth, width), f32),
        in_specs=[anywhere] * 2,
        out_specs=anywhere,
        scratch_shapes=[
            pltpu.VMEM((kinds, count, 2 * rows, depth), bf16),
            pltpu.VMEM((number, 2 * rows, width // 2), bf16),
            pltpu.VMEM((number, 2) + chunk, bf16),
            pltpu.VMEM((number, 2, count - 1) + chunk, bf16),
            pltpu.VMEM((teams, number, 2) + chunk, bf16),
            pltpu.VMEM((number, depth, width // 2), f32),
            DMA((2, number)),
            DMA((2, number)),
            DMA((2, number)),
            DMA((count - 1, 2, number)),
            DMA((count - 1, 2, number)),
            DMA((teams - 1, 2, number)),
            DMA((teams - 1, 2, number)),
            DMA((number,)),
            DMA((number,)),
            DMA((number,)),
        ],
        compiler_params=pltpu.CompilerParams(
            collective_id=collective_id, has_side_effects=True, vmem_limit_bytes=48 * 2**20
        ),
    )(xs, gs)


def norm_back(resid, gain, grad):
    _, back = jax.vjp(layer_norm, resid, gain)
    return back(grad)


def ffn(resid, gain, up_t, down):
    normed = layer_norm(resid, gain).astype(bf16)
    pre = mm_nt(normed, up_t)
    hidden = jax.nn.gelu(pre).astype(bf16)
    return resid + mm(hidden, down), (normed, pre, hidden)


def ffn_back(resid, gain, up_t, down, saved, grad):
    normed, pre, hidden = saved
    branch = grad.astype(bf16)
    _, gelu_back = jax.vjp(jax.nn.gelu, pre)
    grad_pre = gelu_back(mm_nt(branch, down))[0].astype(bf16)
    grad_input, grad_gain = norm_back(resid, gain, mm(grad_pre, up_t))
    return grad + grad_input, grad_gain, grad_pre, branch


def local(
    rgb_pixels,
    keep_mask,
    latent_array,
    gain_input,
    gain_latent,
    w_query,
    w_key,
    w_value,
    w_cross_out,
    gain_mlp_one,
    w_up_one,
    w_down_one,
    gain_self,
    w_self_query,
    w_self_key,
    w_self_value,
    w_self_out,
    gain_mlp_two,
    w_up_two,
    w_down_two,
    cotangent,
):
    images, _, pixels = rgb_pixels.shape
    rows_here, width = latent_array.shape
    count = lax.axis_size("pix")
    me = lax.axis_index("pix")
    latents = rows_here * count
    sharers = count // images
    rows_own = latents // sharers
    slot = me % sharers
    depth = w_query.shape[0]
    channels = gain_input.shape[0]
    width_scale = width ** (-0.5)
    head_scale = HEAD_DIM ** (-0.5)
    groups = [[i * sharers + j for j in range(sharers)] for i in range(images)]

    side = -(-channels // 512) * 512
    key_t = jnp.pad(w_key.T, ((0, 0), (0, side - channels)))
    latent_full, query_mat, key_full = ring_gather([latent_array[None], w_query[None], key_t[None]], 0)
    latent_full = latent_full.reshape(latents, width)
    query_mat = query_mat.reshape(width, width)
    key_full = key_full.reshape(width, side)
    key_mat = key_full[:, :channels].T
    value_out = lax.psum(mm(w_value, w_cross_out).astype(bf16), "pix")
    shards = jnp.stack(
        [
            w_up_one.T,
            w_down_one,
            w_self_query,
            w_self_key,
            w_self_value,
            w_self_out,
            w_up_two.T,
            w_down_two,
        ]
    )
    (whole,) = ring_gather([shards], 1)
    up_one, down_one, self_query, self_key, self_value, self_out, up_two, down_two = [
        whole[k].reshape(width, width) for k in range(8)
    ]

    lines = pixels // SIDE
    u, sin_u, cos_u = angles(me * lines + lax.iota(jnp.int32, lines))
    w, sin_w, cos_w = angles(lax.iota(jnp.int32, SIDE))

    def zeros(rows, columns):
        return jnp.zeros((rows, columns), f32)

    pad = CHANNELS - 4 - SIDE - lines
    table = jnp.concatenate(
        [
            jnp.concatenate(
                [zeros(SIDE, 4), w, zeros(SIDE, BANDS), sin_w, zeros(SIDE, BANDS), cos_w], axis=1
            ),
            jnp.concatenate(
                [zeros(lines, 3), u, zeros(lines, 1), sin_u, zeros(lines, BANDS), cos_u, zeros(lines, BANDS)],
                axis=1,
            ),
            zeros(pad, channels),
            jnp.eye(3, channels, dtype=f32),
            jnp.ones((1, channels), f32),
        ],
        axis=0,
    )
    row_sum = u[:, 0] + jnp.sum(sin_u + cos_u, axis=1)
    col_sum = w[:, 0] + jnp.sum(sin_w + cos_w, axis=1)
    row_square = u[:, 0] ** 2 + jnp.sum(sin_u**2 + cos_u**2, axis=1)
    col_square = w[:, 0] ** 2 + jnp.sum(sin_w**2 + cos_w**2, axis=1)
    feature_sum = (row_sum[:, None] + col_sum[None, :]).reshape(1, pixels)
    feature_square = (row_square[:, None] + col_square[None, :]).reshape(1, pixels)
    colours = rgb_pixels.astype(f32)
    average = (jnp.sum(colours, axis=1) + feature_sum) / channels
    spread = (jnp.sum(colours**2, axis=1) + feature_square) / channels - average**2
    scale = lax.rsqrt(spread + eps)
    keep = keep_mask.astype(f32)

    position = lax.iota(jnp.int32, pixels)
    column, line = position % SIDE, position // SIDE + SIDE
    channel = lax.iota(jnp.int32, CHANNELS - 4)
    hot = (channel[:, None] == column[None, :]) | (channel[:, None] == line[None, :])
    small = jnp.concatenate(
        [colours * scale[:, None, :], (-average * scale)[:, None, :]], axis=1
    )
    xt = jnp.concatenate(
        [
            jnp.where(hot[None], (scale * keep)[:, None, :], 0.0).astype(bf16),
            (small * keep[:, None, :]).astype(bf16),
            keep[:, None, :].astype(bf16),
            jnp.zeros((images, 15, pixels), bf16),
        ],
        axis=1,
    )
    x = jnp.concatenate(
        [
            jnp.where(hot.T[None], scale[:, :, None], 0.0).astype(bf16),
            jnp.swapaxes(small, 1, 2).astype(bf16),
        ],
        axis=2,
    ).reshape(images * pixels, CHANNELS)

    latent_float = latent_full.astype(f32)
    latent_normed = layer_norm(latent_float, gain_latent).astype(bf16)
    queries = mm(latent_normed, query_mat).astype(bf16)
    gained = table * gain_input[None, :]
    score_mat = mm_nt(queries, key_mat) * width_scale
    score_x = exact(score_mat, gained.T)
    at = (score_x.T * LOG2E).astype(bf16)
    a_low = score_x.astype(bf16)

    weighted, tops = score_pass(x, xt, at)
    tops = tops[:, 0, :]
    totals = weighted[:, CHANNELS, :]
    raw = jnp.einsum(
        "kc,ikq->icq",
        table,
        weighted[:, :CHANNELS, :],
        precision=lax.Precision.HIGHEST,
        preferred_element_type=f32,
    )

    def by_owner(value):
        lead = value.shape[1]
        split = value.reshape(images, lead, sharers, rows_own)
        return jnp.swapaxes(split, 1, 2).reshape(count, lead, rows_own)

    raw_parts = lax.all_to_all(
        by_owner(raw).astype(bf16), "pix", split_axis=0, concat_axis=0, tiled=True
    )
    stat_parts = lax.all_to_all(
        by_owner(jnp.stack([tops, totals], axis=1)), "pix", split_axis=0, concat_axis=0, tiled=True
    )
    top = jnp.max(stat_parts[:, 0, :], axis=0)
    share = jnp.exp2(stat_parts[:, 0, :] - top[None, :])
    total = jnp.sum(share * stat_parts[:, 1, :], axis=0)
    share = share / total[None, :]
    raw_t = jnp.sum(raw_parts.astype(f32) * share[:, None, :], axis=0)
    norm_log = top + jnp.log2(total)

    mean_t = raw_t * gain_input[:, None]
    mean_low = mean_t.astype(bf16)
    own = lax.dynamic_slice_in_dim(latent_float, slot * rows_own, rows_own, 0)
    resid_one = own + mm_tn(mean_low, value_out)
    resid_two, saved_one = ffn(resid_one, gain_mlp_one, up_one, down_one)
    normed_two = layer_norm(resid_two, gain_self).astype(bf16)
    heads_q = mm(normed_two, self_query).astype(bf16).reshape(rows_own, HEADS, HEAD_DIM)
    own_kv = jnp.stack([mm(normed_two, self_key), mm(normed_two, self_value)]).astype(bf16)
    all_kv = lax.all_gather(own_kv, "pix", axis=1, tiled=True, axis_index_groups=groups)
    heads_k, heads_v = [all_kv[k].reshape(latents, HEADS, HEAD_DIM) for k in range(2)]
    scores = jnp.einsum("rhd,khd->hrk", heads_q, heads_k, preferred_element_type=f32) * head_scale
    shifted = jnp.exp(scores - jnp.max(scores, axis=2, keepdims=True))
    probs = shifted / jnp.sum(shifted, axis=2, keepdims=True)
    probs_low = probs.astype(bf16)
    mixed = (
        jnp.einsum("hrk,khd->rhd", probs_low, heads_v, preferred_element_type=f32)
        .reshape(rows_own, width)
        .astype(bf16)
    )
    resid_three = resid_two + mm(mixed, self_out)
    final, saved_two = ffn(resid_three, gain_mlp_two, up_two, down_two)

    per = rows_own // rows_here
    pieces = final.astype(bf16).reshape(per, rows_here, width)
    target = lax.iota(jnp.int32, count)
    mine = (target // per == slot)[:, None, None]
    outgoing = jnp.where(mine, jnp.tile(pieces, (count // per, 1, 1)), jnp.zeros((), bf16))
    incoming = lax.all_to_all(outgoing, "pix", split_axis=0, concat_axis=0, tiled=True)
    incoming = incoming.reshape(images, sharers, rows_here, width)
    latent_out = lax.dynamic_index_in_dim(incoming, me // per, axis=1, keepdims=False)

    outgoing = jnp.where(
        (lax.iota(jnp.int32, sharers) == me // per)[None, :, None, None],
        cotangent[:, None],
        jnp.zeros((), bf16),
    ).reshape(count, rows_here, width)
    incoming = lax.all_to_all(outgoing, "pix", split_axis=0, concat_axis=0, tiled=True)
    grad_final = lax.dynamic_slice_in_dim(incoming, slot * per, per, 0).reshape(rows_own, width)
    grad_final = grad_final.astype(f32)

    grad_three, grad_gain_two, grad_pre_two, branch_two = ffn_back(
        resid_three, gain_mlp_two, up_two, down_two, saved_two, grad_final
    )
    branch = grad_three.astype(bf16)
    grad_mixed = mm_nt(branch, self_out).astype(bf16).reshape(rows_own, HEADS, HEAD_DIM)
    grad_probs = jnp.einsum("rhd,khd->hrk", grad_mixed, heads_v, preferred_element_type=f32)
    grad_v_all = jnp.einsum("hrk,rhd->khd", probs_low, grad_mixed, preferred_element_type=f32)
    delta = jnp.sum(probs * grad_probs, axis=2, keepdims=True)
    grad_scores = (probs * (grad_probs - delta)).astype(bf16)
    grad_q = (
        (jnp.einsum("hrk,khd->rhd", grad_scores, heads_k, preferred_element_type=f32) * head_scale)
        .astype(bf16)
        .reshape(rows_own, width)
    )
    grad_k_all = (
        jnp.einsum("hrk,rhd->khd", grad_scores, heads_q, preferred_element_type=f32) * head_scale
    )
    grad_kv = lax.psum_scatter(
        jnp.stack([grad_k_all, grad_v_all]).reshape(2, latents, width).astype(bf16),
        "pix",
        scatter_dimension=1,
        tiled=True,
        axis_index_groups=groups,
    )
    grad_k, grad_v = grad_kv[0], grad_kv[1]
    grad_normed_two = (
        mm_nt(grad_q, self_query) + mm_nt(grad_k, self_key) + mm_nt(grad_v, self_value)
    )
    grad_in_two, grad_gain_attn = norm_back(resid_two, gain_self, grad_normed_two)
    grad_two = grad_three + grad_in_two
    grad_one, grad_gain_one, grad_pre_one, branch_one = ffn_back(
        resid_one, gain_mlp_one, up_one, down_one, saved_one, grad_two
    )
    grad_cross = grad_one.astype(bf16)
    back_mat = mm_nt(grad_cross, value_out)
    delta_one = jnp.sum(back_mat * mean_t.T, axis=1)
    gain_part = jnp.sum(back_mat * raw_t.T, axis=0)

    back_all = lax.all_gather(back_mat.astype(bf16), "pix", axis=0, tiled=True)
    stats = lax.all_gather(jnp.stack([norm_log, delta_one]), "pix", axis=0)
    stats = jnp.swapaxes(stats, 0, 1).reshape(2, images, latents)
    stats = jnp.pad(jnp.swapaxes(stats, 0, 1), ((0, 0), (0, 6), (0, 0)))
    back_x = exact(back_all.astype(f32), gained.T).astype(bf16).reshape(images, latents, CHANNELS)
    grad_t, pixel_out = grad_pass(x, xt, at, jnp.swapaxes(back_x, 1, 2), a_low, back_x, stats)
    moved = (pixel_out[:, 4:7] - pixel_out[:, 7:8] / channels) - (
        (colours - average[:, None, :]) * scale[:, None, :]
    ) * (pixel_out[:, 0:1] / channels)
    grad_pixels = moved * (scale * keep)[:, None, :]

    grad_raw = exact(grad_t[:CHANNELS].T, table)
    gain_part = gain_part + jnp.sum(score_mat * grad_raw, axis=0)
    grad_raw, gain_in, gain_one, gain_attn, gain_two = lax.psum(
        (grad_raw, gain_part, grad_gain_one, grad_gain_attn, grad_gain_two), ("img", "pix")
    )
    grad_x = (grad_raw * (gain_input * width_scale)[None, :]).astype(bf16)
    query_grad = mm(grad_x, key_mat).astype(bf16)
    latent_cols = lax.dynamic_slice_in_dim(latent_normed, me * depth, depth, 1)
    grad_w_query = mm_tn(latent_cols, query_grad)
    grad_latent_full, grad_gain_latent = norm_back(
        latent_float, gain_latent, mm_nt(query_grad, query_mat)
    )
    grad_latent_own = lax.dynamic_slice_in_dim(grad_latent_full, me * rows_here, rows_here, 0)
    key_cols = w_key.shape[1]
    grad_w_key = mm_tn(grad_x, lax.dynamic_slice_in_dim(queries, me * key_cols, key_cols, 1))

    share_rows = -(-channels // count)
    picks = jnp.eye(rows_own, latents, dtype=bf16)
    picks = jnp.roll(picks, slot * rows_own, axis=1).reshape(rows_own, count, rows_here)
    mean_rows = jnp.pad(mean_low.T, ((0, 0), (0, share_rows * count - channels)))
    mean_rows = mean_rows.reshape(rows_own, count, share_rows)
    last = jnp.concatenate(
        [picks, mean_rows, jnp.zeros((rows_own, count, depth - rows_here - share_rows), bf16)],
        axis=2,
    ).reshape(rows_own, width)
    normed_one, _, hidden_one = saved_one
    normed_last, _, hidden_last = saved_two
    xs = jnp.stack(
        [normed_two, mixed, grad_pre_one, hidden_one, grad_pre_two, hidden_last, last]
    )
    gs = jnp.stack(
        [
            grad_q,
            grad_k,
            grad_v,
            branch,
            normed_one,
            branch_one,
            normed_last,
            branch_two,
            grad_cross,
        ]
    )
    summed = ring_reduce(xs, gs, 2)
    g_sq, g_sk, g_sv, g_so, g_up_one, g_down_one, g_up_two, g_down_two, rest = [
        summed[k] for k in range(9)
    ]
    cross_sum = lax.all_gather(
        rest[rows_here : rows_here + share_rows].astype(bf16), "pix", axis=0, tiled=True
    )[:channels]
    grad_w_value = mm_nt(cross_sum, w_cross_out)
    grad_w_cross_out = mm_tn(w_value, cross_sum)
    grad_latent_array = rest[:rows_here] + grad_latent_own
    return (
        latent_out,
        grad_pixels,
        grad_latent_array,
        gain_in,
        grad_gain_latent,
        grad_w_query,
        grad_w_key,
        grad_w_value,
        grad_w_cross_out,
        gain_one,
        g_up_one.T,
        g_down_one,
        gain_attn,
        g_sq,
        g_sk,
        g_sv,
        g_so,
        gain_two,
        g_up_two.T,
        g_down_two,
    )


def solution(mesh):
    rows, columns, copied = P("pix", None), P(None, "pix"), P()
    return jax.shard_map(
        local,
        mesh=mesh,
        in_specs=(
            P("img", None, "pix"),
            P("img", "pix"),
            rows,
            copied,
            copied,
            rows,
            columns,
            columns,
            rows,
            copied,
            columns,
            rows,
            copied,
            rows,
            rows,
            rows,
            rows,
            copied,
            columns,
            rows,
            P("img", "pix", None),
        ),
        out_specs=(
            P("img", "pix", None),
            P("img", None, "pix"),
            rows,
            copied,
            copied,
            rows,
            columns,
            columns,
            rows,
            copied,
            columns,
            rows,
            copied,
            rows,
            rows,
            rows,
            rows,
            copied,
            columns,
            rows,
        ),
        check_vma=False,
    )
```

```python
import functools

import jax
import jax.numpy as jnp
from jax import lax
from jax.experimental import pallas as pl
from jax.experimental.pallas import tpu as pltpu
from jax.sharding import PartitionSpec as P

HEADS = 8
HEAD_DIM = 128
BANDS = 64
SIDE = 224
CHANNELS = 256
LOG2E = 1.4426950408889634

eps = 1e-05
f32 = jnp.float32
bf16 = jnp.bfloat16


def exact(left, right):
    return jnp.dot(left, right, precision=lax.Precision.HIGHEST, preferred_element_type=f32)


def mm(left, right):
    return jnp.dot(left, right, preferred_element_type=f32)


def mm_nt(left, right):
    return lax.dot_general(left, right, (((1,), (1,)), ((), ())), preferred_element_type=f32)


def mm_tn(left, right):
    return lax.dot_general(left, right, (((0,), (0,)), ((), ())), preferred_element_type=f32)


def layer_norm(rows, gain):
    average = jnp.mean(rows, axis=-1, keepdims=True)
    centred = rows - average
    spread = jnp.mean(centred * centred, axis=-1, keepdims=True)
    return centred * lax.rsqrt(spread + eps) * gain


def angles(index):
    place = index.astype(f32) * (2.0 / (SIDE - 1)) - 1.0
    steps = lax.iota(jnp.int32, BANDS).astype(f32)
    frequency = 1.0 + steps * ((SIDE / 2.0 - 1.0) / (BANDS - 1))
    angle = jnp.pi * place[:, None] * frequency[None, :]
    return place[:, None], jnp.sin(angle), jnp.cos(angle)


def pixel_tile(pixels):
    return 896 if pixels % 896 == 0 else pixels


def score_kernel(x_ref, xt_ref, at_ref, u_ref, m_ref, acc, top):
    step = pl.program_id(1)

    @pl.when(step == 0)
    def _():
        acc[...] = jnp.zeros_like(acc)
        top[...] = jnp.full_like(top, -jnp.inf)

    scores = mm(x_ref[...], at_ref[...])
    old = top[0:1, :]
    new = jnp.maximum(old, jnp.max(scores, axis=0, keepdims=True))
    weights = jnp.exp2(scores - new).astype(bf16)
    acc[...] = acc[...] * jnp.exp2(old - new) + mm(xt_ref[0], weights)
    top[...] = jnp.broadcast_to(new, top.shape)

    @pl.when(step == pl.num_programs(1) - 1)
    def _():
        u_ref[0] = acc[...]
        m_ref[0] = top[...]


def score_pass(x, xt, at):
    images, rows, pixels = xt.shape
    tile = pixel_tile(pixels)
    steps = pixels // tile
    latents = at.shape[1]
    return pl.pallas_call(
        score_kernel,
        grid=(images, steps),
        in_specs=[
            pl.BlockSpec((tile, CHANNELS), lambda i, t: (i * steps + t, 0)),
            pl.BlockSpec((1, rows, tile), lambda i, t: (i, 0, t)),
            pl.BlockSpec((CHANNELS, latents), lambda i, t: (0, 0)),
        ],
        out_specs=[
            pl.BlockSpec((1, rows, latents), lambda i, t: (i, 0, 0)),
            pl.BlockSpec((1, 8, latents), lambda i, t: (i, 0, 0)),
        ],
        out_shape=[
            jax.ShapeDtypeStruct((images, rows, latents), f32),
            jax.ShapeDtypeStruct((images, 8, latents), f32),
        ],
        scratch_shapes=[pltpu.VMEM((rows, latents), f32), pltpu.VMEM((8, latents), f32)],
        compiler_params=pltpu.CompilerParams(vmem_limit_bytes=40 * 2**20),
        cost_estimate=pl.CostEstimate(
            flops=4 * images * pixels * CHANNELS * latents,
            bytes_accessed=4 * images * pixels * CHANNELS,
            transcendentals=images * pixels * latents,
        ),
    )(x, xt, at)


def grad_kernel(x_ref, xt_ref, at_ref, bt_ref, a_ref, b_ref, stat_ref, t_ref, out_ref):
    first = (pl.program_id(0) == 0) & (pl.program_id(1) == 0)

    @pl.when(first)
    def _():
        t_ref[...] = jnp.zeros_like(t_ref)

    x = x_ref[...]
    scores = mm(x, at_ref[...])
    grad_p = mm(x, bt_ref[0])
    probs = jnp.exp2(scores - stat_ref[0, 0:1, :])
    grad_s = (probs * (grad_p - stat_ref[0, 1:2, :])).astype(bf16)
    probs = probs.astype(bf16)
    t_ref[...] += mm(xt_ref[0], grad_s)
    back = mm(grad_s, a_ref[...]) + mm(probs, b_ref[0])
    along = jnp.sum(back * x.astype(f32), axis=1, keepdims=True)
    half = back[:, CHANNELS - 128 :]
    lane = lax.broadcasted_iota(jnp.int32, half.shape, 1)
    half = jnp.where(lane == 120, along, half)
    out_ref[0] = half.T[120:128, :]


def grad_pass(x, xt, at, bt, a, b, stat):
    images, rows, pixels = xt.shape
    tile = pixel_tile(pixels)
    steps = pixels // tile
    latents = at.shape[1]
    return pl.pallas_call(
        grad_kernel,
        grid=(images, steps),
        in_specs=[
            pl.BlockSpec((tile, CHANNELS), lambda i, t: (i * steps + t, 0)),
            pl.BlockSpec((1, rows, tile), lambda i, t: (i, 0, t)),
            pl.BlockSpec((CHANNELS, latents), lambda i, t: (0, 0)),
            pl.BlockSpec((1, CHANNELS, latents), lambda i, t: (i, 0, 0)),
            pl.BlockSpec((latents, CHANNELS), lambda i, t: (0, 0)),
            pl.BlockSpec((1, latents, CHANNELS), lambda i, t: (i, 0, 0)),
            pl.BlockSpec((1, 8, latents), lambda i, t: (i, 0, 0)),
        ],
        out_specs=[
            pl.BlockSpec((rows, latents), lambda i, t: (0, 0)),
            pl.BlockSpec((1, 8, tile), lambda i, t: (i, 0, t)),
        ],
        out_shape=[
            jax.ShapeDtypeStruct((rows, latents), f32),
            jax.ShapeDtypeStruct((images, 8, pixels), f32),
        ],
        compiler_params=pltpu.CompilerParams(vmem_limit_bytes=40 * 2**20),
        cost_estimate=pl.CostEstimate(
            flops=10 * images * pixels * CHANNELS * latents,
            bytes_accessed=4 * images * pixels * CHANNELS,
            transcendentals=images * pixels * latents,
        ),
    )(x, xt, at, bt, a, b, stat)


MESH = pl.DeviceIdType.MESH
DMA = pltpu.SemaphoreType.DMA


def ring_place(count):
    me = lax.axis_index("pix")
    return jnp.where(me % 2 == 0, me // 2, count - 1 - me // 2)


def ring_device(place, count):
    place = lax.rem(place + 2 * count, count)
    return jnp.where(place < count // 2, 2 * place, 2 * (count - 1 - place) + 1)


def greet(devices):
    barrier = pltpu.get_barrier_semaphore()
    for device in devices:
        pl.semaphore_signal(barrier, inc=1, device_id=device, device_id_type=MESH)
    pl.semaphore_wait(barrier, len(devices))


def gather_kernel(count, shapes, *refs):
    number = len(shapes)
    sources, fulls = refs[:number], refs[number : 2 * number]
    local_sem, send_sem, recv_sem, hand_send, hand_recv = refs[2 * number :]
    group, me = lax.axis_index("img"), lax.axis_index("pix")
    core = lax.rem(group, 2)
    place = ring_place(count)
    sides = ((group, ring_device(place + 1, count)), (group, ring_device(place - 1, count)))
    other = (group + 1 - 2 * core, me)
    greet(sides + (other,))
    own = [
        pltpu.make_async_copy(sources[a], fulls[a].at[:, me], local_sem.at[a])
        for a in range(number)
    ]
    for copy in own:
        copy.start()
    first = [sum(shape[0] for shape in shapes[:a]) for a in range(number)]

    def spot(a, k, stage, way, source):
        wide = shapes[a][2] // 4
        columns = pl.ds(pl.multiple_of((core * 2 + way) * wide, 128), wide)
        if source:
            return sources[a].at[k, :, columns]
        origin = ring_device(place - stage if way == 0 else place + stage, count)
        return fulls[a].at[k, origin, :, columns]

    def hop(a, k, stage, way):
        return pltpu.make_async_remote_copy(
            spot(a, k, stage, way, stage == 0),
            spot(a, k, stage, way, False),
            send_sem.at[stage, way, first[a] + k],
            recv_sem.at[stage, way, first[a] + k],
            device_id=sides[way],
            device_id_type=MESH,
        )

    def hand(a, k, stage, way):
        part = spot(a, k, stage, way, False)
        return pltpu.make_async_remote_copy(
            part,
            part,
            hand_send.at[stage - 1, way, first[a] + k],
            hand_recv.at[stage - 1, way, first[a] + k],
            device_id=other,
            device_id_type=MESH,
        )

    for stage in range(count):
        for a in range(number):

            @pl.loop(0, shapes[a][0])
            def _(k):
                for way in range(2):
                    if stage > 0:
                        hop(a, k, stage - 1, way).wait_recv()
                    if stage < count - 1:
                        hop(a, k, stage, way).start()
                    if stage > 0:
                        hand(a, k, stage, way).start()

    for copy in own:
        copy.wait()
    for stage in range(count):
        for a in range(number):

            @pl.loop(0, shapes[a][0])
            def _(k):
                for way in range(2):
                    if stage < count - 1:
                        hop(a, k, stage, way).wait_send()
                    if stage > 0:
                        hand(a, k, stage, way).wait()


def ring_gather(arrays, collective_id):
    count = lax.axis_size("pix")
    shapes = [array.shape for array in arrays]
    total = sum(shape[0] for shape in shapes)
    anywhere = pl.BlockSpec(memory_space=pl.ANY)
    return pl.pallas_call(
        functools.partial(gather_kernel, count, shapes),
        out_shape=[
            jax.ShapeDtypeStruct((shape[0], count) + shape[1:], array.dtype)
            for shape, array in zip(shapes, arrays)
        ],
        in_specs=[anywhere] * len(arrays),
        out_specs=[anywhere] * len(arrays),
        scratch_shapes=[DMA((len(arrays),))] + [DMA((count - 1, 2, total))] * 4,
        compiler_params=pltpu.CompilerParams(collective_id=collective_id, has_side_effects=True),
    )(*arrays)


def reduce_kernel(
    count,
    teams,
    xs_ref,
    gs_ref,
    out_ref,
    xv,
    gv,
    first,
    held,
    across,
    done,
    load_sem,
    pair_send,
    pair_recv,
    send_sem,
    recv_sem,
    cross_send,
    cross_recv,
    out_sem,
    hand_send,
    hand_recv,
):
    number, rows, width = gs_ref.shape
    kinds = xs_ref.shape[0]
    depth = xs_ref.shape[3]
    half, wide = width // 2, width // 4
    group, me = lax.axis_index("img"), lax.axis_index("pix")
    core, team = lax.rem(group, 2), group // 2
    place = ring_place(count)
    sides = ((group, ring_device(place + 1, count)), (group, ring_device(place - 1, count)))
    other = (group + 1 - 2 * core, me)
    partners = [(lax.rem(team + d, teams) * 2 + core, me) for d in range(1, teams)]
    greet(sides + (other,) + tuple(partners))

    mine = pl.ds(pl.multiple_of(core * rows, 16), rows)

    def load_x(j):
        return pltpu.make_async_copy(xs_ref.at[j], xv.at[j, :, mine], load_sem.at[0, j])

    def load_g(k):
        part = gs_ref.at[k, :, pl.ds(pl.multiple_of(core * half, 128), half)]
        return pltpu.make_async_copy(part, gv.at[k, mine], load_sem.at[1, k])

    def pair_x(j):
        return pltpu.make_async_remote_copy(
            xs_ref.at[j],
            xv.at[j, :, mine],
            pair_send.at[0, j],
            pair_recv.at[0, j],
            device_id=other,
            device_id_type=MESH,
        )

    def pair_g(k):
        part = gs_ref.at[k, :, pl.ds(pl.multiple_of((1 - core) * half, 128), half)]
        return pltpu.make_async_remote_copy(
            part,
            gv.at[k, mine],
            pair_send.at[1, k],
            pair_recv.at[1, k],
            device_id=other,
            device_id_type=MESH,
        )

    for j in range(number):
        if j < kinds:
            load_x(j).start()
            pair_x(j).start()
        load_g(j).start()
        pair_g(j).start()

    def part(k, owner, way):
        j = jnp.maximum(k - (number - kinds), 0)
        return mm_tn(xv[j, owner], gv[k, :, way * wide : (way + 1) * wide])

    def hop(k, stage, way):
        source = first.at[k, way] if stage == 0 else held.at[k, way, stage - 1]
        return pltpu.make_async_remote_copy(
            source,
            held.at[k, way, stage],
            send_sem.at[stage, way, k],
            recv_sem.at[stage, way, k],
            device_id=sides[way],
            device_id_type=MESH,
        )

    def cross(k, way, d):
        return pltpu.make_async_remote_copy(
            across.at[team, k, way],
            across.at[team, k, way],
            cross_send.at[d, way, k],
            cross_recv.at[d, way, k],
            device_id=partners[d],
            device_id_type=MESH,
        )

    for stage in range(count):

        @pl.loop(0, number)
        def _(k):
            if stage == 0:
                j = jnp.maximum(k - (number - kinds), 0)

                @pl.when((k == 0) | (k > number - kinds))
                def _():
                    load_x(j).wait()
                    pair_x(j).wait_recv()

                load_g(k).wait()
                pair_g(k).wait_recv()
            for way in range(2):
                step = stage + 1
                owner = ring_device(place - step if way == 0 else place + step, count)
                total = part(k, owner, way)
                if stage == 0:
                    first[k, way] = total.astype(bf16)
                    hop(k, 0, way).start()
                else:
                    hop(k, stage - 1, way).wait_recv()
                    total = total + held[k, way, stage - 1].astype(f32)
                    if stage < count - 1:
                        held[k, way, stage - 1] = total.astype(bf16)
                        hop(k, stage, way).start()
                    else:
                        across[team, k, way] = total.astype(bf16)
                        for d in range(teams - 1):
                            cross(k, way, d).start()

    def finish(k):
        columns = pl.ds(pl.multiple_of(core * half, 128), half)
        return pltpu.make_async_copy(done.at[k], out_ref.at[k, :, columns], out_sem.at[k])

    def hand(k):
        columns = pl.ds(pl.multiple_of(core * half, 128), half)
        return pltpu.make_async_remote_copy(
            done.at[k],
            out_ref.at[k, :, columns],
            hand_send.at[k],
            hand_recv.at[k],
            device_id=other,
            device_id_type=MESH,
        )

    @pl.loop(0, number)
    def _(k):
        for way in range(2):
            for d in range(teams - 1):
                cross(k, way, d).wait_recv()
            total = across[0, k, way].astype(f32)
            for t in range(1, teams):
                total = total + across[t, k, way].astype(f32)
            done[k, :, way * wide : (way + 1) * wide] = total
        finish(k).start()
        hand(k).start()

    @pl.loop(0, number)
    def _(k):
        finish(k).wait()
        hand(k).wait()
        pair_g(k).wait_send()
        for way in range(2):
            for stage in range(count - 1):
                hop(k, stage, way).wait_send()
            for d in range(teams - 1):
                cross(k, way, d).wait_send()

    @pl.loop(0, kinds)
    def _(j):
        pair_x(j).wait_send()


def ring_reduce(xs, gs, collective_id):
    count = lax.axis_size("pix")
    teams = lax.axis_size("img") // 2
    kinds, _, rows, depth = xs.shape
    number, _, width = gs.shape
    anywhere = pl.BlockSpec(memory_space=pl.ANY)
    chunk = (depth, width // 4)
    return pl.pallas_call(
        functools.partial(reduce_kernel, count, teams),
        out_shape=jax.ShapeDtypeStruct((number, depth, width), f32),
        in_specs=[anywhere] * 2,
        out_specs=anywhere,
        scratch_shapes=[
            pltpu.VMEM((kinds, count, 2 * rows, depth), bf16),
            pltpu.VMEM((number, 2 * rows, width // 2), bf16),
            pltpu.VMEM((number, 2) + chunk, bf16),
            pltpu.VMEM((number, 2, count - 1) + chunk, bf16),
            pltpu.VMEM((teams, number, 2) + chunk, bf16),
            pltpu.VMEM((number, depth, width // 2), f32),
            DMA((2, number)),
            DMA((2, number)),
            DMA((2, number)),
            DMA((count - 1, 2, number)),
            DMA((count - 1, 2, number)),
            DMA((teams - 1, 2, number)),
            DMA((teams - 1, 2, number)),
            DMA((number,)),
            DMA((number,)),
            DMA((number,)),
        ],
        compiler_params=pltpu.CompilerParams(
            collective_id=collective_id, has_side_effects=True, vmem_limit_bytes=48 * 2**20
        ),
    )(xs, gs)


def peers(count):
    group, me = lax.axis_index("img"), lax.axis_index("pix")
    return [(group, lax.rem(me + d, count)) for d in range(1, count)]


def exchange_kernel(count, number, spread, *refs):
    sources, targets = refs[:number], refs[number : 2 * number]
    own_sem, send_sem, recv_sem = refs[2 * number :]
    me = lax.axis_index("pix")
    others = peers(count)
    greet(others)

    def piece(a, to):
        return sources[a] if spread[a] else sources[a].at[to]

    def push(a, d):
        return pltpu.make_async_remote_copy(
            piece(a, others[d][1]),
            targets[a].at[me],
            send_sem.at[a, d],
            recv_sem.at[a, d],
            device_id=others[d],
            device_id_type=MESH,
        )

    def keep(a):
        return pltpu.make_async_copy(piece(a, me), targets[a].at[me], own_sem.at[a])

    for d in range(count - 1):
        for a in range(number):
            push(a, d).start()
    for a in range(number):
        keep(a).start()
    for a in range(number):
        keep(a).wait()
        for d in range(count - 1):
            push(a, d).wait()


def exchange(arrays, spread, collective_id):
    count = lax.axis_size("pix")
    number = len(arrays)
    anywhere = pl.BlockSpec(memory_space=pl.ANY)
    shapes = [((count,) if flag else ()) + a.shape for a, flag in zip(arrays, spread)]
    return pl.pallas_call(
        functools.partial(exchange_kernel, count, number, spread),
        out_shape=[jax.ShapeDtypeStruct(s, a.dtype) for s, a in zip(shapes, arrays)],
        in_specs=[anywhere] * number,
        out_specs=[anywhere] * number,
        scratch_shapes=[DMA((number,)), DMA((number, count - 1)), DMA((number, count - 1))],
        compiler_params=pltpu.CompilerParams(collective_id=collective_id, has_side_effects=True),
    )(*arrays)


def sum_kernel(
    count,
    crowd,
    t_ref,
    g_ref,
    z_ref,
    t_out,
    g_out,
    z_out,
    t_in,
    g_in,
    t_img,
    g_img,
    own_sem,
    send_sem,
    recv_sem,
    img_send,
    img_recv,
    last_send,
    last_recv,
):
    group, me = lax.axis_index("img"), lax.axis_index("pix")
    others = peers(count)
    across = [(lax.rem(group + d, crowd), me) for d in range(1, crowd)]
    greet(others + across)

    def copy(source, target, sems, index, device):
        return pltpu.make_async_remote_copy(
            source,
            target,
            sems[0].at[index],
            sems[1].at[index],
            device_id=device,
            device_id_type=MESH,
        )

    def scatter(d):
        to = others[d][1]
        sems = (send_sem, recv_sem)
        return (
            copy(t_ref.at[to], t_in.at[d], sems, (0, d), others[d]),
            copy(g_ref.at[to], g_in.at[d], sems, (1, d), others[d]),
        )

    def spread(d):
        return copy(z_ref, z_out.at[me], (send_sem, recv_sem), (2, d), others[d])

    def over(d):
        sems = (img_send, img_recv)
        return (
            copy(t_img.at[group], t_img.at[group], sems, (0, d), across[d]),
            copy(g_img.at[group], g_img.at[group], sems, (1, d), across[d]),
        )

    def gather(d):
        sems = (last_send, last_recv)
        return (
            copy(t_out.at[me], t_out.at[me], sems, (0, d), others[d]),
            copy(g_out.at[me], g_out.at[me], sems, (1, d), others[d]),
        )

    for d in range(count - 1):
        for part in scatter(d):
            part.start()
    for d in range(count - 1):
        spread(d).start()
    keep = pltpu.make_async_copy(z_ref, z_out.at[me], own_sem)
    keep.start()
    t_sum = t_ref[me].astype(f32)
    g_sum = g_ref[me]
    for d in range(count - 1):
        for part in scatter(d):
            part.wait_recv()
        t_sum = t_sum + t_in[d].astype(f32)
        g_sum = g_sum + g_in[d]
    t_img[group] = t_sum.astype(bf16)
    g_img[group] = g_sum
    for d in range(crowd - 1):
        for part in over(d):
            part.start()
    for d in range(crowd - 1):
        for part in over(d):
            part.wait_recv()
    t_sum = t_img[0].astype(f32)
    g_sum = g_img[0]
    for i in range(1, crowd):
        t_sum = t_sum + t_img[i].astype(f32)
        g_sum = g_sum + g_img[i]
    t_out[me] = t_sum.astype(bf16)
    g_out[me] = g_sum
    for d in range(count - 1):
        for part in gather(d):
            part.start()
    keep.wait()
    for d in range(count - 1):
        for part in gather(d):
            part.wait()
        for part in scatter(d):
            part.wait_send()
        spread(d).wait()
    for d in range(crowd - 1):
        for part in over(d):
            part.wait_send()


def small_sums(t, g, z, collective_id):
    count, crowd = lax.axis_size("pix"), lax.axis_size("img")
    inside = pl.BlockSpec(memory_space=pltpu.VMEM)
    return pl.pallas_call(
        functools.partial(sum_kernel, count, crowd),
        out_shape=[
            jax.ShapeDtypeStruct(t.shape, bf16),
            jax.ShapeDtypeStruct(g.shape, f32),
            jax.ShapeDtypeStruct((count,) + z.shape, bf16),
        ],
        in_specs=[inside] * 3,
        out_specs=[inside] * 3,
        scratch_shapes=[
            pltpu.VMEM((count - 1,) + t.shape[1:], bf16),
            pltpu.VMEM((count - 1,) + g.shape[1:], f32),
            pltpu.VMEM((crowd,) + t.shape[1:], bf16),
            pltpu.VMEM((crowd,) + g.shape[1:], f32),
            DMA,
            DMA((3, count - 1)),
            DMA((3, count - 1)),
            DMA((2, crowd - 1)),
            DMA((2, crowd - 1)),
            DMA((2, count - 1)),
            DMA((2, count - 1)),
        ],
        compiler_params=pltpu.CompilerParams(
            collective_id=collective_id, has_side_effects=True, vmem_limit_bytes=24 * 2**20
        ),
    )(t, g, z)


def gelu_parts(z):
    slope = (2.0 / jnp.pi) ** 0.5
    square = z * z
    bend = jnp.tanh(slope * z * (1.0 + 0.044715 * square))
    half = 0.5 * (1.0 + bend)
    return z * half, half + 0.5 * z * (1.0 - bend * bend) * slope * (1.0 + 0.134145 * square)


def latent_kernel(
    count,
    images,
    part_ref,
    stat_ref,
    own_ref,
    cot_ref,
    mix_ref,
    gain_ref,
    in_gain_ref,
    w_ref,
    out_ref,
    xs_ref,
    gs_ref,
    back_ref,
    row_ref,
    gain_out,
    in_gain_out,
    wv,
    one,
    two,
    three,
    pre,
    grad,
    flow,
    low,
    heads_q,
    kv,
    probs,
    kv_out,
    kv_in,
    cot,
    final,
    mean,
    w_sem,
    kv_send,
    kv_recv,
    gkv_send,
    gkv_recv,
    cot_own,
    cot_send,
    cot_recv,
    out_own,
    out_send,
    out_recv,
):
    rows, width = own_ref.shape
    depth = xs_ref.shape[3]
    sharers = count // images
    latents = rows * sharers
    per = count // sharers
    rows_here = latents // count
    spare = xs_ref.shape[3] - rows_here
    group, me = lax.axis_index("img"), lax.axis_index("pix")
    slot, image = lax.rem(me, sharers), me // sharers
    block = 256
    blocks = width // block
    row_block = min(rows, 64)
    up_one, down_one, m_query, m_key, m_value, m_out, up_two, down_two = range(8)
    scale = HEAD_DIM ** (-0.5)

    def load(k):
        return pltpu.make_async_copy(w_ref.at[k], wv.at[k], w_sem.at[k])

    for k in range(8):
        load(k).start()
    greet(peers(count))

    def cot_push(i):
        to = i * sharers + me // per
        return to, pltpu.make_async_remote_copy(
            cot_ref.at[i],
            cot.at[lax.rem(me, per)],
            cot_send.at[i],
            cot_recv.at[lax.rem(me, per)],
            device_id=(group, to),
            device_id_type=MESH,
        )

    def cot_keep():
        return pltpu.make_async_copy(cot_ref.at[image], cot.at[lax.rem(me, per)], cot_own)

    for i in range(images):
        to, copy = cot_push(i)

        @pl.when(to != me)
        def _():
            copy.start()

        @pl.when(to == me)
        def _():
            cot_keep().start()

    def columns(j, wide=block):
        return pl.ds(pl.multiple_of(j * wide, wide), wide)

    def over_columns(body):
        pl.loop(0, blocks)(body)

    def over_rows(body):
        @pl.loop(0, rows // row_block)
        def _(r):
            body(pl.ds(pl.multiple_of(r * row_block, 16), row_block))

    def put_x(j, c, value):
        for b in range(block // depth):
            xs_ref[j, c * (block // depth) + b] = value[:, b * depth : (b + 1) * depth]

    def centre(rows_f32):
        average = jnp.mean(rows_f32, axis=1, keepdims=True)
        centred = rows_f32 - average
        spread = jnp.mean(centred * centred, axis=1, keepdims=True)
        scale_rows = lax.rsqrt(spread + eps)
        return centred * scale_rows, scale_rows

    def norm(source, k, target):
        def body(r):
            target[r] = (centre(source[r])[0] * gain_ref[k : k + 1, :]).astype(bf16)

        over_rows(body)

    def norm_grad(source, k):
        def body(r):
            hat, scale_rows = centre(source[r])
            given = flow[r]
            gain_out[k : k + 1, :] += jnp.sum(given * hat, axis=0, keepdims=True)
            given = given * gain_ref[k : k + 1, :]
            along = jnp.mean(given * hat, axis=1, keepdims=True)
            grad[r] += scale_rows * (given - jnp.mean(given, axis=1, keepdims=True) - hat * along)

        over_rows(body)

    gain_out[...] = jnp.zeros_like(gain_out)

    top = jnp.max(stat_ref[:, 0:1, :], axis=0)
    total = jnp.zeros_like(top)
    for d in range(count):
        total = total + jnp.exp2(stat_ref[d, 0:1, :] - top) * stat_ref[d, 1:2, :]
    raw = jnp.zeros(part_ref.shape[1:], f32)
    for d in range(count):
        raw = raw + part_ref[d].astype(f32) * (jnp.exp2(stat_ref[d, 0:1, :] - top) / total)
    mean[0] = raw
    mean[1] = raw * in_gain_ref[...]
    row_ref[...] = jnp.zeros_like(row_ref)
    row_ref[0:1, :] = top + jnp.log(total) * LOG2E

    tall = count * spare
    mean_tall = mean[1]
    if tall > mean_tall.shape[0]:
        mean_tall = jnp.concatenate(
            [mean_tall, jnp.zeros((tall - mean_tall.shape[0], rows), f32)], axis=0
        )
    share_rows = -(-mean.shape[1] // count)
    share_rows = -(-share_rows // 8) * 8
    place = lax.broadcasted_iota(jnp.int32, (rows_here, rows), 0)
    source_row = lax.broadcasted_iota(jnp.int32, (rows_here, rows), 1) + slot * rows
    for o in range(count):
        picks = jnp.where(place + o * rows_here == source_row, 1.0, 0.0)
        piece = [picks, mean_tall[o * share_rows : (o + 1) * share_rows]]
        if spare > share_rows:
            piece.append(jnp.zeros((spare - share_rows, rows), f32))
        xs_ref[6, o] = jnp.concatenate(piece, axis=0).T.astype(bf16)

    mean_low = mean[1].astype(bf16)

    @over_columns
    def _(j):
        one[:, columns(j)] = own_ref[:, columns(j)] + mm_tn(mean_low, mix_ref[:, columns(j)])

    def feed(source, target, k, up, down, normed, x_hidden, keep):
        norm(source, k, normed)
        load(up).wait()

        @over_columns
        def _(j):
            value = mm_nt(normed[...], wv[up, columns(j), :])
            pre[keep, :, columns(j)] = value
            hidden = gelu_parts(value)[0].astype(bf16)
            low[:, columns(j)] = hidden
            put_x(x_hidden, j, hidden)

        load(down).wait()

        @over_columns
        def _(j):
            value = source[:, columns(j)] + mm(low[...], wv[down, :, columns(j)])
            target[:, columns(j)] = value.astype(target.dtype)

    def feed_back(source, k, up, down, branch, x_pre, keep):
        @over_columns
        def _(j):
            value = mm_nt(branch[...], wv[down, columns(j), :])
            value = (value * gelu_parts(pre[keep, :, columns(j)])[1]).astype(bf16)
            low[:, columns(j)] = value
            put_x(x_pre, j, value)

        @over_columns
        def _(j):
            flow[:, columns(j)] = mm(low[...], wv[up, :, columns(j)])

        norm_grad(source, k)

    feed(one, two, 0, up_one, down_one, gs_ref.at[4], 3, 0)

    norm(two, 1, low)

    def write_blocks(j, value):
        put_x(0, j, value)

    @over_columns
    def _(j):
        write_blocks(j, low[:, columns(j)])

    load(m_key).wait()
    load(m_value).wait()

    @over_columns
    def _(j):
        kv[0, slot, :, columns(j)] = mm(low[...], wv[m_key, :, columns(j)]).astype(bf16)
        kv[1, slot, :, columns(j)] = mm(low[...], wv[m_value, :, columns(j)]).astype(bf16)

    def sharer(d):
        return (group, image * sharers + lax.rem(slot + d, sharers))

    def kv_push(d):
        return pltpu.make_async_remote_copy(
            kv.at[:, slot],
            kv.at[:, slot],
            kv_send.at[d - 1],
            kv_recv.at[d - 1],
            device_id=sharer(d),
            device_id_type=MESH,
        )

    for d in range(1, sharers):
        kv_push(d).start()
    load(m_query).wait()

    @over_columns
    def _(j):
        heads_q[:, columns(j)] = mm(low[...], wv[m_query, :, columns(j)]).astype(bf16)

    for d in range(1, sharers):
        kv_push(d).wait_recv()

    @pl.loop(0, HEADS)
    def _(h):
        c = columns(h, HEAD_DIM)
        k_all = kv[0, :, :, c].reshape(latents, HEAD_DIM)
        v_all = kv[1, :, :, c].reshape(latents, HEAD_DIM)
        scores = mm_nt(heads_q[:, c], k_all) * scale
        shifted = jnp.exp(scores - jnp.max(scores, axis=1, keepdims=True))
        p = shifted / jnp.sum(shifted, axis=1, keepdims=True)
        probs[h] = p
        low[:, c] = mm(p.astype(bf16), v_all).astype(bf16)

    @over_columns
    def _(j):
        put_x(1, j, low[:, columns(j)])

    load(m_out).wait()

    @over_columns
    def _(j):
        three[:, columns(j)] = two[:, columns(j)] + mm(low[...], wv[m_out, :, columns(j)])

    feed(three, final, 2, up_two, down_two, gs_ref.at[6], 5, 1)

    def out_push(b):
        to = slot * per + b
        return to, pltpu.make_async_remote_copy(
            final.at[pl.ds(b * rows_here, rows_here)],
            out_ref.at[image],
            out_send.at[b],
            out_recv.at[image],
            device_id=(group, to),
            device_id_type=MESH,
        )

    def out_keep():
        mine = pl.ds(pl.multiple_of(lax.rem(me, per) * rows_here, 16), rows_here)
        return pltpu.make_async_copy(final.at[mine], out_ref.at[image], out_own)

    for b in range(per):
        to, copy = out_push(b)

        @pl.when(to != me)
        def _():
            copy.start()

        @pl.when(to == me)
        def _():
            out_keep().start()

    def cot_from(b):
        return pltpu.make_async_remote_copy(
            cot_ref.at[0],
            cot.at[b],
            cot_send.at[0],
            cot_recv.at[b],
            device_id=(group, me),
            device_id_type=MESH,
        )

    for b in range(per):

        @pl.when(slot * per + b != me)
        def _():
            cot_from(b).wait_recv()

        @pl.when(slot * per + b == me)
        def _():
            cot_keep().wait()

    given = cot[...].reshape(rows, width)
    gs_ref[7] = given
    grad[...] = given.astype(f32)
    feed_back(three, 2, up_two, down_two, gs_ref.at[7], 4, 1)

    gs_ref[3] = grad[...].astype(bf16)

    @over_columns
    def _(j):
        low[:, columns(j)] = mm_nt(gs_ref[3], wv[m_out, columns(j), :]).astype(bf16)

    @pl.loop(0, HEADS)
    def _(h):
        c = columns(h, HEAD_DIM)
        k_all = kv[0, :, :, c].reshape(latents, HEAD_DIM)
        v_all = kv[1, :, :, c].reshape(latents, HEAD_DIM)
        p = probs[h]
        g_mixed = low[:, c]
        g_p = mm_nt(g_mixed, v_all)
        g_v = mm_tn(p.astype(bf16), g_mixed)
        delta = jnp.sum(p * g_p, axis=1, keepdims=True)
        g_s = (p * (g_p - delta)).astype(bf16)
        gs_ref[0, :, c] = (mm(g_s, k_all) * scale).astype(bf16)
        g_k = mm_tn(g_s, heads_q[:, c]) * scale
        kv_out[:, 0, :, c] = g_k.reshape(sharers, rows, HEAD_DIM).astype(bf16)
        kv_out[:, 1, :, c] = g_v.reshape(sharers, rows, HEAD_DIM).astype(bf16)

    def gkv_push(d):
        to = lax.rem(slot + d, sharers)
        return pltpu.make_async_remote_copy(
            kv_out.at[to],
            kv_in.at[d - 1],
            gkv_send.at[d - 1],
            gkv_recv.at[d - 1],
            device_id=sharer(d),
            device_id_type=MESH,
        )

    for d in range(1, sharers):
        gkv_push(d).start()

    @over_columns
    def _(j):
        flow[:, columns(j)] = mm_nt(gs_ref[0], wv[m_query, columns(j), :])

    for d in range(1, sharers):
        gkv_push(d).wait_recv()
    for which in range(2):

        @over_columns
        def _(j):
            value = kv_out[slot, which, :, columns(j)].astype(f32)
            for d in range(1, sharers):
                value = value + kv_in[d - 1, which, :, columns(j)].astype(f32)
            gs_ref[1 + which, :, columns(j)] = value.astype(bf16)

    @over_columns
    def _(j):
        flow[:, columns(j)] += mm_nt(gs_ref[1], wv[m_key, columns(j), :]) + mm_nt(
            gs_ref[2], wv[m_value, columns(j), :]
        )

    norm_grad(two, 1)
    gs_ref[5] = grad[...].astype(bf16)
    feed_back(one, 0, up_one, down_one, gs_ref.at[5], 2, 0)
    gs_ref[8] = grad[...].astype(bf16)
    back = mm_nt(mix_ref[...], gs_ref[8])
    back_ref[...] = back.astype(bf16)
    row_ref[1:2, :] = jnp.sum(back * mean[1], axis=0, keepdims=True)
    in_gain_out[...] = jnp.broadcast_to(
        jnp.sum(back * mean[0], axis=1, keepdims=True), in_gain_out.shape
    )

    for i in range(images):
        to, copy = cot_push(i)

        @pl.when(to != me)
        def _():
            copy.wait_send()

    for d in range(1, sharers):
        kv_push(d).wait_send()
        gkv_push(d).wait_send()

    def out_from(i):
        return pltpu.make_async_remote_copy(
            final.at[pl.ds(0, rows_here)],
            out_ref.at[i],
            out_send.at[0],
            out_recv.at[i],
            device_id=(group, me),
            device_id_type=MESH,
        )

    for b in range(per):
        to, copy = out_push(b)

        @pl.when(to != me)
        def _():
            copy.wait_send()

    for i in range(images):
        owner = i * sharers + me // per

        @pl.when(owner != me)
        def _():
            out_from(i).wait_recv()

        @pl.when(owner == me)
        def _():
            out_keep().wait()


def latent_pass(parts, stats, own, cotangent, mix, gains, in_gain, whole, collective_id):
    count = lax.axis_size("pix")
    images, rows_here, width = cotangent.shape
    rows = own.shape[0]
    channels = mix.shape[0]
    depth = width // count
    sharers = count // images
    per = count // sharers
    inside = pl.BlockSpec(memory_space=pltpu.VMEM)
    anywhere = pl.BlockSpec(memory_space=pl.ANY)
    whole_f32 = pltpu.VMEM((rows, width), f32)
    whole_low = pltpu.VMEM((rows, width), bf16)
    shape = jax.ShapeDtypeStruct
    return pl.pallas_call(
        functools.partial(latent_kernel, count, images),
        out_shape=[
            shape((images, rows_here, width), bf16),
            shape((7, count, rows, depth), bf16),
            shape((9, rows, width), bf16),
            shape((channels, rows), bf16),
            shape((8, rows), f32),
            shape((8, width), f32),
            shape((channels, 128), f32),
        ],
        in_specs=[inside, inside, inside, anywhere, inside, inside, inside, anywhere],
        out_specs=[anywhere] + [inside] * 6,
        scratch_shapes=[
            pltpu.VMEM((8, width, width), bf16),
            whole_f32,
            whole_f32,
            whole_f32,
            pltpu.VMEM((2, rows, width), f32),
            whole_f32,
            whole_f32,
            whole_low,
            whole_low,
            pltpu.VMEM((2, sharers, rows, width), bf16),
            pltpu.VMEM((HEADS, rows, rows * sharers), f32),
            pltpu.VMEM((sharers, 2, rows, width), bf16),
            pltpu.VMEM((max(sharers - 1, 1), 2, rows, width), bf16),
            pltpu.VMEM((per, rows_here, width), bf16),
            whole_low,
            pltpu.VMEM((2, channels, rows), f32),
            DMA((8,)),
            DMA((sharers,)),
            DMA((sharers,)),
            DMA((sharers,)),
            DMA((sharers,)),
            DMA,
            DMA((images,)),
            DMA((per,)),
            DMA,
            DMA((per,)),
            DMA((images,)),
        ],
        compiler_params=pltpu.CompilerParams(
            collective_id=collective_id, has_side_effects=True, vmem_limit_bytes=60 * 2**20
        ),
    )(parts, stats, own, cotangent, mix, gains, in_gain, whole)


def norm_back(resid, gain, grad):
    _, back = jax.vjp(layer_norm, resid, gain)
    return back(grad)


def local(
    rgb_pixels,
    keep_mask,
    latent_array,
    gain_input,
    gain_latent,
    w_query,
    w_key,
    w_value,
    w_cross_out,
    gain_mlp_one,
    w_up_one,
    w_down_one,
    gain_self,
    w_self_query,
    w_self_key,
    w_self_value,
    w_self_out,
    gain_mlp_two,
    w_up_two,
    w_down_two,
    cotangent,
):
    images, _, pixels = rgb_pixels.shape
    rows_here, width = latent_array.shape
    count = lax.axis_size("pix")
    me = lax.axis_index("pix")
    latents = rows_here * count
    sharers = count // images
    rows_own = latents // sharers
    slot = me % sharers
    depth = w_query.shape[0]
    channels = gain_input.shape[0]
    width_scale = width ** (-0.5)
    tall = -(-channels // 16) * 16

    side = -(-channels // 512) * 512
    key_t = jnp.pad(w_key.T, ((0, 0), (0, side - channels)))
    latent_full, query_mat, key_full = ring_gather([latent_array[None], w_query[None], key_t[None]], 0)
    latent_full = latent_full.reshape(latents, width)
    query_mat = query_mat.reshape(width, width)
    key_full = key_full.reshape(width, side)
    key_mat = key_full[:, :channels].T
    value_out = lax.psum(mm(w_value, w_cross_out).astype(bf16), "pix")
    shards = jnp.stack(
        [
            w_up_one.T,
            w_down_one,
            w_self_query,
            w_self_key,
            w_self_value,
            w_self_out,
            w_up_two.T,
            w_down_two,
        ]
    )
    (whole,) = ring_gather([shards], 1)
    whole = whole.reshape(8, width, width)

    lines = pixels // SIDE
    u, sin_u, cos_u = angles(me * lines + lax.iota(jnp.int32, lines))
    w, sin_w, cos_w = angles(lax.iota(jnp.int32, SIDE))

    def zeros(rows, columns):
        return jnp.zeros((rows, columns), f32)

    pad = CHANNELS - 4 - SIDE - lines
    table = jnp.concatenate(
        [
            jnp.concatenate(
                [zeros(SIDE, 4), w, zeros(SIDE, BANDS), sin_w, zeros(SIDE, BANDS), cos_w], axis=1
            ),
            jnp.concatenate(
                [zeros(lines, 3), u, zeros(lines, 1), sin_u, zeros(lines, BANDS), cos_u, zeros(lines, BANDS)],
                axis=1,
            ),
            zeros(pad, channels),
            jnp.eye(3, channels, dtype=f32),
            jnp.ones((1, channels), f32),
        ],
        axis=0,
    )
    row_sum = u[:, 0] + jnp.sum(sin_u + cos_u, axis=1)
    col_sum = w[:, 0] + jnp.sum(sin_w + cos_w, axis=1)
    row_square = u[:, 0] ** 2 + jnp.sum(sin_u**2 + cos_u**2, axis=1)
    col_square = w[:, 0] ** 2 + jnp.sum(sin_w**2 + cos_w**2, axis=1)
    feature_sum = (row_sum[:, None] + col_sum[None, :]).reshape(1, pixels)
    feature_square = (row_square[:, None] + col_square[None, :]).reshape(1, pixels)
    colours = rgb_pixels.astype(f32)
    average = (jnp.sum(colours, axis=1) + feature_sum) / channels
    spread = (jnp.sum(colours**2, axis=1) + feature_square) / channels - average**2
    scale = lax.rsqrt(spread + eps)
    keep = keep_mask.astype(f32)

    position = lax.iota(jnp.int32, pixels)
    column, line = position % SIDE, position // SIDE + SIDE
    channel = lax.iota(jnp.int32, CHANNELS - 4)
    hot = (channel[:, None] == column[None, :]) | (channel[:, None] == line[None, :])
    small = jnp.concatenate(
        [colours * scale[:, None, :], (-average * scale)[:, None, :]], axis=1
    )
    xt = jnp.concatenate(
        [
            jnp.where(hot[None], (scale * keep)[:, None, :], 0.0).astype(bf16),
            (small * keep[:, None, :]).astype(bf16),
            keep[:, None, :].astype(bf16),
            jnp.zeros((images, 15, pixels), bf16),
        ],
        axis=1,
    )
    x = jnp.concatenate(
        [
            jnp.where(hot.T[None], scale[:, :, None], 0.0).astype(bf16),
            jnp.swapaxes(small, 1, 2).astype(bf16),
        ],
        axis=2,
    ).reshape(images * pixels, CHANNELS)

    latent_float = latent_full.astype(f32)
    latent_normed = layer_norm(latent_float, gain_latent).astype(bf16)
    queries = mm(latent_normed, query_mat).astype(bf16)
    gained = table * gain_input[None, :]
    score_mat = mm_nt(queries, key_mat) * width_scale
    score_x = exact(score_mat, gained.T)
    at = (score_x.T * LOG2E).astype(bf16)
    a_low = score_x.astype(bf16)

    weighted, tops = score_pass(x, xt, at)
    tops = tops[:, 0, :]
    totals = weighted[:, CHANNELS, :]
    raw = jnp.einsum(
        "kc,ikq->icq",
        table,
        weighted[:, :CHANNELS, :],
        precision=lax.Precision.HIGHEST,
        preferred_element_type=f32,
    )

    def by_owner(value):
        lead = value.shape[1]
        split = value.reshape(images, lead, sharers, rows_own)
        return jnp.swapaxes(split, 1, 2).reshape(count, lead, rows_own)

    raw = jnp.pad(raw, ((0, 0), (0, tall - channels), (0, 0)))
    stat = jnp.pad(jnp.stack([tops, totals], axis=1), ((0, 0), (0, 6), (0, 0)))
    raw_parts, stat_parts = exchange(
        [by_owner(raw).astype(bf16), by_owner(stat)], (False, False), 3
    )

    own = lax.dynamic_slice_in_dim(latent_float, slot * rows_own, rows_own, 0)
    latent_out, xs, gs, back_t, row_stats, gain_grads, in_gain = latent_pass(
        raw_parts,
        stat_parts,
        own,
        cotangent,
        jnp.pad(value_out, ((0, tall - channels), (0, 0))),
        jnp.stack([gain_mlp_one, gain_self, gain_mlp_two]),
        jnp.pad(gain_input, (0, tall - channels))[:, None],
        whole,
        4,
    )
    summed = ring_reduce(xs, gs, 2)

    back_all, row_all = exchange([back_t, row_stats], (True, True), 5)

    def by_image(value):
        lead = value.shape[1]
        split = value.reshape(images, sharers, lead, rows_own)
        return jnp.swapaxes(split, 1, 2).reshape(images, lead, latents)

    back_all = by_image(back_all)[:, :channels].astype(f32)
    bt = jnp.einsum(
        "kc,icq->ikq",
        gained,
        back_all,
        precision=lax.Precision.HIGHEST,
        preferred_element_type=f32,
    ).astype(bf16)
    grad_t, pixel_out = grad_pass(
        x, xt, at, bt, a_low, jnp.swapaxes(bt, 1, 2), by_image(row_all)
    )
    moved = (pixel_out[:, 4:7] - pixel_out[:, 7:8] / channels) - (
        (colours - average[:, None, :]) * scale[:, None, :]
    ) * (pixel_out[:, 0:1] / channels)
    grad_pixels = moved * (scale * keep)[:, None, :]

    grad_raw = exact(grad_t[:CHANNELS].T, table)
    across = -(-channels // 128) * 128
    cells = -(-(3 * width + channels) // (count * 1024)) * 1024
    loose = jnp.concatenate([gain_grads[:3].reshape(-1), in_gain[:channels, 0]])
    loose = jnp.pad(loose, (0, count * cells - loose.shape[0])).reshape(count, 8, cells // 8)
    share_rows = -(-(-(-tall // count)) // 8) * 8
    rest = summed[8]
    spare = -(-share_rows // 16) * 16
    cross_rows = jnp.pad(
        rest[rows_here : rows_here + share_rows].astype(bf16), ((0, spare - share_rows), (0, 0))
    )
    grad_raw, loose, cross_sum = small_sums(
        jnp.pad(grad_raw, ((0, 0), (0, across - channels)))
        .astype(bf16)
        .reshape(count, rows_here, across),
        loose,
        cross_rows,
        6,
    )
    grad_raw = grad_raw.reshape(latents, across)[:, :channels].astype(f32)
    loose = loose.reshape(-1)
    gain_one, gain_attn, gain_two = [loose[k * width : (k + 1) * width] for k in range(3)]
    gain_in = loose[3 * width : 3 * width + channels] + jnp.sum(score_mat * grad_raw, axis=0)
    cross_sum = cross_sum[:, :share_rows].reshape(-1, width)[:channels]

    grad_x = (grad_raw * (gain_input * width_scale)[None, :]).astype(bf16)
    query_grad = mm(grad_x, key_mat).astype(bf16)
    latent_cols = lax.dynamic_slice_in_dim(latent_normed, me * depth, depth, 1)
    grad_w_query = mm_tn(latent_cols, query_grad)
    grad_latent_full, grad_gain_latent = norm_back(
        latent_float, gain_latent, mm_nt(query_grad, query_mat)
    )
    grad_latent_own = lax.dynamic_slice_in_dim(grad_latent_full, me * rows_here, rows_here, 0)
    key_cols = w_key.shape[1]
    grad_w_key = mm_tn(grad_x, lax.dynamic_slice_in_dim(queries, me * key_cols, key_cols, 1))

    g_sq, g_sk, g_sv, g_so, g_up_one, g_down_one, g_up_two, g_down_two, rest = [
        summed[k] for k in range(9)
    ]
    grad_w_value = mm_nt(cross_sum, w_cross_out)
    grad_w_cross_out = mm_tn(w_value, cross_sum)
    grad_latent_array = rest[:rows_here] + grad_latent_own
    return (
        latent_out,
        grad_pixels,
        grad_latent_array,
        gain_in,
        grad_gain_latent,
        grad_w_query,
        grad_w_key,
        grad_w_value,
        grad_w_cross_out,
        gain_one,
        g_up_one.T,
        g_down_one,
        gain_attn,
        g_sq,
        g_sk,
        g_sv,
        g_so,
        gain_two,
        g_up_two.T,
        g_down_two,
    )


def solution(mesh):
    rows, columns, copied = P("pix", None), P(None, "pix"), P()
    return jax.shard_map(
        local,
        mesh=mesh,
        in_specs=(
            P("img", None, "pix"),
            P("img", "pix"),
            rows,
            copied,
            copied,
            rows,
            columns,
            columns,
            rows,
            copied,
            columns,
            rows,
            copied,
            rows,
            rows,
            rows,
            rows,
            copied,
            columns,
            rows,
            P("img", "pix", None),
        ),
        out_specs=(
            P("img", "pix", None),
            P("img", None, "pix"),
            rows,
            copied,
            copied,
            rows,
            columns,
            columns,
            rows,
            copied,
            columns,
            rows,
            copied,
            rows,
            rows,
            rows,
            rows,
            copied,
            columns,
            rows,
        ),
        check_vma=False,
    )
```

```python
import functools

import jax
import jax.numpy as jnp
from jax import lax
from jax.experimental import pallas as pl
from jax.experimental.pallas import tpu as pltpu
from jax.sharding import PartitionSpec as P

HEADS = 8
HEAD_DIM = 128
BANDS = 64
SIDE = 224
CHANNELS = 256
LOG2E = 1.4426950408889634

eps = 1e-05
f32 = jnp.float32
bf16 = jnp.bfloat16


def exact(left, right):
    return jnp.dot(left, right, precision=lax.Precision.HIGHEST, preferred_element_type=f32)


def mm(left, right):
    return jnp.dot(left, right, preferred_element_type=f32)


def mm_nt(left, right):
    return lax.dot_general(left, right, (((1,), (1,)), ((), ())), preferred_element_type=f32)


def mm_tn(left, right):
    return lax.dot_general(left, right, (((0,), (0,)), ((), ())), preferred_element_type=f32)


def layer_norm(rows, gain):
    average = jnp.mean(rows, axis=-1, keepdims=True)
    centred = rows - average
    spread = jnp.mean(centred * centred, axis=-1, keepdims=True)
    return centred * lax.rsqrt(spread + eps) * gain


def angles(index):
    place = index.astype(f32) * (2.0 / (SIDE - 1)) - 1.0
    steps = lax.iota(jnp.int32, BANDS).astype(f32)
    frequency = 1.0 + steps * ((SIDE / 2.0 - 1.0) / (BANDS - 1))
    angle = jnp.pi * place[:, None] * frequency[None, :]
    return place[:, None], jnp.sin(angle), jnp.cos(angle)


def pixel_tile(pixels):
    return 896 if pixels % 896 == 0 else pixels


MESH = pl.DeviceIdType.MESH
DMA = pltpu.SemaphoreType.DMA


def ring_place(count):
    me = lax.axis_index("pix")
    return jnp.where(me % 2 == 0, me // 2, count - 1 - me // 2)


def ring_device(place, count):
    place = lax.rem(place + 2 * count, count)
    return jnp.where(place < count // 2, 2 * place, 2 * (count - 1 - place) + 1)


def greet(devices):
    barrier = pltpu.get_barrier_semaphore()
    for device in devices:
        pl.semaphore_signal(barrier, inc=1, device_id=device, device_id_type=MESH)
    pl.semaphore_wait(barrier, len(devices))


def hot_codes(tile):
    pixel = lax.broadcasted_iota(jnp.int32, (tile, CHANNELS), 0)
    channel = lax.broadcasted_iota(jnp.int32, (tile, CHANNELS), 1)
    start = channel - SIDE - pixel // SIDE
    code = jnp.where(start >= 0, start, -2)
    code = jnp.where(channel < SIDE, jnp.where(channel == pixel % SIDE, -1, -2), code)
    rows = jnp.where(channel >= CHANNELS - 4, -1, code)
    return rows, jnp.where(channel >= CHANNELS - 4, -2, code).T


def selector():
    k = lax.broadcasted_iota(jnp.int32, (8, CHANNELS), 0)
    channel = lax.broadcasted_iota(jnp.int32, (8, CHANNELS), 1)
    own = channel - (CHANNELS - 8)
    return jnp.where(jnp.where(own >= 4, own, 0) == k, 1.0, 0.0).astype(bf16)


def build_x(values, base, code_ref, select_ref):
    spread = mm_tn(values.astype(bf16), select_ref[...])
    code = code_ref[...]
    return jnp.where((code == -1) | (code == base), spread, 0.0).astype(bf16)


def build_xt(values, base, code_ref):
    code = code_ref[...]
    hot = jnp.where((code == -1) | (code == base), values[0:1, :], 0.0)
    last = hot[CHANNELS - 8 :, :]
    k = lax.broadcasted_iota(jnp.int32, last.shape, 0)
    last = jnp.where(k >= 4, values, last)
    return jnp.concatenate([hot[: CHANNELS - 8, :], last], axis=0)


def masked_xt(values, base, code_ref):
    keep = values[1:2, :]
    xt = (build_xt(values, base, code_ref) * keep).astype(bf16)
    k = lax.broadcasted_iota(jnp.int32, (16, values.shape[1]), 0)
    return jnp.concatenate([xt, jnp.where(k == 0, keep, 0.0).astype(bf16)], axis=0)


def forward_kernel(
    count,
    images,
    tile,
    v_ref,
    code_ref,
    code_t_ref,
    select_ref,
    table_ref,
    gained_ref,
    gain_ref,
    lat_ref,
    wq_ref,
    wk_ref,
    w_ref,
    lat_full,
    wq_full,
    wk_full,
    w_full,
    normed_ref,
    query_ref,
    a_ref,
    at_ref,
    alow_ref,
    part_ref,
    stat_ref,
    lat_v,
    wq_v,
    wk_v,
    acc,
    top,
    u_send,
    s_send,
    own_sem,
    load_sem,
    send_sem,
    recv_sem,
    hand_send,
    hand_recv,
    u_own,
    u_out,
    u_in,
):
    pixels = v_ref.shape[2]
    steps = pixels // tile
    lines = tile // SIDE
    sharers = count // images
    rows = part_ref.shape[2]
    width = wq_ref.shape[2]
    latents = normed_ref.shape[0]
    group, me = lax.axis_index("img"), lax.axis_index("pix")
    core = lax.rem(group, 2)
    place = ring_place(count)
    sides = ((group, ring_device(place + 1, count)), (group, ring_device(place - 1, count)))
    other = (group + 1 - 2 * core, me)
    greet([other] + peers(count))
    sources = (lat_ref, wq_ref, wk_ref, w_ref)
    fulls = (lat_full, wq_full, wk_full, w_full)
    mats = w_ref.shape[0]

    def spot(a, k, stage, way, source):
        wide = sources[a].shape[2] // 4
        columns = pl.ds(pl.multiple_of((core * 2 + way) * wide, 128), wide)
        if source:
            return sources[a].at[k, :, columns]
        origin = ring_device(place - stage if way == 0 else place + stage, count)
        return fulls[a].at[k, origin, :, columns]

    def hop(a, k, stage, way, first=False):
        return pltpu.make_async_remote_copy(
            spot(a, k, stage, way, first),
            spot(a, k, stage, way, False),
            send_sem.at[stage, way, a + k],
            recv_sem.at[stage, way, a + k],
            device_id=sides[way],
            device_id_type=MESH,
        )

    def hand(a, k, stage, way):
        part = spot(a, k, stage, way, False)
        return pltpu.make_async_remote_copy(
            part,
            part,
            hand_send.at[stage - 1, way, a + k],
            hand_recv.at[stage - 1, way, a + k],
            device_id=other,
            device_id_type=MESH,
        )

    def relay(a, k, stage, onward=True):
        for way in range(2):
            hop(a, k, stage - 1, way).wait_recv()
            if onward:
                hop(a, k, stage, way).start()
            hand(a, k, stage, way).start()

    own = [
        pltpu.make_async_copy(sources[a], fulls[a].at[:, me], own_sem.at[a]) for a in range(4)
    ]
    for a in range(3):
        for way in range(2):
            hop(a, 0, 0, way, True).start()
    for copy in own:
        copy.start()
    for stage in range(1, count):
        for a in range(3):
            relay(a, 0, stage, stage < count - 1)
        if stage <= mats:
            for way in range(2):
                hop(3, stage - 1, 0, way, True).start()
    for k in range(count - 1, mats):
        for way in range(2):
            hop(3, k, 0, way, True).start()
    for a in range(3):
        own[a].wait()
        for stage in range(1, count):
            for way in range(2):
                hand(a, 0, stage, way).wait_recv()

    loads = [
        pltpu.make_async_copy(full.at[0], held, load_sem.at[j])
        for j, (full, held) in enumerate(((lat_full, lat_v), (wq_full, wq_v), (wk_full, wk_v)))
    ]
    for copy in loads:
        copy.start()
    loads[0].wait()
    rows_here = lat_v.shape[1]

    @pl.loop(0, count)
    def _(o):
        block = lat_v[o].astype(f32)
        average = jnp.mean(block, axis=1, keepdims=True)
        centred = block - average
        spread = jnp.mean(centred * centred, axis=1, keepdims=True)
        normed = (centred * lax.rsqrt(spread + eps) * gain_ref[...]).astype(bf16)
        normed_ref[pl.ds(pl.multiple_of(o * rows_here, rows_here), rows_here), :] = normed

    loads[1].wait()

    @pl.loop(0, width // 256)
    def _(j):
        columns = pl.ds(pl.multiple_of(j * 256, 256), 256)
        weight = wq_v[:, :, columns].reshape(width, 256)
        query_ref[:, columns] = mm(normed_ref[...], weight).astype(bf16)

    loads[2].wait()
    a_ref[...] = mm(query_ref[...], wk_v[...].reshape(width, wk_v.shape[2])) * (width ** (-0.5))

    def exact_nt(left, right):
        return lax.dot_general(
            left,
            right,
            (((1,), (1,)), ((), ())),
            precision=lax.Precision.HIGHEST,
            preferred_element_type=f32,
        )

    at_ref[...] = (exact_nt(gained_ref[...], a_ref[...]) * LOG2E).astype(bf16)
    alow_ref[...] = exact_nt(a_ref[...], gained_ref[...]).astype(bf16)

    relays = (count - 2) * mats

    def relay_number(e):
        relay(3, lax.rem(e, mats), 1 + e // mats)

    def u_push(i, h):
        to = i * sharers + h
        sems = lambda which: dict(
            send_sem=u_out.at[which, to],
            recv_sem=u_in.at[which, me],
            device_id=(group, to),
            device_id_type=MESH,
        )
        return to, (
            pltpu.make_async_remote_copy(u_send.at[i, h], part_ref.at[me], **sems(0)),
            pltpu.make_async_remote_copy(s_send.at[i, h], stat_ref.at[me], **sems(1)),
        )

    def u_keep():
        i, h = me // sharers, lax.rem(me, sharers)
        return (
            pltpu.make_async_copy(u_send.at[i, h], part_ref.at[me], u_own.at[0]),
            pltpu.make_async_copy(s_send.at[i, h], stat_ref.at[me], u_own.at[1]),
        )

    @pl.loop(0, images * steps)
    def _(t):
        i, step = t // steps, lax.rem(t, steps)

        @pl.when(t < relays)
        def _():
            relay_number(t)

        @pl.when(step == 0)
        def _():
            acc[...] = jnp.zeros_like(acc)
            top[...] = jnp.full_like(top, -jnp.inf)

        values = v_ref[i, :, pl.ds(pl.multiple_of(step * tile, 128), tile)]
        base = step * lines
        x = build_x(values, base, code_ref, select_ref)
        scores = mm(x, at_ref[...])
        xt = masked_xt(values, base, code_t_ref)
        old = top[0:1, :]
        new = jnp.maximum(old, jnp.max(scores, axis=0, keepdims=True))
        weights = jnp.exp2(scores - new).astype(bf16)
        acc[...] = acc[...] * jnp.exp2(old - new) + mm(xt, weights)
        top[...] = jnp.broadcast_to(new, top.shape)

        @pl.when(step == steps - 1)
        def _():
            raw = jnp.dot(
                table_ref[...],
                acc[:CHANNELS, :],
                precision=lax.Precision.HIGHEST,
                preferred_element_type=f32,
            ).astype(bf16)
            stats = jnp.concatenate([top[0:1, :], acc[CHANNELS : CHANNELS + 1, :], top[0:6, :]], axis=0)
            for h in range(sharers):
                u_send[i, h] = raw[:, h * rows : (h + 1) * rows]
                s_send[i, h] = stats[:, h * rows : (h + 1) * rows]
            for h in range(sharers):
                to, copies = u_push(i, h)

                @pl.when(to != me)
                def _():
                    for copy in copies:
                        copy.start()

                @pl.when(to == me)
                def _():
                    for copy in u_keep():
                        copy.start()

    if images * steps < relays:

        @pl.loop(images * steps, relays)
        def _(e):
            relay_number(e)

    @pl.loop(0, mats)
    def _(k):
        relay(3, k, count - 1, False)

    own[3].wait()
    for a in range(3):
        for way in range(2):
            for stage in range(count - 1):
                hop(a, 0, stage, way).wait_send()
                hand(a, 0, stage + 1, way).wait_send()

    @pl.loop(0, mats)
    def _(k):
        for way in range(2):
            for stage in range(count - 1):
                hop(3, k, stage, way).wait_send()
                hand(3, k, stage + 1, way).wait()

    def u_from(d):
        source = lax.rem(me + d, count)
        sems = lambda which: dict(
            send_sem=u_out.at[which, source],
            recv_sem=u_in.at[which, source],
            device_id=(group, source),
            device_id_type=MESH,
        )
        return (
            pltpu.make_async_remote_copy(u_send.at[0, 0], part_ref.at[source], **sems(0)),
            pltpu.make_async_remote_copy(s_send.at[0, 0], stat_ref.at[source], **sems(1)),
        )

    for copy in u_keep():
        copy.wait()
    for d in range(1, count):
        for copy in u_from(d):
            copy.wait()


def forward_pass(values, table, gained, gain_latent, lat, wq, wk, shards, collective_id):
    count = lax.axis_size("pix")
    images, _, pixels = values.shape
    tile = pixel_tile(pixels)
    rows_here, width = lat.shape[1:]
    latents = rows_here * count
    sharers = count // images
    rows = latents // sharers
    tall = table.shape[0]
    mats = shards.shape[0]
    inside = pl.BlockSpec(memory_space=pltpu.VMEM)
    anywhere = pl.BlockSpec(memory_space=pl.ANY)
    shape = jax.ShapeDtypeStruct
    codes, codes_t = hot_codes(tile)

    def full(array):
        return shape((array.shape[0], count) + array.shape[1:], array.dtype)

    ring = DMA((count - 1, 2, 3 + mats))
    return pl.pallas_call(
        functools.partial(forward_kernel, count, images, tile),
        out_shape=[full(lat), full(wq), full(wk), full(shards)]
        + [
            shape((latents, width), bf16),
            shape((latents, width), bf16),
            shape((latents, wk.shape[2]), f32),
            shape((CHANNELS, latents), bf16),
            shape((latents, CHANNELS), bf16),
            shape((count, tall, rows), bf16),
            shape((count, 8, rows), f32),
        ],
        in_specs=[inside] * 7 + [anywhere] * 4,
        out_specs=[anywhere] * 4 + [inside] * 5 + [anywhere] * 2,
        scratch_shapes=[
            pltpu.VMEM((count,) + lat.shape[1:], bf16),
            pltpu.VMEM((count,) + wq.shape[1:], bf16),
            pltpu.VMEM((count,) + wk.shape[1:], bf16),
            pltpu.VMEM((CHANNELS + 16, latents), f32),
            pltpu.VMEM((8, latents), f32),
            pltpu.VMEM((images, sharers, tall, rows), bf16),
            pltpu.VMEM((images, sharers, 8, rows), f32),
            DMA((4,)),
            DMA((3,)),
            ring,
            ring,
            ring,
            ring,
            DMA((2,)),
            DMA((2, count)),
            DMA((2, count)),
        ],
        compiler_params=pltpu.CompilerParams(
            collective_id=collective_id, has_side_effects=True, vmem_limit_bytes=48 * 2**20
        ),
    )(values, codes, codes_t, selector(), table, gained, gain_latent[None], lat, wq, wk, shards)


def backward_kernel(
    count,
    teams,
    images,
    tile,
    v_ref,
    code_ref,
    code_t_ref,
    select_ref,
    table_ref,
    gained_ref,
    at_ref,
    a_ref,
    back_ref,
    row_ref,
    xs_ref,
    gs_ref,
    t_ref,
    pixel_ref,
    out_ref,
    t_acc,
    bt,
    b_low,
    stat,
    back_all,
    row_all,
    xv,
    gv,
    first,
    held,
    across,
    done,
    load_sem,
    pair_send,
    pair_recv,
    send_sem,
    recv_sem,
    cross_send,
    cross_recv,
    out_sem,
    hand_send,
    hand_recv,
    back_send,
    back_recv,
):
    number, rows, width = gs_ref.shape
    kinds = xs_ref.shape[0]
    sharers = count // images
    steps = v_ref.shape[2] // tile
    lines = tile // SIDE
    depth = xs_ref.shape[3]
    half, wide = width // 2, width // 4
    group, me = lax.axis_index("img"), lax.axis_index("pix")
    core, team = lax.rem(group, 2), group // 2
    place = ring_place(count)
    sides = ((group, ring_device(place + 1, count)), (group, ring_device(place - 1, count)))
    other = (group + 1 - 2 * core, me)
    partners = [(lax.rem(team + d, teams) * 2 + core, me) for d in range(1, teams)]
    others = peers(count)
    greet([other] + partners + others)

    def back_push(d):
        sems = lambda which: dict(
            send_sem=back_send.at[which, d],
            recv_sem=back_recv.at[which, me],
            device_id=others[d],
            device_id_type=MESH,
        )
        return (
            pltpu.make_async_remote_copy(back_ref, back_all.at[me], **sems(0)),
            pltpu.make_async_remote_copy(row_ref, row_all.at[me], **sems(1)),
        )

    def back_from(source):
        sems = lambda which: dict(
            send_sem=back_send.at[which, 0],
            recv_sem=back_recv.at[which, source],
            device_id=(group, source),
            device_id_type=MESH,
        )
        return (
            pltpu.make_async_remote_copy(back_ref, back_all.at[source], **sems(0)),
            pltpu.make_async_remote_copy(row_ref, row_all.at[source], **sems(1)),
        )

    for d in range(count - 1):
        for copy in back_push(d):
            copy.start()
    back_all[me] = back_ref[...]
    row_all[me] = row_ref[...]

    mine = pl.ds(pl.multiple_of(core * rows, 16), rows)

    def load_x(j):
        return pltpu.make_async_copy(xs_ref.at[j], xv.at[j, :, mine], load_sem.at[0, j])

    def load_g(k):
        part = gs_ref.at[k, :, pl.ds(pl.multiple_of(core * half, 128), half)]
        return pltpu.make_async_copy(part, gv.at[k, mine], load_sem.at[1, k])

    def pair_x(j):
        return pltpu.make_async_remote_copy(
            xs_ref.at[j],
            xv.at[j, :, mine],
            pair_send.at[0, j],
            pair_recv.at[0, j],
            device_id=other,
            device_id_type=MESH,
        )

    def pair_g(k):
        part = gs_ref.at[k, :, pl.ds(pl.multiple_of((1 - core) * half, 128), half)]
        return pltpu.make_async_remote_copy(
            part,
            gv.at[k, mine],
            pair_send.at[1, k],
            pair_recv.at[1, k],
            device_id=other,
            device_id_type=MESH,
        )

    for j in range(number):
        if j < kinds:
            load_x(j).start()
            pair_x(j).start()
        load_g(j).start()
        pair_g(j).start()

    def part(k, owner, way):
        j = jnp.maximum(k - (number - kinds), 0)
        return mm_tn(xv[j, owner], gv[k, :, way * wide : (way + 1) * wide])

    def hop(k, stage, way, start=False):
        source = first.at[k, way] if start else held.at[k, way, stage - 1]
        return pltpu.make_async_remote_copy(
            source,
            held.at[k, way, stage],
            send_sem.at[stage, way, k],
            recv_sem.at[stage, way, k],
            device_id=sides[way],
            device_id_type=MESH,
        )

    def cross(k, way, d):
        return pltpu.make_async_remote_copy(
            across.at[team, k, way],
            across.at[team, k, way],
            cross_send.at[d, way, k],
            cross_recv.at[d, way, k],
            device_id=partners[d],
            device_id_type=MESH,
        )

    def owner_at(stage, way):
        return ring_device(place - stage - 1 if way == 0 else place + stage + 1, count)

    @pl.loop(0, number)
    def _(k):
        j = jnp.maximum(k - (number - kinds), 0)

        @pl.when((k == 0) | (k > number - kinds))
        def _():
            load_x(j).wait()
            pair_x(j).wait_recv()

        load_g(k).wait()
        pair_g(k).wait_recv()
        for way in range(2):
            first[k, way] = part(k, owner_at(0, way), way).astype(bf16)
            hop(k, 0, way, True).start()

    def relay(k, stage):
        for way in range(2):
            own = part(k, owner_at(stage, way), way)
            hop(k, stage - 1, way, True).wait_recv()
            held[k, way, stage - 1] = (own + held[k, way, stage - 1].astype(f32)).astype(bf16)
            hop(k, stage, way).start()

    def relay_number(e):
        relay(lax.rem(e, number), 1 + e // number)

    relays = (count - 2) * number
    tiles = images * steps
    pace = min(2, relays // tiles)
    t_acc[...] = jnp.zeros_like(t_acc)

    @pl.loop(0, tiles)
    def _(t):
        image = lax.rem(t // steps + me // sharers, images)
        step = lax.rem(t, steps)
        for e in range(pace):
            relay_number(t * pace + e)

        @pl.when(step == 0)
        def _():
            for h in range(sharers):
                source = image * sharers + h

                @pl.when(source != me)
                def _():
                    for copy in back_from(source):
                        copy.wait_recv()

                here = slice(h * rows, (h + 1) * rows)
                wide = jnp.dot(
                    gained_ref[...],
                    back_all[source].astype(f32),
                    precision=lax.Precision.HIGHEST,
                    preferred_element_type=f32,
                )
                bt[:, here] = wide.astype(bf16)
                b_low[here, :] = wide.T.astype(bf16)
                stat[:, here] = row_all[source]

        span = pl.ds(pl.multiple_of(step * tile, 128), tile)
        values = v_ref[image, :, span]
        x = build_x(values, step * lines, code_ref, select_ref)
        xt = masked_xt(values, step * lines, code_t_ref)
        scores = mm(x, at_ref[...])
        grad_p = mm(x, bt[...])
        probs = jnp.exp2(scores - stat[0:1, :])
        grad_s = (probs * (grad_p - stat[1:2, :])).astype(bf16)
        probs = probs.astype(bf16)
        t_acc[...] += mm(xt, grad_s)
        back = mm(grad_s, a_ref[...]) + mm(probs, b_low[...])
        along = jnp.sum(back * x.astype(f32), axis=1, keepdims=True)
        half_back = back[:, CHANNELS - 128 :]
        lane = lax.broadcasted_iota(jnp.int32, half_back.shape, 1)
        half_back = jnp.where(lane == 120, along, half_back)
        pixel_ref[image, :, span] = half_back.T[120:128, :]

    t_ref[...] = lax.dot_general(
        t_acc[:CHANNELS, :],
        table_ref[...],
        (((0,), (0,)), ((), ())),
        precision=lax.Precision.HIGHEST,
        preferred_element_type=f32,
    ).astype(bf16)

    if tiles * pace < relays:

        @pl.loop(tiles * pace, relays)
        def _(e):
            relay_number(e)

    @pl.loop(0, number)
    def _(k):
        for way in range(2):
            own = part(k, me, way)
            hop(k, count - 2, way, True).wait_recv()
            across[team, k, way] = (own + held[k, way, count - 2].astype(f32)).astype(bf16)
            for d in range(teams - 1):
                cross(k, way, d).start()

    def finish(k):
        columns = pl.ds(pl.multiple_of(core * half, 128), half)
        return pltpu.make_async_copy(done.at[k], out_ref.at[k, :, columns], out_sem.at[k])

    def hand(k):
        columns = pl.ds(pl.multiple_of(core * half, 128), half)
        return pltpu.make_async_remote_copy(
            done.at[k],
            out_ref.at[k, :, columns],
            hand_send.at[k],
            hand_recv.at[k],
            device_id=other,
            device_id_type=MESH,
        )

    @pl.loop(0, number)
    def _(k):
        for way in range(2):
            for d in range(teams - 1):
                cross(k, way, d).wait_recv()
            total = across[0, k, way].astype(f32)
            for t in range(1, teams):
                total = total + across[t, k, way].astype(f32)
            done[k, :, way * wide : (way + 1) * wide] = total
        finish(k).start()
        hand(k).start()

    @pl.loop(0, number)
    def _(k):
        finish(k).wait()
        hand(k).wait()
        pair_g(k).wait_send()
        for way in range(2):
            for stage in range(count - 1):
                hop(k, stage, way, stage == 0).wait_send()
            for d in range(teams - 1):
                cross(k, way, d).wait_send()

    @pl.loop(0, kinds)
    def _(j):
        pair_x(j).wait_send()

    for d in range(count - 1):
        for copy in back_push(d):
            copy.wait_send()


def backward_pass(values, table, gained, at, a, back, rows_in, xs, gs, collective_id):
    count = lax.axis_size("pix")
    teams = lax.axis_size("img") // 2
    kinds, _, rows, depth = xs.shape
    number, _, width = gs.shape
    anywhere = pl.BlockSpec(memory_space=pl.ANY)
    inside = pl.BlockSpec(memory_space=pltpu.VMEM)
    chunk = (depth, width // 4)
    images, _, pixels = values.shape
    tile = pixel_tile(pixels)
    latents = at.shape[1]
    tall = back.shape[0]
    codes, codes_t = hot_codes(tile)
    shape = jax.ShapeDtypeStruct
    return pl.pallas_call(
        functools.partial(backward_kernel, count, teams, images, tile),
        out_shape=[
            shape((latents, table.shape[1]), bf16),
            shape((images, 8, pixels), f32),
            shape((number, depth, width), f32),
        ],
        in_specs=[inside] * 10 + [anywhere] * 2,
        out_specs=[inside] * 2 + [anywhere],
        scratch_shapes=[
            pltpu.VMEM((CHANNELS + 16, latents), f32),
            pltpu.VMEM((CHANNELS, latents), bf16),
            pltpu.VMEM((latents, CHANNELS), bf16),
            pltpu.VMEM((8, latents), f32),
            pltpu.VMEM((count, tall, rows), bf16),
            pltpu.VMEM((count, 8, rows), f32),
            pltpu.VMEM((kinds, count, 2 * rows, depth), bf16),
            pltpu.VMEM((number, 2 * rows, width // 2), bf16),
            pltpu.VMEM((number, 2) + chunk, bf16),
            pltpu.VMEM((number, 2, count - 1) + chunk, bf16),
            pltpu.VMEM((teams, number, 2) + chunk, bf16),
            pltpu.VMEM((number, depth, width // 2), f32),
            DMA((2, number)),
            DMA((2, number)),
            DMA((2, number)),
            DMA((count - 1, 2, number)),
            DMA((count - 1, 2, number)),
            DMA((teams - 1, 2, number)),
            DMA((teams - 1, 2, number)),
            DMA((number,)),
            DMA((number,)),
            DMA((number,)),
            DMA((2, count)),
            DMA((2, count)),
        ],
        compiler_params=pltpu.CompilerParams(
            collective_id=collective_id, has_side_effects=True, vmem_limit_bytes=60 * 2**20
        ),
    )(values, codes, codes_t, selector(), table, gained, at, a, back, rows_in, xs, gs)


def peers(count):
    group, me = lax.axis_index("img"), lax.axis_index("pix")
    return [(group, lax.rem(me + d, count)) for d in range(1, count)]


def sum_kernel(
    count,
    crowd,
    t_ref,
    g_ref,
    z_ref,
    t_out,
    g_out,
    z_out,
    t_in,
    g_in,
    t_img,
    g_img,
    own_sem,
    send_sem,
    recv_sem,
    img_send,
    img_recv,
    last_send,
    last_recv,
):
    group, me = lax.axis_index("img"), lax.axis_index("pix")
    others = peers(count)
    across = [(lax.rem(group + d, crowd), me) for d in range(1, crowd)]
    greet(others + across)

    def copy(source, target, sems, index, device):
        return pltpu.make_async_remote_copy(
            source,
            target,
            sems[0].at[index],
            sems[1].at[index],
            device_id=device,
            device_id_type=MESH,
        )

    def scatter(d):
        to = others[d][1]
        sems = (send_sem, recv_sem)
        return (
            copy(t_ref.at[to], t_in.at[d], sems, (0, d), others[d]),
            copy(g_ref.at[to], g_in.at[d], sems, (1, d), others[d]),
        )

    def spread(d):
        return copy(z_ref, z_out.at[me], (send_sem, recv_sem), (2, d), others[d])

    def over(d):
        sems = (img_send, img_recv)
        return (
            copy(t_img.at[group], t_img.at[group], sems, (0, d), across[d]),
            copy(g_img.at[group], g_img.at[group], sems, (1, d), across[d]),
        )

    def gather(d):
        sems = (last_send, last_recv)
        return (
            copy(t_out.at[me], t_out.at[me], sems, (0, d), others[d]),
            copy(g_out.at[me], g_out.at[me], sems, (1, d), others[d]),
        )

    for d in range(count - 1):
        for part in scatter(d):
            part.start()
    for d in range(count - 1):
        spread(d).start()
    keep = pltpu.make_async_copy(z_ref, z_out.at[me], own_sem)
    keep.start()
    t_sum = t_ref[me].astype(f32)
    g_sum = g_ref[me]
    for d in range(count - 1):
        for part in scatter(d):
            part.wait_recv()
        t_sum = t_sum + t_in[d].astype(f32)
        g_sum = g_sum + g_in[d]
    t_img[group] = t_sum.astype(bf16)
    g_img[group] = g_sum
    for d in range(crowd - 1):
        for part in over(d):
            part.start()
    for d in range(crowd - 1):
        for part in over(d):
            part.wait_recv()
    t_sum = t_img[0].astype(f32)
    g_sum = g_img[0]
    for i in range(1, crowd):
        t_sum = t_sum + t_img[i].astype(f32)
        g_sum = g_sum + g_img[i]
    t_out[me] = t_sum.astype(bf16)
    g_out[me] = g_sum
    for d in range(count - 1):
        for part in gather(d):
            part.start()
    keep.wait()
    for d in range(count - 1):
        for part in gather(d):
            part.wait()
        for part in scatter(d):
            part.wait_send()
        spread(d).wait()
    for d in range(crowd - 1):
        for part in over(d):
            part.wait_send()


def small_sums(t, g, z, collective_id):
    count, crowd = lax.axis_size("pix"), lax.axis_size("img")
    inside = pl.BlockSpec(memory_space=pltpu.VMEM)
    return pl.pallas_call(
        functools.partial(sum_kernel, count, crowd),
        out_shape=[
            jax.ShapeDtypeStruct(t.shape, bf16),
            jax.ShapeDtypeStruct(g.shape, f32),
            jax.ShapeDtypeStruct((count,) + z.shape, bf16),
        ],
        in_specs=[inside] * 3,
        out_specs=[inside] * 3,
        scratch_shapes=[
            pltpu.VMEM((count - 1,) + t.shape[1:], bf16),
            pltpu.VMEM((count - 1,) + g.shape[1:], f32),
            pltpu.VMEM((crowd,) + t.shape[1:], bf16),
            pltpu.VMEM((crowd,) + g.shape[1:], f32),
            DMA,
            DMA((3, count - 1)),
            DMA((3, count - 1)),
            DMA((2, crowd - 1)),
            DMA((2, crowd - 1)),
            DMA((2, count - 1)),
            DMA((2, count - 1)),
        ],
        compiler_params=pltpu.CompilerParams(
            collective_id=collective_id, has_side_effects=True, vmem_limit_bytes=24 * 2**20
        ),
    )(t, g, z)


def gelu_parts(z):
    slope = (2.0 / jnp.pi) ** 0.5
    square = z * z
    bend = jnp.tanh(slope * z * (1.0 + 0.044715 * square))
    half = 0.5 * (1.0 + bend)
    return z * half, half + 0.5 * z * (1.0 - bend * bend) * slope * (1.0 + 0.134145 * square)


def latent_kernel(
    count,
    images,
    part_ref,
    stat_ref,
    own_ref,
    cot_ref,
    mix_ref,
    gain_ref,
    in_gain_ref,
    w_ref,
    out_ref,
    xs_ref,
    gs_ref,
    back_ref,
    row_ref,
    gain_out,
    in_gain_out,
    wv,
    one,
    two,
    three,
    pre,
    grad,
    flow,
    low,
    heads_q,
    kv,
    probs,
    kv_out,
    kv_in,
    cot,
    final,
    mean,
    w_sem,
    kv_send,
    kv_recv,
    gkv_send,
    gkv_recv,
    cot_own,
    cot_send,
    cot_recv,
    out_own,
    out_send,
    out_recv,
):
    rows, width = own_ref.shape
    depth = xs_ref.shape[3]
    sharers = count // images
    latents = rows * sharers
    per = count // sharers
    rows_here = latents // count
    spare = xs_ref.shape[3] - rows_here
    group, me = lax.axis_index("img"), lax.axis_index("pix")
    slot, image = lax.rem(me, sharers), me // sharers
    block = 256
    blocks = width // block
    row_block = min(rows, 64)
    up_one, down_one, m_query, m_key, m_value, m_out, up_two, down_two = range(8)
    scale = HEAD_DIM ** (-0.5)

    def load(k):
        return pltpu.make_async_copy(w_ref.at[k], wv.at[k], w_sem.at[k])

    for k in range(8):
        load(k).start()
    greet(peers(count))

    def cot_push(i):
        to = i * sharers + me // per
        return to, pltpu.make_async_remote_copy(
            cot_ref.at[i],
            cot.at[lax.rem(me, per)],
            cot_send.at[i],
            cot_recv.at[lax.rem(me, per)],
            device_id=(group, to),
            device_id_type=MESH,
        )

    def cot_keep():
        return pltpu.make_async_copy(cot_ref.at[image], cot.at[lax.rem(me, per)], cot_own)

    for i in range(images):
        to, copy = cot_push(i)

        @pl.when(to != me)
        def _():
            copy.start()

        @pl.when(to == me)
        def _():
            cot_keep().start()

    def columns(j, wide=block):
        return pl.ds(pl.multiple_of(j * wide, wide), wide)

    def over_columns(body):
        pl.loop(0, blocks)(body)

    def over_rows(body):
        @pl.loop(0, rows // row_block)
        def _(r):
            body(pl.ds(pl.multiple_of(r * row_block, 16), row_block))

    def put_x(j, c, value):
        for b in range(block // depth):
            xs_ref[j, c * (block // depth) + b] = value[:, b * depth : (b + 1) * depth]

    def centre(rows_f32):
        average = jnp.mean(rows_f32, axis=1, keepdims=True)
        centred = rows_f32 - average
        spread = jnp.mean(centred * centred, axis=1, keepdims=True)
        scale_rows = lax.rsqrt(spread + eps)
        return centred * scale_rows, scale_rows

    def norm(source, k, target):
        def body(r):
            target[r] = (centre(source[r])[0] * gain_ref[k : k + 1, :]).astype(bf16)

        over_rows(body)

    def norm_grad(source, k):
        def body(r):
            hat, scale_rows = centre(source[r])
            given = flow[r]
            gain_out[k : k + 1, :] += jnp.sum(given * hat, axis=0, keepdims=True)
            given = given * gain_ref[k : k + 1, :]
            along = jnp.mean(given * hat, axis=1, keepdims=True)
            grad[r] += scale_rows * (given - jnp.mean(given, axis=1, keepdims=True) - hat * along)

        over_rows(body)

    gain_out[...] = jnp.zeros_like(gain_out)

    top = jnp.max(stat_ref[:, 0:1, :], axis=0)
    total = jnp.zeros_like(top)
    for d in range(count):
        total = total + jnp.exp2(stat_ref[d, 0:1, :] - top) * stat_ref[d, 1:2, :]
    raw = jnp.zeros(part_ref.shape[1:], f32)
    for d in range(count):
        raw = raw + part_ref[d].astype(f32) * (jnp.exp2(stat_ref[d, 0:1, :] - top) / total)
    mean[0] = raw
    mean[1] = raw * in_gain_ref[...]
    row_ref[...] = jnp.zeros_like(row_ref)
    row_ref[0:1, :] = top + jnp.log(total) * LOG2E

    tall = count * spare
    mean_tall = mean[1]
    if tall > mean_tall.shape[0]:
        mean_tall = jnp.concatenate(
            [mean_tall, jnp.zeros((tall - mean_tall.shape[0], rows), f32)], axis=0
        )
    share_rows = -(-mean.shape[1] // count)
    share_rows = -(-share_rows // 8) * 8
    place = lax.broadcasted_iota(jnp.int32, (rows_here, rows), 0)
    source_row = lax.broadcasted_iota(jnp.int32, (rows_here, rows), 1) + slot * rows
    for o in range(count):
        picks = jnp.where(place + o * rows_here == source_row, 1.0, 0.0)
        piece = [picks, mean_tall[o * share_rows : (o + 1) * share_rows]]
        if spare > share_rows:
            piece.append(jnp.zeros((spare - share_rows, rows), f32))
        xs_ref[6, o] = jnp.concatenate(piece, axis=0).T.astype(bf16)

    mean_low = mean[1].astype(bf16)

    @over_columns
    def _(j):
        one[:, columns(j)] = own_ref[:, columns(j)] + mm_tn(mean_low, mix_ref[:, columns(j)])

    def feed(source, target, k, up, down, normed, x_hidden, keep):
        norm(source, k, normed)
        load(up).wait()

        @over_columns
        def _(j):
            value = mm_nt(normed[...], wv[up, columns(j), :])
            pre[keep, :, columns(j)] = value
            hidden = gelu_parts(value)[0].astype(bf16)
            low[:, columns(j)] = hidden
            put_x(x_hidden, j, hidden)

        load(down).wait()

        @over_columns
        def _(j):
            value = source[:, columns(j)] + mm(low[...], wv[down, :, columns(j)])
            target[:, columns(j)] = value.astype(target.dtype)

    def feed_back(source, k, up, down, branch, x_pre, keep):
        @over_columns
        def _(j):
            value = mm_nt(branch[...], wv[down, columns(j), :])
            value = (value * gelu_parts(pre[keep, :, columns(j)])[1]).astype(bf16)
            low[:, columns(j)] = value
            put_x(x_pre, j, value)

        @over_columns
        def _(j):
            flow[:, columns(j)] = mm(low[...], wv[up, :, columns(j)])

        norm_grad(source, k)

    feed(one, two, 0, up_one, down_one, gs_ref.at[4], 3, 0)

    norm(two, 1, low)

    def write_blocks(j, value):
        put_x(0, j, value)

    @over_columns
    def _(j):
        write_blocks(j, low[:, columns(j)])

    load(m_key).wait()
    load(m_value).wait()

    @over_columns
    def _(j):
        kv[0, slot, :, columns(j)] = mm(low[...], wv[m_key, :, columns(j)]).astype(bf16)
        kv[1, slot, :, columns(j)] = mm(low[...], wv[m_value, :, columns(j)]).astype(bf16)

    def sharer(d):
        return (group, image * sharers + lax.rem(slot + d, sharers))

    def kv_push(d):
        return pltpu.make_async_remote_copy(
            kv.at[:, slot],
            kv.at[:, slot],
            kv_send.at[d - 1],
            kv_recv.at[d - 1],
            device_id=sharer(d),
            device_id_type=MESH,
        )

    for d in range(1, sharers):
        kv_push(d).start()
    load(m_query).wait()

    @over_columns
    def _(j):
        heads_q[:, columns(j)] = mm(low[...], wv[m_query, :, columns(j)]).astype(bf16)

    for d in range(1, sharers):
        kv_push(d).wait_recv()

    @pl.loop(0, HEADS)
    def _(h):
        c = columns(h, HEAD_DIM)
        k_all = kv[0, :, :, c].reshape(latents, HEAD_DIM)
        v_all = kv[1, :, :, c].reshape(latents, HEAD_DIM)
        scores = mm_nt(heads_q[:, c], k_all) * scale
        shifted = jnp.exp(scores - jnp.max(scores, axis=1, keepdims=True))
        p = shifted / jnp.sum(shifted, axis=1, keepdims=True)
        probs[h] = p
        low[:, c] = mm(p.astype(bf16), v_all).astype(bf16)

    @over_columns
    def _(j):
        put_x(1, j, low[:, columns(j)])

    load(m_out).wait()

    @over_columns
    def _(j):
        three[:, columns(j)] = two[:, columns(j)] + mm(low[...], wv[m_out, :, columns(j)])

    feed(three, final, 2, up_two, down_two, gs_ref.at[6], 5, 1)

    def out_push(b):
        to = slot * per + b
        return to, pltpu.make_async_remote_copy(
            final.at[pl.ds(b * rows_here, rows_here)],
            out_ref.at[image],
            out_send.at[b],
            out_recv.at[image],
            device_id=(group, to),
            device_id_type=MESH,
        )

    def out_keep():
        mine = pl.ds(pl.multiple_of(lax.rem(me, per) * rows_here, 16), rows_here)
        return pltpu.make_async_copy(final.at[mine], out_ref.at[image], out_own)

    for b in range(per):
        to, copy = out_push(b)

        @pl.when(to != me)
        def _():
            copy.start()

        @pl.when(to == me)
        def _():
            out_keep().start()

    def cot_from(b):
        return pltpu.make_async_remote_copy(
            cot_ref.at[0],
            cot.at[b],
            cot_send.at[0],
            cot_recv.at[b],
            device_id=(group, me),
            device_id_type=MESH,
        )

    for b in range(per):

        @pl.when(slot * per + b != me)
        def _():
            cot_from(b).wait_recv()

        @pl.when(slot * per + b == me)
        def _():
            cot_keep().wait()

    given = cot[...].reshape(rows, width)
    gs_ref[7] = given
    grad[...] = given.astype(f32)
    feed_back(three, 2, up_two, down_two, gs_ref.at[7], 4, 1)

    gs_ref[3] = grad[...].astype(bf16)

    @over_columns
    def _(j):
        low[:, columns(j)] = mm_nt(gs_ref[3], wv[m_out, columns(j), :]).astype(bf16)

    @pl.loop(0, HEADS)
    def _(h):
        c = columns(h, HEAD_DIM)
        k_all = kv[0, :, :, c].reshape(latents, HEAD_DIM)
        v_all = kv[1, :, :, c].reshape(latents, HEAD_DIM)
        p = probs[h]
        g_mixed = low[:, c]
        g_p = mm_nt(g_mixed, v_all)
        g_v = mm_tn(p.astype(bf16), g_mixed)
        delta = jnp.sum(p * g_p, axis=1, keepdims=True)
        g_s = (p * (g_p - delta)).astype(bf16)
        gs_ref[0, :, c] = (mm(g_s, k_all) * scale).astype(bf16)
        g_k = mm_tn(g_s, heads_q[:, c]) * scale
        kv_out[:, 0, :, c] = g_k.reshape(sharers, rows, HEAD_DIM).astype(bf16)
        kv_out[:, 1, :, c] = g_v.reshape(sharers, rows, HEAD_DIM).astype(bf16)

    def gkv_push(d):
        to = lax.rem(slot + d, sharers)
        return pltpu.make_async_remote_copy(
            kv_out.at[to],
            kv_in.at[d - 1],
            gkv_send.at[d - 1],
            gkv_recv.at[d - 1],
            device_id=sharer(d),
            device_id_type=MESH,
        )

    for d in range(1, sharers):
        gkv_push(d).start()

    @over_columns
    def _(j):
        flow[:, columns(j)] = mm_nt(gs_ref[0], wv[m_query, columns(j), :])

    for d in range(1, sharers):
        gkv_push(d).wait_recv()
    for which in range(2):

        @over_columns
        def _(j):
            value = kv_out[slot, which, :, columns(j)].astype(f32)
            for d in range(1, sharers):
                value = value + kv_in[d - 1, which, :, columns(j)].astype(f32)
            gs_ref[1 + which, :, columns(j)] = value.astype(bf16)

    @over_columns
    def _(j):
        flow[:, columns(j)] += mm_nt(gs_ref[1], wv[m_key, columns(j), :]) + mm_nt(
            gs_ref[2], wv[m_value, columns(j), :]
        )

    norm_grad(two, 1)
    gs_ref[5] = grad[...].astype(bf16)
    feed_back(one, 0, up_one, down_one, gs_ref.at[5], 2, 0)
    gs_ref[8] = grad[...].astype(bf16)
    back = mm_nt(mix_ref[...], gs_ref[8])
    back_ref[...] = back.astype(bf16)
    row_ref[1:2, :] = jnp.sum(back * mean[1], axis=0, keepdims=True)
    in_gain_out[...] = jnp.broadcast_to(
        jnp.sum(back * mean[0], axis=1, keepdims=True), in_gain_out.shape
    )

    for i in range(images):
        to, copy = cot_push(i)

        @pl.when(to != me)
        def _():
            copy.wait_send()

    for d in range(1, sharers):
        kv_push(d).wait_send()
        gkv_push(d).wait_send()

    def out_from(i):
        return pltpu.make_async_remote_copy(
            final.at[pl.ds(0, rows_here)],
            out_ref.at[i],
            out_send.at[0],
            out_recv.at[i],
            device_id=(group, me),
            device_id_type=MESH,
        )

    for b in range(per):
        to, copy = out_push(b)

        @pl.when(to != me)
        def _():
            copy.wait_send()

    for i in range(images):
        owner = i * sharers + me // per

        @pl.when(owner != me)
        def _():
            out_from(i).wait_recv()

        @pl.when(owner == me)
        def _():
            out_keep().wait()


def latent_pass(parts, stats, own, cotangent, mix, gains, in_gain, whole, collective_id):
    count = lax.axis_size("pix")
    images, rows_here, width = cotangent.shape
    rows = own.shape[0]
    channels = mix.shape[0]
    depth = width // count
    sharers = count // images
    per = count // sharers
    inside = pl.BlockSpec(memory_space=pltpu.VMEM)
    anywhere = pl.BlockSpec(memory_space=pl.ANY)
    whole_f32 = pltpu.VMEM((rows, width), f32)
    whole_low = pltpu.VMEM((rows, width), bf16)
    shape = jax.ShapeDtypeStruct
    return pl.pallas_call(
        functools.partial(latent_kernel, count, images),
        out_shape=[
            shape((images, rows_here, width), bf16),
            shape((7, count, rows, depth), bf16),
            shape((9, rows, width), bf16),
            shape((channels, rows), bf16),
            shape((8, rows), f32),
            shape((8, width), f32),
            shape((channels, 128), f32),
        ],
        in_specs=[inside, inside, inside, anywhere, inside, inside, inside, anywhere],
        out_specs=[anywhere] + [inside] * 6,
        scratch_shapes=[
            pltpu.VMEM((8, width, width), bf16),
            whole_f32,
            whole_f32,
            whole_f32,
            pltpu.VMEM((2, rows, width), f32),
            whole_f32,
            whole_f32,
            whole_low,
            whole_low,
            pltpu.VMEM((2, sharers, rows, width), bf16),
            pltpu.VMEM((HEADS, rows, rows * sharers), f32),
            pltpu.VMEM((sharers, 2, rows, width), bf16),
            pltpu.VMEM((max(sharers - 1, 1), 2, rows, width), bf16),
            pltpu.VMEM((per, rows_here, width), bf16),
            whole_low,
            pltpu.VMEM((2, channels, rows), f32),
            DMA((8,)),
            DMA((sharers,)),
            DMA((sharers,)),
            DMA((sharers,)),
            DMA((sharers,)),
            DMA,
            DMA((images,)),
            DMA((per,)),
            DMA,
            DMA((per,)),
            DMA((images,)),
        ],
        compiler_params=pltpu.CompilerParams(
            collective_id=collective_id, has_side_effects=True, vmem_limit_bytes=60 * 2**20
        ),
    )(parts, stats, own, cotangent, mix, gains, in_gain, whole)


def norm_back(resid, gain, grad):
    _, back = jax.vjp(layer_norm, resid, gain)
    return back(grad)


def local(
    rgb_pixels,
    keep_mask,
    latent_array,
    gain_input,
    gain_latent,
    w_query,
    w_key,
    w_value,
    w_cross_out,
    gain_mlp_one,
    w_up_one,
    w_down_one,
    gain_self,
    w_self_query,
    w_self_key,
    w_self_value,
    w_self_out,
    gain_mlp_two,
    w_up_two,
    w_down_two,
    cotangent,
):
    images, _, pixels = rgb_pixels.shape
    rows_here, width = latent_array.shape
    count = lax.axis_size("pix")
    me = lax.axis_index("pix")
    latents = rows_here * count
    sharers = count // images
    rows_own = latents // sharers
    slot = me % sharers
    depth = w_query.shape[0]
    channels = gain_input.shape[0]
    width_scale = width ** (-0.5)
    tall = -(-channels // 16) * 16

    side = -(-channels // 512) * 512
    key_t = jnp.pad(w_key.T, ((0, 0), (0, side - channels)))
    value_out = lax.psum(mm(w_value, w_cross_out).astype(bf16), "pix")
    shards = jnp.stack(
        [
            w_up_one.T,
            w_down_one,
            w_self_query,
            w_self_key,
            w_self_value,
            w_self_out,
            w_up_two.T,
            w_down_two,
        ]
    )

    lines = pixels // SIDE
    u, sin_u, cos_u = angles(me * lines + lax.iota(jnp.int32, lines))
    w, sin_w, cos_w = angles(lax.iota(jnp.int32, SIDE))

    def zeros(rows, columns):
        return jnp.zeros((rows, columns), f32)

    pad = CHANNELS - 4 - SIDE - lines
    table = jnp.concatenate(
        [
            jnp.concatenate(
                [zeros(SIDE, 4), w, zeros(SIDE, BANDS), sin_w, zeros(SIDE, BANDS), cos_w], axis=1
            ),
            jnp.concatenate(
                [zeros(lines, 3), u, zeros(lines, 1), sin_u, zeros(lines, BANDS), cos_u, zeros(lines, BANDS)],
                axis=1,
            ),
            zeros(pad, channels),
            jnp.eye(3, channels, dtype=f32),
            jnp.ones((1, channels), f32),
        ],
        axis=0,
    )
    row_sum = u[:, 0] + jnp.sum(sin_u + cos_u, axis=1)
    col_sum = w[:, 0] + jnp.sum(sin_w + cos_w, axis=1)
    row_square = u[:, 0] ** 2 + jnp.sum(sin_u**2 + cos_u**2, axis=1)
    col_square = w[:, 0] ** 2 + jnp.sum(sin_w**2 + cos_w**2, axis=1)
    feature_sum = (row_sum[:, None] + col_sum[None, :]).reshape(1, pixels)
    feature_square = (row_square[:, None] + col_square[None, :]).reshape(1, pixels)
    colours = rgb_pixels.astype(f32)
    average = (jnp.sum(colours, axis=1) + feature_sum) / channels
    spread = (jnp.sum(colours**2, axis=1) + feature_square) / channels - average**2
    scale = lax.rsqrt(spread + eps)
    keep = keep_mask.astype(f32)

    own_values = jnp.concatenate([colours, -average[:, None, :]], axis=1) * scale[:, None, :]
    values = jnp.concatenate(
        [scale[:, None], keep[:, None], jnp.zeros((images, 2, pixels), f32), own_values], axis=1
    )
    gained = table * gain_input[None, :]
    (
        latent_full,
        query_mat,
        key_full,
        whole,
        latent_normed,
        queries,
        score_mat,
        at,
        a_low,
        raw_parts,
        stat_parts,
    ) = forward_pass(
        values,
        jnp.pad(table.T, ((0, tall - channels), (0, 0))),
        jnp.pad(gained, ((0, 0), (0, side - channels))),
        gain_latent,
        latent_array[None],
        w_query[None],
        key_t[None],
        shards,
        0,
    )
    latent_float = latent_full.reshape(latents, width).astype(f32)
    query_mat = query_mat.reshape(width, width)
    key_mat = key_full.reshape(width, side)[:, :channels].T
    score_mat = score_mat[:, :channels]
    whole = whole.reshape(8, width, width)

    own = lax.dynamic_slice_in_dim(latent_float, slot * rows_own, rows_own, 0)
    latent_out, xs, gs, back_t, row_stats, gain_grads, in_gain = latent_pass(
        raw_parts,
        stat_parts,
        own,
        cotangent,
        jnp.pad(value_out, ((0, tall - channels), (0, 0))),
        jnp.stack([gain_mlp_one, gain_self, gain_mlp_two]),
        jnp.pad(gain_input, (0, tall - channels))[:, None],
        whole,
        4,
    )
    across = -(-channels // 128) * 128
    grad_raw, pixel_out, summed = backward_pass(
        values,
        jnp.pad(table, ((0, 0), (0, across - channels))),
        jnp.pad(gained, ((0, 0), (0, tall - channels))),
        at,
        a_low,
        back_t,
        row_stats,
        xs,
        gs,
        2,
    )
    moved = (pixel_out[:, 4:7] - pixel_out[:, 7:8] / channels) - (
        (colours - average[:, None, :]) * scale[:, None, :]
    ) * (pixel_out[:, 0:1] / channels)
    grad_pixels = moved * (scale * keep)[:, None, :]

    cells = -(-(3 * width + channels) // (count * 1024)) * 1024
    loose = jnp.concatenate([gain_grads[:3].reshape(-1), in_gain[:channels, 0]])
    loose = jnp.pad(loose, (0, count * cells - loose.shape[0])).reshape(count, 8, cells // 8)
    share_rows = -(-(-(-tall // count)) // 8) * 8
    rest = summed[8]
    spare = -(-share_rows // 16) * 16
    cross_rows = jnp.pad(
        rest[rows_here : rows_here + share_rows].astype(bf16), ((0, spare - share_rows), (0, 0))
    )
    grad_raw, loose, cross_sum = small_sums(
        grad_raw.reshape(count, rows_here, across),
        loose,
        cross_rows,
        6,
    )
    grad_raw = grad_raw.reshape(latents, across)[:, :channels].astype(f32)
    loose = loose.reshape(-1)
    gain_one, gain_attn, gain_two = [loose[k * width : (k + 1) * width] for k in range(3)]
    gain_in = loose[3 * width : 3 * width + channels] + jnp.sum(score_mat * grad_raw, axis=0)
    cross_sum = cross_sum[:, :share_rows].reshape(-1, width)[:channels]

    grad_x = (grad_raw * (gain_input * width_scale)[None, :]).astype(bf16)
    query_grad = mm(grad_x, key_mat).astype(bf16)
    latent_cols = lax.dynamic_slice_in_dim(latent_normed, me * depth, depth, 1)
    grad_w_query = mm_tn(latent_cols, query_grad)
    grad_latent_full, grad_gain_latent = norm_back(
        latent_float, gain_latent, mm_nt(query_grad, query_mat)
    )
    grad_latent_own = lax.dynamic_slice_in_dim(grad_latent_full, me * rows_here, rows_here, 0)
    key_cols = w_key.shape[1]
    grad_w_key = mm_tn(grad_x, lax.dynamic_slice_in_dim(queries, me * key_cols, key_cols, 1))

    g_sq, g_sk, g_sv, g_so, g_up_one, g_down_one, g_up_two, g_down_two, rest = [
        summed[k] for k in range(9)
    ]
    grad_w_value = mm_nt(cross_sum, w_cross_out)
    grad_w_cross_out = mm_tn(w_value, cross_sum)
    grad_latent_array = rest[:rows_here] + grad_latent_own
    return (
        latent_out,
        grad_pixels,
        grad_latent_array,
        gain_in,
        grad_gain_latent,
        grad_w_query,
        grad_w_key,
        grad_w_value,
        grad_w_cross_out,
        gain_one,
        g_up_one.T,
        g_down_one,
        gain_attn,
        g_sq,
        g_sk,
        g_sv,
        g_so,
        gain_two,
        g_up_two.T,
        g_down_two,
    )


def solution(mesh):
    rows, columns, copied = P("pix", None), P(None, "pix"), P()
    return jax.shard_map(
        local,
        mesh=mesh,
        in_specs=(
            P("img", None, "pix"),
            P("img", "pix"),
            rows,
            copied,
            copied,
            rows,
            columns,
            columns,
            rows,
            copied,
            columns,
            rows,
            copied,
            rows,
            rows,
            rows,
            rows,
            copied,
            columns,
            rows,
            P("img", "pix", None),
        ),
        out_specs=(
            P("img", "pix", None),
            P("img", None, "pix"),
            rows,
            copied,
            copied,
            rows,
            columns,
            columns,
            rows,
            copied,
            columns,
            rows,
            copied,
            rows,
            rows,
            rows,
            rows,
            copied,
            columns,
            rows,
        ),
        check_vma=False,
    )
```

```python
import functools

import jax
import jax.numpy as jnp
from jax import lax
from jax.experimental import pallas as pl
from jax.experimental.pallas import tpu as pltpu
from jax.sharding import PartitionSpec as P

HEADS = 8
HEAD_DIM = 128
BANDS = 64
SIDE = 224
CHANNELS = 256
LOG2E = 1.4426950408889634

eps = 1e-05
f32 = jnp.float32
bf16 = jnp.bfloat16


def exact(left, right):
    return jnp.dot(left, right, precision=lax.Precision.HIGHEST, preferred_element_type=f32)


def mm(left, right):
    return jnp.dot(left, right, preferred_element_type=f32)


def mm_nt(left, right):
    return lax.dot_general(left, right, (((1,), (1,)), ((), ())), preferred_element_type=f32)


def mm_tn(left, right):
    return lax.dot_general(left, right, (((0,), (0,)), ((), ())), preferred_element_type=f32)


def layer_norm(rows, gain):
    average = jnp.mean(rows, axis=-1, keepdims=True)
    centred = rows - average
    spread = jnp.mean(centred * centred, axis=-1, keepdims=True)
    return centred * lax.rsqrt(spread + eps) * gain


def angles(index):
    place = index.astype(f32) * (2.0 / (SIDE - 1)) - 1.0
    steps = lax.iota(jnp.int32, BANDS).astype(f32)
    frequency = 1.0 + steps * ((SIDE / 2.0 - 1.0) / (BANDS - 1))
    angle = jnp.pi * place[:, None] * frequency[None, :]
    return place[:, None], jnp.sin(angle), jnp.cos(angle)


def pixel_tile(pixels):
    return 896 if pixels % 896 == 0 else pixels


MESH = pl.DeviceIdType.MESH
DMA = pltpu.SemaphoreType.DMA


def ring_place(count):
    me = lax.axis_index("pix")
    return jnp.where(me % 2 == 0, me // 2, count - 1 - me // 2)


def ring_device(place, count):
    place = lax.rem(place + 2 * count, count)
    return jnp.where(place < count // 2, 2 * place, 2 * (count - 1 - place) + 1)


def greet(devices):
    barrier = pltpu.get_barrier_semaphore()
    for device in devices:
        pl.semaphore_signal(barrier, inc=1, device_id=device, device_id_type=MESH)
    pl.semaphore_wait(barrier, len(devices))


def hot_codes(tile):
    pixel = lax.broadcasted_iota(jnp.int32, (CHANNELS, tile), 1)
    channel = lax.broadcasted_iota(jnp.int32, (CHANNELS, tile), 0)
    start = channel - SIDE - pixel // SIDE
    code = jnp.where((start >= 0) & (channel < CHANNELS - 4), start, -2)
    return jnp.where(channel < SIDE, jnp.where(channel == pixel % SIDE, -1, -2), code)


def build_xt(values, base, code_ref):
    code = code_ref[...]
    hot = jnp.where((code == -1) | (code == base), values[0:1, :], 0.0)
    last = hot[CHANNELS - 8 :, :]
    k = lax.broadcasted_iota(jnp.int32, last.shape, 0)
    last = jnp.where(k >= 4, values, last)
    return jnp.concatenate([hot[: CHANNELS - 8, :], last], axis=0)


def build_both(values, base, code_ref):
    keep = values[1:2, :]
    xt = build_xt(values, base, code_ref).astype(bf16)
    k = lax.broadcasted_iota(jnp.int32, (16, values.shape[1]), 0)
    ones = jnp.where(k == 0, keep, 0.0).astype(bf16)
    return xt.T, jnp.concatenate([xt * keep.astype(bf16), ones], axis=0)


def forward_kernel(
    count,
    images,
    tile,
    v_ref,
    code_ref,
    table_ref,
    gained_ref,
    gain_ref,
    lat_ref,
    wq_ref,
    wk_ref,
    w_ref,
    lat_full,
    wq_full,
    wk_full,
    w_full,
    normed_ref,
    query_ref,
    a_ref,
    at_ref,
    alow_ref,
    part_ref,
    stat_ref,
    lat_v,
    wq_v,
    wk_v,
    acc,
    top,
    u_send,
    s_send,
    own_sem,
    load_sem,
    send_sem,
    recv_sem,
    hand_send,
    hand_recv,
    u_own,
    u_out,
    u_in,
):
    pixels = v_ref.shape[2]
    steps = pixels // tile
    lines = tile // SIDE
    owners = Owners(count, images)
    sharers = owners.sharers
    rows = part_ref.shape[2]
    width = wq_ref.shape[2]
    latents = normed_ref.shape[0]
    group, me = lax.axis_index("img"), lax.axis_index("pix")
    core = lax.rem(group, 2)
    place = ring_place(count)
    sides = ((group, ring_device(place + 1, count)), (group, ring_device(place - 1, count)))
    other = (group + 1 - 2 * core, me)
    greet(plane(count))
    sources = (lat_ref, wq_ref, wk_ref, w_ref)
    fulls = (lat_full, wq_full, wk_full, w_full)
    mats = w_ref.shape[0]

    def spot(a, k, stage, way, source):
        wide = sources[a].shape[2] // 4
        columns = pl.ds(pl.multiple_of((core * 2 + way) * wide, 128), wide)
        if source:
            return sources[a].at[k, :, columns]
        origin = ring_device(place - stage if way == 0 else place + stage, count)
        return fulls[a].at[k, origin, :, columns]

    def hop(a, k, stage, way, first=False):
        return pltpu.make_async_remote_copy(
            spot(a, k, stage, way, first),
            spot(a, k, stage, way, False),
            send_sem.at[stage, way, a + k],
            recv_sem.at[stage, way, a + k],
            device_id=sides[way],
            device_id_type=MESH,
        )

    def hand(a, k, stage, way):
        part = spot(a, k, stage, way, False)
        return pltpu.make_async_remote_copy(
            part,
            part,
            hand_send.at[stage - 1, way, a + k],
            hand_recv.at[stage - 1, way, a + k],
            device_id=other,
            device_id_type=MESH,
        )

    def relay(a, k, stage, onward=True):
        for way in range(2):
            hop(a, k, stage - 1, way).wait_recv()
            if onward:
                hop(a, k, stage, way).start()
            hand(a, k, stage, way).start()

    own = [
        pltpu.make_async_copy(sources[a], fulls[a].at[:, me], own_sem.at[a]) for a in range(4)
    ]
    for a in range(3):
        for way in range(2):
            hop(a, 0, 0, way, True).start()
    for copy in own:
        copy.start()
    for stage in range(1, count):
        for a in range(3):
            relay(a, 0, stage, stage < count - 1)
        if stage <= mats:
            for way in range(2):
                hop(3, stage - 1, 0, way, True).start()
    for k in range(count - 1, mats):
        for way in range(2):
            hop(3, k, 0, way, True).start()
    for a in range(3):
        own[a].wait()
        for stage in range(1, count):
            for way in range(2):
                hand(a, 0, stage, way).wait_recv()

    loads = [
        pltpu.make_async_copy(full.at[0], held, load_sem.at[j])
        for j, (full, held) in enumerate(((lat_full, lat_v), (wq_full, wq_v), (wk_full, wk_v)))
    ]
    for copy in loads:
        copy.start()
    loads[0].wait()
    rows_here = lat_v.shape[1]

    @pl.loop(0, count)
    def _(o):
        block = lat_v[o].astype(f32)
        average = jnp.mean(block, axis=1, keepdims=True)
        centred = block - average
        spread = jnp.mean(centred * centred, axis=1, keepdims=True)
        normed = (centred * lax.rsqrt(spread + eps) * gain_ref[...]).astype(bf16)
        normed_ref[pl.ds(pl.multiple_of(o * rows_here, rows_here), rows_here), :] = normed

    loads[1].wait()

    @pl.loop(0, width // 256)
    def _(j):
        columns = pl.ds(pl.multiple_of(j * 256, 256), 256)
        weight = wq_v[:, :, columns].reshape(width, 256)
        query_ref[:, columns] = mm(normed_ref[...], weight).astype(bf16)

    loads[2].wait()
    a_ref[...] = mm(query_ref[...], wk_v[...].reshape(width, wk_v.shape[2])) * (width ** (-0.5))

    def exact_nt(left, right):
        return lax.dot_general(
            left,
            right,
            (((1,), (1,)), ((), ())),
            precision=lax.Precision.HIGHEST,
            preferred_element_type=f32,
        )

    at_ref[...] = (exact_nt(gained_ref[...], a_ref[...]) * LOG2E).astype(bf16)
    alow_ref[...] = exact_nt(a_ref[...], gained_ref[...]).astype(bf16)

    relays = (count - 2) * mats

    def relay_number(e):
        relay(3, lax.rem(e, mats), 1 + e // mats)

    def u_push(i, h):
        to = owners.device(group, i, jnp.int32(h))
        sems = lambda which: dict(
            send_sem=u_out.at[which, i * sharers + h],
            recv_sem=u_in.at[which, me],
            device_id=to,
            device_id_type=MESH,
        )
        return to, (
            pltpu.make_async_remote_copy(u_send.at[i, h], part_ref.at[me], **sems(0)),
            pltpu.make_async_remote_copy(s_send.at[i, h], stat_ref.at[me], **sems(1)),
        )

    def u_keep():
        i, h = owners.image, owners.slot
        return (
            pltpu.make_async_copy(u_send.at[i, h], part_ref.at[me], u_own.at[0]),
            pltpu.make_async_copy(s_send.at[i, h], stat_ref.at[me], u_own.at[1]),
        )

    @pl.loop(0, images * steps)
    def _(t):
        i, step = t // steps, lax.rem(t, steps)

        @pl.when(t < relays)
        def _():
            relay_number(t)

        @pl.when(step == 0)
        def _():
            acc[...] = jnp.zeros_like(acc)
            top[...] = jnp.full_like(top, -jnp.inf)

        values = v_ref[i, :, pl.ds(pl.multiple_of(step * tile, 128), tile)]
        base = step * lines
        x, xt = build_both(values, base, code_ref)
        first, second = slice(0, tile // 2), slice(tile // 2, tile)
        scores = [mm(x[half], at_ref[...]) for half in (first, second)]
        old, total = top[0:1, :], acc[...]
        for half, score in zip((first, second), scores):
            new = jnp.maximum(old, jnp.max(score, axis=0, keepdims=True))
            weights = jnp.exp2(score - new).astype(bf16)
            total = total * jnp.exp2(old - new) + mm(xt[:, half], weights)
            old = new
        acc[...] = total
        top[...] = jnp.broadcast_to(old, top.shape)

        @pl.when(step == steps - 1)
        def _():
            raw = jnp.dot(
                table_ref[...],
                acc[:CHANNELS, :],
                precision=lax.Precision.HIGHEST,
                preferred_element_type=f32,
            ).astype(bf16)
            stats = jnp.concatenate([top[0:1, :], acc[CHANNELS : CHANNELS + 1, :], top[0:6, :]], axis=0)
            for h in range(sharers):
                u_send[i, h] = raw[:, h * rows : (h + 1) * rows]
                s_send[i, h] = stats[:, h * rows : (h + 1) * rows]
            for h in range(sharers):
                to, copies = u_push(i, h)

                @pl.when(jnp.logical_not(owners.is_me(to)))
                def _():
                    for copy in copies:
                        copy.start()

                @pl.when(owners.is_me(to))
                def _():
                    for copy in u_keep():
                        copy.start()

    if images * steps < relays:

        @pl.loop(images * steps, relays)
        def _(e):
            relay_number(e)

    @pl.loop(0, mats)
    def _(k):
        relay(3, k, count - 1, False)

    own[3].wait()
    for a in range(3):
        for way in range(2):
            for stage in range(count - 1):
                hop(a, 0, stage, way).wait_send()
                hand(a, 0, stage + 1, way).wait_send()

    @pl.loop(0, mats)
    def _(k):
        for way in range(2):
            for stage in range(count - 1):
                hop(3, k, stage, way).wait_send()
                hand(3, k, stage + 1, way).wait()

    def u_from(source):
        sems = lambda which: dict(
            send_sem=u_out.at[which, 0],
            recv_sem=u_in.at[which, source],
            device_id=(owners.home, source),
            device_id_type=MESH,
        )
        return (
            pltpu.make_async_remote_copy(u_send.at[0, 0], part_ref.at[source], **sems(0)),
            pltpu.make_async_remote_copy(s_send.at[0, 0], stat_ref.at[source], **sems(1)),
        )

    for i in range(images):
        for h in range(sharers):
            to, copies = u_push(i, h)

            @pl.when(jnp.logical_not(owners.is_me(to)))
            def _():
                for copy in copies:
                    copy.wait_send()

    for source in range(count):
        local = owners.is_me((owners.home, source))

        @pl.when(local)
        def _():
            for copy in u_keep():
                copy.wait()

        @pl.when(jnp.logical_not(local))
        def _():
            for copy in u_from(source):
                copy.wait_recv()


def forward_pass(values, table, gained, gain_latent, lat, wq, wk, shards, collective_id):
    count = lax.axis_size("pix")
    images, _, pixels = values.shape
    tile = pixel_tile(pixels)
    rows_here, width = lat.shape[1:]
    latents = rows_here * count
    sharers = count // images
    rows = latents // sharers
    tall = table.shape[0]
    mats = shards.shape[0]
    inside = pl.BlockSpec(memory_space=pltpu.VMEM)
    anywhere = pl.BlockSpec(memory_space=pl.ANY)
    shape = jax.ShapeDtypeStruct

    def full(array):
        return shape((array.shape[0], count) + array.shape[1:], array.dtype)

    ring = DMA((count - 1, 2, 3 + mats))
    return pl.pallas_call(
        functools.partial(forward_kernel, count, images, tile),
        out_shape=[full(lat), full(wq), full(wk), full(shards)]
        + [
            shape((latents, width), bf16),
            shape((latents, width), bf16),
            shape((latents, wk.shape[2]), f32),
            shape((CHANNELS, latents), bf16),
            shape((latents, CHANNELS), bf16),
            shape((count, tall, rows), bf16),
            shape((count, 8, rows), f32),
        ],
        in_specs=[inside] * 5 + [anywhere] * 4,
        out_specs=[anywhere] * 4 + [inside] * 5 + [anywhere] * 2,
        scratch_shapes=[
            pltpu.VMEM((count,) + lat.shape[1:], bf16),
            pltpu.VMEM((count,) + wq.shape[1:], bf16),
            pltpu.VMEM((count,) + wk.shape[1:], bf16),
            pltpu.VMEM((CHANNELS + 16, latents), f32),
            pltpu.VMEM((8, latents), f32),
            pltpu.VMEM((images, sharers, tall, rows), bf16),
            pltpu.VMEM((images, sharers, 8, rows), f32),
            DMA((4,)),
            DMA((3,)),
            ring,
            ring,
            ring,
            ring,
            DMA((2,)),
            DMA((2, count)),
            DMA((2, count)),
        ],
        compiler_params=pltpu.CompilerParams(
            collective_id=collective_id, has_side_effects=True, vmem_limit_bytes=48 * 2**20
        ),
    )(values, hot_codes(tile), table, gained, gain_latent[None], lat, wq, wk, shards)


def backward_kernel(
    count,
    teams,
    images,
    tile,
    v_ref,
    code_ref,
    table_ref,
    gained_ref,
    at_ref,
    a_ref,
    back_ref,
    row_ref,
    xs_ref,
    gs_ref,
    t_ref,
    pixel_ref,
    out_ref,
    t_acc,
    bt,
    b_low,
    stat,
    back_all,
    row_all,
    xv,
    gv,
    terms,
    held,
    across,
    done,
    load_sem,
    pair_send,
    pair_recv,
    send_sem,
    recv_sem,
    cross_send,
    cross_recv,
    out_sem,
    hand_send,
    hand_recv,
    back_send,
    back_recv,
):
    number, rows, width = gs_ref.shape
    kinds = xs_ref.shape[0]
    owners = Owners(count, images)
    sharers = owners.sharers
    steps = v_ref.shape[2] // tile
    lines = tile // SIDE
    depth = xs_ref.shape[1] // count
    half, wide = width // 2, width // 4
    group, me = lax.axis_index("img"), lax.axis_index("pix")
    core, team = lax.rem(group, 2), group // 2
    place = ring_place(count)
    sides = ((group, ring_device(place + 1, count)), (group, ring_device(place - 1, count)))
    other = (group + 1 - 2 * core, me)
    partners = [(lax.rem(team + d, teams) * 2 + core, me) for d in range(1, teams)]
    greet(plane(count) + partners)

    own_index = owners.image * sharers + owners.slot

    def back_push(d):
        to = (owners.home, lax.rem(me + d, count))
        sems = lambda which: dict(
            send_sem=back_send.at[which, d],
            recv_sem=back_recv.at[which, own_index],
            device_id=to,
            device_id_type=MESH,
        )
        return to, (
            pltpu.make_async_remote_copy(back_ref, back_all.at[own_index], **sems(0)),
            pltpu.make_async_remote_copy(row_ref, row_all.at[own_index], **sems(1)),
        )

    def back_from(source):
        sems = lambda which: dict(
            send_sem=back_send.at[which, 0],
            recv_sem=back_recv.at[which, source],
            device_id=(group, me),
            device_id_type=MESH,
        )
        return (
            pltpu.make_async_remote_copy(back_ref, back_all.at[source], **sems(0)),
            pltpu.make_async_remote_copy(row_ref, row_all.at[source], **sems(1)),
        )

    for d in range(count):
        to, copies = back_push(d)

        @pl.when(jnp.logical_not(owners.is_me(to)))
        def _():
            for copy in copies:
                copy.start()

        @pl.when(owners.is_me(to))
        def _():
            back_all[own_index] = back_ref[...]
            row_all[own_index] = row_ref[...]

    def load_x(j):
        return pltpu.make_async_copy(xs_ref.at[j], xv.at[j, core], load_sem.at[0, j])

    def load_g(k):
        part = gs_ref.at[k, :, pl.ds(pl.multiple_of(core * half, 128), half)]
        return pltpu.make_async_copy(part, gv.at[k, core], load_sem.at[1, k])

    def pair_x(j):
        return pltpu.make_async_remote_copy(
            xs_ref.at[j],
            xv.at[j, core],
            pair_send.at[0, j],
            pair_recv.at[0, j],
            device_id=other,
            device_id_type=MESH,
        )

    def pair_g(k):
        part = gs_ref.at[k, :, pl.ds(pl.multiple_of((1 - core) * half, 128), half)]
        return pltpu.make_async_remote_copy(
            part,
            gv.at[k, core],
            pair_send.at[1, k],
            pair_recv.at[1, k],
            device_id=other,
            device_id_type=MESH,
        )

    for j in range(number):
        if j < kinds:
            load_x(j).start()
            pair_x(j).start()
        load_g(j).start()
        pair_g(j).start()

    def part(k, owner, way):
        here = pl.ds(pl.multiple_of(owner * depth, depth), depth)
        return terms.at[k, here, way * wide : (way + 1) * wide]

    def hop(k, stage, way, start=False):
        source = part(k, owner_at(0, way), way) if start else held.at[k, way, stage - 1]
        return pltpu.make_async_remote_copy(
            source,
            held.at[k, way, stage],
            send_sem.at[stage, way, k],
            recv_sem.at[stage, way, k],
            device_id=sides[way],
            device_id_type=MESH,
        )

    def cross(k, way, d):
        return pltpu.make_async_remote_copy(
            across.at[team, k, way],
            across.at[team, k, way],
            cross_send.at[d, way, k],
            cross_recv.at[d, way, k],
            device_id=partners[d],
            device_id_type=MESH,
        )

    def owner_at(stage, way):
        return ring_device(place - stage - 1 if way == 0 else place + stage + 1, count)

    @pl.loop(0, number)
    def _(k):
        j = jnp.maximum(k - (number - kinds), 0)

        @pl.when((k == 0) | (k > number - kinds))
        def _():
            load_x(j).wait()
            pair_x(j).wait_recv()

        load_g(k).wait()
        pair_g(k).wait_recv()
        for r in range(0, width, 256):
            piece = slice(r, r + 256)
            terms[k, piece, :] = (
                mm(xv[j, 0, piece, :], gv[k, 0]) + mm(xv[j, 1, piece, :], gv[k, 1])
            ).astype(bf16)
        for way in range(2):
            hop(k, 0, way, True).start()

    def relay(k, stage):
        for way in range(2):
            own = part(k, owner_at(stage, way), way)[...].astype(f32)
            hop(k, stage - 1, way, True).wait_recv()
            held[k, way, stage - 1] = (own + held[k, way, stage - 1].astype(f32)).astype(bf16)
            hop(k, stage, way).start()

    def relay_number(e):
        relay(lax.rem(e, number), 1 + e // number)

    relays = (count - 2) * number
    tiles = images * steps
    pace = min(2, relays // tiles)
    t_acc[...] = jnp.zeros_like(t_acc)

    @pl.loop(0, tiles)
    def _(t):
        image = lax.rem(t // steps + owners.image, images)
        step = lax.rem(t, steps)
        for e in range(pace):
            relay_number(t * pace + e)

        @pl.when(step == 0)
        def _():
            for h in range(sharers):
                source = image * sharers + h

                sender = owners.device(group, image, jnp.int32(h))

                @pl.when(jnp.logical_not(owners.is_me(sender)))
                def _():
                    for copy in back_from(source):
                        copy.wait_recv()

                here = slice(h * rows, (h + 1) * rows)
                wide = jnp.dot(
                    gained_ref[...],
                    back_all[source].astype(f32),
                    precision=lax.Precision.HIGHEST,
                    preferred_element_type=f32,
                )
                bt[:, here] = wide.astype(bf16)
                b_low[here, :] = wide.T.astype(bf16)
                stat[:, here] = row_all[source]

        span = pl.ds(pl.multiple_of(step * tile, 128), tile)
        values = v_ref[image, :, span]
        x, xt = build_both(values, step * lines, code_ref)
        halves = (slice(0, tile // 2), slice(tile // 2, tile))
        products = [(mm(x[half], at_ref[...]), mm(x[half], bt[...])) for half in halves]
        kept, ends = [], []
        for half, (scores, grad_p) in zip(halves, products):
            probs = jnp.exp2(scores - stat[0:1, :])
            grad_s = (probs * (grad_p - stat[1:2, :])).astype(bf16)
            kept.append(grad_s)
            back = mm(grad_s, a_ref[...]) + mm(probs.astype(bf16), b_low[...])
            along = jnp.sum(back * x[half].astype(f32), axis=1, keepdims=True)
            end = back[:, CHANNELS - 128 :]
            lane = lax.broadcasted_iota(jnp.int32, end.shape, 1)
            ends.append(jnp.where(lane == 120, along, end))
        t_acc[...] += mm(xt, jnp.concatenate(kept, axis=0))
        pixel_ref[image, :, span] = jnp.concatenate(ends, axis=0).T[120:128, :]

    t_ref[...] = lax.dot_general(
        t_acc[:CHANNELS, :],
        table_ref[...],
        (((0,), (0,)), ((), ())),
        precision=lax.Precision.HIGHEST,
        preferred_element_type=f32,
    ).astype(bf16)

    if tiles * pace < relays:

        @pl.loop(tiles * pace, relays)
        def _(e):
            relay_number(e)

    @pl.loop(0, number)
    def _(k):
        for way in range(2):
            own = part(k, me, way)[...].astype(f32)
            hop(k, count - 2, way, True).wait_recv()
            across[team, k, way] = (own + held[k, way, count - 2].astype(f32)).astype(bf16)
            for d in range(teams - 1):
                cross(k, way, d).start()

    def finish(k):
        columns = pl.ds(pl.multiple_of(core * half, 128), half)
        return pltpu.make_async_copy(done.at[k], out_ref.at[k, :, columns], out_sem.at[k])

    def hand(k):
        columns = pl.ds(pl.multiple_of(core * half, 128), half)
        return pltpu.make_async_remote_copy(
            done.at[k],
            out_ref.at[k, :, columns],
            hand_send.at[k],
            hand_recv.at[k],
            device_id=other,
            device_id_type=MESH,
        )

    @pl.loop(0, number)
    def _(k):
        for way in range(2):
            for d in range(teams - 1):
                cross(k, way, d).wait_recv()
            total = across[0, k, way].astype(f32)
            for t in range(1, teams):
                total = total + across[t, k, way].astype(f32)
            done[k, :, way * wide : (way + 1) * wide] = total
        finish(k).start()
        hand(k).start()

    @pl.loop(0, number)
    def _(k):
        finish(k).wait()
        hand(k).wait()
        pair_g(k).wait_send()
        for way in range(2):
            for stage in range(count - 1):
                hop(k, stage, way, stage == 0).wait_send()
            for d in range(teams - 1):
                cross(k, way, d).wait_send()

    @pl.loop(0, kinds)
    def _(j):
        pair_x(j).wait_send()

    for d in range(count):
        to, copies = back_push(d)

        @pl.when(jnp.logical_not(owners.is_me(to)))
        def _():
            for copy in copies:
                copy.wait_send()


def backward_pass(values, table, gained, at, a, back, rows_in, xs, gs, collective_id):
    count = lax.axis_size("pix")
    teams = lax.axis_size("img") // 2
    kinds, _, rows = xs.shape
    number, _, width = gs.shape
    depth = xs.shape[1] // count
    anywhere = pl.BlockSpec(memory_space=pl.ANY)
    inside = pl.BlockSpec(memory_space=pltpu.VMEM)
    chunk = (depth, width // 4)
    images, _, pixels = values.shape
    tile = pixel_tile(pixels)
    latents = at.shape[1]
    tall = back.shape[0]
    shape = jax.ShapeDtypeStruct
    return pl.pallas_call(
        functools.partial(backward_kernel, count, teams, images, tile),
        out_shape=[
            shape((latents, table.shape[1]), bf16),
            shape((images, 8, pixels), f32),
            shape((number, depth, width), f32),
        ],
        in_specs=[inside] * 8 + [anywhere] * 2,
        out_specs=[inside] * 2 + [anywhere],
        scratch_shapes=[
            pltpu.VMEM((CHANNELS + 16, latents), f32),
            pltpu.VMEM((CHANNELS, latents), bf16),
            pltpu.VMEM((latents, CHANNELS), bf16),
            pltpu.VMEM((8, latents), f32),
            pltpu.VMEM((count, tall, rows), bf16),
            pltpu.VMEM((count, 8, rows), f32),
            pltpu.VMEM((kinds, 2, xs.shape[1], rows), bf16),
            pltpu.VMEM((number, 2, rows, width // 2), bf16),
            pltpu.VMEM((number, xs.shape[1], width // 2), bf16),
            pltpu.VMEM((number, 2, count - 1) + chunk, bf16),
            pltpu.VMEM((teams, number, 2) + chunk, bf16),
            pltpu.VMEM((number, depth, width // 2), f32),
            DMA((2, number)),
            DMA((2, number)),
            DMA((2, number)),
            DMA((count - 1, 2, number)),
            DMA((count - 1, 2, number)),
            DMA((teams - 1, 2, number)),
            DMA((teams - 1, 2, number)),
            DMA((number,)),
            DMA((number,)),
            DMA((number,)),
            DMA((2, count)),
            DMA((2, count)),
        ],
        compiler_params=pltpu.CompilerParams(
            collective_id=collective_id, has_side_effects=True, vmem_limit_bytes=60 * 2**20
        ),
    )(values, hot_codes(tile), table, gained, at, a, back, rows_in, xs, gs)


def peers(count):
    group, me = lax.axis_index("img"), lax.axis_index("pix")
    return [(group, lax.rem(me + d, count)) for d in range(1, count)]


def plane(count):
    group, me = lax.axis_index("img"), lax.axis_index("pix")
    other = group + 1 - 2 * lax.rem(group, 2)
    return peers(count) + [(other, lax.rem(me + d, count)) for d in range(count)]


class Owners:
    def __init__(self, count, images):
        self.group, self.me = lax.axis_index("img"), lax.axis_index("pix")
        self.core = lax.rem(self.group, 2)
        self.base = self.group - self.core
        self.images = images
        self.chips = count // (2 * images)
        self.sharers = 2 * self.chips
        self.slot = lax.rem(self.me, self.chips) * 2 + self.core
        image = self.me // self.chips
        self.image = lax.rem(image, images)
        self.home = self.base + image // images

    def device(self, group, image, slot):
        core = lax.rem(group, 2)
        chip = (core * self.images + image) * self.chips + slot // 2
        return self.base + lax.rem(slot, 2), chip

    def is_me(self, device):
        return (device[0] == self.group) & (device[1] == self.me)


def sum_kernel(
    count,
    crowd,
    t_ref,
    g_ref,
    z_ref,
    t_out,
    g_out,
    z_out,
    t_in,
    g_in,
    t_img,
    g_img,
    own_sem,
    send_sem,
    recv_sem,
    img_send,
    img_recv,
    last_send,
    last_recv,
):
    group, me = lax.axis_index("img"), lax.axis_index("pix")
    others = peers(count)
    across = [(lax.rem(group + d, crowd), me) for d in range(1, crowd)]
    greet(others + across)

    def copy(source, target, sems, index, device):
        return pltpu.make_async_remote_copy(
            source,
            target,
            sems[0].at[index],
            sems[1].at[index],
            device_id=device,
            device_id_type=MESH,
        )

    def scatter(d):
        to = others[d][1]
        sems = (send_sem, recv_sem)
        return (
            copy(t_ref.at[to], t_in.at[d], sems, (0, d), others[d]),
            copy(g_ref.at[to], g_in.at[d], sems, (1, d), others[d]),
        )

    def spread(d):
        return copy(z_ref, z_out.at[me], (send_sem, recv_sem), (2, d), others[d])

    def over(d):
        sems = (img_send, img_recv)
        return (
            copy(t_img.at[group], t_img.at[group], sems, (0, d), across[d]),
            copy(g_img.at[group], g_img.at[group], sems, (1, d), across[d]),
        )

    def gather(d):
        sems = (last_send, last_recv)
        return (
            copy(t_out.at[me], t_out.at[me], sems, (0, d), others[d]),
            copy(g_out.at[me], g_out.at[me], sems, (1, d), others[d]),
        )

    for d in range(count - 1):
        for part in scatter(d):
            part.start()
    for d in range(count - 1):
        spread(d).start()
    keep = pltpu.make_async_copy(z_ref, z_out.at[me], own_sem)
    keep.start()
    t_sum = t_ref[me].astype(f32)
    g_sum = g_ref[me]
    for d in range(count - 1):
        for part in scatter(d):
            part.wait_recv()
        t_sum = t_sum + t_in[d].astype(f32)
        g_sum = g_sum + g_in[d]
    t_img[group] = t_sum.astype(bf16)
    g_img[group] = g_sum
    for d in range(crowd - 1):
        for part in over(d):
            part.start()
    for d in range(crowd - 1):
        for part in over(d):
            part.wait_recv()
    t_sum = t_img[0].astype(f32)
    g_sum = g_img[0]
    for i in range(1, crowd):
        t_sum = t_sum + t_img[i].astype(f32)
        g_sum = g_sum + g_img[i]
    t_out[me] = t_sum.astype(bf16)
    g_out[me] = g_sum
    for d in range(count - 1):
        for part in gather(d):
            part.start()
    keep.wait()
    for d in range(count - 1):
        for part in gather(d):
            part.wait()
        for part in scatter(d):
            part.wait_send()
        spread(d).wait()
    for d in range(crowd - 1):
        for part in over(d):
            part.wait_send()


def small_sums(t, g, z, collective_id):
    count, crowd = lax.axis_size("pix"), lax.axis_size("img")
    inside = pl.BlockSpec(memory_space=pltpu.VMEM)
    return pl.pallas_call(
        functools.partial(sum_kernel, count, crowd),
        out_shape=[
            jax.ShapeDtypeStruct(t.shape, bf16),
            jax.ShapeDtypeStruct(g.shape, f32),
            jax.ShapeDtypeStruct((count,) + z.shape, bf16),
        ],
        in_specs=[inside] * 3,
        out_specs=[inside] * 3,
        scratch_shapes=[
            pltpu.VMEM((count - 1,) + t.shape[1:], bf16),
            pltpu.VMEM((count - 1,) + g.shape[1:], f32),
            pltpu.VMEM((crowd,) + t.shape[1:], bf16),
            pltpu.VMEM((crowd,) + g.shape[1:], f32),
            DMA,
            DMA((3, count - 1)),
            DMA((3, count - 1)),
            DMA((2, crowd - 1)),
            DMA((2, crowd - 1)),
            DMA((2, count - 1)),
            DMA((2, count - 1)),
        ],
        compiler_params=pltpu.CompilerParams(
            collective_id=collective_id, has_side_effects=True, vmem_limit_bytes=24 * 2**20
        ),
    )(t, g, z)


def gelu_parts(z):
    slope = (2.0 / jnp.pi) ** 0.5
    square = z * z
    bend = jnp.tanh(slope * z * (1.0 + 0.044715 * square))
    half = 0.5 * (1.0 + bend)
    return z * half, half + 0.5 * z * (1.0 - bend * bend) * slope * (1.0 + 0.134145 * square)


def latent_kernel(
    count,
    images,
    part_ref,
    stat_ref,
    own_ref,
    cot_ref,
    mix_ref,
    gain_ref,
    in_gain_ref,
    w_ref,
    out_ref,
    xs_ref,
    gs_ref,
    back_ref,
    row_ref,
    gain_out,
    in_gain_out,
    wv,
    one,
    two,
    three,
    pre,
    grad,
    flow,
    low,
    heads_q,
    kv,
    probs,
    kv_out,
    kv_in,
    cot,
    final,
    mean,
    w_sem,
    kv_send,
    kv_recv,
    gkv_send,
    gkv_recv,
    cot_own,
    cot_send,
    cot_recv,
    out_own,
    out_send,
    out_recv,
):
    rows, width = own_ref.shape
    depth = width // count
    owners = Owners(count, images)
    sharers = owners.sharers
    latents = rows * sharers
    per = count // sharers
    rows_here = latents // count
    spare = depth - rows_here
    group, me = lax.axis_index("img"), lax.axis_index("pix")
    slot, image, home = owners.slot, owners.image, owners.home
    block = 256
    blocks = width // block
    row_block = min(rows, 64)
    up_one, down_one, m_query, m_key, m_value, m_out, up_two, down_two = range(8)
    scale = HEAD_DIM ** (-0.5)

    def load(k):
        return pltpu.make_async_copy(w_ref.at[k], wv.at[k], w_sem.at[k])

    for k in range(8):
        load(k).start()
    greet(plane(count))

    def cot_push(i):
        to = owners.device(group, i, me // per)
        return to, pltpu.make_async_remote_copy(
            cot_ref.at[i],
            cot.at[lax.rem(me, per)],
            cot_send.at[i],
            cot_recv.at[lax.rem(me, per)],
            device_id=to,
            device_id_type=MESH,
        )

    def cot_keep():
        return pltpu.make_async_copy(cot_ref.at[image], cot.at[lax.rem(me, per)], cot_own)

    for i in range(images):
        to, copy = cot_push(i)

        @pl.when(jnp.logical_not(owners.is_me(to)))
        def _():
            copy.start()

        @pl.when(owners.is_me(to))
        def _():
            cot_keep().start()

    def columns(j, wide=block):
        return pl.ds(pl.multiple_of(j * wide, wide), wide)

    def over_columns(body):
        pl.loop(0, blocks)(body)

    def over_rows(body):
        @pl.loop(0, rows // row_block)
        def _(r):
            body(pl.ds(pl.multiple_of(r * row_block, 16), row_block))

    def put_x(j, c, value):
        xs_ref[j, columns(c), :] = value.T

    def centre(rows_f32):
        average = jnp.mean(rows_f32, axis=1, keepdims=True)
        centred = rows_f32 - average
        spread = jnp.mean(centred * centred, axis=1, keepdims=True)
        scale_rows = lax.rsqrt(spread + eps)
        return centred * scale_rows, scale_rows

    def norm(source, k, target):
        def body(r):
            target[r] = (centre(source[r])[0] * gain_ref[k : k + 1, :]).astype(bf16)

        over_rows(body)

    def norm_grad(source, k):
        def body(r):
            hat, scale_rows = centre(source[r])
            given = flow[r]
            gain_out[k : k + 1, :] += jnp.sum(given * hat, axis=0, keepdims=True)
            given = given * gain_ref[k : k + 1, :]
            along = jnp.mean(given * hat, axis=1, keepdims=True)
            grad[r] += scale_rows * (given - jnp.mean(given, axis=1, keepdims=True) - hat * along)

        over_rows(body)

    gain_out[...] = jnp.zeros_like(gain_out)

    top = jnp.max(stat_ref[:, 0:1, :], axis=0)
    total = jnp.zeros_like(top)
    for d in range(count):
        total = total + jnp.exp2(stat_ref[d, 0:1, :] - top) * stat_ref[d, 1:2, :]
    raw = jnp.zeros(part_ref.shape[1:], f32)
    for d in range(count):
        raw = raw + part_ref[d].astype(f32) * (jnp.exp2(stat_ref[d, 0:1, :] - top) / total)
    mean[0] = raw
    mean[1] = raw * in_gain_ref[...]
    row_ref[...] = jnp.zeros_like(row_ref)
    row_ref[0:1, :] = top + jnp.log(total) * LOG2E

    tall = count * spare
    mean_tall = mean[1]
    if tall > mean_tall.shape[0]:
        mean_tall = jnp.concatenate(
            [mean_tall, jnp.zeros((tall - mean_tall.shape[0], rows), f32)], axis=0
        )
    share_rows = -(-mean.shape[1] // count)
    share_rows = -(-share_rows // 8) * 8
    place = lax.broadcasted_iota(jnp.int32, (rows_here, rows), 0)
    source_row = lax.broadcasted_iota(jnp.int32, (rows_here, rows), 1) + slot * rows
    for o in range(count):
        picks = jnp.where(place + o * rows_here == source_row, 1.0, 0.0)
        piece = [picks, mean_tall[o * share_rows : (o + 1) * share_rows]]
        if spare > share_rows:
            piece.append(jnp.zeros((spare - share_rows, rows), f32))
        xs_ref[6, o * depth : (o + 1) * depth, :] = jnp.concatenate(piece, axis=0).astype(bf16)

    mean_low = mean[1].astype(bf16)

    @over_columns
    def _(j):
        one[:, columns(j)] = own_ref[:, columns(j)] + mm_tn(mean_low, mix_ref[:, columns(j)])

    def feed(source, target, k, up, down, normed, x_hidden, keep):
        norm(source, k, normed)
        load(up).wait()

        @over_columns
        def _(j):
            value = mm_nt(normed[...], wv[up, columns(j), :])
            pre[keep, :, columns(j)] = value
            hidden = gelu_parts(value)[0].astype(bf16)
            low[:, columns(j)] = hidden
            put_x(x_hidden, j, hidden)

        load(down).wait()

        @over_columns
        def _(j):
            value = source[:, columns(j)] + mm(low[...], wv[down, :, columns(j)])
            target[:, columns(j)] = value.astype(target.dtype)

    def feed_back(source, k, up, down, branch, x_pre, keep):
        @over_columns
        def _(j):
            value = mm_nt(branch[...], wv[down, columns(j), :])
            value = (value * gelu_parts(pre[keep, :, columns(j)])[1]).astype(bf16)
            low[:, columns(j)] = value
            put_x(x_pre, j, value)

        @over_columns
        def _(j):
            flow[:, columns(j)] = mm(low[...], wv[up, :, columns(j)])

        norm_grad(source, k)

    feed(one, two, 0, up_one, down_one, gs_ref.at[4], 3, 0)

    norm(two, 1, low)

    def write_blocks(j, value):
        put_x(0, j, value)

    @over_columns
    def _(j):
        write_blocks(j, low[:, columns(j)])

    load(m_key).wait()
    load(m_value).wait()

    @over_columns
    def _(j):
        kv[0, slot, :, columns(j)] = mm(low[...], wv[m_key, :, columns(j)]).astype(bf16)
        kv[1, slot, :, columns(j)] = mm(low[...], wv[m_value, :, columns(j)]).astype(bf16)

    def sharer(d):
        return owners.device(home, image, lax.rem(slot + d, sharers))

    def kv_push(d):
        return pltpu.make_async_remote_copy(
            kv.at[:, slot],
            kv.at[:, slot],
            kv_send.at[d - 1],
            kv_recv.at[d - 1],
            device_id=sharer(d),
            device_id_type=MESH,
        )

    for d in range(1, sharers):
        kv_push(d).start()
    load(m_query).wait()

    @over_columns
    def _(j):
        heads_q[:, columns(j)] = mm(low[...], wv[m_query, :, columns(j)]).astype(bf16)

    for d in range(1, sharers):
        kv_push(d).wait_recv()

    @pl.loop(0, HEADS)
    def _(h):
        c = columns(h, HEAD_DIM)
        k_all = kv[0, :, :, c].reshape(latents, HEAD_DIM)
        v_all = kv[1, :, :, c].reshape(latents, HEAD_DIM)
        scores = mm_nt(heads_q[:, c], k_all) * scale
        shifted = jnp.exp(scores - jnp.max(scores, axis=1, keepdims=True))
        p = shifted / jnp.sum(shifted, axis=1, keepdims=True)
        probs[h] = p
        low[:, c] = mm(p.astype(bf16), v_all).astype(bf16)

    @over_columns
    def _(j):
        put_x(1, j, low[:, columns(j)])

    load(m_out).wait()

    @over_columns
    def _(j):
        three[:, columns(j)] = two[:, columns(j)] + mm(low[...], wv[m_out, :, columns(j)])

    feed(three, final, 2, up_two, down_two, gs_ref.at[6], 5, 1)

    def out_push(b):
        to = (home, slot * per + b)
        return to, pltpu.make_async_remote_copy(
            final.at[pl.ds(b * rows_here, rows_here)],
            out_ref.at[image],
            out_send.at[b],
            out_recv.at[image],
            device_id=to,
            device_id_type=MESH,
        )

    def out_keep():
        mine = pl.ds(pl.multiple_of(lax.rem(me, per) * rows_here, 16), rows_here)
        return pltpu.make_async_copy(final.at[mine], out_ref.at[image], out_own)

    for b in range(per):
        to, copy = out_push(b)

        @pl.when(jnp.logical_not(owners.is_me(to)))
        def _():
            copy.start()

        @pl.when(owners.is_me(to))
        def _():
            out_keep().start()

    def cot_from(b):
        return pltpu.make_async_remote_copy(
            cot_ref.at[0],
            cot.at[b],
            cot_send.at[0],
            cot_recv.at[b],
            device_id=(group, me),
            device_id_type=MESH,
        )

    for b in range(per):

        local = owners.is_me((home, slot * per + b))

        @pl.when(jnp.logical_not(local))
        def _():
            cot_from(b).wait_recv()

        @pl.when(local)
        def _():
            cot_keep().wait()

    given = cot[...].reshape(rows, width)
    gs_ref[7] = given
    grad[...] = given.astype(f32)
    feed_back(three, 2, up_two, down_two, gs_ref.at[7], 4, 1)

    gs_ref[3] = grad[...].astype(bf16)

    @over_columns
    def _(j):
        low[:, columns(j)] = mm_nt(gs_ref[3], wv[m_out, columns(j), :]).astype(bf16)

    @pl.loop(0, HEADS)
    def _(h):
        c = columns(h, HEAD_DIM)
        k_all = kv[0, :, :, c].reshape(latents, HEAD_DIM)
        v_all = kv[1, :, :, c].reshape(latents, HEAD_DIM)
        p = probs[h]
        g_mixed = low[:, c]
        g_p = mm_nt(g_mixed, v_all)
        g_v = mm_tn(p.astype(bf16), g_mixed)
        delta = jnp.sum(p * g_p, axis=1, keepdims=True)
        g_s = (p * (g_p - delta)).astype(bf16)
        gs_ref[0, :, c] = (mm(g_s, k_all) * scale).astype(bf16)
        g_k = mm_tn(g_s, heads_q[:, c]) * scale
        kv_out[:, 0, :, c] = g_k.reshape(sharers, rows, HEAD_DIM).astype(bf16)
        kv_out[:, 1, :, c] = g_v.reshape(sharers, rows, HEAD_DIM).astype(bf16)

    def gkv_push(d):
        to = lax.rem(slot + d, sharers)
        return pltpu.make_async_remote_copy(
            kv_out.at[to],
            kv_in.at[d - 1],
            gkv_send.at[d - 1],
            gkv_recv.at[d - 1],
            device_id=sharer(d),
            device_id_type=MESH,
        )

    for d in range(1, sharers):
        gkv_push(d).start()

    @over_columns
    def _(j):
        flow[:, columns(j)] = mm_nt(gs_ref[0], wv[m_query, columns(j), :])

    for d in range(1, sharers):
        gkv_push(d).wait_recv()
    for which in range(2):

        @over_columns
        def _(j):
            value = kv_out[slot, which, :, columns(j)].astype(f32)
            for d in range(1, sharers):
                value = value + kv_in[d - 1, which, :, columns(j)].astype(f32)
            gs_ref[1 + which, :, columns(j)] = value.astype(bf16)

    @over_columns
    def _(j):
        flow[:, columns(j)] += mm_nt(gs_ref[1], wv[m_key, columns(j), :]) + mm_nt(
            gs_ref[2], wv[m_value, columns(j), :]
        )

    norm_grad(two, 1)
    gs_ref[5] = grad[...].astype(bf16)
    feed_back(one, 0, up_one, down_one, gs_ref.at[5], 2, 0)
    gs_ref[8] = grad[...].astype(bf16)
    back = mm_nt(mix_ref[...], gs_ref[8])
    back_ref[...] = back.astype(bf16)
    row_ref[1:2, :] = jnp.sum(back * mean[1], axis=0, keepdims=True)
    in_gain_out[...] = jnp.broadcast_to(
        jnp.sum(back * mean[0], axis=1, keepdims=True), in_gain_out.shape
    )

    for i in range(images):
        to, copy = cot_push(i)

        @pl.when(jnp.logical_not(owners.is_me(to)))
        def _():
            copy.wait_send()

    for d in range(1, sharers):
        kv_push(d).wait_send()
        gkv_push(d).wait_send()

    def out_from(i):
        return pltpu.make_async_remote_copy(
            final.at[pl.ds(0, rows_here)],
            out_ref.at[i],
            out_send.at[0],
            out_recv.at[i],
            device_id=(group, me),
            device_id_type=MESH,
        )

    for b in range(per):
        to, copy = out_push(b)

        @pl.when(jnp.logical_not(owners.is_me(to)))
        def _():
            copy.wait_send()

    for i in range(images):
        local = owners.is_me(owners.device(group, i, me // per))

        @pl.when(jnp.logical_not(local))
        def _():
            out_from(i).wait_recv()

        @pl.when(local)
        def _():
            out_keep().wait()


def latent_pass(parts, stats, own, cotangent, mix, gains, in_gain, whole, collective_id):
    count = lax.axis_size("pix")
    images, rows_here, width = cotangent.shape
    rows = own.shape[0]
    channels = mix.shape[0]
    sharers = count // images
    per = count // sharers
    inside = pl.BlockSpec(memory_space=pltpu.VMEM)
    anywhere = pl.BlockSpec(memory_space=pl.ANY)
    whole_f32 = pltpu.VMEM((rows, width), f32)
    whole_low = pltpu.VMEM((rows, width), bf16)
    shape = jax.ShapeDtypeStruct
    return pl.pallas_call(
        functools.partial(latent_kernel, count, images),
        out_shape=[
            shape((images, rows_here, width), bf16),
            shape((7, width, rows), bf16),
            shape((9, rows, width), bf16),
            shape((channels, rows), bf16),
            shape((8, rows), f32),
            shape((8, width), f32),
            shape((channels, 128), f32),
        ],
        in_specs=[inside, inside, inside, anywhere, inside, inside, inside, anywhere],
        out_specs=[anywhere] + [inside] * 6,
        scratch_shapes=[
            pltpu.VMEM((8, width, width), bf16),
            whole_f32,
            whole_f32,
            whole_f32,
            pltpu.VMEM((2, rows, width), f32),
            whole_f32,
            whole_f32,
            whole_low,
            whole_low,
            pltpu.VMEM((2, sharers, rows, width), bf16),
            pltpu.VMEM((HEADS, rows, rows * sharers), f32),
            pltpu.VMEM((sharers, 2, rows, width), bf16),
            pltpu.VMEM((max(sharers - 1, 1), 2, rows, width), bf16),
            pltpu.VMEM((per, rows_here, width), bf16),
            whole_low,
            pltpu.VMEM((2, channels, rows), f32),
            DMA((8,)),
            DMA((sharers,)),
            DMA((sharers,)),
            DMA((sharers,)),
            DMA((sharers,)),
            DMA,
            DMA((images,)),
            DMA((per,)),
            DMA,
            DMA((per,)),
            DMA((images,)),
        ],
        compiler_params=pltpu.CompilerParams(
            collective_id=collective_id, has_side_effects=True, vmem_limit_bytes=60 * 2**20
        ),
    )(parts, stats, own, cotangent, mix, gains, in_gain, whole)


def norm_back(resid, gain, grad):
    _, back = jax.vjp(layer_norm, resid, gain)
    return back(grad)


def local(
    rgb_pixels,
    keep_mask,
    latent_array,
    gain_input,
    gain_latent,
    w_query,
    w_key,
    w_value,
    w_cross_out,
    gain_mlp_one,
    w_up_one,
    w_down_one,
    gain_self,
    w_self_query,
    w_self_key,
    w_self_value,
    w_self_out,
    gain_mlp_two,
    w_up_two,
    w_down_two,
    cotangent,
):
    images, _, pixels = rgb_pixels.shape
    rows_here, width = latent_array.shape
    count = lax.axis_size("pix")
    me = lax.axis_index("pix")
    latents = rows_here * count
    sharers = count // images
    rows_own = latents // sharers
    slot = (me % (sharers // 2)) * 2 + lax.axis_index("img") % 2
    depth = w_query.shape[0]
    channels = gain_input.shape[0]
    width_scale = width ** (-0.5)
    tall = -(-channels // 16) * 16

    side = -(-channels // 512) * 512
    key_t = jnp.pad(w_key.T, ((0, 0), (0, side - channels)))
    value_out = lax.psum(mm(w_value, w_cross_out).astype(bf16), "pix")
    shards = jnp.stack(
        [
            w_up_one.T,
            w_down_one,
            w_self_query,
            w_self_key,
            w_self_value,
            w_self_out,
            w_up_two.T,
            w_down_two,
        ]
    )

    lines = pixels // SIDE
    u, sin_u, cos_u = angles(me * lines + lax.iota(jnp.int32, lines))
    w, sin_w, cos_w = angles(lax.iota(jnp.int32, SIDE))

    def zeros(rows, columns):
        return jnp.zeros((rows, columns), f32)

    pad = CHANNELS - 4 - SIDE - lines
    table = jnp.concatenate(
        [
            jnp.concatenate(
                [zeros(SIDE, 4), w, zeros(SIDE, BANDS), sin_w, zeros(SIDE, BANDS), cos_w], axis=1
            ),
            jnp.concatenate(
                [zeros(lines, 3), u, zeros(lines, 1), sin_u, zeros(lines, BANDS), cos_u, zeros(lines, BANDS)],
                axis=1,
            ),
            zeros(pad, channels),
            jnp.eye(3, channels, dtype=f32),
            jnp.ones((1, channels), f32),
        ],
        axis=0,
    )
    row_sum = u[:, 0] + jnp.sum(sin_u + cos_u, axis=1)
    col_sum = w[:, 0] + jnp.sum(sin_w + cos_w, axis=1)
    row_square = u[:, 0] ** 2 + jnp.sum(sin_u**2 + cos_u**2, axis=1)
    col_square = w[:, 0] ** 2 + jnp.sum(sin_w**2 + cos_w**2, axis=1)
    feature_sum = (row_sum[:, None] + col_sum[None, :]).reshape(1, pixels)
    feature_square = (row_square[:, None] + col_square[None, :]).reshape(1, pixels)
    colours = rgb_pixels.astype(f32)
    average = (jnp.sum(colours, axis=1) + feature_sum) / channels
    spread = (jnp.sum(colours**2, axis=1) + feature_square) / channels - average**2
    scale = lax.rsqrt(spread + eps)
    keep = keep_mask.astype(f32)

    own_values = jnp.concatenate([colours, -average[:, None, :]], axis=1) * scale[:, None, :]
    values = jnp.concatenate(
        [scale[:, None], keep[:, None], jnp.zeros((images, 2, pixels), f32), own_values], axis=1
    )
    gained = table * gain_input[None, :]
    (
        latent_full,
        query_mat,
        key_full,
        whole,
        latent_normed,
        queries,
        score_mat,
        at,
        a_low,
        raw_parts,
        stat_parts,
    ) = forward_pass(
        values,
        jnp.pad(table.T, ((0, tall - channels), (0, 0))),
        jnp.pad(gained, ((0, 0), (0, side - channels))),
        gain_latent,
        latent_array[None],
        w_query[None],
        key_t[None],
        shards,
        0,
    )
    latent_float = latent_full.reshape(latents, width).astype(f32)
    query_mat = query_mat.reshape(width, width)
    key_mat = key_full.reshape(width, side)[:, :channels].T
    score_mat = score_mat[:, :channels]
    whole = whole.reshape(8, width, width)

    own = lax.dynamic_slice_in_dim(latent_float, slot * rows_own, rows_own, 0)
    latent_out, xs, gs, back_t, row_stats, gain_grads, in_gain = latent_pass(
        raw_parts,
        stat_parts,
        own,
        cotangent,
        jnp.pad(value_out, ((0, tall - channels), (0, 0))),
        jnp.stack([gain_mlp_one, gain_self, gain_mlp_two]),
        jnp.pad(gain_input, (0, tall - channels))[:, None],
        whole,
        4,
    )
    across = -(-channels // 128) * 128
    grad_raw, pixel_out, summed = backward_pass(
        values,
        jnp.pad(table, ((0, 0), (0, across - channels))),
        jnp.pad(gained, ((0, 0), (0, tall - channels))),
        at,
        a_low,
        back_t,
        row_stats,
        xs,
        gs,
        2,
    )
    moved = (pixel_out[:, 4:7] - pixel_out[:, 7:8] / channels) - (
        (colours - average[:, None, :]) * scale[:, None, :]
    ) * (pixel_out[:, 0:1] / channels)
    grad_pixels = moved * (scale * keep)[:, None, :]

    cells = -(-(3 * width + channels) // (count * 1024)) * 1024
    loose = jnp.concatenate([gain_grads[:3].reshape(-1), in_gain[:channels, 0]])
    loose = jnp.pad(loose, (0, count * cells - loose.shape[0])).reshape(count, 8, cells // 8)
    share_rows = -(-(-(-tall // count)) // 8) * 8
    rest = summed[8]
    spare = -(-share_rows // 16) * 16
    cross_rows = jnp.pad(
        rest[rows_here : rows_here + share_rows].astype(bf16), ((0, spare - share_rows), (0, 0))
    )
    grad_raw, loose, cross_sum = small_sums(
        grad_raw.reshape(count, rows_here, across),
        loose,
        cross_rows,
        6,
    )
    grad_raw = grad_raw.reshape(latents, across)[:, :channels].astype(f32)
    loose = loose.reshape(-1)
    gain_one, gain_attn, gain_two = [loose[k * width : (k + 1) * width] for k in range(3)]
    gain_in = loose[3 * width : 3 * width + channels] + jnp.sum(score_mat * grad_raw, axis=0)
    cross_sum = cross_sum[:, :share_rows].reshape(-1, width)[:channels]

    grad_x = (grad_raw * (gain_input * width_scale)[None, :]).astype(bf16)
    query_grad = mm(grad_x, key_mat).astype(bf16)
    latent_cols = lax.dynamic_slice_in_dim(latent_normed, me * depth, depth, 1)
    grad_w_query = mm_tn(latent_cols, query_grad)
    grad_latent_full, grad_gain_latent = norm_back(
        latent_float, gain_latent, mm_nt(query_grad, query_mat)
    )
    grad_latent_own = lax.dynamic_slice_in_dim(grad_latent_full, me * rows_here, rows_here, 0)
    key_cols = w_key.shape[1]
    grad_w_key = mm_tn(grad_x, lax.dynamic_slice_in_dim(queries, me * key_cols, key_cols, 1))

    g_sq, g_sk, g_sv, g_so, g_up_one, g_down_one, g_up_two, g_down_two, rest = [
        summed[k] for k in range(9)
    ]
    grad_w_value = mm_nt(cross_sum, w_cross_out)
    grad_w_cross_out = mm_tn(w_value, cross_sum)
    grad_latent_array = rest[:rows_here] + grad_latent_own
    return (
        latent_out,
        grad_pixels,
        grad_latent_array,
        gain_in,
        grad_gain_latent,
        grad_w_query,
        grad_w_key,
        grad_w_value,
        grad_w_cross_out,
        gain_one,
        g_up_one.T,
        g_down_one,
        gain_attn,
        g_sq,
        g_sk,
        g_sv,
        g_so,
        gain_two,
        g_up_two.T,
        g_down_two,
    )


def solution(mesh):
    rows, columns, copied = P("pix", None), P(None, "pix"), P()
    return jax.shard_map(
        local,
        mesh=mesh,
        in_specs=(
            P("img", None, "pix"),
            P("img", "pix"),
            rows,
            copied,
            copied,
            rows,
            columns,
            columns,
            rows,
            copied,
            columns,
            rows,
            copied,
            rows,
            rows,
            rows,
            rows,
            copied,
            columns,
            rows,
            P("img", "pix", None),
        ),
        out_specs=(
            P("img", "pix", None),
            P("img", None, "pix"),
            rows,
            copied,
            copied,
            rows,
            columns,
            columns,
            rows,
            copied,
            columns,
            rows,
            copied,
            rows,
            rows,
            rows,
            rows,
            copied,
            columns,
            rows,
        ),
        check_vma=False,
    )
```

```python
import functools

import jax
import jax.numpy as jnp
from jax import lax
from jax.experimental import pallas as pl
from jax.experimental.pallas import tpu as pltpu
from jax.sharding import PartitionSpec as P

HEADS = 8
HEAD_DIM = 128
BANDS = 64
SIDE = 224
CHANNELS = 256
LOG2E = 1.4426950408889634

eps = 1e-05
f32 = jnp.float32
bf16 = jnp.bfloat16


def exact(left, right):
    return jnp.dot(left, right, precision=lax.Precision.HIGHEST, preferred_element_type=f32)


def mm(left, right):
    return jnp.dot(left, right, preferred_element_type=f32)


def mm_nt(left, right):
    return lax.dot_general(left, right, (((1,), (1,)), ((), ())), preferred_element_type=f32)


def mm_tn(left, right):
    return lax.dot_general(left, right, (((0,), (0,)), ((), ())), preferred_element_type=f32)


def angles(index):
    place = index.astype(f32) * (2.0 / (SIDE - 1)) - 1.0
    steps = lax.iota(jnp.int32, BANDS).astype(f32)
    frequency = 1.0 + steps * ((SIDE / 2.0 - 1.0) / (BANDS - 1))
    angle = jnp.pi * place[:, None] * frequency[None, :]
    return place[:, None], jnp.sin(angle), jnp.cos(angle)


def pixel_tile(pixels):
    return 896 if pixels % 896 == 0 else pixels


MESH = pl.DeviceIdType.MESH
DMA = pltpu.SemaphoreType.DMA


def ring_place(count):
    me = lax.axis_index("pix")
    return jnp.where(me % 2 == 0, me // 2, count - 1 - me // 2)


def ring_device(place, count):
    place = lax.rem(place + 2 * count, count)
    return jnp.where(place < count // 2, 2 * place, 2 * (count - 1 - place) + 1)


def greet(devices):
    barrier = pltpu.get_barrier_semaphore()
    for device in devices:
        pl.semaphore_signal(barrier, inc=1, device_id=device, device_id_type=MESH)
    pl.semaphore_wait(barrier, len(devices))


def hot_codes(tile):
    pixel = lax.broadcasted_iota(jnp.int32, (CHANNELS, tile), 1)
    channel = lax.broadcasted_iota(jnp.int32, (CHANNELS, tile), 0)
    start = channel - SIDE - pixel // SIDE
    code = jnp.where((start >= 0) & (channel < CHANNELS - 4), start, -2)
    return jnp.where(channel < SIDE, jnp.where(channel == pixel % SIDE, -1, -2), code)


def build_xt(values, base, code_ref):
    code = code_ref[...]
    hot = jnp.where((code == -1) | (code == base), values[0:1, :], 0.0)
    last = hot[CHANNELS - 8 :, :]
    k = lax.broadcasted_iota(jnp.int32, last.shape, 0)
    last = jnp.where(k >= 4, values, last)
    return jnp.concatenate([hot[: CHANNELS - 8, :], last], axis=0)


def build_both(values, base, code_ref):
    keep = values[1:2, :]
    xt = build_xt(values, base, code_ref).astype(bf16)
    k = lax.broadcasted_iota(jnp.int32, (16, values.shape[1]), 0)
    ones = jnp.where(k == 0, keep, 0.0).astype(bf16)
    return xt.T, jnp.concatenate([xt * keep.astype(bf16), ones], axis=0)


def forward_kernel(
    count,
    images,
    tile,
    mats,
    v_ref,
    code_ref,
    table_ref,
    gained_ref,
    gain_ref,
    lat_ref,
    wq_ref,
    wk_ref,
    *refs,
):
    shards = refs[:mats]
    forward_body(
        count,
        images,
        tile,
        v_ref,
        code_ref,
        table_ref,
        gained_ref,
        gain_ref,
        lat_ref,
        wq_ref,
        wk_ref,
        shards,
        *refs[mats:],
    )


def forward_body(
    count,
    images,
    tile,
    v_ref,
    code_ref,
    table_ref,
    gained_ref,
    gain_ref,
    lat_ref,
    wq_ref,
    wk_ref,
    shards,
    lat_full,
    wq_full,
    wk_full,
    w_full,
    normed_ref,
    query_ref,
    a_ref,
    at_ref,
    alow_ref,
    part_ref,
    stat_ref,
    acc,
    top,
    u_send,
    s_send,
    own_sem,
    send_sem,
    recv_sem,
    hand_send,
    hand_recv,
    u_own,
    u_out,
    u_in,
):
    pixels = v_ref.shape[2]
    steps = pixels // tile
    lines = tile // SIDE
    owners = Owners(count, images)
    sharers = owners.sharers
    rows = part_ref.shape[2]
    width = wq_ref.shape[1]
    latents = normed_ref.shape[0]
    group, me = lax.axis_index("img"), lax.axis_index("pix")
    core = lax.rem(group, 2)
    place = ring_place(count)
    sides = ((group, ring_device(place + 1, count)), (group, ring_device(place - 1, count)))
    other = (group + 1 - 2 * core, me)
    greet(plane(count))
    sources = (lat_ref, wq_ref, wk_ref)
    fulls = (lat_full, wq_full, wk_full, w_full)
    mats = len(shards)

    reach = count // 2

    def spot(a, k, stage, way, last, source=False):
        wide = fulls[a].shape[3] // 4
        begin = (core * 2 + way) * wide if last else core * 2 * wide
        columns = pl.ds(pl.multiple_of(begin, 128), wide if last else 2 * wide)
        if source:
            return (sources[a] if a < 3 else shards[k]).at[:, columns]
        origin = ring_device(place - stage if way == 0 else place + stage, count)
        return fulls[a].at[k, origin, :, columns]

    def hop(a, k, stage, way, first=False, last=False):
        return pltpu.make_async_remote_copy(
            spot(a, k, stage, way, last, first),
            spot(a, k, stage, way, last),
            send_sem.at[stage, way, a + k],
            recv_sem.at[stage, way, a + k],
            device_id=sides[way],
            device_id_type=MESH,
        )

    def hand(a, k, stage, way, last=False):
        part = spot(a, k, stage, way, last)
        return pltpu.make_async_remote_copy(
            part,
            part,
            hand_send.at[stage - 1, way, a + k],
            hand_recv.at[stage - 1, way, a + k],
            device_id=other,
            device_id_type=MESH,
        )

    def relay(a, k, stage):
        for way in range(2):
            hop(a, k, stage - 1, way).wait_recv()

            @pl.when(stage == reach - 1)
            def _():
                hop(a, k, stage, way, last=True).start()

            @pl.when(stage != reach - 1)
            def _():
                hop(a, k, stage, way).start()

            hand(a, k, stage, way).start()

    def relay_end(a, k):
        for way in range(2):
            hop(a, k, reach - 1, way, last=True).wait_recv()
            hand(a, k, reach, way, last=True).start()

    def start_ring(a, k):
        for way in range(2):
            hop(a, k, 0, way, True, reach == 1).start()

    def sent(a, k):
        for way in range(2):
            for stage in range(reach):
                last = stage == reach - 1
                hop(a, k, stage, way, stage == 0, last).wait_send()
                hand(a, k, stage + 1, way, last).wait_send()

    def handed(a, k):
        for way in range(2):
            for stage in range(1, reach + 1):
                hand(a, k, stage, way, stage == reach).wait_recv()

    own = [
        pltpu.make_async_copy(shards[k], fulls[3].at[k, me], own_sem.at[k]) for k in range(mats)
    ]
    for a in range(3):
        start_ring(a, 0)
    for a in range(3):
        fulls[a][0, me] = sources[a][...]
    for copy in own:
        copy.start()
    each = -(-mats // reach)
    for stage in range(1, reach + 1):
        for a in range(3):
            if stage < reach:
                relay(a, 0, jnp.int32(stage))
            else:
                relay_end(a, 0)
        for k in range((stage - 1) * each, min(stage * each, mats)):
            start_ring(3, k)
    for a in range(3):
        handed(a, 0)

    rows_here = lat_ref.shape[0]

    @pl.loop(0, count)
    def _(o):
        block = lat_full[0, o].astype(f32)
        average = jnp.mean(block, axis=1, keepdims=True)
        centred = block - average
        spread = jnp.mean(centred * centred, axis=1, keepdims=True)
        normed = (centred * lax.rsqrt(spread + eps) * gain_ref[...]).astype(bf16)
        normed_ref[pl.ds(pl.multiple_of(o * rows_here, rows_here), rows_here), :] = normed

    @pl.loop(0, width // 256)
    def _(j):
        columns = pl.ds(pl.multiple_of(j * 256, 256), 256)
        weight = wq_full[0, :, :, columns].reshape(width, 256)
        query_ref[:, columns] = mm(normed_ref[...], weight).astype(bf16)

    a_ref[...] = mm(query_ref[...], wk_full[0].reshape(width, wk_ref.shape[1])) * (width ** (-0.5))

    def exact_nt(left, right):
        return lax.dot_general(
            left,
            right,
            (((1,), (1,)), ((), ())),
            precision=lax.Precision.HIGHEST,
            preferred_element_type=f32,
        )

    at_ref[...] = (exact_nt(gained_ref[...], a_ref[...]) * LOG2E).astype(bf16)
    alow_ref[...] = exact_nt(a_ref[...], gained_ref[...]).astype(bf16)

    table_t = table_ref[...].T[: part_ref.shape[1], :]

    relays = (reach - 1) * mats

    def relay_number(e):
        relay(3, lax.rem(e, mats), 1 + e // mats)

    def u_push(i, h):
        to = owners.device(group, i, jnp.int32(h))
        sems = lambda which: dict(
            send_sem=u_out.at[which, i * sharers + h],
            recv_sem=u_in.at[which, me],
            device_id=to,
            device_id_type=MESH,
        )
        return to, (
            pltpu.make_async_remote_copy(u_send.at[i, h], part_ref.at[me], **sems(0)),
            pltpu.make_async_remote_copy(s_send.at[i, h], stat_ref.at[me], **sems(1)),
        )

    def u_keep():
        i, h = owners.image, owners.slot
        return (
            pltpu.make_async_copy(u_send.at[i, h], part_ref.at[me], u_own.at[0]),
            pltpu.make_async_copy(s_send.at[i, h], stat_ref.at[me], u_own.at[1]),
        )

    @pl.loop(0, images * steps)
    def _(t):
        i, step = t // steps, lax.rem(t, steps)

        @pl.when(t < relays)
        def _():
            relay_number(t)

        @pl.when(step == 0)
        def _():
            acc[...] = jnp.zeros_like(acc)
            top[...] = jnp.full_like(top, -jnp.inf)

        values = v_ref[i, :, pl.ds(pl.multiple_of(step * tile, 128), tile)]
        base = step * lines
        x, xt = build_both(values, base, code_ref)
        first, second = slice(0, tile // 2), slice(tile // 2, tile)
        scores = [mm(x[half], at_ref[...]) for half in (first, second)]
        old, total = top[0:1, :], acc[...]
        for half, score in zip((first, second), scores):
            new = jnp.maximum(old, jnp.max(score, axis=0, keepdims=True))
            weights = jnp.exp2(score - new).astype(bf16)
            total = total * jnp.exp2(old - new) + mm(xt[:, half], weights)
            old = new
        acc[...] = total
        top[...] = jnp.broadcast_to(old, top.shape)

        @pl.when(step == steps - 1)
        def _():
            raw = jnp.dot(
                table_t,
                acc[:CHANNELS, :],
                precision=lax.Precision.HIGHEST,
                preferred_element_type=f32,
            ).astype(bf16)
            stats = jnp.concatenate([top[0:1, :], acc[CHANNELS : CHANNELS + 1, :], top[0:6, :]], axis=0)
            for h in range(sharers):
                u_send[i, h] = raw[:, h * rows : (h + 1) * rows]
                s_send[i, h] = stats[:, h * rows : (h + 1) * rows]
            for h in range(sharers):
                to, copies = u_push(i, h)

                @pl.when(jnp.logical_not(owners.is_me(to)))
                def _():
                    for copy in copies:
                        copy.start()

                @pl.when(owners.is_me(to))
                def _():
                    for copy in u_keep():
                        copy.start()

    if images * steps < relays:

        @pl.loop(images * steps, relays)
        def _(e):
            relay_number(e)

    @pl.loop(0, mats)
    def _(k):
        relay_end(3, k)

    for copy in own:
        copy.wait()
    for a in range(3):
        sent(a, 0)

    for k in range(mats):
        sent(3, k)
        handed(3, k)

    def u_from(source):
        sems = lambda which: dict(
            send_sem=u_out.at[which, 0],
            recv_sem=u_in.at[which, source],
            device_id=(owners.home, source),
            device_id_type=MESH,
        )
        return (
            pltpu.make_async_remote_copy(u_send.at[0, 0], part_ref.at[source], **sems(0)),
            pltpu.make_async_remote_copy(s_send.at[0, 0], stat_ref.at[source], **sems(1)),
        )

    for i in range(images):
        for h in range(sharers):
            to, copies = u_push(i, h)

            @pl.when(jnp.logical_not(owners.is_me(to)))
            def _():
                for copy in copies:
                    copy.wait_send()

    for source in range(count):
        local = owners.is_me((owners.home, source))

        @pl.when(local)
        def _():
            for copy in u_keep():
                copy.wait()

        @pl.when(jnp.logical_not(local))
        def _():
            for copy in u_from(source):
                copy.wait_recv()


def forward_pass(values, table, gained, gain_latent, lat, wq, wk, shards, tall, collective_id):
    count = lax.axis_size("pix")
    images, _, pixels = values.shape
    tile = pixel_tile(pixels)
    rows_here, width = lat.shape
    latents = rows_here * count
    sharers = count // images
    rows = latents // sharers
    mats = len(shards)
    inside = pl.BlockSpec(memory_space=pltpu.VMEM)
    anywhere = pl.BlockSpec(memory_space=pl.ANY)
    shape = jax.ShapeDtypeStruct

    def full(array, number=1):
        return shape((number, count) + array.shape, array.dtype)

    ring = DMA((count // 2, 2, 3 + mats))
    return pl.pallas_call(
        functools.partial(forward_kernel, count, images, tile, mats),
        out_shape=[full(lat), full(wq), full(wk), full(shards[0], mats)]
        + [
            shape((latents, width), bf16),
            shape((latents, width), bf16),
            shape((latents, wk.shape[1]), f32),
            shape((CHANNELS, latents), bf16),
            shape((latents, CHANNELS), bf16),
            shape((count, tall, rows), bf16),
            shape((count, 8, rows), f32),
        ],
        in_specs=[inside] * (8 + mats),
        out_specs=[inside] * 3 + [anywhere] + [inside] * 5 + [anywhere] * 2,
        scratch_shapes=[
            pltpu.VMEM((CHANNELS + 16, latents), f32),
            pltpu.VMEM((8, latents), f32),
            pltpu.VMEM((images, sharers, tall, rows), bf16),
            pltpu.VMEM((images, sharers, 8, rows), f32),
            DMA((mats,)),
            ring,
            ring,
            ring,
            ring,
            DMA((2,)),
            DMA((2, count)),
            DMA((2, count)),
        ],
        compiler_params=pltpu.CompilerParams(
            collective_id=collective_id, has_side_effects=True, vmem_limit_bytes=48 * 2**20
        ),
    )(values, hot_codes(tile), table, gained, gain_latent[None], lat, wq, wk, *shards)


def backward_kernel(
    count,
    teams,
    images,
    tile,
    channels,
    v_ref,
    code_ref,
    table_ref,
    gained_ref,
    at_ref,
    a_ref,
    back_ref,
    row_ref,
    gain_ref,
    xs_ref,
    gs_ref,
    t_out,
    g_out,
    z_out,
    pixel_ref,
    out_ref,
    t_raw,
    t_in,
    t_img,
    g_raw,
    g_in,
    g_img,
    z_own,
    t_acc,
    bt,
    b_low,
    stat,
    back_all,
    row_all,
    xv,
    gv,
    terms,
    held,
    across,
    done,
    load_sem,
    pair_send,
    pair_recv,
    send_sem,
    recv_sem,
    cross_send,
    cross_recv,
    out_sem,
    hand_send,
    hand_recv,
    back_send,
    back_recv,
    sum_send,
    sum_recv,
    img_send,
    img_recv,
    last_send,
    last_recv,
    z_send,
    z_recv,
    z_hand_send,
    z_hand_recv,
):
    number, rows, width = gs_ref.shape
    kinds = xs_ref.shape[0]
    owners = Owners(count, images)
    sharers = owners.sharers
    steps = v_ref.shape[2] // tile
    lines = tile // SIDE
    depth = xs_ref.shape[1] // count
    half, wide = width // 2, width // 4
    group, me = lax.axis_index("img"), lax.axis_index("pix")
    core, team = lax.rem(group, 2), group // 2
    place = ring_place(count)
    sides = ((group, ring_device(place + 1, count)), (group, ring_device(place - 1, count)))
    other = (group + 1 - 2 * core, me)
    partners = [(lax.rem(team + d, teams) * 2 + core, me) for d in range(1, teams)]
    crowd = 2 * teams
    others = peers(count)
    same_place = [(lax.rem(group + d, crowd), me) for d in range(1, crowd)]
    far = [
        (lax.rem(team + d, teams) * 2 + c, me) for d in range(1, teams) for c in range(2)
    ]
    greet(plane(count) + far)

    def send(source, target, sems, index, device):
        return pltpu.make_async_remote_copy(
            source,
            target,
            sems[0].at[index],
            sems[1].at[index],
            device_id=device,
            device_id_type=MESH,
        )

    def scatter(d):
        to, sems = others[d][1], (sum_send, sum_recv)
        return (
            send(t_raw.at[to], t_in.at[d], sems, (0, d), others[d]),
            send(g_raw.at[to], g_in.at[d], sems, (1, d), others[d]),
        )

    def over(d):
        sems = (img_send, img_recv)
        return (
            send(t_img.at[group], t_img.at[group], sems, (0, d), same_place[d]),
            send(g_img.at[group], g_img.at[group], sems, (1, d), same_place[d]),
        )

    def gather(d):
        sems = (last_send, last_recv)
        return (
            send(t_out.at[me], t_out.at[me], sems, (0, d), others[d]),
            send(g_out.at[me], g_out.at[me], sems, (1, d), others[d]),
        )

    def z_push(d):
        return send(z_own, z_out.at[core, me], (z_send, z_recv), d, others[d])

    def z_hand():
        return pltpu.make_async_remote_copy(
            z_out.at[core],
            z_out.at[core],
            z_hand_send,
            z_hand_recv,
            device_id=other,
            device_id_type=MESH,
        )

    for o in range(count):
        g_raw[o] = gain_ref[:, o * depth : (o + 1) * depth]

    own_index = owners.image * sharers + owners.slot

    def back_push(d):
        to = (owners.home, lax.rem(me + d, count))
        sems = lambda which: dict(
            send_sem=back_send.at[which, d],
            recv_sem=back_recv.at[which, own_index],
            device_id=to,
            device_id_type=MESH,
        )
        return to, (
            pltpu.make_async_remote_copy(back_ref, back_all.at[own_index], **sems(0)),
            pltpu.make_async_remote_copy(row_ref, row_all.at[own_index], **sems(1)),
        )

    def back_from(source):
        sems = lambda which: dict(
            send_sem=back_send.at[which, 0],
            recv_sem=back_recv.at[which, source],
            device_id=(group, me),
            device_id_type=MESH,
        )
        return (
            pltpu.make_async_remote_copy(back_ref, back_all.at[source], **sems(0)),
            pltpu.make_async_remote_copy(row_ref, row_all.at[source], **sems(1)),
        )

    for d in range(count):
        to, copies = back_push(d)

        @pl.when(jnp.logical_not(owners.is_me(to)))
        def _():
            for copy in copies:
                copy.start()

        @pl.when(owners.is_me(to))
        def _():
            back_all[own_index] = back_ref[...]
            row_all[own_index] = row_ref[...]

    def load_x(j):
        return pltpu.make_async_copy(xs_ref.at[j], xv.at[j, core], load_sem.at[0, j])

    def load_g(k):
        part = gs_ref.at[k, :, pl.ds(pl.multiple_of(core * half, 128), half)]
        return pltpu.make_async_copy(part, gv.at[k, core], load_sem.at[1, k])

    def pair_x(j):
        return pltpu.make_async_remote_copy(
            xs_ref.at[j],
            xv.at[j, core],
            pair_send.at[0, j],
            pair_recv.at[0, j],
            device_id=other,
            device_id_type=MESH,
        )

    def pair_g(k):
        part = gs_ref.at[k, :, pl.ds(pl.multiple_of((1 - core) * half, 128), half)]
        return pltpu.make_async_remote_copy(
            part,
            gv.at[k, core],
            pair_send.at[1, k],
            pair_recv.at[1, k],
            device_id=other,
            device_id_type=MESH,
        )

    order = [number - 1] + list(range(number - 1))
    for k in order:
        j = max(k - (number - kinds), 0)
        if k == 0 or k > number - kinds:
            load_x(j).start()
            pair_x(j).start()
        load_g(k).start()
        pair_g(k).start()

    def turn(k):
        return lax.rem(k + number - 1, number)

    reach = count // 2

    def owner_at(stage, way):
        ahead = reach - stage
        return ring_device(place + ahead if way == 0 else place - ahead, count)

    def rows_of(owner):
        return pl.ds(pl.multiple_of(owner * depth, depth), depth)

    def quarter(q):
        return slice(q * wide, (q + 1) * wide)

    def hop(k, stage, way, start=False):
        if start:
            source = terms.at[k, rows_of(owner_at(0, way)), quarter(way)]
            target = held.at[k, way, 0, :, quarter(way)]
        else:
            source = held.at[k, way, stage - 1]
            target = held.at[k, way, stage]
        return pltpu.make_async_remote_copy(
            source,
            target,
            send_sem.at[stage, way, k],
            recv_sem.at[stage, way, k],
            device_id=sides[way],
            device_id_type=MESH,
        )

    def cross(k, d):
        return pltpu.make_async_remote_copy(
            across.at[team, k],
            across.at[team, k],
            cross_send.at[d, k],
            cross_recv.at[d, k],
            device_id=partners[d],
            device_id_type=MESH,
        )

    @pl.loop(0, number)
    def _(k):
        k = turn(k)
        j = jnp.maximum(k - (number - kinds), 0)

        @pl.when((k == 0) | (k > number - kinds))
        def _():
            load_x(j).wait()
            pair_x(j).wait_recv()

        load_g(k).wait()
        pair_g(k).wait_recv()
        for r in range(0, width, 256):
            piece = slice(r, r + 256)
            terms[k, piece, :] = (
                mm(xv[j, 0, piece, :], gv[k, 0]) + mm(xv[j, 1, piece, :], gv[k, 1])
            ).astype(bf16)
        for way in range(2):
            hop(k, 0, way, True).start()

    def relay(k, stage):
        for way in range(2):
            here = rows_of(owner_at(stage, way))

            @pl.when(stage == 1)
            def _():
                hop(k, 0, way, True).wait_recv()
                both = terms[k, here, quarter(way)].astype(f32)
                both = both + held[k, way, 0, :, quarter(way)].astype(f32)
                held[k, way, 0, :, quarter(way)] = both.astype(bf16)
                held[k, way, 0, :, quarter(1 - way)] = terms[k, here, quarter(1 - way)]

            @pl.when(stage > 1)
            def _():
                hop(k, stage - 1, way).wait_recv()
                both = terms[k, here, :].astype(f32) + held[k, way, stage - 1].astype(f32)
                held[k, way, stage - 1] = both.astype(bf16)

            hop(k, stage, way).start()

    def relay_number(e):
        relay(turn(lax.rem(e, number)), 1 + e // number)

    relays = (reach - 1) * number
    tiles = images * steps
    pace = min(-(-relays // tiles), 2)
    t_acc[...] = jnp.zeros_like(t_acc)

    @pl.loop(0, tiles)
    def _(t):
        image = lax.rem(t // steps + owners.image, images)
        step = lax.rem(t, steps)
        for e in range(pace):

            @pl.when(t * pace + e < relays)
            def _():
                relay_number(t * pace + e)

        @pl.when(step == 0)
        def _():
            for h in range(sharers):
                source = image * sharers + h

                sender = owners.device(group, image, jnp.int32(h))

                @pl.when(jnp.logical_not(owners.is_me(sender)))
                def _():
                    for copy in back_from(source):
                        copy.wait_recv()

                here = slice(h * rows, (h + 1) * rows)
                wide = jnp.dot(
                    gained_ref[:, : back_ref.shape[0]],
                    back_all[source].astype(f32),
                    precision=lax.Precision.HIGHEST,
                    preferred_element_type=f32,
                )
                bt[:, here] = wide.astype(bf16)
                b_low[here, :] = wide.T.astype(bf16)
                stat[:, here] = row_all[source]

        span = pl.ds(pl.multiple_of(step * tile, 128), tile)
        values = v_ref[image, :, span]
        x, xt = build_both(values, step * lines, code_ref)
        halves = (slice(0, tile // 2), slice(tile // 2, tile))
        products = [(mm(x[half], at_ref[...]), mm(x[half], bt[...])) for half in halves]
        kept, ends = [], []
        for half, (scores, grad_p) in zip(halves, products):
            probs = jnp.exp2(scores - stat[0:1, :])
            grad_s = (probs * (grad_p - stat[1:2, :])).astype(bf16)
            kept.append(grad_s)
            back = mm(grad_s, a_ref[...]) + mm(probs.astype(bf16), b_low[...])
            along = jnp.sum(back * x[half].astype(f32), axis=1, keepdims=True)
            end = back[:, CHANNELS - 128 :]
            lane = lax.broadcasted_iota(jnp.int32, end.shape, 1)
            ends.append(jnp.where(lane == 120, along, end))
        t_acc[...] += mm(xt, jnp.concatenate(kept, axis=0))
        ends = jnp.concatenate(ends, axis=0).T[120:128, :] * (values[0:1, :] * values[1:2, :])
        hat = values[4:7, :] + values[7:8, :]
        mean_part = ends[7:8, :] + hat * ends[0:1, :]
        pixel_ref[image, :, span] = ends[4:7, :] - mean_part * (1.0 / channels)

    t_sum = lax.dot_general(
        t_acc[:CHANNELS, :],
        table_ref[:, : t_raw.shape[2]],
        (((0,), (0,)), ((), ())),
        precision=lax.Precision.HIGHEST,
        preferred_element_type=f32,
    )
    t_raw[...] = t_sum.astype(bf16).reshape(t_raw.shape)
    for d in range(count - 1):
        for copy in scatter(d):
            copy.start()

    if tiles * pace < relays:

        @pl.loop(tiles * pace, relays)
        def _(e):
            relay_number(e)

    @pl.loop(0, number)
    def _(k):
        k = turn(k)
        for way in range(2):
            hop(k, reach - 1, way, reach == 1).wait_recv()
        total = terms[k, rows_of(me), :].astype(f32)
        for way in range(2):
            total = total + held[k, way, reach - 1].astype(f32)
        across[team, k] = total.astype(bf16)
        for d in range(teams - 1):
            cross(k, d).start()

    t_sum, g_sum = t_raw[me].astype(f32), g_raw[me]
    for d in range(count - 1):
        for copy in scatter(d):
            copy.wait_recv()
        t_sum = t_sum + t_in[d].astype(f32)
        g_sum = g_sum + g_in[d]
    t_img[group] = t_sum.astype(bf16)
    g_img[group] = g_sum
    for d in range(crowd - 1):
        for copy in over(d):
            copy.start()

    def finish(k):
        columns = pl.ds(pl.multiple_of(core * half, 128), half)
        return pltpu.make_async_copy(done.at[k], out_ref.at[k, :, columns], out_sem.at[k])

    def hand(k):
        columns = pl.ds(pl.multiple_of(core * half, 128), half)
        return pltpu.make_async_remote_copy(
            done.at[k],
            out_ref.at[k, :, columns],
            hand_send.at[k],
            hand_recv.at[k],
            device_id=other,
            device_id_type=MESH,
        )

    @pl.loop(0, number)
    def _(k):
        k = turn(k)
        for d in range(teams - 1):
            cross(k, d).wait_recv()
        total = across[0, k].astype(f32)
        for t in range(1, teams):
            total = total + across[t, k].astype(f32)
        done[k] = total
        finish(k).start()
        hand(k).start()

        @pl.when(k == number - 1)
        def _():
            rows_here = t_raw.shape[1]
            mine = done[number - 1, rows_here : rows_here + z_own.shape[0], :].astype(bf16)
            z_own[...] = mine
            z_out[core, me] = mine
            for d in range(count - 1):
                z_push(d).start()

    for d in range(crowd - 1):
        for copy in over(d):
            copy.wait_recv()
    t_sum, g_sum = t_img[0].astype(f32), g_img[0]
    for i in range(1, crowd):
        t_sum = t_sum + t_img[i].astype(f32)
        g_sum = g_sum + g_img[i]
    t_out[me] = t_sum.astype(bf16)
    g_out[me] = g_sum
    for d in range(count - 1):
        for copy in gather(d):
            copy.start()
    for d in range(count - 1):
        z_push(d).wait()
    z_hand().start()
    for d in range(count - 1):
        for copy in gather(d):
            copy.wait()
        for copy in scatter(d):
            copy.wait_send()
    for d in range(crowd - 1):
        for copy in over(d):
            copy.wait_send()
    z_hand().wait()

    @pl.loop(0, number)
    def _(k):
        finish(k).wait()
        hand(k).wait()
        pair_g(k).wait_send()
        for way in range(2):
            for stage in range(reach):
                hop(k, stage, way, stage == 0).wait_send()
        for d in range(teams - 1):
            cross(k, d).wait_send()

    @pl.loop(0, kinds)
    def _(j):
        pair_x(j).wait_send()

    for d in range(count):
        to, copies = back_push(d)

        @pl.when(jnp.logical_not(owners.is_me(to)))
        def _():
            for copy in copies:
                copy.wait_send()


def backward_pass(
    values, table, gained, at, a, back, rows_in, gains, xs, gs, channels, collective_id
):
    count = lax.axis_size("pix")
    teams = lax.axis_size("img") // 2
    kinds, _, rows = xs.shape
    number, _, width = gs.shape
    depth = xs.shape[1] // count
    anywhere = pl.BlockSpec(memory_space=pl.ANY)
    inside = pl.BlockSpec(memory_space=pltpu.VMEM)
    chunk = (depth, width // 2)
    images, _, pixels = values.shape
    tile = pixel_tile(pixels)
    latents = at.shape[1]
    tall = back.shape[0]
    shape = jax.ShapeDtypeStruct
    rows_here = latents // count
    t_shape = shape((count, rows_here, -(-channels // 128) * 128), bf16)
    g_shape = shape((count, 8, depth), f32)
    spare = min(-(-share_rows(channels, count) // 16) * 16, depth - rows_here)
    return pl.pallas_call(
        functools.partial(backward_kernel, count, teams, images, tile, channels),
        out_shape=[
            t_shape,
            g_shape,
            shape((2, count, spare, width // 2), bf16),
            shape((images, 3, pixels), f32),
            shape((number, depth, width), f32),
        ],
        in_specs=[inside] * 9 + [anywhere] * 2,
        out_specs=[inside] * 4 + [anywhere],
        scratch_shapes=[
            pltpu.VMEM(t_shape.shape, bf16),
            pltpu.VMEM((count - 1,) + t_shape.shape[1:], bf16),
            pltpu.VMEM((2 * teams,) + t_shape.shape[1:], bf16),
            pltpu.VMEM(g_shape.shape, f32),
            pltpu.VMEM((count - 1,) + g_shape.shape[1:], f32),
            pltpu.VMEM((2 * teams,) + g_shape.shape[1:], f32),
            pltpu.VMEM((spare, width // 2), bf16),
            pltpu.VMEM((CHANNELS + 16, latents), f32),
            pltpu.VMEM((CHANNELS, latents), bf16),
            pltpu.VMEM((latents, CHANNELS), bf16),
            pltpu.VMEM((8, latents), f32),
            pltpu.VMEM((count, tall, rows), bf16),
            pltpu.VMEM((count, 8, rows), f32),
            pltpu.VMEM((kinds, 2, xs.shape[1], rows), bf16),
            pltpu.VMEM((number, 2, rows, width // 2), bf16),
            pltpu.VMEM((number, xs.shape[1], width // 2), bf16),
            pltpu.VMEM((number, 2, count // 2) + chunk, bf16),
            pltpu.VMEM((teams, number) + chunk, bf16),
            pltpu.VMEM((number, depth, width // 2), f32),
            DMA((2, number)),
            DMA((2, number)),
            DMA((2, number)),
            DMA((count // 2, 2, number)),
            DMA((count // 2, 2, number)),
            DMA((teams - 1, number)),
            DMA((teams - 1, number)),
            DMA((number,)),
            DMA((number,)),
            DMA((number,)),
            DMA((2, count)),
            DMA((2, count)),
            DMA((2, count - 1)),
            DMA((2, count - 1)),
            DMA((2, 2 * teams - 1)),
            DMA((2, 2 * teams - 1)),
            DMA((2, count - 1)),
            DMA((2, count - 1)),
            DMA((count - 1,)),
            DMA((count - 1,)),
            DMA,
            DMA,
        ],
        compiler_params=pltpu.CompilerParams(
            collective_id=collective_id, has_side_effects=True, vmem_limit_bytes=60 * 2**20
        ),
    )(values, hot_codes(tile), table, gained, at, a, back, rows_in, gains, xs, gs)


def peers(count):
    group, me = lax.axis_index("img"), lax.axis_index("pix")
    return [(group, lax.rem(me + d, count)) for d in range(1, count)]


def plane(count):
    group, me = lax.axis_index("img"), lax.axis_index("pix")
    other = group + 1 - 2 * lax.rem(group, 2)
    return peers(count) + [(other, lax.rem(me + d, count)) for d in range(count)]


class Owners:
    def __init__(self, count, images):
        self.group, self.me = lax.axis_index("img"), lax.axis_index("pix")
        self.core = lax.rem(self.group, 2)
        self.base = self.group - self.core
        self.images = images
        self.chips = count // (2 * images)
        self.sharers = 2 * self.chips
        self.slot = lax.rem(self.me, self.chips) * 2 + self.core
        image = self.me // self.chips
        self.image = lax.rem(image, images)
        self.home = self.base + image // images

    def device(self, group, image, slot):
        core = lax.rem(group, 2)
        chip = (core * self.images + image) * self.chips + slot // 2
        return self.base + lax.rem(slot, 2), chip

    def is_me(self, device):
        return (device[0] == self.group) & (device[1] == self.me)


def share_rows(channels, count):
    channels = -(-channels // 16) * 16
    return -(-(-(-channels // count)) // 8) * 8


def gelu_parts(z):
    slope = (2.0 / jnp.pi) ** 0.5
    square = z * z
    bend = jnp.tanh(slope * z * (1.0 + 0.044715 * square))
    half = 0.5 * (1.0 + bend)
    return z * half, half + 0.5 * z * (1.0 - bend * bend) * slope * (1.0 + 0.134145 * square)


def latent_kernel(
    count,
    images,
    part_ref,
    stat_ref,
    own_ref,
    cot_ref,
    mix_ref,
    gain_ref,
    in_gain_ref,
    w_ref,
    late_up,
    late_down,
    out_ref,
    xs_ref,
    gs_ref,
    back_ref,
    row_ref,
    gain_out,
    wv,
    one,
    two,
    three,
    pre,
    grad,
    flow,
    low,
    heads_q,
    kv,
    probs,
    kv_out,
    kv_in,
    cot,
    final,
    mean,
    own_v,
    own_sem,
    w_sem,
    ring_own,
    ring_send,
    ring_recv,
    hand_send,
    hand_recv,
    kv_send,
    kv_recv,
    gkv_send,
    gkv_recv,
    cot_own,
    cot_send,
    cot_recv,
    out_own,
    out_send,
    out_recv,
):
    rows, width = one.shape
    depth = width // count
    owners = Owners(count, images)
    sharers = owners.sharers
    latents = rows * sharers
    per = count // sharers
    rows_here = latents // count
    spare = depth - rows_here
    group, me = lax.axis_index("img"), lax.axis_index("pix")
    slot, image, home = owners.slot, owners.image, owners.home
    block = 256
    blocks = width // block
    row_block = min(rows, 64)
    up_one, down_one, m_query, m_key, m_value, m_out, up_two, down_two = range(8)
    scale = HEAD_DIM ** (-0.5)

    def load(k):
        return pltpu.make_async_copy(w_ref.at[k], wv.at[k], w_sem.at[k])

    early, late_refs = w_ref.shape[0], (late_up, late_down)
    late = len(late_refs)
    own_copy = pltpu.make_async_copy(
        own_ref.at[pl.ds(pl.multiple_of(slot * rows, 16), rows)], own_v, own_sem
    )
    own_copy.start()
    for k in range(early):
        load(k).start()
    greet(plane(count))

    core = lax.rem(group, 2)
    ring = ring_place(count)
    sides = ((group, ring_device(ring + 1, count)), (group, ring_device(ring - 1, count)))
    other = (group + 1 - 2 * core, me)

    reach = count // 2

    def spot(k, stage, way, last, source=False):
        begin = (core * 2 + way) * (width // 4) if last else core * (width // 2)
        some = pl.ds(pl.multiple_of(begin, 128), width // 4 if last else width // 2)
        if source:
            return late_refs[k].at[:, some]
        origin = ring_device(ring - stage if way == 0 else ring + stage, count)
        here = pl.ds(pl.multiple_of(origin * depth, depth), depth)
        return wv.at[early + k, here, some]

    def hop(k, stage, way, start=False, last=False):
        return pltpu.make_async_remote_copy(
            spot(k, stage, way, last, start),
            spot(k, stage, way, last),
            ring_send.at[stage, way, k],
            ring_recv.at[stage, way, k],
            device_id=sides[way],
            device_id_type=MESH,
        )

    def hand(k, stage, way, last=False):
        return pltpu.make_async_remote_copy(
            spot(k, stage, way, last),
            spot(k, stage, way, last),
            hand_send.at[stage - 1, way, k],
            hand_recv.at[stage - 1, way, k],
            device_id=other,
            device_id_type=MESH,
        )

    def ring_keep(k):
        here = pl.ds(pl.multiple_of(me * depth, depth), depth)
        return pltpu.make_async_copy(late_refs[k], wv.at[early + k, here], ring_own.at[k])

    for k in range(late):
        for way in range(2):
            hop(k, 0, way, True, reach == 1).start()
        ring_keep(k).start()

    def relays(first, end):
        for stage in range(first, min(end, reach + 1)):
            for k in range(late):
                for way in range(2):
                    last = stage == reach
                    hop(k, stage - 1, way, last=last).wait_recv()
                    if stage < reach:
                        hop(k, stage, way, last=stage == reach - 1).start()
                    hand(k, stage, way, last).start()

    def arrived(k):
        ring_keep(k).wait()
        for stage in range(1, reach + 1):
            for way in range(2):
                hand(k, stage, way, stage == reach).wait_recv()

    def cot_push(i):
        to = owners.device(group, i, me // per)
        return to, pltpu.make_async_remote_copy(
            cot_ref.at[i],
            cot.at[lax.rem(me, per)],
            cot_send.at[i],
            cot_recv.at[lax.rem(me, per)],
            device_id=to,
            device_id_type=MESH,
        )

    def cot_keep():
        return pltpu.make_async_copy(cot_ref.at[image], cot.at[lax.rem(me, per)], cot_own)

    for i in range(images):
        to, copy = cot_push(i)

        @pl.when(jnp.logical_not(owners.is_me(to)))
        def _():
            copy.start()

        @pl.when(owners.is_me(to))
        def _():
            cot_keep().start()

    def columns(j, wide=block):
        return pl.ds(pl.multiple_of(j * wide, wide), wide)

    def over_columns(body, times=blocks):
        pl.loop(0, times)(body)

    def over_rows(body):
        @pl.loop(0, rows // row_block)
        def _(r):
            body(pl.ds(pl.multiple_of(r * row_block, 16), row_block))

    def put_x(j, c, value):
        xs_ref[j, columns(c), :] = value.T

    def centre(rows_f32):
        average = jnp.mean(rows_f32, axis=1, keepdims=True)
        centred = rows_f32 - average
        spread = jnp.mean(centred * centred, axis=1, keepdims=True)
        scale_rows = lax.rsqrt(spread + eps)
        return centred * scale_rows, scale_rows

    def norm(source, k, target):
        def body(r):
            target[r] = (centre(source[r])[0] * gain_ref[k : k + 1, :]).astype(bf16)

        over_rows(body)

    def norm_grad(source, k):
        def body(r):
            hat, scale_rows = centre(source[r])
            given = flow[r]
            gain_out[k : k + 1, :] += jnp.sum(given * hat, axis=0, keepdims=True)
            given = given * gain_ref[k : k + 1, :]
            along = jnp.mean(given * hat, axis=1, keepdims=True)
            grad[r] += scale_rows * (given - jnp.mean(given, axis=1, keepdims=True) - hat * along)

        over_rows(body)

    gain_out[...] = jnp.zeros_like(gain_out)

    top = jnp.max(stat_ref[:, 0:1, :], axis=0)
    total = jnp.zeros_like(top)
    for d in range(count):
        total = total + jnp.exp2(stat_ref[d, 0:1, :] - top) * stat_ref[d, 1:2, :]
    raw = jnp.zeros(part_ref.shape[1:], f32)
    for d in range(count):
        raw = raw + part_ref[d].astype(f32) * (jnp.exp2(stat_ref[d, 0:1, :] - top) / total)
    mean[0] = raw
    mean[1] = raw * in_gain_ref[...]
    row_ref[...] = jnp.zeros_like(row_ref)
    row_ref[0:1, :] = top + jnp.log(total) * LOG2E

    tall = count * spare
    mean_tall = mean[1]
    if tall > mean_tall.shape[0]:
        mean_tall = jnp.concatenate(
            [mean_tall, jnp.zeros((tall - mean_tall.shape[0], rows), f32)], axis=0
        )
    share = share_rows(mean.shape[1], count)
    place = lax.broadcasted_iota(jnp.int32, (rows_here, rows), 0)
    source_row = lax.broadcasted_iota(jnp.int32, (rows_here, rows), 1) + slot * rows
    for o in range(count):
        picks = jnp.where(place + o * rows_here == source_row, 1.0, 0.0)
        piece = [picks, mean_tall[o * share : (o + 1) * share]]
        if spare > share:
            piece.append(jnp.zeros((spare - share, rows), f32))
        xs_ref[6, o * depth : (o + 1) * depth, :] = jnp.concatenate(piece, axis=0).astype(bf16)

    mean_low = mean[1].astype(bf16)

    def make_one(j):
        one[:, columns(j)] = own_v[:, columns(j)].astype(f32) + mm_tn(mean_low, mix_ref[:, columns(j)])

    own_copy.wait()
    over_columns(make_one)

    def ready(k):
        if k < early:
            load(k).wait()
        else:
            arrived(k - early)

    def feed(source, target, k, up, down, normed, x_hidden, keep):
        norm(source, k, normed)
        ready(up)

        def make_hidden(j):
            value = mm_nt(normed[...], wv[up, columns(j), :])
            pre[keep, :, columns(j)] = value
            hidden = gelu_parts(value)[0].astype(bf16)
            low[:, columns(j)] = hidden
            put_x(x_hidden, j, hidden)

        over_columns(make_hidden)
        ready(down)

        def make_branch(j):
            value = source[:, columns(j)] + mm(low[...], wv[down, :, columns(j)])
            target[:, columns(j)] = value.astype(target.dtype)

        over_columns(make_branch)

    def feed_back(source, k, up, down, branch, x_pre, keep):
        @over_columns
        def _(j):
            value = mm_nt(branch[...], wv[down, columns(j), :])
            value = (value * gelu_parts(pre[keep, :, columns(j)])[1]).astype(bf16)
            low[:, columns(j)] = value
            put_x(x_pre, j, value)

        @over_columns
        def _(j):
            flow[:, columns(j)] = mm(low[...], wv[up, :, columns(j)])

        norm_grad(source, k)

    feed(one, two, 0, up_one, down_one, gs_ref.at[4], 3, 0)
    relays(1, 2)

    norm(two, 1, low)

    load(m_key).wait()
    load(m_value).wait()

    def make_kv(j):
        put_x(0, j, low[:, columns(j)])
        kv[0, slot, :, columns(j)] = mm(low[...], wv[m_key, :, columns(j)]).astype(bf16)
        kv[1, slot, :, columns(j)] = mm(low[...], wv[m_value, :, columns(j)]).astype(bf16)

    over_columns(make_kv)

    def sharer(d):
        return owners.device(home, image, lax.rem(slot + d, sharers))

    def kv_push(d):
        return pltpu.make_async_remote_copy(
            kv.at[:, slot],
            kv.at[:, slot],
            kv_send.at[d - 1],
            kv_recv.at[d - 1],
            device_id=sharer(d),
            device_id_type=MESH,
        )

    for d in range(1, sharers):
        kv_push(d).start()
    load(m_query).wait()

    @over_columns
    def _(j):
        heads_q[:, columns(j)] = mm(low[...], wv[m_query, :, columns(j)]).astype(bf16)

    for d in range(1, sharers):
        kv_push(d).wait_recv()

    def attend(h):
        c = columns(h, HEAD_DIM)
        k_all = kv[0, :, :, c].reshape(latents, HEAD_DIM)
        v_all = kv[1, :, :, c].reshape(latents, HEAD_DIM)
        scores = mm_nt(heads_q[:, c], k_all) * scale
        shifted = jnp.exp(scores - jnp.max(scores, axis=1, keepdims=True))
        p = shifted / jnp.sum(shifted, axis=1, keepdims=True)
        probs[h] = p
        low[:, c] = mm(p.astype(bf16), v_all).astype(bf16)

    relays(2, 3)
    pl.loop(0, HEADS // 2)(attend)
    relays(3, 4)
    pl.loop(HEADS // 2, HEADS)(attend)

    @over_columns
    def _(j):
        put_x(1, j, low[:, columns(j)])

    ready(m_out)

    @over_columns
    def _(j):
        three[:, columns(j)] = two[:, columns(j)] + mm(low[...], wv[m_out, :, columns(j)])

    relays(4, reach + 1)
    feed(three, final, 2, up_two, down_two, gs_ref.at[6], 5, 1)

    def out_push(b):
        to = (home, slot * per + b)
        return to, pltpu.make_async_remote_copy(
            final.at[pl.ds(b * rows_here, rows_here)],
            out_ref.at[image],
            out_send.at[b],
            out_recv.at[image],
            device_id=to,
            device_id_type=MESH,
        )

    def out_keep():
        mine = pl.ds(pl.multiple_of(lax.rem(me, per) * rows_here, 16), rows_here)
        return pltpu.make_async_copy(final.at[mine], out_ref.at[image], out_own)

    for b in range(per):
        to, copy = out_push(b)

        @pl.when(jnp.logical_not(owners.is_me(to)))
        def _():
            copy.start()

        @pl.when(owners.is_me(to))
        def _():
            out_keep().start()

    def cot_from(b):
        return pltpu.make_async_remote_copy(
            cot_ref.at[0],
            cot.at[b],
            cot_send.at[0],
            cot_recv.at[b],
            device_id=(group, me),
            device_id_type=MESH,
        )

    for b in range(per):

        local = owners.is_me((home, slot * per + b))

        @pl.when(jnp.logical_not(local))
        def _():
            cot_from(b).wait_recv()

        @pl.when(local)
        def _():
            cot_keep().wait()

    given = cot[...].reshape(rows, width)
    gs_ref[7] = given
    grad[...] = given.astype(f32)
    feed_back(three, 2, up_two, down_two, gs_ref.at[7], 4, 1)

    gs_ref[3] = grad[...].astype(bf16)

    @over_columns
    def _(j):
        low[:, columns(j)] = mm_nt(gs_ref[3], wv[m_out, columns(j), :]).astype(bf16)

    @pl.loop(0, HEADS)
    def _(h):
        c = columns(h, HEAD_DIM)
        k_all = kv[0, :, :, c].reshape(latents, HEAD_DIM)
        v_all = kv[1, :, :, c].reshape(latents, HEAD_DIM)
        p = probs[h]
        g_mixed = low[:, c]
        g_p = mm_nt(g_mixed, v_all)
        g_v = mm_tn(p.astype(bf16), g_mixed)
        delta = jnp.sum(p * g_p, axis=1, keepdims=True)
        g_s = (p * (g_p - delta)).astype(bf16)
        gs_ref[0, :, c] = (mm(g_s, k_all) * scale).astype(bf16)
        g_k = mm_tn(g_s, heads_q[:, c]) * scale
        kv_out[:, 0, :, c] = g_k.reshape(sharers, rows, HEAD_DIM).astype(bf16)
        kv_out[:, 1, :, c] = g_v.reshape(sharers, rows, HEAD_DIM).astype(bf16)

    def gkv_push(d):
        to = lax.rem(slot + d, sharers)
        return pltpu.make_async_remote_copy(
            kv_out.at[to],
            kv_in.at[d - 1],
            gkv_send.at[d - 1],
            gkv_recv.at[d - 1],
            device_id=sharer(d),
            device_id_type=MESH,
        )

    for d in range(1, sharers):
        gkv_push(d).start()

    @over_columns
    def _(j):
        flow[:, columns(j)] = mm_nt(gs_ref[0], wv[m_query, columns(j), :])

    for d in range(1, sharers):
        gkv_push(d).wait_recv()
    for which in range(2):

        @over_columns
        def _(j):
            value = kv_out[slot, which, :, columns(j)].astype(f32)
            for d in range(1, sharers):
                value = value + kv_in[d - 1, which, :, columns(j)].astype(f32)
            gs_ref[1 + which, :, columns(j)] = value.astype(bf16)

    @over_columns
    def _(j):
        flow[:, columns(j)] += mm_nt(gs_ref[1], wv[m_key, columns(j), :]) + mm_nt(
            gs_ref[2], wv[m_value, columns(j), :]
        )

    norm_grad(two, 1)
    gs_ref[5] = grad[...].astype(bf16)
    feed_back(one, 0, up_one, down_one, gs_ref.at[5], 2, 0)
    gs_ref[8] = grad[...].astype(bf16)
    back = mm_nt(mix_ref[...], gs_ref[8])
    back_ref[...] = back.astype(bf16)
    row_ref[1:2, :] = jnp.sum(back * mean[1], axis=0, keepdims=True)
    in_gain = jnp.broadcast_to(
        jnp.sum(back * mean[0], axis=1, keepdims=True), (back.shape[0], 128)
    )
    gain_out[3:4, : back.shape[0]] = in_gain.T[0:1, :]

    for i in range(images):
        to, copy = cot_push(i)

        @pl.when(jnp.logical_not(owners.is_me(to)))
        def _():
            copy.wait_send()

    for d in range(1, sharers):
        kv_push(d).wait_send()
        gkv_push(d).wait_send()
    for k in range(late):
        for stage in range(reach):
            for way in range(2):
                last = stage == reach - 1
                hop(k, stage, way, stage == 0, last).wait_send()
                hand(k, stage + 1, way, last).wait_send()

    def out_from(i):
        return pltpu.make_async_remote_copy(
            final.at[pl.ds(0, rows_here)],
            out_ref.at[i],
            out_send.at[0],
            out_recv.at[i],
            device_id=(group, me),
            device_id_type=MESH,
        )

    for b in range(per):
        to, copy = out_push(b)

        @pl.when(jnp.logical_not(owners.is_me(to)))
        def _():
            copy.wait_send()

    for i in range(images):
        local = owners.is_me(owners.device(group, i, me // per))

        @pl.when(jnp.logical_not(local))
        def _():
            out_from(i).wait_recv()

        @pl.when(local)
        def _():
            out_keep().wait()


def latent_pass(parts, stats, own, cotangent, mix, gains, in_gain, whole, late, rows, collective_id):
    count = lax.axis_size("pix")
    images, rows_here, width = cotangent.shape
    channels = mix.shape[0]
    sharers = count // images
    per = count // sharers
    inside = pl.BlockSpec(memory_space=pltpu.VMEM)
    anywhere = pl.BlockSpec(memory_space=pl.ANY)
    whole_f32 = pltpu.VMEM((rows, width), f32)
    whole_low = pltpu.VMEM((rows, width), bf16)
    ring = DMA((count // 2, 2, len(late)))
    shape = jax.ShapeDtypeStruct
    return pl.pallas_call(
        functools.partial(latent_kernel, count, images),
        out_shape=[
            shape((images, rows_here, width), bf16),
            shape((7, width, rows), bf16),
            shape((9, rows, width), bf16),
            shape((channels, rows), bf16),
            shape((8, rows), f32),
            shape((8, width), f32),
        ],
        in_specs=[inside] * 2 + [anywhere] * 2 + [inside] * 3 + [anywhere] * 3,
        out_specs=[anywhere] + [inside] * 5,
        scratch_shapes=[
            pltpu.VMEM((8, width, width), bf16),
            whole_f32,
            whole_f32,
            whole_f32,
            pltpu.VMEM((2, rows, width), f32),
            whole_f32,
            whole_f32,
            whole_low,
            whole_low,
            pltpu.VMEM((2, sharers, rows, width), bf16),
            pltpu.VMEM((HEADS, rows, rows * sharers), f32),
            pltpu.VMEM((sharers, 2, rows, width), bf16),
            pltpu.VMEM((max(sharers - 1, 1), 2, rows, width), bf16),
            pltpu.VMEM((per, rows_here, width), bf16),
            whole_low,
            pltpu.VMEM((2, channels, rows), f32),
            whole_low,
            DMA,
            DMA((whole.shape[0],)),
            DMA((len(late),)),
            ring,
            ring,
            ring,
            ring,
            DMA((sharers,)),
            DMA((sharers,)),
            DMA((sharers,)),
            DMA((sharers,)),
            DMA,
            DMA((images,)),
            DMA((per,)),
            DMA,
            DMA((per,)),
            DMA((images,)),
        ],
        compiler_params=pltpu.CompilerParams(
            collective_id=collective_id, has_side_effects=True, vmem_limit_bytes=60 * 2**20
        ),
    )(parts, stats, own, cotangent, mix, gains, in_gain, whole, *late)


def tail_kernel(
    count,
    channels,
    t_ref,
    g_ref,
    z_ref,
    a_ref,
    lat_ref,
    qcols_ref,
    ncols_ref,
    wq_ref,
    wk_ref,
    wv_ref,
    wco_ref,
    gain_ref,
    lat_gain_ref,
    sum_ref,
    lat_out,
    lat_gain_out,
    gains_out,
    wq_out,
    wk_out,
    wv_out,
    wco_out,
    up_one_out,
    up_two_out,
    down_one_out,
    down_two_out,
    sq_out,
    sk_out,
    sv_out,
    so_out,
    z_v,
    query_grad,
    flow,
):
    me = lax.axis_index("pix")
    width = wq_ref.shape[0]
    depth = wco_ref.shape[0]
    rows_here = lat_out.shape[0]
    latents = lat_ref.shape[0]
    across = t_ref.shape[1]
    for k, to in (
        (0, sq_out),
        (1, sk_out),
        (2, sv_out),
        (3, so_out),
        (5, down_one_out),
        (7, down_two_out),
    ):
        to[...] = sum_ref[k]
    t = t_ref[...].astype(f32)
    tx = (t * (gain_ref[...] * width ** (-0.5))).astype(bf16)
    for o in range(count):
        gains_out[:, o * depth : (o + 1) * depth] = g_ref[o]
    row = jnp.sum(a_ref[:, :across] * t, axis=0, keepdims=True)
    gains_out[3:4, :across] += row
    wk_out[...] = mm_tn(tx, qcols_ref[...])[:channels]

    @pl.loop(0, width // 256)
    def _(j):
        columns = pl.ds(pl.multiple_of(j * 256, 256), 256)
        query_grad[:, columns] = mm_nt(tx, wk_ref[columns, :across]).astype(bf16)

    @pl.loop(0, width // 256)
    def _(j):
        columns = pl.ds(pl.multiple_of(j * 256, 256), 256)
        wq_out[:, columns] = mm_tn(ncols_ref[...], query_grad[:, columns])
        flow[:, columns] = mm_nt(query_grad[...], wq_ref[columns, :])

    share = share_rows(channels, count)
    half = width // 2
    for o in range(count):
        for h in range(2):
            z_v[o * share : (o + 1) * share, h * half : (h + 1) * half] = z_ref[h, o, :share].astype(f32)
    cross = z_v[...].astype(bf16)
    wv_out[...] = mm_nt(cross, wco_ref[...])[:channels]
    wco_out[...] = mm_tn(wv_ref[...], cross)

    up_one_out[...] = sum_ref[4].T
    up_two_out[...] = sum_ref[6].T
    lat_gain_out[...] = jnp.zeros_like(lat_gain_out)

    @pl.loop(0, count)
    def _(o):
        here = pl.ds(pl.multiple_of(o * rows_here, rows_here), rows_here)
        rows = lat_ref[here, :].astype(f32)
        average = jnp.mean(rows, axis=1, keepdims=True)
        centred = rows - average
        scale = lax.rsqrt(jnp.mean(centred * centred, axis=1, keepdims=True) + eps)
        hat = centred * scale
        given = flow[here, :]
        lat_gain_out[...] += jnp.sum(given * hat, axis=0, keepdims=True)

        @pl.when(o == me)
        def _():
            gained = given * lat_gain_ref[...]
            along = jnp.mean(gained * hat, axis=1, keepdims=True)
            moved = scale * (gained - jnp.mean(gained, axis=1, keepdims=True) - hat * along)
            lat_out[...] = moved + sum_ref[8, :rows_here, :]


def tail_pass(t, g, z, a, lat, qcols, ncols, wq, wk, wv, wco, gain, lat_gain, summed, channels):
    count = z.shape[1]
    _, depth, width = summed.shape
    latents = lat.shape[0]
    share = share_rows(channels, count)
    inside = pl.BlockSpec(memory_space=pltpu.VMEM)
    anywhere = pl.BlockSpec(memory_space=pl.ANY)
    shape = lambda *dims: jax.ShapeDtypeStruct(dims, f32)
    plain = shape(depth, width)
    return pl.pallas_call(
        functools.partial(tail_kernel, count, channels),
        out_shape=[
            shape(latents // count, width),
            shape(1, width),
            shape(8, width),
            plain,
            shape(channels, depth),
            shape(channels, depth),
            plain,
            shape(width, depth),
            shape(width, depth),
        ]
        + [plain] * 6,
        in_specs=[inside] * 14,
        out_specs=[inside] * 15,
        scratch_shapes=[
            pltpu.VMEM((count * share, width), f32),
            pltpu.VMEM((latents, width), bf16),
            pltpu.VMEM((latents, width), f32),
        ],
        compiler_params=pltpu.CompilerParams(vmem_limit_bytes=48 * 2**20),
    )(t, g, z, a, lat, qcols, ncols, wq, wk, wv, wco, gain, lat_gain, summed)


def local(
    rgb_pixels,
    keep_mask,
    latent_array,
    gain_input,
    gain_latent,
    w_query,
    w_key,
    w_value,
    w_cross_out,
    gain_mlp_one,
    w_up_one,
    w_down_one,
    gain_self,
    w_self_query,
    w_self_key,
    w_self_value,
    w_self_out,
    gain_mlp_two,
    w_up_two,
    w_down_two,
    cotangent,
):
    images, _, pixels = rgb_pixels.shape
    rows_here, width = latent_array.shape
    count = lax.axis_size("pix")
    me = lax.axis_index("pix")
    latents = rows_here * count
    sharers = count // images
    rows_own = latents // sharers
    depth = w_query.shape[0]
    channels = gain_input.shape[0]
    tall = -(-channels // 16) * 16

    side = -(-channels // 512) * 512
    key_t = jnp.pad(w_key.T, ((0, 0), (0, side - channels)))
    value_pad = jnp.pad(w_value, ((0, tall - channels), (0, 0)))
    value_out = lax.psum(mm(value_pad, w_cross_out).astype(bf16), "pix")
    shards = [w_up_one.T, w_down_one, w_self_query, w_self_key, w_self_value, w_self_out]
    late = [w_up_two.T, w_down_two]

    lines = pixels // SIDE
    u, sin_u, cos_u = angles(me * lines + lax.iota(jnp.int32, lines))
    w, sin_w, cos_w = angles(lax.iota(jnp.int32, SIDE))

    def zeros(rows, columns):
        return jnp.zeros((rows, columns), f32)

    pad = CHANNELS - 4 - SIDE - lines
    table = jnp.concatenate(
        [
            jnp.concatenate(
                [zeros(SIDE, 4), w, zeros(SIDE, BANDS), sin_w, zeros(SIDE, BANDS), cos_w], axis=1
            ),
            jnp.concatenate(
                [zeros(lines, 3), u, zeros(lines, 1), sin_u, zeros(lines, BANDS), cos_u, zeros(lines, BANDS)],
                axis=1,
            ),
            zeros(pad, channels),
            jnp.eye(3, channels, dtype=f32),
            jnp.ones((1, channels), f32),
        ],
        axis=0,
    )
    row_sum = u[:, 0] + jnp.sum(sin_u + cos_u, axis=1)
    col_sum = w[:, 0] + jnp.sum(sin_w + cos_w, axis=1)
    row_square = u[:, 0] ** 2 + jnp.sum(sin_u**2 + cos_u**2, axis=1)
    col_square = w[:, 0] ** 2 + jnp.sum(sin_w**2 + cos_w**2, axis=1)
    feature_sum = (row_sum[:, None] + col_sum[None, :]).reshape(1, pixels)
    feature_square = (row_square[:, None] + col_square[None, :]).reshape(1, pixels)
    colours = rgb_pixels.astype(f32)
    average = (jnp.sum(colours, axis=1) + feature_sum) / channels
    spread = (jnp.sum(colours**2, axis=1) + feature_square) / channels - average**2
    scale = lax.rsqrt(spread + eps)
    keep = keep_mask.astype(f32)

    own_values = jnp.concatenate([colours, -average[:, None, :]], axis=1) * scale[:, None, :]
    values = jnp.concatenate(
        [scale[:, None], keep[:, None], jnp.zeros((images, 2, pixels), f32), own_values], axis=1
    )
    table = jnp.pad(table, ((0, 0), (0, side - channels)))
    gained = table * jnp.pad(gain_input, (0, side - channels))[None, :]
    (
        latent_full,
        query_mat,
        key_full,
        whole,
        latent_normed,
        queries,
        score_mat,
        at,
        a_low,
        raw_parts,
        stat_parts,
    ) = forward_pass(
        values,
        table,
        gained,
        gain_latent,
        latent_array,
        w_query,
        key_t,
        shards,
        tall,
        0,
    )
    latent_full = latent_full.reshape(latents, width)
    whole = whole.reshape(-1, width, width)

    latent_out, xs, gs, back_t, row_stats, gain_grads = latent_pass(
        raw_parts,
        stat_parts,
        latent_full,
        cotangent,
        value_out,
        jnp.stack([gain_mlp_one, gain_self, gain_mlp_two]),
        jnp.pad(gain_input, (0, tall - channels))[:, None],
        whole,
        late,
        rows_own,
        4,
    )
    across = -(-channels // 128) * 128
    grad_raw, gain_sums, cross_sum, grad_pixels, summed = backward_pass(
        values,
        table,
        gained,
        at,
        a_low,
        back_t,
        row_stats,
        gain_grads,
        xs,
        gs,
        channels,
        2,
    )

    share = share_rows(channels, count)
    (
        grad_latent_array,
        gain_latent_sum,
        gain_sums,
        grad_w_query,
        grad_w_key,
        grad_w_value,
        grad_w_cross_out,
        g_up_one,
        g_up_two,
        g_down_one,
        g_down_two,
        g_sq,
        g_sk,
        g_sv,
        g_so,
    ) = tail_pass(
        grad_raw.reshape(latents, across),
        gain_sums,
        cross_sum,
        score_mat,
        latent_full,
        lax.dynamic_slice_in_dim(queries, me * depth, depth, 1),
        lax.dynamic_slice_in_dim(latent_normed, me * depth, depth, 1),
        query_mat.reshape(width, width),
        key_full.reshape(width, side),
        jnp.pad(w_value, ((0, share * count - channels), (0, 0))),
        w_cross_out,
        jnp.pad(gain_input, (0, across - channels))[None],
        gain_latent[None],
        summed,
        channels,
    )
    gain_one, gain_attn, gain_two = gain_sums[0], gain_sums[1], gain_sums[2]
    gain_in = gain_sums[3, :channels]
    grad_gain_latent = gain_latent_sum[0]
    return (
        latent_out,
        grad_pixels,
        grad_latent_array,
        gain_in,
        grad_gain_latent,
        grad_w_query,
        grad_w_key,
        grad_w_value,
        grad_w_cross_out,
        gain_one,
        g_up_one,
        g_down_one,
        gain_attn,
        g_sq,
        g_sk,
        g_sv,
        g_so,
        gain_two,
        g_up_two,
        g_down_two,
    )


def solution(mesh):
    rows, columns, copied = P("pix", None), P(None, "pix"), P()
    return jax.shard_map(
        local,
        mesh=mesh,
        in_specs=(
            P("img", None, "pix"),
            P("img", "pix"),
            rows,
            copied,
            copied,
            rows,
            columns,
            columns,
            rows,
            copied,
            columns,
            rows,
            copied,
            rows,
            rows,
            rows,
            rows,
            copied,
            columns,
            rows,
            P("img", "pix", None),
        ),
        out_specs=(
            P("img", "pix", None),
            P("img", None, "pix"),
            rows,
            copied,
            copied,
            rows,
            columns,
            columns,
            rows,
            copied,
            columns,
            rows,
            copied,
            rows,
            rows,
            rows,
            rows,
            copied,
            columns,
            rows,
        ),
        check_vma=False,
    )
```

```python
import functools

import jax
import jax.numpy as jnp
from jax import lax
from jax.experimental import pallas as pl
from jax.experimental.pallas import tpu as pltpu
from jax.sharding import PartitionSpec as P

HEADS = 8
HEAD_DIM = 128
BANDS = 64
SIDE = 224
CHANNELS = 256
LOG2E = 1.4426950408889634

eps = 1e-05
f32 = jnp.float32
bf16 = jnp.bfloat16


def exact(left, right):
    return jnp.dot(left, right, precision=lax.Precision.HIGHEST, preferred_element_type=f32)


def mm(left, right):
    return jnp.dot(left, right, preferred_element_type=f32)


def mm_nt(left, right):
    return lax.dot_general(left, right, (((1,), (1,)), ((), ())), preferred_element_type=f32)


def mm_tn(left, right):
    return lax.dot_general(left, right, (((0,), (0,)), ((), ())), preferred_element_type=f32)


def angles(index):
    place = index.astype(f32) * (2.0 / (SIDE - 1)) - 1.0
    steps = lax.iota(jnp.int32, BANDS).astype(f32)
    frequency = 1.0 + steps * ((SIDE / 2.0 - 1.0) / (BANDS - 1))
    angle = jnp.pi * place[:, None] * frequency[None, :]
    return place[:, None], jnp.sin(angle), jnp.cos(angle)


def pixel_tile(pixels):
    return 896 if pixels % 896 == 0 else pixels


MESH = pl.DeviceIdType.MESH
DMA = pltpu.SemaphoreType.DMA


def ring_place(count):
    me = lax.axis_index("pix")
    return jnp.where(me % 2 == 0, me // 2, count - 1 - me // 2)


def ring_device(place, count):
    place = lax.rem(place + 2 * count, count)
    return jnp.where(place < count // 2, 2 * place, 2 * (count - 1 - place) + 1)


def greet(devices):
    barrier = pltpu.get_barrier_semaphore()
    for device in devices:
        pl.semaphore_signal(barrier, inc=1, device_id=device, device_id_type=MESH)
    pl.semaphore_wait(barrier, len(devices))


def hot_codes(tile):
    pixel = lax.broadcasted_iota(jnp.int32, (CHANNELS, tile), 1)
    channel = lax.broadcasted_iota(jnp.int32, (CHANNELS, tile), 0)
    start = channel - SIDE - pixel // SIDE
    code = jnp.where((start >= 0) & (channel < CHANNELS - 4), start, -2)
    return jnp.where(channel < SIDE, jnp.where(channel == pixel % SIDE, -1, -2), code)


def build_xt(values, base, code_ref):
    code = code_ref[...]
    hot = jnp.where((code == -1) | (code == base), values[0:1, :], 0.0)
    last = hot[CHANNELS - 8 :, :]
    k = lax.broadcasted_iota(jnp.int32, last.shape, 0)
    last = jnp.where(k >= 4, values, last)
    return jnp.concatenate([hot[: CHANNELS - 8, :], last], axis=0)


def build_both(values, base, code_ref):
    keep = values[1:2, :]
    xt = build_xt(values, base, code_ref).astype(bf16)
    k = lax.broadcasted_iota(jnp.int32, (16, values.shape[1]), 0)
    ones = jnp.where(k == 0, keep, 0.0).astype(bf16)
    return xt.T, jnp.concatenate([xt * keep.astype(bf16), ones], axis=0)


def forward_kernel(
    count,
    teams,
    images,
    tile,
    mats,
    v_ref,
    code_ref,
    table_ref,
    gained_ref,
    gain_ref,
    lat_ref,
    wq_ref,
    wk_ref,
    wv_ref,
    wco_ref,
    *refs,
):
    shards = refs[:mats]
    forward_body(
        count,
        teams,
        images,
        tile,
        v_ref,
        code_ref,
        table_ref,
        gained_ref,
        gain_ref,
        lat_ref,
        wq_ref,
        wk_ref,
        wv_ref,
        wco_ref,
        shards,
        *refs[mats:],
    )


def forward_body(
    count,
    teams,
    images,
    tile,
    v_ref,
    code_ref,
    table_ref,
    gained_ref,
    gain_ref,
    lat_ref,
    wq_ref,
    wk_ref,
    wv_ref,
    wco_ref,
    shards,
    lat_full,
    wq_full,
    wk_full,
    w_full,
    normed_ref,
    query_ref,
    a_ref,
    at_ref,
    alow_ref,
    mix_ref,
    part_ref,
    stat_ref,
    mix_raw,
    mix_in,
    acc,
    top,
    u_send,
    s_send,
    own_sem,
    send_sem,
    recv_sem,
    hand_send,
    hand_recv,
    mix_send,
    mix_recv,
    mix_hand,
    x_send,
    x_recv,
    u_own,
    u_out,
    u_in,
):
    pixels = v_ref.shape[2]
    steps = pixels // tile
    lines = tile // SIDE
    owners = Owners(count, images)
    sharers = owners.sharers
    rows = part_ref.shape[2]
    width = wq_ref.shape[1]
    latents = normed_ref.shape[0]
    group, me = lax.axis_index("img"), lax.axis_index("pix")
    core = lax.rem(group, 2)
    place = ring_place(count)
    sides = ((group, ring_device(place + 1, count)), (group, ring_device(place - 1, count)))
    other = (group + 1 - 2 * core, me)
    team = group // 2
    partners = [(lax.rem(team + d, teams) * 2 + core, me) for d in range(1, teams)]
    greet(plane(count) + partners)
    sources = (lat_ref, wq_ref, wk_ref)
    fulls = (lat_full, wq_full, wk_full, w_full)
    mats = len(shards)

    reach = count // 2

    def spot(a, k, stage, way, last, source=False):
        wide = fulls[a].shape[3] // 4
        begin = (core * 2 + way) * wide if last else core * 2 * wide
        columns = pl.ds(pl.multiple_of(begin, 128), wide if last else 2 * wide)
        if source:
            return (sources[a] if a < 3 else shards[k]).at[:, columns]
        origin = ring_device(place - stage if way == 0 else place + stage, count)
        return fulls[a].at[k, origin, :, columns]

    def hop(a, k, stage, way, first=False, last=False):
        return pltpu.make_async_remote_copy(
            spot(a, k, stage, way, last, first),
            spot(a, k, stage, way, last),
            send_sem.at[stage, way, a + k],
            recv_sem.at[stage, way, a + k],
            device_id=sides[way],
            device_id_type=MESH,
        )

    def hand(a, k, stage, way, last=False):
        part = spot(a, k, stage, way, last)
        return pltpu.make_async_remote_copy(
            part,
            part,
            hand_send.at[stage - 1, way, a + k],
            hand_recv.at[stage - 1, way, a + k],
            device_id=other,
            device_id_type=MESH,
        )

    def relay(a, k, stage):
        for way in range(2):
            hop(a, k, stage - 1, way).wait_recv()

            @pl.when(stage == reach - 1)
            def _():
                hop(a, k, stage, way, last=True).start()

            @pl.when(stage != reach - 1)
            def _():
                hop(a, k, stage, way).start()

            hand(a, k, stage, way).start()

    def relay_end(a, k):
        for way in range(2):
            hop(a, k, reach - 1, way, last=True).wait_recv()
            hand(a, k, reach, way, last=True).start()

    def start_ring(a, k):
        for way in range(2):
            hop(a, k, 0, way, True, reach == 1).start()

    alone = 2

    def at_home(k):
        return (k < alone) | (lax.rem(jnp.int32(k), teams) == team)

    def over_x(k, stage, way, d, last=False):
        part = spot(3, k, stage, way, last)
        return pltpu.make_async_remote_copy(
            part,
            part,
            x_send.at[d, stage - 1, way, k],
            x_recv.at[stage - 1, way, k],
            device_id=partners[d],
            device_id_type=MESH,
        )

    def pass_x(k, stage, last=False):
        @pl.when(k >= alone)
        def _():
            for way in range(2):
                for d in range(teams - 1):
                    over_x(k, stage, way, d, last).start()

    def take_x(k, stage, last=False):
        for way in range(2):
            over_x(k, stage, way, 0, last).wait_recv()
            hand(3, k, stage, way, last).start()

    def relay_weight(k, stage):
        home = at_home(k)

        @pl.when(home)
        def _():
            relay(3, k, stage)
            pass_x(k, stage)

        @pl.when(jnp.logical_not(home) & (stage > 1))
        def _():
            take_x(k, stage - 1)

    def relay_weight_end(k):
        home = at_home(k)

        @pl.when(home)
        def _():
            relay_end(3, k)
            pass_x(k, reach, True)

        @pl.when(jnp.logical_not(home))
        def _():
            take_x(k, reach - 1)

    def sent(a, k):
        for way in range(2):
            for stage in range(reach):
                last = stage == reach - 1
                hop(a, k, stage, way, stage == 0, last).wait_send()
                hand(a, k, stage + 1, way, last).wait_send()

    def handed(a, k):
        for way in range(2):
            for stage in range(1, reach + 1):
                hand(a, k, stage, way, stage == reach).wait_recv()

    own = [
        pltpu.make_async_copy(shards[k], fulls[3].at[k, me], own_sem.at[k]) for k in range(mats)
    ]
    for a in range(3):
        start_ring(a, 0)
    others = peers(count)
    used = -(-part_ref.shape[1] // mix_raw.shape[1])

    def mix_copy(source, target, stage, index, device):
        return pltpu.make_async_remote_copy(
            source,
            target,
            mix_send.at[stage, index],
            mix_recv.at[stage, index],
            device_id=device,
            device_id_type=MESH,
        )

    def mix_scatter(d):
        return mix_copy(mix_raw.at[others[d][1]], mix_in.at[d], 0, d, others[d])

    def mix_gather(d):
        return mix_copy(mix_ref.at[core, me], mix_ref.at[core, me], 1, d, others[d])

    def mix_from(d):
        source = lax.rem(me + count - 1 - d, count)
        return source, mix_copy(mix_ref.at[core, source], mix_ref.at[core, source], 1, d, others[d])

    def mix_pass():
        return pltpu.make_async_remote_copy(
            mix_ref.at[core],
            mix_ref.at[core],
            mix_hand.at[0],
            mix_hand.at[1],
            device_id=other,
            device_id_type=MESH,
        )

    half = width // 2
    columns = pl.ds(pl.multiple_of(core * half, 128), half)
    mix_raw[...] = mm(wv_ref[...], wco_ref[:, columns]).astype(bf16).reshape(mix_raw.shape)
    for d in range(count - 1):

        @pl.when(others[d][1] < used)
        def _():
            mix_scatter(d).start()

    for a in range(3):
        fulls[a][0, me] = sources[a][...]
    for copy in own:
        copy.start()
    each = -(-mats // reach)
    for stage in range(1, reach + 1):
        for a in range(3):
            if stage < reach:
                relay(a, 0, jnp.int32(stage))
            else:
                relay_end(a, 0)
        for k in range((stage - 1) * each, min(stage * each, mats)):

            @pl.when(at_home(k))
            def _():
                start_ring(3, k)


    @pl.when(me < used)
    def _():
        total = mix_raw[me].astype(f32)
        for d in range(count - 1):
            mix_scatter(d).wait_recv()
            total = total + mix_in[d].astype(f32)
        mix_ref[core, me] = total.astype(bf16)
        for d in range(count - 1):
            mix_gather(d).start()

    for a in range(3):
        handed(a, 0)

    rows_here = lat_ref.shape[0]
    relays = (reach - 1) * mats
    early = min(relays, width // 256)

    def relay_number(e):
        relay_weight(lax.rem(e, mats), 1 + e // mats)

    @pl.loop(0, count)
    def _(o):
        block = lat_full[0, o].astype(f32)
        average = jnp.mean(block, axis=1, keepdims=True)
        centred = block - average
        spread = jnp.mean(centred * centred, axis=1, keepdims=True)
        normed = (centred * lax.rsqrt(spread + eps) * gain_ref[...]).astype(bf16)
        normed_ref[pl.ds(pl.multiple_of(o * rows_here, rows_here), rows_here), :] = normed

    @pl.loop(0, width // 256)
    def _(j):
        @pl.when(j < early)
        def _():
            relay_number(j)

        columns = pl.ds(pl.multiple_of(j * 256, 256), 256)
        weight = wq_full[0, :, :, columns].reshape(width, 256)
        query_ref[:, columns] = mm(normed_ref[...], weight).astype(bf16)

    a_ref[...] = mm(query_ref[...], wk_full[0].reshape(width, wk_ref.shape[1])) * (width ** (-0.5))

    def exact_nt(left, right):
        return lax.dot_general(
            left,
            right,
            (((1,), (1,)), ((), ())),
            precision=lax.Precision.HIGHEST,
            preferred_element_type=f32,
        )

    at_ref[...] = (exact_nt(gained_ref[...], a_ref[...]) * LOG2E).astype(bf16)
    alow_ref[...] = exact_nt(a_ref[...], gained_ref[...]).astype(bf16)

    table_t = table_ref[...].T[: part_ref.shape[1], :]

    def u_push(i, h):
        to = owners.device(group, i, jnp.int32(h))
        sems = lambda which: dict(
            send_sem=u_out.at[which, i * sharers + h],
            recv_sem=u_in.at[which, me],
            device_id=to,
            device_id_type=MESH,
        )
        return to, (
            pltpu.make_async_remote_copy(u_send.at[i, h], part_ref.at[me], **sems(0)),
            pltpu.make_async_remote_copy(s_send.at[i, h], stat_ref.at[me], **sems(1)),
        )

    def u_keep():
        i, h = owners.image, owners.slot
        return (
            pltpu.make_async_copy(u_send.at[i, h], part_ref.at[me], u_own.at[0]),
            pltpu.make_async_copy(s_send.at[i, h], stat_ref.at[me], u_own.at[1]),
        )

    @pl.loop(0, images * steps)
    def _(t):
        i, step = t // steps, lax.rem(t, steps)

        @pl.when(t + early < relays)
        def _():
            relay_number(t + early)

        @pl.when(step == 0)
        def _():
            acc[...] = jnp.zeros_like(acc)
            top[...] = jnp.full_like(top, -jnp.inf)

        values = v_ref[i, :, pl.ds(pl.multiple_of(step * tile, 128), tile)]
        base = step * lines
        x, xt = build_both(values, base, code_ref)
        first, second = slice(0, tile // 2), slice(tile // 2, tile)
        scores = [mm(x[half], at_ref[...]) for half in (first, second)]
        old, total = top[0:1, :], acc[...]
        for half, score in zip((first, second), scores):
            new = jnp.maximum(old, jnp.max(score, axis=0, keepdims=True))
            weights = jnp.exp2(score - new).astype(bf16)
            total = total * jnp.exp2(old - new) + mm(xt[:, half], weights)
            old = new
        acc[...] = total
        top[...] = jnp.broadcast_to(old, top.shape)

        @pl.when(step == steps - 1)
        def _():
            raw = jnp.dot(
                table_t,
                acc[:CHANNELS, :],
                precision=lax.Precision.HIGHEST,
                preferred_element_type=f32,
            ).astype(bf16)
            stats = jnp.concatenate([top[0:1, :], acc[CHANNELS : CHANNELS + 1, :], top[0:6, :]], axis=0)
            for h in range(sharers):
                u_send[i, h] = raw[:, h * rows : (h + 1) * rows]
                s_send[i, h] = stats[:, h * rows : (h + 1) * rows]
            for h in range(sharers):
                to, copies = u_push(i, h)

                @pl.when(jnp.logical_not(owners.is_me(to)))
                def _():
                    for copy in copies:
                        copy.start()

                @pl.when(owners.is_me(to))
                def _():
                    for copy in u_keep():
                        copy.start()

    if images * steps + early < relays:

        @pl.loop(images * steps + early, relays)
        def _(e):
            relay_number(e)

    for d in range(count - 1):
        source, copy = mix_from(d)

        @pl.when(source < used)
        def _():
            copy.wait_recv()

    for o in range(used, count):
        mix_ref[core, o] = jnp.zeros_like(mix_raw[0])
    mix_pass().start()

    pl.loop(0, mats)(relay_weight_end)

    @pl.loop(alone, mats)
    def _(k):
        @pl.when(jnp.logical_not(at_home(k)))
        def _():
            take_x(k, reach, True)

    for copy in own:
        copy.wait()
    mix_pass().wait()
    for d in range(count - 1):

        @pl.when(others[d][1] < used)
        def _():
            mix_scatter(d).wait_send()

        @pl.when(me < used)
        def _():
            mix_gather(d).wait_send()

    for a in range(3):
        sent(a, 0)

    for k in range(mats):
        home = at_home(k)

        @pl.when(home)
        def _():
            sent(3, k)
            if k >= alone:
                for stage in range(1, reach + 1):
                    for way in range(2):
                        for d in range(teams - 1):
                            over_x(k, stage, way, d, stage == reach).wait_send()

        @pl.when(jnp.logical_not(home))
        def _():
            for way in range(2):
                for stage in range(1, reach + 1):
                    hand(3, k, stage, way, stage == reach).wait_send()

        handed(3, k)

    def u_from(source):
        sems = lambda which: dict(
            send_sem=u_out.at[which, 0],
            recv_sem=u_in.at[which, source],
            device_id=(owners.home, source),
            device_id_type=MESH,
        )
        return (
            pltpu.make_async_remote_copy(u_send.at[0, 0], part_ref.at[source], **sems(0)),
            pltpu.make_async_remote_copy(s_send.at[0, 0], stat_ref.at[source], **sems(1)),
        )

    for i in range(images):
        for h in range(sharers):
            to, copies = u_push(i, h)

            @pl.when(jnp.logical_not(owners.is_me(to)))
            def _():
                for copy in copies:
                    copy.wait_send()

    for source in range(count):
        local = owners.is_me((owners.home, source))

        @pl.when(local)
        def _():
            for copy in u_keep():
                copy.wait()

        @pl.when(jnp.logical_not(local))
        def _():
            for copy in u_from(source):
                copy.wait_recv()


def forward_pass(
    values, table, gained, gain_latent, lat, wq, wk, wv, wco, shards, tall, collective_id
):
    count = lax.axis_size("pix")
    images, _, pixels = values.shape
    tile = pixel_tile(pixels)
    rows_here, width = lat.shape
    latents = rows_here * count
    sharers = count // images
    rows = latents // sharers
    mats = len(shards)
    inside = pl.BlockSpec(memory_space=pltpu.VMEM)
    anywhere = pl.BlockSpec(memory_space=pl.ANY)
    shape = jax.ShapeDtypeStruct

    def full(array, number=1):
        return shape((number, count) + array.shape, array.dtype)

    ring = DMA((count // 2, 2, 3 + mats))
    return pl.pallas_call(
        functools.partial(forward_kernel, count, lax.axis_size("img") // 2, images, tile, mats),
        out_shape=[full(lat), full(wq), full(wk), full(shards[0], mats)]
        + [
            shape((latents, width), bf16),
            shape((latents, width), bf16),
            shape((latents, wk.shape[1]), f32),
            shape((CHANNELS, latents), bf16),
            shape((latents, CHANNELS), bf16),
            shape((2, count, wv.shape[0] // count, width // 2), bf16),
            shape((count, tall, rows), bf16),
            shape((count, 8, rows), f32),
        ],
        in_specs=[inside] * (10 + mats),
        out_specs=[inside] * 3 + [anywhere] + [inside] * 6 + [anywhere] * 2,
        scratch_shapes=[
            pltpu.VMEM((count, wv.shape[0] // count, width // 2), bf16),
            pltpu.VMEM((count - 1, wv.shape[0] // count, width // 2), bf16),
            pltpu.VMEM((CHANNELS + 16, latents), f32),
            pltpu.VMEM((8, latents), f32),
            pltpu.VMEM((images, sharers, tall, rows), bf16),
            pltpu.VMEM((images, sharers, 8, rows), f32),
            DMA((mats,)),
            ring,
            ring,
            ring,
            ring,
            DMA((2, count - 1)),
            DMA((2, count - 1)),
            DMA((2,)),
            DMA((max(lax.axis_size("img") // 2 - 1, 1), count // 2, 2, mats)),
            DMA((count // 2, 2, mats)),
            DMA((2,)),
            DMA((2, count)),
            DMA((2, count)),
        ],
        compiler_params=pltpu.CompilerParams(
            collective_id=collective_id, has_side_effects=True, vmem_limit_bytes=48 * 2**20
        ),
    )(values, hot_codes(tile), table, gained, gain_latent[None], lat, wq, wk, wv, wco, *shards)


def backward_kernel(
    count,
    teams,
    images,
    tile,
    channels,
    v_ref,
    code_ref,
    table_ref,
    gained_ref,
    at_ref,
    a_ref,
    back_ref,
    row_ref,
    gain_ref,
    xs_ref,
    gs_ref,
    t_out,
    g_out,
    z_out,
    pixel_ref,
    out_ref,
    t_raw,
    t_in,
    t_img,
    g_raw,
    g_in,
    g_img,
    z_own,
    t_acc,
    bt,
    b_low,
    stat,
    back_all,
    row_all,
    xv,
    gv,
    terms,
    held,
    across,
    done,
    load_sem,
    pair_send,
    pair_recv,
    send_sem,
    recv_sem,
    cross_send,
    cross_recv,
    out_sem,
    hand_send,
    hand_recv,
    back_send,
    back_recv,
    pass_send,
    sum_send,
    sum_recv,
    img_send,
    img_recv,
    last_send,
    last_recv,
    z_send,
    z_recv,
    z_hand_send,
    z_hand_recv,
):
    number, rows, width = gs_ref.shape
    kinds = xs_ref.shape[0]
    owners = Owners(count, images)
    sharers = owners.sharers
    steps = v_ref.shape[2] // tile
    lines = tile // SIDE
    depth = xs_ref.shape[1] // count
    half, wide = width // 2, width // 4
    group, me = lax.axis_index("img"), lax.axis_index("pix")
    core, team = lax.rem(group, 2), group // 2
    place = ring_place(count)
    sides = ((group, ring_device(place + 1, count)), (group, ring_device(place - 1, count)))
    other = (group + 1 - 2 * core, me)
    partners = [(lax.rem(team + d, teams) * 2 + core, me) for d in range(1, teams)]
    crowd = 2 * teams
    others = peers(count)
    same_place = [(lax.rem(group + d, crowd), me) for d in range(1, crowd)]
    far = [
        (lax.rem(team + d, teams) * 2 + c, me) for d in range(1, teams) for c in range(2)
    ]
    greet(plane(count) + far)

    def send(source, target, sems, index, device):
        return pltpu.make_async_remote_copy(
            source,
            target,
            sems[0].at[index],
            sems[1].at[index],
            device_id=device,
            device_id_type=MESH,
        )

    def scatter(d):
        to, sems = others[d][1], (sum_send, sum_recv)
        return (
            send(t_raw.at[to], t_in.at[d], sems, (0, d), others[d]),
            send(g_raw.at[to], g_in.at[d], sems, (1, d), others[d]),
        )

    def over(d):
        sems = (img_send, img_recv)
        return (
            send(t_img.at[group], t_img.at[group], sems, (0, d), same_place[d]),
            send(g_img.at[group], g_img.at[group], sems, (1, d), same_place[d]),
        )

    def gather(d):
        sems = (last_send, last_recv)
        return (
            send(t_out.at[me], t_out.at[me], sems, (0, d), others[d]),
            send(g_out.at[me], g_out.at[me], sems, (1, d), others[d]),
        )

    def z_push(d):
        return send(z_own, z_out.at[core, me], (z_send, z_recv), d, others[d])

    def z_hand():
        return pltpu.make_async_remote_copy(
            z_out.at[core],
            z_out.at[core],
            z_hand_send,
            z_hand_recv,
            device_id=other,
            device_id_type=MESH,
        )

    for o in range(count):
        g_raw[o] = gain_ref[:, o * depth : (o + 1) * depth]

    own_index = owners.image * sharers + owners.slot

    def back_push(d):
        to = (owners.home, lax.rem(me + 2 * d, count))
        sems = lambda which: dict(
            send_sem=back_send.at[which, d],
            recv_sem=back_recv.at[which, own_index],
            device_id=to,
            device_id_type=MESH,
        )
        return to, (
            pltpu.make_async_remote_copy(back_ref, back_all.at[own_index], **sems(0)),
            pltpu.make_async_remote_copy(row_ref, row_all.at[own_index], **sems(1)),
        )

    def back_from(source):
        sems = lambda which: dict(
            send_sem=back_send.at[which, 0],
            recv_sem=back_recv.at[which, source],
            device_id=(group, me),
            device_id_type=MESH,
        )
        return (
            pltpu.make_async_remote_copy(back_ref, back_all.at[source], **sems(0)),
            pltpu.make_async_remote_copy(row_ref, row_all.at[source], **sems(1)),
        )

    def back_hand(block):
        to = (group, me + 1 - 2 * lax.rem(me, 2))
        sems = lambda which: dict(
            send_sem=pass_send.at[which, block],
            recv_sem=back_recv.at[which, block],
            device_id=to,
            device_id_type=MESH,
        )
        return (
            pltpu.make_async_remote_copy(back_all.at[block], back_all.at[block], **sems(0)),
            pltpu.make_async_remote_copy(row_all.at[block], row_all.at[block], **sems(1)),
        )

    def back_owner(image, slot):
        sender = owners.device(group, image, slot)
        return sender, lax.rem(sender[1], 2) == lax.rem(me, 2)

    for d in range(count // 2):
        to, copies = back_push(d)

        @pl.when(jnp.logical_not(owners.is_me(to)))
        def _():
            for copy in copies:
                copy.start()

        @pl.when(owners.is_me(to))
        def _():
            back_all[own_index] = back_ref[...]
            row_all[own_index] = row_ref[...]

    def load_x(j):
        return pltpu.make_async_copy(xs_ref.at[j], xv.at[j, core], load_sem.at[0, j])

    def load_g(k):
        part = gs_ref.at[k, :, pl.ds(pl.multiple_of(core * half, 128), half)]
        return pltpu.make_async_copy(part, gv.at[k, core], load_sem.at[1, k])

    def pair_x(j):
        return pltpu.make_async_remote_copy(
            xs_ref.at[j],
            xv.at[j, core],
            pair_send.at[0, j],
            pair_recv.at[0, j],
            device_id=other,
            device_id_type=MESH,
        )

    def pair_g(k):
        part = gs_ref.at[k, :, pl.ds(pl.multiple_of((1 - core) * half, 128), half)]
        return pltpu.make_async_remote_copy(
            part,
            gv.at[k, core],
            pair_send.at[1, k],
            pair_recv.at[1, k],
            device_id=other,
            device_id_type=MESH,
        )

    order = [number - 1] + list(range(number - 1))
    for k in order:
        j = max(k - (number - kinds), 0)
        if k == 0 or k > number - kinds:
            load_x(j).start()
            pair_x(j).start()
        load_g(k).start()
        pair_g(k).start()

    def turn(k):
        return lax.rem(k + number - 1, number)

    reach = count // 2

    def owner_at(stage, way):
        ahead = reach - stage
        return ring_device(place + ahead if way == 0 else place - ahead, count)

    def rows_of(owner):
        return pl.ds(pl.multiple_of(owner * depth, depth), depth)

    def quarter(q):
        return slice(q * wide, (q + 1) * wide)

    def hop(k, stage, way, start=False):
        if start:
            source = terms.at[k, rows_of(owner_at(0, way)), quarter(way)]
            target = held.at[k, way, 0, :, quarter(way)]
        else:
            source = held.at[k, way, stage - 1]
            target = held.at[k, way, stage]
        return pltpu.make_async_remote_copy(
            source,
            target,
            send_sem.at[stage, way, k],
            recv_sem.at[stage, way, k],
            device_id=sides[way],
            device_id_type=MESH,
        )

    def cross(k, d):
        return pltpu.make_async_remote_copy(
            across.at[team, k],
            across.at[team, k],
            cross_send.at[d, k],
            cross_recv.at[d, k],
            device_id=partners[d],
            device_id_type=MESH,
        )

    @pl.loop(0, number)
    def _(k):
        k = turn(k)
        j = jnp.maximum(k - (number - kinds), 0)

        @pl.when((k == 0) | (k > number - kinds))
        def _():
            load_x(j).wait()
            pair_x(j).wait_recv()

        load_g(k).wait()
        pair_g(k).wait_recv()
        for r in range(0, width, 256):
            piece = slice(r, r + 256)
            terms[k, piece, :] = (
                mm(xv[j, 0, piece, :], gv[k, 0]) + mm(xv[j, 1, piece, :], gv[k, 1])
            ).astype(bf16)
        for way in range(2):
            hop(k, 0, way, True).start()

    for block in range(count):
        sender, direct = back_owner(block // sharers, jnp.int32(block % sharers))

        @pl.when(direct)
        def _():
            @pl.when(jnp.logical_not(owners.is_me(sender)))
            def _():
                for copy in back_from(block):
                    copy.wait_recv()

            for copy in back_hand(block):
                copy.start()

    def relay(k, stage):
        for way in range(2):
            here = rows_of(owner_at(stage, way))

            @pl.when(stage == 1)
            def _():
                hop(k, 0, way, True).wait_recv()
                both = terms[k, here, quarter(way)].astype(f32)
                both = both + held[k, way, 0, :, quarter(way)].astype(f32)
                held[k, way, 0, :, quarter(way)] = both.astype(bf16)
                held[k, way, 0, :, quarter(1 - way)] = terms[k, here, quarter(1 - way)]

            @pl.when(stage > 1)
            def _():
                hop(k, stage - 1, way).wait_recv()
                both = terms[k, here, :].astype(f32) + held[k, way, stage - 1].astype(f32)
                held[k, way, stage - 1] = both.astype(bf16)

            hop(k, stage, way).start()

    def finish(k):
        columns = pl.ds(pl.multiple_of(core * half, 128), half)
        return pltpu.make_async_copy(done.at[k], out_ref.at[k, :, columns], out_sem.at[k])

    def hand(k):
        columns = pl.ds(pl.multiple_of(core * half, 128), half)
        return pltpu.make_async_remote_copy(
            done.at[k],
            out_ref.at[k, :, columns],
            hand_send.at[k],
            hand_recv.at[k],
            device_id=other,
            device_id_type=MESH,
        )

    def settle(k):
        for way in range(2):
            hop(k, reach - 1, way, reach == 1).wait_recv()
        total = terms[k, rows_of(me), :].astype(f32)
        for way in range(2):
            total = total + held[k, way, reach - 1].astype(f32)
        across[team, k] = total.astype(bf16)
        for d in range(teams - 1):
            cross(k, d).start()

    span_k = 3 if number % 3 == 0 else number
    groups = number // span_k
    events = reach * number

    def complete(k):
        for d in range(teams - 1):
            cross(k, d).wait_recv()
        total = across[0, k].astype(f32)
        for t in range(1, teams):
            total = total + across[t, k].astype(f32)
        done[k] = total
        finish(k).start()
        hand(k).start()

        @pl.when(k == number - 1)
        def _():
            rows_here = t_raw.shape[1]
            mine = done[number - 1, rows_here : rows_here + z_own.shape[0], :].astype(bf16)
            z_own[...] = mine
            z_out[core, me] = mine
            for d in range(count - 1):
                z_push(d).start()

    def event(e):
        block, k = e // span_k, lax.rem(e, span_k)
        block = jnp.where(block == 0, 0, block + 1)
        g, slot = block // reach, lax.rem(block, reach)
        settles = (slot == 1) | (g == groups)

        @pl.when(settles)
        def _():
            settle(turn((g - 1) * span_k + k))

            @pl.when(g > 1)
            def _():
                complete(turn((g - 2) * span_k + k))

        @pl.when(jnp.logical_not(settles))
        def _():
            relay(turn(g * span_k + k), jnp.maximum(slot, 1))

    tiles = images * steps
    paced = tiles * 5 // 8
    middle = (paced + events) // 2
    t_acc[...] = jnp.zeros_like(t_acc)

    @pl.loop(0, tiles)
    def _(t):
        image = lax.rem(t // steps + owners.image, images)
        step = lax.rem(t, steps)
        e = t * 5 // 8

        @pl.when((t + 1) * 5 // 8 > e)
        def _():
            event(e)

        @pl.when(step == 0)
        def _():
            for h in range(sharers):
                source = image * sharers + h

                _, direct = back_owner(image, jnp.int32(h))

                @pl.when(jnp.logical_not(direct))
                def _():
                    for copy in back_from(source):
                        copy.wait_recv()

                here = slice(h * rows, (h + 1) * rows)
                wide = jnp.dot(
                    gained_ref[:, : back_ref.shape[0]],
                    back_all[source].astype(f32),
                    precision=lax.Precision.HIGHEST,
                    preferred_element_type=f32,
                )
                bt[:, here] = wide.astype(bf16)
                b_low[here, :] = wide.T.astype(bf16)
                stat[:, here] = row_all[source]

        span = pl.ds(pl.multiple_of(step * tile, 128), tile)
        values = v_ref[image, :, span]
        x, xt = build_both(values, step * lines, code_ref)
        halves = (slice(0, tile // 2), slice(tile // 2, tile))
        products = [(mm(x[half], at_ref[...]), mm(x[half], bt[...])) for half in halves]
        kept, ends = [], []
        for half, (scores, grad_p) in zip(halves, products):
            probs = jnp.exp2(scores - stat[0:1, :])
            grad_s = (probs * (grad_p - stat[1:2, :])).astype(bf16)
            kept.append(grad_s)
            back = mm(grad_s, a_ref[...]) + mm(probs.astype(bf16), b_low[...])
            along = jnp.sum(back * x[half].astype(f32), axis=1, keepdims=True)
            end = back[:, CHANNELS - 128 :]
            lane = lax.broadcasted_iota(jnp.int32, end.shape, 1)
            ends.append(jnp.where(lane == 120, along, end))
        t_acc[...] += mm(xt, jnp.concatenate(kept, axis=0))
        ends = jnp.concatenate(ends, axis=0).T[120:128, :] * (values[0:1, :] * values[1:2, :])
        hat = values[4:7, :] + values[7:8, :]
        mean_part = ends[7:8, :] + hat * ends[0:1, :]
        pixel_ref[image, :, span] = ends[4:7, :] - mean_part * (1.0 / channels)

    t_sum = lax.dot_general(
        t_acc[:CHANNELS, :],
        table_ref[:, : t_raw.shape[2]],
        (((0,), (0,)), ((), ())),
        precision=lax.Precision.HIGHEST,
        preferred_element_type=f32,
    )
    t_raw[...] = t_sum.astype(bf16).reshape(t_raw.shape)
    for d in range(count - 1):
        for copy in scatter(d):
            copy.start()

    pl.loop(paced, middle)(event)
    t_sum, g_sum = t_raw[me].astype(f32), g_raw[me]
    for d in range(count - 1):
        for copy in scatter(d):
            copy.wait_recv()
        t_sum = t_sum + t_in[d].astype(f32)
        g_sum = g_sum + g_in[d]
    t_img[group] = t_sum.astype(bf16)
    g_img[group] = g_sum
    for d in range(crowd - 1):
        for copy in over(d):
            copy.start()

    pl.loop(middle, events)(event)

    @pl.loop((groups - 1) * span_k, number)
    def _(k):
        complete(turn(k))

    for d in range(crowd - 1):
        for copy in over(d):
            copy.wait_recv()
    t_sum, g_sum = t_img[0].astype(f32), g_img[0]
    for i in range(1, crowd):
        t_sum = t_sum + t_img[i].astype(f32)
        g_sum = g_sum + g_img[i]
    t_out[me] = t_sum.astype(bf16)
    g_out[me] = g_sum
    for d in range(count - 1):
        for copy in gather(d):
            copy.start()
    for d in range(count - 1):
        z_push(d).wait()
    z_hand().start()
    for d in range(count - 1):
        for copy in gather(d):
            copy.wait()
        for copy in scatter(d):
            copy.wait_send()
    for d in range(crowd - 1):
        for copy in over(d):
            copy.wait_send()
    z_hand().wait()

    @pl.loop(0, number)
    def _(k):
        finish(k).wait()
        hand(k).wait()
        pair_g(k).wait_send()
        for way in range(2):
            for stage in range(reach):
                hop(k, stage, way, stage == 0).wait_send()
        for d in range(teams - 1):
            cross(k, d).wait_send()

    @pl.loop(0, kinds)
    def _(j):
        pair_x(j).wait_send()

    for d in range(count // 2):
        to, copies = back_push(d)

        @pl.when(jnp.logical_not(owners.is_me(to)))
        def _():
            for copy in copies:
                copy.wait_send()

    for block in range(count):
        _, direct = back_owner(block // sharers, jnp.int32(block % sharers))

        @pl.when(direct)
        def _():
            for copy in back_hand(block):
                copy.wait_send()


def backward_pass(
    values, table, gained, at, a, back, rows_in, gains, xs, gs, channels, collective_id
):
    count = lax.axis_size("pix")
    teams = lax.axis_size("img") // 2
    kinds, _, rows = xs.shape
    number, _, width = gs.shape
    depth = xs.shape[1] // count
    anywhere = pl.BlockSpec(memory_space=pl.ANY)
    inside = pl.BlockSpec(memory_space=pltpu.VMEM)
    chunk = (depth, width // 2)
    images, _, pixels = values.shape
    tile = pixel_tile(pixels)
    latents = at.shape[1]
    tall = back.shape[0]
    shape = jax.ShapeDtypeStruct
    rows_here = latents // count
    t_shape = shape((count, rows_here, -(-channels // 128) * 128), bf16)
    g_shape = shape((count, 8, depth), f32)
    spare = min(-(-share_rows(channels, count) // 16) * 16, depth - rows_here)
    return pl.pallas_call(
        functools.partial(backward_kernel, count, teams, images, tile, channels),
        out_shape=[
            t_shape,
            g_shape,
            shape((2, count, spare, width // 2), bf16),
            shape((images, 3, pixels), f32),
            shape((number, depth, width), f32),
        ],
        in_specs=[inside] * 9 + [anywhere] * 2,
        out_specs=[inside] * 4 + [anywhere],
        scratch_shapes=[
            pltpu.VMEM(t_shape.shape, bf16),
            pltpu.VMEM((count - 1,) + t_shape.shape[1:], bf16),
            pltpu.VMEM((2 * teams,) + t_shape.shape[1:], bf16),
            pltpu.VMEM(g_shape.shape, f32),
            pltpu.VMEM((count - 1,) + g_shape.shape[1:], f32),
            pltpu.VMEM((2 * teams,) + g_shape.shape[1:], f32),
            pltpu.VMEM((spare, width // 2), bf16),
            pltpu.VMEM((CHANNELS + 16, latents), f32),
            pltpu.VMEM((CHANNELS, latents), bf16),
            pltpu.VMEM((latents, CHANNELS), bf16),
            pltpu.VMEM((8, latents), f32),
            pltpu.VMEM((count, tall, rows), bf16),
            pltpu.VMEM((count, 8, rows), f32),
            pltpu.VMEM((kinds, 2, xs.shape[1], rows), bf16),
            pltpu.VMEM((number, 2, rows, width // 2), bf16),
            pltpu.VMEM((number, xs.shape[1], width // 2), bf16),
            pltpu.VMEM((number, 2, count // 2) + chunk, bf16),
            pltpu.VMEM((teams, number) + chunk, bf16),
            pltpu.VMEM((number, depth, width // 2), f32),
            DMA((2, number)),
            DMA((2, number)),
            DMA((2, number)),
            DMA((count // 2, 2, number)),
            DMA((count // 2, 2, number)),
            DMA((teams - 1, number)),
            DMA((teams - 1, number)),
            DMA((number,)),
            DMA((number,)),
            DMA((number,)),
            DMA((2, count)),
            DMA((2, count)),
            DMA((2, count)),
            DMA((2, count - 1)),
            DMA((2, count - 1)),
            DMA((2, 2 * teams - 1)),
            DMA((2, 2 * teams - 1)),
            DMA((2, count - 1)),
            DMA((2, count - 1)),
            DMA((count - 1,)),
            DMA((count - 1,)),
            DMA,
            DMA,
        ],
        compiler_params=pltpu.CompilerParams(
            collective_id=collective_id, has_side_effects=True, vmem_limit_bytes=60 * 2**20
        ),
    )(values, hot_codes(tile), table, gained, at, a, back, rows_in, gains, xs, gs)


def peers(count):
    group, me = lax.axis_index("img"), lax.axis_index("pix")
    return [(group, lax.rem(me + d, count)) for d in range(1, count)]


def plane(count):
    group, me = lax.axis_index("img"), lax.axis_index("pix")
    other = group + 1 - 2 * lax.rem(group, 2)
    return peers(count) + [(other, lax.rem(me + d, count)) for d in range(count)]


class Owners:
    def __init__(self, count, images):
        self.group, self.me = lax.axis_index("img"), lax.axis_index("pix")
        self.core = lax.rem(self.group, 2)
        self.base = self.group - self.core
        self.images = images
        self.chips = count // (2 * images)
        self.sharers = 2 * self.chips
        self.slot = lax.rem(self.me, self.chips) * 2 + self.core
        image = self.me // self.chips
        self.image = lax.rem(image, images)
        self.home = self.base + image // images

    def device(self, group, image, slot):
        core = lax.rem(group, 2)
        chip = (core * self.images + image) * self.chips + slot // 2
        return self.base + lax.rem(slot, 2), chip

    def is_me(self, device):
        return (device[0] == self.group) & (device[1] == self.me)


def share_rows(channels, count):
    channels = -(-channels // 16) * 16
    return -(-(-(-channels // count)) // 8) * 8


def gelu_parts(z):
    slope = (2.0 / jnp.pi) ** 0.5
    square = z * z
    bend = jnp.tanh(slope * z * (1.0 + 0.044715 * square))
    half = 0.5 * (1.0 + bend)
    return z * half, half + 0.5 * z * (1.0 - bend * bend) * slope * (1.0 + 0.134145 * square)


def latent_kernel(
    count,
    images,
    part_ref,
    stat_ref,
    own_ref,
    cot_ref,
    mix_ref,
    gain_ref,
    in_gain_ref,
    w_ref,
    late_up,
    late_down,
    out_ref,
    xs_ref,
    gs_ref,
    back_ref,
    row_ref,
    gain_out,
    wv,
    one,
    two,
    three,
    pre,
    grad,
    flow,
    low,
    heads_q,
    kv,
    probs,
    kv_out,
    kv_in,
    cot,
    final,
    mean,
    own_v,
    own_sem,
    w_sem,
    ring_own,
    ring_send,
    ring_recv,
    hand_send,
    hand_recv,
    kv_send,
    kv_recv,
    gkv_send,
    gkv_recv,
    cot_own,
    cot_send,
    cot_recv,
    out_own,
    out_send,
    out_recv,
):
    rows, width = one.shape
    depth = width // count
    owners = Owners(count, images)
    sharers = owners.sharers
    latents = rows * sharers
    per = count // sharers
    rows_here = latents // count
    spare = depth - rows_here
    group, me = lax.axis_index("img"), lax.axis_index("pix")
    slot, image, home = owners.slot, owners.image, owners.home
    block = 256
    blocks = width // block
    row_block = min(rows, 64)
    up_one, down_one, m_query, m_key, m_value, m_out, up_two, down_two = range(8)
    scale = HEAD_DIM ** (-0.5)

    def load(k):
        return pltpu.make_async_copy(w_ref.at[k], wv.at[k], w_sem.at[k])

    early, late_refs = w_ref.shape[0], (late_up, late_down)
    late = len(late_refs)
    own_copy = pltpu.make_async_copy(
        own_ref.at[pl.ds(pl.multiple_of(slot * rows, 16), rows)], own_v, own_sem
    )
    own_copy.start()
    for k in range(early):
        load(k).start()
    greet(plane(count))

    core = lax.rem(group, 2)
    ring = ring_place(count)
    sides = ((group, ring_device(ring + 1, count)), (group, ring_device(ring - 1, count)))
    other = (group + 1 - 2 * core, me)

    reach = count // 2

    def spot(k, stage, way, last, source=False):
        begin = (core * 2 + way) * (width // 4) if last else core * (width // 2)
        some = pl.ds(pl.multiple_of(begin, 128), width // 4 if last else width // 2)
        if source:
            return late_refs[k].at[:, some]
        origin = ring_device(ring - stage if way == 0 else ring + stage, count)
        here = pl.ds(pl.multiple_of(origin * depth, depth), depth)
        return wv.at[early + k, here, some]

    def hop(k, stage, way, start=False, last=False):
        return pltpu.make_async_remote_copy(
            spot(k, stage, way, last, start),
            spot(k, stage, way, last),
            ring_send.at[stage, way, k],
            ring_recv.at[stage, way, k],
            device_id=sides[way],
            device_id_type=MESH,
        )

    def hand(k, stage, way, last=False):
        return pltpu.make_async_remote_copy(
            spot(k, stage, way, last),
            spot(k, stage, way, last),
            hand_send.at[stage - 1, way, k],
            hand_recv.at[stage - 1, way, k],
            device_id=other,
            device_id_type=MESH,
        )

    def ring_keep(k):
        here = pl.ds(pl.multiple_of(me * depth, depth), depth)
        return pltpu.make_async_copy(late_refs[k], wv.at[early + k, here], ring_own.at[k])

    for k in range(late):
        for way in range(2):
            hop(k, 0, way, True, reach == 1).start()
        ring_keep(k).start()

    def relays(first, end):
        for stage in range(first, min(end, reach + 1)):
            for k in range(late):
                for way in range(2):
                    last = stage == reach
                    hop(k, stage - 1, way, last=last).wait_recv()
                    if stage < reach:
                        hop(k, stage, way, last=stage == reach - 1).start()
                    hand(k, stage, way, last).start()

    def arrived(k):
        ring_keep(k).wait()
        for stage in range(1, reach + 1):
            for way in range(2):
                hand(k, stage, way, stage == reach).wait_recv()

    def cot_push(i):
        to = owners.device(group, i, me // per)
        return to, pltpu.make_async_remote_copy(
            cot_ref.at[i],
            cot.at[lax.rem(me, per)],
            cot_send.at[i],
            cot_recv.at[lax.rem(me, per)],
            device_id=to,
            device_id_type=MESH,
        )

    def cot_keep():
        return pltpu.make_async_copy(cot_ref.at[image], cot.at[lax.rem(me, per)], cot_own)

    for i in range(images):
        to, copy = cot_push(i)

        @pl.when(jnp.logical_not(owners.is_me(to)))
        def _():
            copy.start()

        @pl.when(owners.is_me(to))
        def _():
            cot_keep().start()

    def columns(j, wide=block):
        return pl.ds(pl.multiple_of(j * wide, wide), wide)

    def over_columns(body, times=blocks):
        pl.loop(0, times)(body)

    def over_rows(body):
        @pl.loop(0, rows // row_block)
        def _(r):
            body(pl.ds(pl.multiple_of(r * row_block, 16), row_block))

    def put_x(j, c, value):
        xs_ref[j, columns(c), :] = value.T

    def centre(rows_f32):
        average = jnp.mean(rows_f32, axis=1, keepdims=True)
        centred = rows_f32 - average
        spread = jnp.mean(centred * centred, axis=1, keepdims=True)
        scale_rows = lax.rsqrt(spread + eps)
        return centred * scale_rows, scale_rows

    def norm(source, k, target):
        def body(r):
            target[r] = (centre(source[r])[0] * gain_ref[k : k + 1, :]).astype(bf16)

        over_rows(body)

    def norm_grad(source, k):
        def body(r):
            hat, scale_rows = centre(source[r])
            given = flow[r]
            gain_out[k : k + 1, :] += jnp.sum(given * hat, axis=0, keepdims=True)
            given = given * gain_ref[k : k + 1, :]
            along = jnp.mean(given * hat, axis=1, keepdims=True)
            grad[r] += scale_rows * (given - jnp.mean(given, axis=1, keepdims=True) - hat * along)

        over_rows(body)

    gain_out[...] = jnp.zeros_like(gain_out)

    top = jnp.max(stat_ref[:, 0:1, :], axis=0)
    total = jnp.zeros_like(top)
    for d in range(count):
        total = total + jnp.exp2(stat_ref[d, 0:1, :] - top) * stat_ref[d, 1:2, :]
    raw = jnp.zeros(part_ref.shape[1:], f32)
    for d in range(count):
        raw = raw + part_ref[d].astype(f32) * (jnp.exp2(stat_ref[d, 0:1, :] - top) / total)
    mean[0] = raw
    mean[1] = raw * in_gain_ref[...]
    row_ref[...] = jnp.zeros_like(row_ref)
    row_ref[0:1, :] = top + jnp.log(total) * LOG2E

    tall = count * spare
    mean_tall = mean[1]
    if tall > mean_tall.shape[0]:
        mean_tall = jnp.concatenate(
            [mean_tall, jnp.zeros((tall - mean_tall.shape[0], rows), f32)], axis=0
        )
    share = share_rows(mean.shape[1], count)
    place = lax.broadcasted_iota(jnp.int32, (rows_here, rows), 0)
    source_row = lax.broadcasted_iota(jnp.int32, (rows_here, rows), 1) + slot * rows
    for o in range(count):
        picks = jnp.where(place + o * rows_here == source_row, 1.0, 0.0)
        piece = [picks, mean_tall[o * share : (o + 1) * share]]
        if spare > share:
            piece.append(jnp.zeros((spare - share, rows), f32))
        xs_ref[6, o * depth : (o + 1) * depth, :] = jnp.concatenate(piece, axis=0).astype(bf16)

    mean_low = mean[1].astype(bf16)

    def make_one(j):
        one[:, columns(j)] = own_v[:, columns(j)].astype(f32) + mm_tn(
            mean_low,
            mix_ref[j // (blocks // 2), : mean.shape[1], columns(lax.rem(j, blocks // 2))],
        )

    own_copy.wait()
    over_columns(make_one)

    def ready(k):
        if k < early:
            load(k).wait()
        else:
            arrived(k - early)

    def feed(source, target, k, up, down, normed, x_hidden, keep):
        norm(source, k, normed)
        ready(up)

        def make_hidden(j):
            value = mm_nt(normed[...], wv[up, columns(j), :])
            pre[keep, :, columns(j)] = value
            hidden = gelu_parts(value)[0].astype(bf16)
            low[:, columns(j)] = hidden
            put_x(x_hidden, j, hidden)

        over_columns(make_hidden)
        ready(down)

        def make_branch(j):
            value = source[:, columns(j)] + mm(low[...], wv[down, :, columns(j)])
            target[:, columns(j)] = value.astype(target.dtype)

        over_columns(make_branch)

    def feed_back(source, k, up, down, branch, x_pre, keep):
        @over_columns
        def _(j):
            value = mm_nt(branch[...], wv[down, columns(j), :])
            value = (value * gelu_parts(pre[keep, :, columns(j)])[1]).astype(bf16)
            low[:, columns(j)] = value
            put_x(x_pre, j, value)

        @over_columns
        def _(j):
            flow[:, columns(j)] = mm(low[...], wv[up, :, columns(j)])

        norm_grad(source, k)

    feed(one, two, 0, up_one, down_one, gs_ref.at[4], 3, 0)
    relays(1, 2)

    norm(two, 1, low)

    load(m_key).wait()
    load(m_value).wait()

    def make_kv(j):
        put_x(0, j, low[:, columns(j)])
        kv[0, slot, :, columns(j)] = mm(low[...], wv[m_key, :, columns(j)]).astype(bf16)
        kv[1, slot, :, columns(j)] = mm(low[...], wv[m_value, :, columns(j)]).astype(bf16)

    over_columns(make_kv)

    def sharer(d):
        return owners.device(home, image, lax.rem(slot + d, sharers))

    def kv_push(d):
        return pltpu.make_async_remote_copy(
            kv.at[:, slot],
            kv.at[:, slot],
            kv_send.at[d - 1],
            kv_recv.at[d - 1],
            device_id=sharer(d),
            device_id_type=MESH,
        )

    for d in range(1, sharers):
        kv_push(d).start()
    load(m_query).wait()

    @over_columns
    def _(j):
        heads_q[:, columns(j)] = mm(low[...], wv[m_query, :, columns(j)]).astype(bf16)

    for d in range(1, sharers):
        kv_push(d).wait_recv()

    def attend(h):
        c = columns(h, HEAD_DIM)
        k_all = kv[0, :, :, c].reshape(latents, HEAD_DIM)
        v_all = kv[1, :, :, c].reshape(latents, HEAD_DIM)
        scores = mm_nt(heads_q[:, c], k_all) * scale
        shifted = jnp.exp(scores - jnp.max(scores, axis=1, keepdims=True))
        p = shifted / jnp.sum(shifted, axis=1, keepdims=True)
        probs[h] = p
        low[:, c] = mm(p.astype(bf16), v_all).astype(bf16)

    pl.loop(0, HEADS // 2)(attend)
    relays(2, 3)
    pl.loop(HEADS // 2, HEADS)(attend)
    relays(3, 4)

    @over_columns
    def _(j):
        put_x(1, j, low[:, columns(j)])

    ready(m_out)

    @over_columns
    def _(j):
        three[:, columns(j)] = two[:, columns(j)] + mm(low[...], wv[m_out, :, columns(j)])

    relays(4, reach + 1)
    feed(three, final, 2, up_two, down_two, gs_ref.at[6], 5, 1)

    def out_push(b):
        to = (home, slot * per + b)
        return to, pltpu.make_async_remote_copy(
            final.at[pl.ds(b * rows_here, rows_here)],
            out_ref.at[image],
            out_send.at[b],
            out_recv.at[image],
            device_id=to,
            device_id_type=MESH,
        )

    def out_keep():
        mine = pl.ds(pl.multiple_of(lax.rem(me, per) * rows_here, 16), rows_here)
        return pltpu.make_async_copy(final.at[mine], out_ref.at[image], out_own)

    for b in range(per):
        to, copy = out_push(b)

        @pl.when(jnp.logical_not(owners.is_me(to)))
        def _():
            copy.start()

        @pl.when(owners.is_me(to))
        def _():
            out_keep().start()

    def cot_from(b):
        return pltpu.make_async_remote_copy(
            cot_ref.at[0],
            cot.at[b],
            cot_send.at[0],
            cot_recv.at[b],
            device_id=(group, me),
            device_id_type=MESH,
        )

    for b in range(per):

        local = owners.is_me((home, slot * per + b))

        @pl.when(jnp.logical_not(local))
        def _():
            cot_from(b).wait_recv()

        @pl.when(local)
        def _():
            cot_keep().wait()

    given = cot[...].reshape(rows, width)
    gs_ref[7] = given
    grad[...] = given.astype(f32)
    feed_back(three, 2, up_two, down_two, gs_ref.at[7], 4, 1)

    gs_ref[3] = grad[...].astype(bf16)

    @over_columns
    def _(j):
        low[:, columns(j)] = mm_nt(gs_ref[3], wv[m_out, columns(j), :]).astype(bf16)

    @pl.loop(0, HEADS)
    def _(h):
        c = columns(h, HEAD_DIM)
        k_all = kv[0, :, :, c].reshape(latents, HEAD_DIM)
        v_all = kv[1, :, :, c].reshape(latents, HEAD_DIM)
        p = probs[h]
        g_mixed = low[:, c]
        g_p = mm_nt(g_mixed, v_all)
        g_v = mm_tn(p.astype(bf16), g_mixed)
        delta = jnp.sum(p * g_p, axis=1, keepdims=True)
        g_s = (p * (g_p - delta)).astype(bf16)
        gs_ref[0, :, c] = (mm(g_s, k_all) * scale).astype(bf16)
        g_k = mm_tn(g_s, heads_q[:, c]) * scale
        kv_out[:, 0, :, c] = g_k.reshape(sharers, rows, HEAD_DIM).astype(bf16)
        kv_out[:, 1, :, c] = g_v.reshape(sharers, rows, HEAD_DIM).astype(bf16)

    def gkv_push(d):
        to = lax.rem(slot + d, sharers)
        return pltpu.make_async_remote_copy(
            kv_out.at[to],
            kv_in.at[d - 1],
            gkv_send.at[d - 1],
            gkv_recv.at[d - 1],
            device_id=sharer(d),
            device_id_type=MESH,
        )

    for d in range(1, sharers):
        gkv_push(d).start()

    @over_columns
    def _(j):
        flow[:, columns(j)] = mm_nt(gs_ref[0], wv[m_query, columns(j), :])

    for d in range(1, sharers):
        gkv_push(d).wait_recv()
    for which in range(2):

        @over_columns
        def _(j):
            value = kv_out[slot, which, :, columns(j)].astype(f32)
            for d in range(1, sharers):
                value = value + kv_in[d - 1, which, :, columns(j)].astype(f32)
            gs_ref[1 + which, :, columns(j)] = value.astype(bf16)

    @over_columns
    def _(j):
        flow[:, columns(j)] += mm_nt(gs_ref[1], wv[m_key, columns(j), :]) + mm_nt(
            gs_ref[2], wv[m_value, columns(j), :]
        )

    norm_grad(two, 1)
    gs_ref[5] = grad[...].astype(bf16)
    feed_back(one, 0, up_one, down_one, gs_ref.at[5], 2, 0)
    gs_ref[8] = grad[...].astype(bf16)
    half = width // 2
    back = mm_nt(mix_ref[0, : mean.shape[1], :], gs_ref[8, :, :half])
    back = back + mm_nt(mix_ref[1, : mean.shape[1], :], gs_ref[8, :, half:])
    back_ref[...] = back.astype(bf16)
    row_ref[1:2, :] = jnp.sum(back * mean[1], axis=0, keepdims=True)
    in_gain = jnp.broadcast_to(
        jnp.sum(back * mean[0], axis=1, keepdims=True), (back.shape[0], 128)
    )
    gain_out[3:4, : back.shape[0]] = in_gain.T[0:1, :]

    for i in range(images):
        to, copy = cot_push(i)

        @pl.when(jnp.logical_not(owners.is_me(to)))
        def _():
            copy.wait_send()

    for d in range(1, sharers):
        kv_push(d).wait_send()
        gkv_push(d).wait_send()
    for k in range(late):
        for stage in range(reach):
            for way in range(2):
                last = stage == reach - 1
                hop(k, stage, way, stage == 0, last).wait_send()
                hand(k, stage + 1, way, last).wait_send()

    def out_from(i):
        return pltpu.make_async_remote_copy(
            final.at[pl.ds(0, rows_here)],
            out_ref.at[i],
            out_send.at[0],
            out_recv.at[i],
            device_id=(group, me),
            device_id_type=MESH,
        )

    for b in range(per):
        to, copy = out_push(b)

        @pl.when(jnp.logical_not(owners.is_me(to)))
        def _():
            copy.wait_send()

    for i in range(images):
        local = owners.is_me(owners.device(group, i, me // per))

        @pl.when(jnp.logical_not(local))
        def _():
            out_from(i).wait_recv()

        @pl.when(local)
        def _():
            out_keep().wait()


def latent_pass(parts, stats, own, cotangent, mix, gains, in_gain, whole, late, rows, collective_id):
    count = lax.axis_size("pix")
    images, rows_here, width = cotangent.shape
    channels = parts.shape[1]
    sharers = count // images
    per = count // sharers
    inside = pl.BlockSpec(memory_space=pltpu.VMEM)
    anywhere = pl.BlockSpec(memory_space=pl.ANY)
    whole_f32 = pltpu.VMEM((rows, width), f32)
    whole_low = pltpu.VMEM((rows, width), bf16)
    ring = DMA((count // 2, 2, len(late)))
    shape = jax.ShapeDtypeStruct
    return pl.pallas_call(
        functools.partial(latent_kernel, count, images),
        out_shape=[
            shape((images, rows_here, width), bf16),
            shape((7, width, rows), bf16),
            shape((9, rows, width), bf16),
            shape((channels, rows), bf16),
            shape((8, rows), f32),
            shape((8, width), f32),
        ],
        in_specs=[inside] * 2 + [anywhere] * 2 + [inside] * 3 + [anywhere] * 3,
        out_specs=[anywhere] + [inside] * 5,
        scratch_shapes=[
            pltpu.VMEM((8, width, width), bf16),
            whole_f32,
            whole_f32,
            whole_f32,
            pltpu.VMEM((2, rows, width), f32),
            whole_f32,
            whole_f32,
            whole_low,
            whole_low,
            pltpu.VMEM((2, sharers, rows, width), bf16),
            pltpu.VMEM((HEADS, rows, rows * sharers), f32),
            pltpu.VMEM((sharers, 2, rows, width), bf16),
            pltpu.VMEM((max(sharers - 1, 1), 2, rows, width), bf16),
            pltpu.VMEM((per, rows_here, width), bf16),
            whole_low,
            pltpu.VMEM((2, channels, rows), f32),
            whole_low,
            DMA,
            DMA((whole.shape[0],)),
            DMA((len(late),)),
            ring,
            ring,
            ring,
            ring,
            DMA((sharers,)),
            DMA((sharers,)),
            DMA((sharers,)),
            DMA((sharers,)),
            DMA,
            DMA((images,)),
            DMA((per,)),
            DMA,
            DMA((per,)),
            DMA((images,)),
        ],
        compiler_params=pltpu.CompilerParams(
            collective_id=collective_id, has_side_effects=True, vmem_limit_bytes=60 * 2**20
        ),
    )(parts, stats, own, cotangent, mix, gains, in_gain, whole, *late)


def tail_kernel(
    count,
    channels,
    t_ref,
    g_ref,
    z_ref,
    a_ref,
    lat_ref,
    qcols_ref,
    ncols_ref,
    wq_ref,
    wk_ref,
    wv_ref,
    wco_ref,
    gain_ref,
    lat_gain_ref,
    sum_ref,
    lat_out,
    lat_gain_out,
    gains_out,
    wq_out,
    wk_out,
    wv_out,
    wco_out,
    up_one_out,
    up_two_out,
    down_one_out,
    down_two_out,
    sq_out,
    sk_out,
    sv_out,
    so_out,
    z_v,
    query_grad,
    flow,
):
    me = lax.axis_index("pix")
    width = wq_ref.shape[0]
    depth = wco_ref.shape[0]
    rows_here = lat_out.shape[0]
    latents = lat_ref.shape[0]
    across = t_ref.shape[1]
    for k, to in (
        (0, sq_out),
        (1, sk_out),
        (2, sv_out),
        (3, so_out),
        (5, down_one_out),
        (7, down_two_out),
    ):
        to[...] = sum_ref[k]
    t = t_ref[...].astype(f32)
    tx = (t * (gain_ref[...] * width ** (-0.5))).astype(bf16)
    for o in range(count):
        gains_out[:, o * depth : (o + 1) * depth] = g_ref[o]
    row = jnp.sum(a_ref[:, :across] * t, axis=0, keepdims=True)
    gains_out[3:4, :across] += row
    wk_out[...] = mm_tn(tx, qcols_ref[...])[:channels]

    @pl.loop(0, width // 256)
    def _(j):
        columns = pl.ds(pl.multiple_of(j * 256, 256), 256)
        query_grad[:, columns] = mm_nt(tx, wk_ref[columns, :across]).astype(bf16)

    @pl.loop(0, width // 256)
    def _(j):
        columns = pl.ds(pl.multiple_of(j * 256, 256), 256)
        wq_out[:, columns] = mm_tn(ncols_ref[...], query_grad[:, columns])
        flow[:, columns] = mm_nt(query_grad[...], wq_ref[columns, :])

    share = share_rows(channels, count)
    half = width // 2
    for o in range(count):
        for h in range(2):
            z_v[o * share : (o + 1) * share, h * half : (h + 1) * half] = z_ref[h, o, :share].astype(f32)
    cross = z_v[...].astype(bf16)
    wv_out[...] = mm_nt(cross, wco_ref[...])[:channels]
    wco_out[...] = mm_tn(wv_ref[...], cross)

    up_one_out[...] = sum_ref[4].T
    up_two_out[...] = sum_ref[6].T
    lat_gain_out[...] = jnp.zeros_like(lat_gain_out)

    @pl.loop(0, count)
    def _(o):
        here = pl.ds(pl.multiple_of(o * rows_here, rows_here), rows_here)
        rows = lat_ref[here, :].astype(f32)
        average = jnp.mean(rows, axis=1, keepdims=True)
        centred = rows - average
        scale = lax.rsqrt(jnp.mean(centred * centred, axis=1, keepdims=True) + eps)
        hat = centred * scale
        given = flow[here, :]
        lat_gain_out[...] += jnp.sum(given * hat, axis=0, keepdims=True)

        @pl.when(o == me)
        def _():
            gained = given * lat_gain_ref[...]
            along = jnp.mean(gained * hat, axis=1, keepdims=True)
            moved = scale * (gained - jnp.mean(gained, axis=1, keepdims=True) - hat * along)
            lat_out[...] = moved + sum_ref[8, :rows_here, :]


def tail_pass(t, g, z, a, lat, qcols, ncols, wq, wk, wv, wco, gain, lat_gain, summed, channels):
    count = z.shape[1]
    _, depth, width = summed.shape
    latents = lat.shape[0]
    share = share_rows(channels, count)
    inside = pl.BlockSpec(memory_space=pltpu.VMEM)
    anywhere = pl.BlockSpec(memory_space=pl.ANY)
    shape = lambda *dims: jax.ShapeDtypeStruct(dims, f32)
    plain = shape(depth, width)
    return pl.pallas_call(
        functools.partial(tail_kernel, count, channels),
        out_shape=[
            shape(latents // count, width),
            shape(1, width),
            shape(8, width),
            plain,
            shape(channels, depth),
            shape(channels, depth),
            plain,
            shape(width, depth),
            shape(width, depth),
        ]
        + [plain] * 6,
        in_specs=[inside] * 14,
        out_specs=[inside] * 15,
        scratch_shapes=[
            pltpu.VMEM((count * share, width), f32),
            pltpu.VMEM((latents, width), bf16),
            pltpu.VMEM((latents, width), f32),
        ],
        compiler_params=pltpu.CompilerParams(vmem_limit_bytes=48 * 2**20),
    )(t, g, z, a, lat, qcols, ncols, wq, wk, wv, wco, gain, lat_gain, summed)


def local(
    rgb_pixels,
    keep_mask,
    latent_array,
    gain_input,
    gain_latent,
    w_query,
    w_key,
    w_value,
    w_cross_out,
    gain_mlp_one,
    w_up_one,
    w_down_one,
    gain_self,
    w_self_query,
    w_self_key,
    w_self_value,
    w_self_out,
    gain_mlp_two,
    w_up_two,
    w_down_two,
    cotangent,
):
    images, _, pixels = rgb_pixels.shape
    rows_here, width = latent_array.shape
    count = lax.axis_size("pix")
    me = lax.axis_index("pix")
    latents = rows_here * count
    sharers = count // images
    rows_own = latents // sharers
    depth = w_query.shape[0]
    channels = gain_input.shape[0]
    tall = -(-channels // 16) * 16

    side = -(-channels // 512) * 512
    key_t = jnp.pad(w_key.T, ((0, 0), (0, side - channels)))
    blocks = -(-tall // (16 * count)) * 16 * count
    value_pad = jnp.pad(w_value, ((0, blocks - channels), (0, 0)))
    shards = [w_up_one.T, w_down_one, w_self_query, w_self_key, w_self_value, w_self_out]
    late = [w_up_two.T, w_down_two]

    lines = pixels // SIDE
    u, sin_u, cos_u = angles(me * lines + lax.iota(jnp.int32, lines))
    w, sin_w, cos_w = angles(lax.iota(jnp.int32, SIDE))

    def zeros(rows, columns):
        return jnp.zeros((rows, columns), f32)

    pad = CHANNELS - 4 - SIDE - lines
    table = jnp.concatenate(
        [
            jnp.concatenate(
                [zeros(SIDE, 4), w, zeros(SIDE, BANDS), sin_w, zeros(SIDE, BANDS), cos_w], axis=1
            ),
            jnp.concatenate(
                [zeros(lines, 3), u, zeros(lines, 1), sin_u, zeros(lines, BANDS), cos_u, zeros(lines, BANDS)],
                axis=1,
            ),
            zeros(pad, channels),
            jnp.eye(3, channels, dtype=f32),
            jnp.ones((1, channels), f32),
        ],
        axis=0,
    )
    row_sum = u[:, 0] + jnp.sum(sin_u + cos_u, axis=1)
    col_sum = w[:, 0] + jnp.sum(sin_w + cos_w, axis=1)
    row_square = u[:, 0] ** 2 + jnp.sum(sin_u**2 + cos_u**2, axis=1)
    col_square = w[:, 0] ** 2 + jnp.sum(sin_w**2 + cos_w**2, axis=1)
    feature_sum = (row_sum[:, None] + col_sum[None, :]).reshape(1, pixels)
    feature_square = (row_square[:, None] + col_square[None, :]).reshape(1, pixels)
    colours = rgb_pixels.astype(f32)
    average = (jnp.sum(colours, axis=1) + feature_sum) / channels
    spread = (jnp.sum(colours**2, axis=1) + feature_square) / channels - average**2
    scale = lax.rsqrt(spread + eps)
    keep = keep_mask.astype(f32)

    own_values = jnp.concatenate([colours, -average[:, None, :]], axis=1) * scale[:, None, :]
    values = jnp.concatenate(
        [scale[:, None], keep[:, None], jnp.zeros((images, 2, pixels), f32), own_values], axis=1
    )
    table = jnp.pad(table, ((0, 0), (0, side - channels)))
    gained = table * jnp.pad(gain_input, (0, side - channels))[None, :]
    (
        latent_full,
        query_mat,
        key_full,
        whole,
        latent_normed,
        queries,
        score_mat,
        at,
        a_low,
        value_out,
        raw_parts,
        stat_parts,
    ) = forward_pass(
        values,
        table,
        gained,
        gain_latent,
        latent_array,
        w_query,
        key_t,
        value_pad,
        w_cross_out,
        shards,
        tall,
        0,
    )
    latent_full = latent_full.reshape(latents, width)
    whole = whole.reshape(-1, width, width)

    latent_out, xs, gs, back_t, row_stats, gain_grads = latent_pass(
        raw_parts,
        stat_parts,
        latent_full,
        cotangent,
        value_out.reshape(2, blocks, width // 2),
        jnp.stack([gain_mlp_one, gain_self, gain_mlp_two]),
        jnp.pad(gain_input, (0, tall - channels))[:, None],
        whole,
        late,
        rows_own,
        4,
    )
    across = -(-channels // 128) * 128
    grad_raw, gain_sums, cross_sum, grad_pixels, summed = backward_pass(
        values,
        table,
        gained,
        at,
        a_low,
        back_t,
        row_stats,
        gain_grads,
        xs,
        gs,
        channels,
        2,
    )

    share = share_rows(channels, count)
    (
        grad_latent_array,
        gain_latent_sum,
        gain_sums,
        grad_w_query,
        grad_w_key,
        grad_w_value,
        grad_w_cross_out,
        g_up_one,
        g_up_two,
        g_down_one,
        g_down_two,
        g_sq,
        g_sk,
        g_sv,
        g_so,
    ) = tail_pass(
        grad_raw.reshape(latents, across),
        gain_sums,
        cross_sum,
        score_mat,
        latent_full,
        lax.dynamic_slice_in_dim(queries, me * depth, depth, 1),
        lax.dynamic_slice_in_dim(latent_normed, me * depth, depth, 1),
        query_mat.reshape(width, width),
        key_full.reshape(width, side),
        jnp.pad(w_value, ((0, share * count - channels), (0, 0))),
        w_cross_out,
        jnp.pad(gain_input, (0, across - channels))[None],
        gain_latent[None],
        summed,
        channels,
    )
    gain_one, gain_attn, gain_two = gain_sums[0], gain_sums[1], gain_sums[2]
    gain_in = gain_sums[3, :channels]
    grad_gain_latent = gain_latent_sum[0]
    return (
        latent_out,
        grad_pixels,
        grad_latent_array,
        gain_in,
        grad_gain_latent,
        grad_w_query,
        grad_w_key,
        grad_w_value,
        grad_w_cross_out,
        gain_one,
        g_up_one,
        g_down_one,
        gain_attn,
        g_sq,
        g_sk,
        g_sv,
        g_so,
        gain_two,
        g_up_two,
        g_down_two,
    )


def solution(mesh):
    rows, columns, copied = P("pix", None), P(None, "pix"), P()
    return jax.shard_map(
        local,
        mesh=mesh,
        in_specs=(
            P("img", None, "pix"),
            P("img", "pix"),
            rows,
            copied,
            copied,
            rows,
            columns,
            columns,
            rows,
            copied,
            columns,
            rows,
            copied,
            rows,
            rows,
            rows,
            rows,
            copied,
            columns,
            rows,
            P("img", "pix", None),
        ),
        out_specs=(
            P("img", "pix", None),
            P("img", None, "pix"),
            rows,
            copied,
            copied,
            rows,
            columns,
            columns,
            rows,
            copied,
            columns,
            rows,
            copied,
            rows,
            rows,
            rows,
            rows,
            copied,
            columns,
            rows,
        ),
        check_vma=False,
    )
```

```python
import functools

import jax
import jax.numpy as jnp
from jax import lax
from jax.experimental import pallas as pl
from jax.experimental.pallas import tpu as pltpu
from jax.sharding import PartitionSpec as P

HEADS = 8
HEAD_DIM = 128
BANDS = 64
SIDE = 224
CHANNELS = 256
LOG2E = 1.4426950408889634

eps = 1e-05
f32 = jnp.float32
bf16 = jnp.bfloat16


def exact(left, right):
    return jnp.dot(left, right, precision=lax.Precision.HIGHEST, preferred_element_type=f32)


def mm(left, right):
    return jnp.dot(left, right, preferred_element_type=f32)


def mm_nt(left, right):
    return lax.dot_general(left, right, (((1,), (1,)), ((), ())), preferred_element_type=f32)


def mm_tn(left, right):
    return lax.dot_general(left, right, (((0,), (0,)), ((), ())), preferred_element_type=f32)


def angles(index):
    place = index.astype(f32) * (2.0 / (SIDE - 1)) - 1.0
    steps = lax.iota(jnp.int32, BANDS).astype(f32)
    frequency = 1.0 + steps * ((SIDE / 2.0 - 1.0) / (BANDS - 1))
    angle = jnp.pi * place[:, None] * frequency[None, :]
    return place[:, None], jnp.sin(angle), jnp.cos(angle)


def pixel_tile(pixels):
    return 896 if pixels % 896 == 0 else pixels


MESH = pl.DeviceIdType.MESH
DMA = pltpu.SemaphoreType.DMA


def ring_place(count):
    me = lax.axis_index("pix")
    return jnp.where(me % 2 == 0, me // 2, count - 1 - me // 2)


def ring_device(place, count):
    place = lax.rem(place + 2 * count, count)
    return jnp.where(place < count // 2, 2 * place, 2 * (count - 1 - place) + 1)


def greet(devices):
    barrier = pltpu.get_barrier_semaphore()
    for device in devices:
        pl.semaphore_signal(barrier, inc=1, device_id=device, device_id_type=MESH)
    pl.semaphore_wait(barrier, len(devices))


def hot_codes(tile):
    pixel = lax.broadcasted_iota(jnp.int32, (CHANNELS, tile), 1)
    channel = lax.broadcasted_iota(jnp.int32, (CHANNELS, tile), 0)
    start = channel - SIDE - pixel // SIDE
    code = jnp.where((start >= 0) & (channel < CHANNELS - 4), start, -2)
    return jnp.where(channel < SIDE, jnp.where(channel == pixel % SIDE, -1, -2), code)


def build_xt(values, base, code_ref):
    code = code_ref[...]
    hot = jnp.where((code == -1) | (code == base), values[0:1, :], 0.0)
    last = hot[CHANNELS - 8 :, :]
    k = lax.broadcasted_iota(jnp.int32, last.shape, 0)
    last = jnp.where(k >= 4, values, last)
    return jnp.concatenate([hot[: CHANNELS - 8, :], last], axis=0)


def build_both(values, base, code_ref):
    keep = values[1:2, :]
    xt = build_xt(values, base, code_ref).astype(bf16)
    k = lax.broadcasted_iota(jnp.int32, (16, values.shape[1]), 0)
    ones = jnp.where(k == 0, keep, 0.0).astype(bf16)
    return xt.T, jnp.concatenate([xt * keep.astype(bf16), ones], axis=0)


def forward_kernel(
    count,
    teams,
    images,
    tile,
    mats,
    v_ref,
    code_ref,
    table_ref,
    gained_ref,
    gain_ref,
    lat_ref,
    wq_ref,
    wk_ref,
    wv_ref,
    wco_ref,
    *refs,
):
    shards = refs[:mats]
    forward_body(
        count,
        teams,
        images,
        tile,
        v_ref,
        code_ref,
        table_ref,
        gained_ref,
        gain_ref,
        lat_ref,
        wq_ref,
        wk_ref,
        wv_ref,
        wco_ref,
        shards,
        *refs[mats:],
    )


def forward_body(
    count,
    teams,
    images,
    tile,
    v_ref,
    code_ref,
    table_ref,
    gained_ref,
    gain_ref,
    lat_ref,
    wq_ref,
    wk_ref,
    wv_ref,
    wco_ref,
    shards,
    lat_full,
    wq_full,
    wk_full,
    w_full,
    normed_ref,
    query_ref,
    a_ref,
    at_ref,
    alow_ref,
    mix_ref,
    part_ref,
    stat_ref,
    mix_raw,
    mix_in,
    acc,
    top,
    u_send,
    s_send,
    own_sem,
    send_sem,
    recv_sem,
    hand_send,
    hand_recv,
    mix_send,
    mix_recv,
    mix_hand,
    x_send,
    x_recv,
    u_own,
    u_out,
    u_in,
):
    pixels = v_ref.shape[2]
    steps = pixels // tile
    lines = tile // SIDE
    owners = Owners(count, images)
    sharers = owners.sharers
    rows = part_ref.shape[2]
    width = wq_ref.shape[1]
    latents = normed_ref.shape[0]
    group, me = lax.axis_index("img"), lax.axis_index("pix")
    core = lax.rem(group, 2)
    place = ring_place(count)
    sides = ((group, ring_device(place + 1, count)), (group, ring_device(place - 1, count)))
    other = (group + 1 - 2 * core, me)
    team = group // 2
    partners = [(lax.rem(team + d, teams) * 2 + core, me) for d in range(1, teams)]
    greet(plane(count) + partners)
    sources = (lat_ref, wq_ref, wk_ref)
    fulls = (lat_full, wq_full, wk_full, w_full)
    mats = len(shards)

    reach = count // 2

    def spot(a, k, stage, way, last, source=False):
        wide = fulls[a].shape[3] // 4
        begin = (core * 2 + way) * wide if last else core * 2 * wide
        columns = pl.ds(pl.multiple_of(begin, 128), wide if last else 2 * wide)
        if source:
            return (sources[a] if a < 3 else shards[k]).at[:, columns]
        origin = ring_device(place - stage if way == 0 else place + stage, count)
        return fulls[a].at[k, origin, :, columns]

    def hop(a, k, stage, way, first=False, last=False):
        return pltpu.make_async_remote_copy(
            spot(a, k, stage, way, last, first),
            spot(a, k, stage, way, last),
            send_sem.at[stage, way, a + k],
            recv_sem.at[stage, way, a + k],
            device_id=sides[way],
            device_id_type=MESH,
        )

    def hand(a, k, stage, way, last=False):
        part = spot(a, k, stage, way, last)
        return pltpu.make_async_remote_copy(
            part,
            part,
            hand_send.at[stage - 1, way, a + k],
            hand_recv.at[stage - 1, way, a + k],
            device_id=other,
            device_id_type=MESH,
        )

    def relay(a, k, stage):
        for way in range(2):
            hop(a, k, stage - 1, way).wait_recv()

            @pl.when(stage == reach - 1)
            def _():
                hop(a, k, stage, way, last=True).start()

            @pl.when(stage != reach - 1)
            def _():
                hop(a, k, stage, way).start()

            hand(a, k, stage, way).start()

    def relay_end(a, k):
        for way in range(2):
            hop(a, k, reach - 1, way, last=True).wait_recv()
            hand(a, k, reach, way, last=True).start()

    def start_ring(a, k):
        for way in range(2):
            hop(a, k, 0, way, True, reach == 1).start()

    alone = 0

    def at_home(k):
        return (k < alone) | (lax.rem(jnp.int32(k), teams) == team)

    def over_x(k, stage, way, d, last=False):
        part = spot(3, k, stage, way, last)
        return pltpu.make_async_remote_copy(
            part,
            part,
            x_send.at[d, stage - 1, way, k],
            x_recv.at[stage - 1, way, k],
            device_id=partners[d],
            device_id_type=MESH,
        )

    def pass_x(k, stage, last=False):
        @pl.when(k >= alone)
        def _():
            for way in range(2):
                for d in range(teams - 1):
                    over_x(k, stage, way, d, last).start()

    def take_x(k, stage, last=False):
        for way in range(2):
            over_x(k, stage, way, 0, last).wait_recv()
            hand(3, k, stage, way, last).start()

    def relay_weight(k, stage):
        home = at_home(k)

        @pl.when(home)
        def _():
            relay(3, k, stage)
            pass_x(k, stage)

        @pl.when(jnp.logical_not(home) & (stage > 1))
        def _():
            take_x(k, stage - 1)

    def relay_weight_end(k):
        home = at_home(k)

        @pl.when(home)
        def _():
            relay_end(3, k)
            pass_x(k, reach, True)

        @pl.when(jnp.logical_not(home))
        def _():
            take_x(k, reach - 1)

    def sent(a, k):
        for way in range(2):
            for stage in range(reach):
                last = stage == reach - 1
                hop(a, k, stage, way, stage == 0, last).wait_send()
                hand(a, k, stage + 1, way, last).wait_send()

    def handed(a, k):
        for way in range(2):
            for stage in range(1, reach + 1):
                hand(a, k, stage, way, stage == reach).wait_recv()

    own = [
        pltpu.make_async_copy(shards[k], fulls[3].at[k, me], own_sem.at[k]) for k in range(mats)
    ]
    for a in range(3):
        start_ring(a, 0)
    others = peers(count)
    used = -(-part_ref.shape[1] // mix_raw.shape[1])

    def mix_copy(source, target, stage, index, device):
        return pltpu.make_async_remote_copy(
            source,
            target,
            mix_send.at[stage, index],
            mix_recv.at[stage, index],
            device_id=device,
            device_id_type=MESH,
        )

    def mix_scatter(d):
        return mix_copy(mix_raw.at[others[d][1]], mix_in.at[d], 0, d, others[d])

    def mix_gather(d):
        return mix_copy(mix_ref.at[core, me], mix_ref.at[core, me], 1, d, others[d])

    def mix_from(d):
        source = lax.rem(me + count - 1 - d, count)
        return source, mix_copy(mix_ref.at[core, source], mix_ref.at[core, source], 1, d, others[d])

    def mix_pass():
        return pltpu.make_async_remote_copy(
            mix_ref.at[core],
            mix_ref.at[core],
            mix_hand.at[0],
            mix_hand.at[1],
            device_id=other,
            device_id_type=MESH,
        )

    half = width // 2
    columns = pl.ds(pl.multiple_of(core * half, 128), half)
    mix_raw[...] = mm(wv_ref[...], wco_ref[:, columns]).astype(bf16).reshape(mix_raw.shape)
    for a in range(3):
        fulls[a][0, me] = sources[a][...]
    for copy in own:
        copy.start()
    each = -(-mats // reach)
    for stage in range(1, reach + 1):
        for a in range(3):
            if stage < reach:
                relay(a, 0, jnp.int32(stage))
            else:
                relay_end(a, 0)
        for k in range((stage - 1) * each, min(stage * each, mats)):

            @pl.when(at_home(k))
            def _():
                start_ring(3, k)


    for d in range(count - 1):

        @pl.when(others[d][1] < used)
        def _():
            mix_scatter(d).start()

    for a in range(3):
        handed(a, 0)

    rows_here = lat_ref.shape[0]
    relays = (reach - 1) * mats
    early = min(relays, width // 256)

    def relay_number(e):
        relay_weight(lax.rem(e, mats), 1 + e // mats)

    @pl.loop(0, count)
    def _(o):
        block = lat_full[0, o].astype(f32)
        average = jnp.mean(block, axis=1, keepdims=True)
        centred = block - average
        spread = jnp.mean(centred * centred, axis=1, keepdims=True)
        normed = (centred * lax.rsqrt(spread + eps) * gain_ref[...]).astype(bf16)
        normed_ref[pl.ds(pl.multiple_of(o * rows_here, rows_here), rows_here), :] = normed

    @pl.loop(0, width // 256)
    def _(j):
        @pl.when(j < early)
        def _():
            relay_number(j)

        columns = pl.ds(pl.multiple_of(j * 256, 256), 256)
        weight = wq_full[0, :, :, columns].reshape(width, 256)
        query_ref[:, columns] = mm(normed_ref[...], weight).astype(bf16)

    a_ref[...] = mm(query_ref[...], wk_full[0].reshape(width, wk_ref.shape[1])) * (width ** (-0.5))

    def exact_nt(left, right):
        return lax.dot_general(
            left,
            right,
            (((1,), (1,)), ((), ())),
            precision=lax.Precision.HIGHEST,
            preferred_element_type=f32,
        )

    at_ref[...] = (exact_nt(gained_ref[...], a_ref[...]) * LOG2E).astype(bf16)
    alow_ref[...] = exact_nt(a_ref[...], gained_ref[...]).astype(bf16)

    table_t = table_ref[...].T[: part_ref.shape[1], :]

    @pl.when(me < used)
    def _():
        total = mix_raw[me].astype(f32)
        for d in range(count - 1):
            mix_scatter(d).wait_recv()
            total = total + mix_in[d].astype(f32)
        mix_ref[core, me] = total.astype(bf16)
        for d in range(count - 1):
            mix_gather(d).start()

    def u_push(i, h):
        to = owners.device(group, i, jnp.int32(h))
        sems = lambda which: dict(
            send_sem=u_out.at[which, i * sharers + h],
            recv_sem=u_in.at[which, me],
            device_id=to,
            device_id_type=MESH,
        )
        return to, (
            pltpu.make_async_remote_copy(u_send.at[i, h], part_ref.at[me], **sems(0)),
            pltpu.make_async_remote_copy(s_send.at[i, h], stat_ref.at[me], **sems(1)),
        )

    def u_keep():
        i, h = owners.image, owners.slot
        return (
            pltpu.make_async_copy(u_send.at[i, h], part_ref.at[me], u_own.at[0]),
            pltpu.make_async_copy(s_send.at[i, h], stat_ref.at[me], u_own.at[1]),
        )

    @pl.loop(0, images * steps)
    def _(t):
        i, step = t // steps, lax.rem(t, steps)

        @pl.when(t + early < relays)
        def _():
            relay_number(t + early)

        @pl.when(step == 0)
        def _():
            acc[...] = jnp.zeros_like(acc)
            top[...] = jnp.full_like(top, -jnp.inf)

        values = v_ref[i, :, pl.ds(pl.multiple_of(step * tile, 128), tile)]
        base = step * lines
        x, xt = build_both(values, base, code_ref)
        first, second = slice(0, tile // 2), slice(tile // 2, tile)
        scores = [mm(x[half], at_ref[...]) for half in (first, second)]
        old, total = top[0:1, :], acc[...]
        for half, score in zip((first, second), scores):
            new = jnp.maximum(old, jnp.max(score, axis=0, keepdims=True))
            weights = jnp.exp2(score - new).astype(bf16)
            total = total * jnp.exp2(old - new) + mm(xt[:, half], weights)
            old = new
        acc[...] = total
        top[...] = jnp.broadcast_to(old, top.shape)

        @pl.when(step == steps - 1)
        def _():
            raw = jnp.dot(
                table_t,
                acc[:CHANNELS, :],
                precision=lax.Precision.HIGHEST,
                preferred_element_type=f32,
            ).astype(bf16)
            stats = jnp.concatenate([top[0:1, :], acc[CHANNELS : CHANNELS + 1, :], top[0:6, :]], axis=0)
            for h in range(sharers):
                u_send[i, h] = raw[:, h * rows : (h + 1) * rows]
                s_send[i, h] = stats[:, h * rows : (h + 1) * rows]
            for h in range(sharers):
                to, copies = u_push(i, h)

                @pl.when(jnp.logical_not(owners.is_me(to)))
                def _():
                    for copy in copies:
                        copy.start()

                @pl.when(owners.is_me(to))
                def _():
                    for copy in u_keep():
                        copy.start()

    if images * steps + early < relays:

        @pl.loop(images * steps + early, relays)
        def _(e):
            relay_number(e)

    for d in range(count - 1):
        source, copy = mix_from(d)

        @pl.when(source < used)
        def _():
            copy.wait_recv()

    for o in range(used, count):
        mix_ref[core, o] = jnp.zeros_like(mix_raw[0])
    mix_pass().start()

    pl.loop(0, mats)(relay_weight_end)

    @pl.loop(alone, mats)
    def _(k):
        @pl.when(jnp.logical_not(at_home(k)))
        def _():
            take_x(k, reach, True)

    for copy in own:
        copy.wait()
    mix_pass().wait()
    for d in range(count - 1):

        @pl.when(others[d][1] < used)
        def _():
            mix_scatter(d).wait_send()

        @pl.when(me < used)
        def _():
            mix_gather(d).wait_send()

    for a in range(3):
        sent(a, 0)

    for k in range(mats):
        home = at_home(k)

        @pl.when(home)
        def _():
            sent(3, k)
            if k >= alone:
                for stage in range(1, reach + 1):
                    for way in range(2):
                        for d in range(teams - 1):
                            over_x(k, stage, way, d, stage == reach).wait_send()

        @pl.when(jnp.logical_not(home))
        def _():
            for way in range(2):
                for stage in range(1, reach + 1):
                    hand(3, k, stage, way, stage == reach).wait_send()

        handed(3, k)

    def u_from(source):
        sems = lambda which: dict(
            send_sem=u_out.at[which, 0],
            recv_sem=u_in.at[which, source],
            device_id=(owners.home, source),
            device_id_type=MESH,
        )
        return (
            pltpu.make_async_remote_copy(u_send.at[0, 0], part_ref.at[source], **sems(0)),
            pltpu.make_async_remote_copy(s_send.at[0, 0], stat_ref.at[source], **sems(1)),
        )

    for i in range(images):
        for h in range(sharers):
            to, copies = u_push(i, h)

            @pl.when(jnp.logical_not(owners.is_me(to)))
            def _():
                for copy in copies:
                    copy.wait_send()

    for source in range(count):
        local = owners.is_me((owners.home, source))

        @pl.when(local)
        def _():
            for copy in u_keep():
                copy.wait()

        @pl.when(jnp.logical_not(local))
        def _():
            for copy in u_from(source):
                copy.wait_recv()


def forward_pass(
    values, table, gained, gain_latent, lat, wq, wk, wv, wco, shards, tall, collective_id
):
    count = lax.axis_size("pix")
    images, _, pixels = values.shape
    tile = pixel_tile(pixels)
    rows_here, width = lat.shape
    latents = rows_here * count
    sharers = count // images
    rows = latents // sharers
    mats = len(shards)
    inside = pl.BlockSpec(memory_space=pltpu.VMEM)
    anywhere = pl.BlockSpec(memory_space=pl.ANY)
    shape = jax.ShapeDtypeStruct

    def full(array, number=1):
        return shape((number, count) + array.shape, array.dtype)

    ring = DMA((count // 2, 2, 3 + mats))
    return pl.pallas_call(
        functools.partial(forward_kernel, count, lax.axis_size("img") // 2, images, tile, mats),
        out_shape=[full(lat), full(wq), full(wk), full(shards[0], mats)]
        + [
            shape((latents, width), bf16),
            shape((latents, width), bf16),
            shape((latents, wk.shape[1]), f32),
            shape((CHANNELS, latents), bf16),
            shape((latents, CHANNELS), bf16),
            shape((2, count, wv.shape[0] // count, width // 2), bf16),
            shape((count, tall, rows), bf16),
            shape((count, 8, rows), f32),
        ],
        in_specs=[inside] * (10 + mats),
        out_specs=[inside] * 3 + [anywhere] + [inside] * 6 + [anywhere] * 2,
        scratch_shapes=[
            pltpu.VMEM((count, wv.shape[0] // count, width // 2), bf16),
            pltpu.VMEM((count - 1, wv.shape[0] // count, width // 2), bf16),
            pltpu.VMEM((CHANNELS + 16, latents), f32),
            pltpu.VMEM((8, latents), f32),
            pltpu.VMEM((images, sharers, tall, rows), bf16),
            pltpu.VMEM((images, sharers, 8, rows), f32),
            DMA((mats,)),
            ring,
            ring,
            ring,
            ring,
            DMA((2, count - 1)),
            DMA((2, count - 1)),
            DMA((2,)),
            DMA((max(lax.axis_size("img") // 2 - 1, 1), count // 2, 2, mats)),
            DMA((count // 2, 2, mats)),
            DMA((2,)),
            DMA((2, count)),
            DMA((2, count)),
        ],
        compiler_params=pltpu.CompilerParams(
            collective_id=collective_id, has_side_effects=True, vmem_limit_bytes=48 * 2**20
        ),
    )(values, hot_codes(tile), table, gained, gain_latent[None], lat, wq, wk, wv, wco, *shards)


def backward_kernel(
    count,
    teams,
    images,
    tile,
    channels,
    v_ref,
    code_ref,
    table_ref,
    gained_ref,
    at_ref,
    a_ref,
    back_ref,
    row_ref,
    gain_ref,
    xs_ref,
    gs_ref,
    t_out,
    g_out,
    z_out,
    pixel_ref,
    out_ref,
    t_raw,
    t_in,
    t_img,
    g_raw,
    g_in,
    g_img,
    z_own,
    t_acc,
    bt,
    b_low,
    stat,
    back_all,
    row_all,
    xv,
    gv,
    terms,
    held,
    across,
    done,
    load_sem,
    pair_send,
    pair_recv,
    send_sem,
    recv_sem,
    cross_send,
    cross_recv,
    out_sem,
    hand_send,
    hand_recv,
    back_send,
    back_recv,
    pass_send,
    foreign_send,
    foreign_recv,
    sum_send,
    sum_recv,
    img_send,
    img_recv,
    last_send,
    last_recv,
    z_send,
    z_recv,
    z_hand_send,
    z_hand_recv,
):
    number, rows, width = gs_ref.shape
    kinds = xs_ref.shape[0]
    owners = Owners(count, images)
    sharers = owners.sharers
    steps = v_ref.shape[2] // tile
    lines = tile // SIDE
    depth = xs_ref.shape[1] // count
    half, wide = width // 2, width // 4
    group, me = lax.axis_index("img"), lax.axis_index("pix")
    core, team = lax.rem(group, 2), group // 2
    place = ring_place(count)
    sides = ((group, ring_device(place + 1, count)), (group, ring_device(place - 1, count)))
    other = (group + 1 - 2 * core, me)
    partners = [(lax.rem(team + d, teams) * 2 + core, me) for d in range(1, teams)]
    crowd = 2 * teams
    others = peers(count)
    same_place = [(lax.rem(group + d, crowd), me) for d in range(1, crowd)]
    far = [
        (lax.rem(team + d, teams) * 2 + c, me) for d in range(1, teams) for c in range(2)
    ]
    greet(plane(count) + far)

    def send(source, target, sems, index, device):
        return pltpu.make_async_remote_copy(
            source,
            target,
            sems[0].at[index],
            sems[1].at[index],
            device_id=device,
            device_id_type=MESH,
        )

    def scatter(d):
        to, sems = others[d][1], (sum_send, sum_recv)
        return (
            send(t_raw.at[to], t_in.at[d], sems, (0, d), others[d]),
            send(g_raw.at[to], g_in.at[d], sems, (1, d), others[d]),
        )

    def over(d):
        sems = (img_send, img_recv)
        return (
            send(t_img.at[group], t_img.at[group], sems, (0, d), same_place[d]),
            send(g_img.at[group], g_img.at[group], sems, (1, d), same_place[d]),
        )

    def gather(d):
        sems = (last_send, last_recv)
        return (
            send(t_out.at[me], t_out.at[me], sems, (0, d), others[d]),
            send(g_out.at[me], g_out.at[me], sems, (1, d), others[d]),
        )

    def z_push(d):
        return send(z_own, z_out.at[core, me], (z_send, z_recv), d, others[d])

    def z_hand():
        return pltpu.make_async_remote_copy(
            z_out.at[core],
            z_out.at[core],
            z_hand_send,
            z_hand_recv,
            device_id=other,
            device_id_type=MESH,
        )

    for o in range(count):
        g_raw[o] = gain_ref[:, o * depth : (o + 1) * depth]

    own_index = owners.image * sharers + owners.slot

    def back_push(d):
        to = (owners.home, lax.rem(me + 2 * d, count))
        sems = lambda which: dict(
            send_sem=back_send.at[which, d],
            recv_sem=back_recv.at[which, own_index],
            device_id=to,
            device_id_type=MESH,
        )
        return to, (
            pltpu.make_async_remote_copy(back_ref, back_all.at[own_index], **sems(0)),
            pltpu.make_async_remote_copy(row_ref, row_all.at[own_index], **sems(1)),
        )

    def back_from(source):
        sems = lambda which: dict(
            send_sem=back_send.at[which, 0],
            recv_sem=back_recv.at[which, source],
            device_id=(group, me),
            device_id_type=MESH,
        )
        return (
            pltpu.make_async_remote_copy(back_ref, back_all.at[source], **sems(0)),
            pltpu.make_async_remote_copy(row_ref, row_all.at[source], **sems(1)),
        )

    def back_hand(block):
        to = (group, me + 1 - 2 * lax.rem(me, 2))
        sems = lambda which: dict(
            send_sem=pass_send.at[which, block],
            recv_sem=back_recv.at[which, block],
            device_id=to,
            device_id_type=MESH,
        )
        return (
            pltpu.make_async_remote_copy(back_all.at[block], back_all.at[block], **sems(0)),
            pltpu.make_async_remote_copy(row_all.at[block], row_all.at[block], **sems(1)),
        )

    def back_owner(image, slot):
        sender = owners.device(group, image, slot)
        return sender, lax.rem(sender[1], 2) == lax.rem(me, 2)

    for d in range(count // 2):
        to, copies = back_push(d)

        @pl.when(jnp.logical_not(owners.is_me(to)))
        def _():
            for copy in copies:
                copy.start()

        @pl.when(owners.is_me(to))
        def _():
            back_all[own_index] = back_ref[...]
            row_all[own_index] = row_ref[...]

    def load_x(j):
        return pltpu.make_async_copy(xs_ref.at[j], xv.at[j, core], load_sem.at[0, j])

    def load_g(k):
        part = gs_ref.at[k, :, pl.ds(pl.multiple_of(core * half, 128), half)]
        return pltpu.make_async_copy(part, gv.at[k, core], load_sem.at[1, k])

    def pair_x(j):
        return pltpu.make_async_remote_copy(
            xs_ref.at[j],
            xv.at[j, core],
            pair_send.at[0, j],
            pair_recv.at[0, j],
            device_id=other,
            device_id_type=MESH,
        )

    def pair_g(k):
        part = gs_ref.at[k, :, pl.ds(pl.multiple_of((1 - core) * half, 128), half)]
        return pltpu.make_async_remote_copy(
            part,
            gv.at[k, core],
            pair_send.at[1, k],
            pair_recv.at[1, k],
            device_id=other,
            device_id_type=MESH,
        )

    low, high = (4, 8) if number == 9 and count > 4 and 4 % teams == 0 else (0, 0)
    if teams == 1:
        low, high = 0, 0
    reach = count // 2

    def alone(k):
        return (k >= low) & (k < high)

    def at_home(k):
        return jnp.logical_not(alone(k)) | (lax.rem(k, teams) == team)

    def foreign(k, sender, way, stage):
        slot = (k // teams) * teams + sender
        rows_in = pl.ds((way * reach + stage) * depth, depth)
        return pltpu.make_async_remote_copy(
            terms.at[k, rows_in],
            held.at[slot, way, stage],
            foreign_send.at[way, stage, k],
            foreign_recv.at[sender, way, stage, k],
            device_id=(lax.rem(k, teams) * 2 + core, me),
            device_id_type=MESH,
        )

    pieces = [(way, stage) for way in range(2) for stage in range(reach)]
    order = [(i + low) % number for i in range(number)] if high else list(range(number))
    for k in order:
        j = max(k - (number - kinds), 0)
        if k == 0 or k > number - kinds:
            load_x(j).start()
            pair_x(j).start()
        load_g(k).start()
        pair_g(k).start()

    def turn(k):
        return lax.rem(k + number - 1, number)

    def owner_at(stage, way):
        ahead = reach - stage
        return ring_device(place + ahead if way == 0 else place - ahead, count)

    def rows_of(owner):
        return pl.ds(pl.multiple_of(owner * depth, depth), depth)

    def quarter(q):
        return slice(q * wide, (q + 1) * wide)

    def hop(k, stage, way, start=False):
        if start:
            source = terms.at[k, rows_of(owner_at(0, way)), quarter(way)]
            target = held.at[k, way, 0, :, quarter(way)]
        else:
            source = held.at[k, way, stage - 1]
            target = held.at[k, way, stage]
        return pltpu.make_async_remote_copy(
            source,
            target,
            send_sem.at[stage, way, k],
            recv_sem.at[stage, way, k],
            device_id=sides[way],
            device_id_type=MESH,
        )

    def cross(k, d):
        return pltpu.make_async_remote_copy(
            across.at[team, k],
            across.at[team, k],
            cross_send.at[d, k],
            cross_recv.at[d, k],
            device_id=partners[d],
            device_id_type=MESH,
        )

    @pl.loop(0, number)
    def _(i):
        k = lax.rem(i + low, number)
        j = jnp.maximum(k - (number - kinds), 0)

        @pl.when((k == 0) | (k > number - kinds))
        def _():
            load_x(j).wait()
            pair_x(j).wait_recv()

        load_g(k).wait()
        pair_g(k).wait_recv()
        for r in range(0, width, 256):
            piece = slice(r, r + 256)
            terms[k, piece, :] = (
                mm(xv[j, 0, piece, :], gv[k, 0]) + mm(xv[j, 1, piece, :], gv[k, 1])
            ).astype(bf16)

        @pl.when(jnp.logical_not(alone(k)))
        def _():
            for way in range(2):
                hop(k, 0, way, True).start()

        @pl.when(jnp.logical_not(at_home(k)))
        def _():
            for way, stage in pieces:
                foreign(k, team, way, stage).start()

    def launch(k):
        @pl.when(at_home(k))
        def _():
            for way, stage in pieces:
                here = pl.ds((way * reach + stage) * depth, depth)
                total = terms[k, here, :].astype(f32)
                for d in range(1, teams):
                    sender = lax.rem(team + d, teams)
                    foreign(k, sender, way, stage).wait_recv()
                    slot = (k // teams) * teams + sender
                    total = total + held[slot, way, stage].astype(f32)
                terms[k, here, :] = total.astype(bf16)
            for way in range(2):
                hop(k, 0, way, True).start()

    for block in range(count):
        sender, direct = back_owner(block // sharers, jnp.int32(block % sharers))

        @pl.when(direct)
        def _():
            @pl.when(jnp.logical_not(owners.is_me(sender)))
            def _():
                for copy in back_from(block):
                    copy.wait_recv()

            for copy in back_hand(block):
                copy.start()

    def relay(k, stage):
        for way in range(2):
            here = rows_of(owner_at(stage, way))

            @pl.when(stage == 1)
            def _():
                hop(k, 0, way, True).wait_recv()
                both = terms[k, here, quarter(way)].astype(f32)
                both = both + held[k, way, 0, :, quarter(way)].astype(f32)
                held[k, way, 0, :, quarter(way)] = both.astype(bf16)
                held[k, way, 0, :, quarter(1 - way)] = terms[k, here, quarter(1 - way)]

            @pl.when(stage > 1)
            def _():
                hop(k, stage - 1, way).wait_recv()
                both = terms[k, here, :].astype(f32) + held[k, way, stage - 1].astype(f32)
                held[k, way, stage - 1] = both.astype(bf16)

            hop(k, stage, way).start()

    def finish(k):
        columns = pl.ds(pl.multiple_of(core * half, 128), half)
        return pltpu.make_async_copy(done.at[k], out_ref.at[k, :, columns], out_sem.at[k])

    def hand(k):
        columns = pl.ds(pl.multiple_of(core * half, 128), half)
        return pltpu.make_async_remote_copy(
            done.at[k],
            out_ref.at[k, :, columns],
            hand_send.at[k],
            hand_recv.at[k],
            device_id=other,
            device_id_type=MESH,
        )

    def settle(k):
        for way in range(2):
            hop(k, reach - 1, way, reach == 1).wait_recv()
        total = terms[k, rows_of(me), :].astype(f32)
        for way in range(2):
            total = total + held[k, way, reach - 1].astype(f32)
        across[team, k] = total.astype(bf16)
        for d in range(teams - 1):
            cross(k, d).start()

    span_k = 3 if number % 3 == 0 else number
    groups = number // span_k
    events = reach * number

    def cross_from(k, d):
        return pltpu.make_async_remote_copy(
            across.at[team, k],
            across.at[team, k],
            cross_send.at[0, k],
            cross_recv.at[d, k],
            device_id=partners[0] if teams > 1 else other,
            device_id_type=MESH,
        )

    def complete(k):
        @pl.when(jnp.logical_not(alone(k)))
        def _():
            for d in range(teams - 1):
                cross(k, d).wait_recv()
            total = across[0, k].astype(f32)
            for t in range(1, teams):
                total = total + across[t, k].astype(f32)
            done[k] = total

        @pl.when(alone(k))
        def _():
            home = lax.rem(k, teams)

            @pl.when(home != team)
            def _():
                cross_from(k, lax.rem(team + 2 * teams - home - 1, teams)).wait_recv()

            done[k] = across[home, k].astype(f32)

        finish(k).start()
        hand(k).start()

        @pl.when(k == number - 1)
        def _():
            rows_here = t_raw.shape[1]
            mine = done[number - 1, rows_here : rows_here + z_own.shape[0], :].astype(bf16)
            z_own[...] = mine
            z_out[core, me] = mine
            for d in range(count - 1):
                z_push(d).start()

    def event(e):
        block, k = e // span_k, lax.rem(e, span_k)
        block = jnp.where(block == 0, 0, block + 1)
        g, slot = block // reach, lax.rem(block, reach)
        settles = (slot == 1) | (g == groups)

        @pl.when(settles)
        def _():
            one = turn((g - 1) * span_k + k)

            @pl.when(at_home(one))
            def _():
                settle(one)

            @pl.when(g > 1)
            def _():
                complete(turn((g - 2) * span_k + k))

        @pl.when(jnp.logical_not(settles))
        def _():
            one = turn(g * span_k + k)

            @pl.when(at_home(one))
            def _():
                relay(one, jnp.maximum(slot, 1))

            if high:

                @pl.when((g == 0) & (slot == reach - 1) & (k == span_k - 1))
                def _():
                    launch(jnp.int32(low))

                @pl.when((g == 1) & (slot == 2))
                def _():
                    launch(low + 1 + k)

    tiles = images * steps
    paced = tiles
    middle = (paced + events) // 2
    t_acc[...] = jnp.zeros_like(t_acc)

    @pl.loop(0, tiles)
    def _(t):
        image = lax.rem(t // steps + owners.image, images)
        step = lax.rem(t, steps)
        e = t

        @pl.when(t + 1 > e)
        def _():
            event(e)

        @pl.when(step == 0)
        def _():
            for h in range(sharers):
                source = image * sharers + h

                _, direct = back_owner(image, jnp.int32(h))

                @pl.when(jnp.logical_not(direct))
                def _():
                    for copy in back_from(source):
                        copy.wait_recv()

                here = slice(h * rows, (h + 1) * rows)
                wide = jnp.dot(
                    gained_ref[:, : back_ref.shape[0]],
                    back_all[source].astype(f32),
                    precision=lax.Precision.HIGHEST,
                    preferred_element_type=f32,
                )
                bt[:, here] = wide.astype(bf16)
                b_low[here, :] = wide.T.astype(bf16)
                stat[:, here] = row_all[source]

        span = pl.ds(pl.multiple_of(step * tile, 128), tile)
        values = v_ref[image, :, span]
        x, xt = build_both(values, step * lines, code_ref)
        halves = (slice(0, tile // 2), slice(tile // 2, tile))
        products = [(mm(x[half], at_ref[...]), mm(x[half], bt[...])) for half in halves]
        kept, ends = [], []
        for half, (scores, grad_p) in zip(halves, products):
            probs = jnp.exp2(scores - stat[0:1, :])
            grad_s = (probs * (grad_p - stat[1:2, :])).astype(bf16)
            kept.append(grad_s)
            back = mm(grad_s, a_ref[...]) + mm(probs.astype(bf16), b_low[...])
            along = jnp.sum(back * x[half].astype(f32), axis=1, keepdims=True)
            end = back[:, CHANNELS - 128 :]
            lane = lax.broadcasted_iota(jnp.int32, end.shape, 1)
            ends.append(jnp.where(lane == 120, along, end))
        t_acc[...] += mm(xt, jnp.concatenate(kept, axis=0))
        ends = jnp.concatenate(ends, axis=0).T[120:128, :] * (values[0:1, :] * values[1:2, :])
        hat = values[4:7, :] + values[7:8, :]
        mean_part = ends[7:8, :] + hat * ends[0:1, :]
        pixel_ref[image, :, span] = ends[4:7, :] - mean_part * (1.0 / channels)

    t_sum = lax.dot_general(
        t_acc[:CHANNELS, :],
        table_ref[:, : t_raw.shape[2]],
        (((0,), (0,)), ((), ())),
        precision=lax.Precision.HIGHEST,
        preferred_element_type=f32,
    )
    t_raw[...] = t_sum.astype(bf16).reshape(t_raw.shape)
    for d in range(count - 1):
        for copy in scatter(d):
            copy.start()

    pl.loop(paced, middle)(event)
    t_sum, g_sum = t_raw[me].astype(f32), g_raw[me]
    for d in range(count - 1):
        for copy in scatter(d):
            copy.wait_recv()
        t_sum = t_sum + t_in[d].astype(f32)
        g_sum = g_sum + g_in[d]
    t_img[group] = t_sum.astype(bf16)
    g_img[group] = g_sum
    for d in range(crowd - 1):
        for copy in over(d):
            copy.start()

    pl.loop(middle, events)(event)

    @pl.loop((groups - 1) * span_k, number)
    def _(k):
        complete(turn(k))

    for d in range(crowd - 1):
        for copy in over(d):
            copy.wait_recv()
    t_sum, g_sum = t_img[0].astype(f32), g_img[0]
    for i in range(1, crowd):
        t_sum = t_sum + t_img[i].astype(f32)
        g_sum = g_sum + g_img[i]
    t_out[me] = t_sum.astype(bf16)
    g_out[me] = g_sum
    for d in range(count - 1):
        for copy in gather(d):
            copy.start()
    for d in range(count - 1):
        z_push(d).wait()
    z_hand().start()
    for d in range(count - 1):
        for copy in gather(d):
            copy.wait()
        for copy in scatter(d):
            copy.wait_send()
    for d in range(crowd - 1):
        for copy in over(d):
            copy.wait_send()
    z_hand().wait()

    @pl.loop(0, number)
    def _(k):
        finish(k).wait()
        hand(k).wait()
        pair_g(k).wait_send()

        @pl.when(at_home(k))
        def _():
            for way in range(2):
                for stage in range(reach):
                    hop(k, stage, way, stage == 0).wait_send()
            for d in range(teams - 1):
                cross(k, d).wait_send()

        @pl.when(jnp.logical_not(at_home(k)))
        def _():
            for way, stage in pieces:
                foreign(k, team, way, stage).wait_send()

    @pl.loop(0, kinds)
    def _(j):
        pair_x(j).wait_send()

    for d in range(count // 2):
        to, copies = back_push(d)

        @pl.when(jnp.logical_not(owners.is_me(to)))
        def _():
            for copy in copies:
                copy.wait_send()

    for block in range(count):
        _, direct = back_owner(block // sharers, jnp.int32(block % sharers))

        @pl.when(direct)
        def _():
            for copy in back_hand(block):
                copy.wait_send()


def backward_pass(
    values, table, gained, at, a, back, rows_in, gains, xs, gs, channels, collective_id
):
    count = lax.axis_size("pix")
    teams = lax.axis_size("img") // 2
    kinds, _, rows = xs.shape
    number, _, width = gs.shape
    depth = xs.shape[1] // count
    anywhere = pl.BlockSpec(memory_space=pl.ANY)
    inside = pl.BlockSpec(memory_space=pltpu.VMEM)
    chunk = (depth, width // 2)
    images, _, pixels = values.shape
    tile = pixel_tile(pixels)
    latents = at.shape[1]
    tall = back.shape[0]
    shape = jax.ShapeDtypeStruct
    rows_here = latents // count
    t_shape = shape((count, rows_here, -(-channels // 128) * 128), bf16)
    g_shape = shape((count, 8, depth), f32)
    spare = min(-(-share_rows(channels, count) // 16) * 16, depth - rows_here)
    return pl.pallas_call(
        functools.partial(backward_kernel, count, teams, images, tile, channels),
        out_shape=[
            t_shape,
            g_shape,
            shape((2, count, spare, width // 2), bf16),
            shape((images, 3, pixels), f32),
            shape((number, depth, width), f32),
        ],
        in_specs=[inside] * 9 + [anywhere] * 2,
        out_specs=[inside] * 4 + [anywhere],
        scratch_shapes=[
            pltpu.VMEM(t_shape.shape, bf16),
            pltpu.VMEM((count - 1,) + t_shape.shape[1:], bf16),
            pltpu.VMEM((2 * teams,) + t_shape.shape[1:], bf16),
            pltpu.VMEM(g_shape.shape, f32),
            pltpu.VMEM((count - 1,) + g_shape.shape[1:], f32),
            pltpu.VMEM((2 * teams,) + g_shape.shape[1:], f32),
            pltpu.VMEM((spare, width // 2), bf16),
            pltpu.VMEM((CHANNELS + 16, latents), f32),
            pltpu.VMEM((CHANNELS, latents), bf16),
            pltpu.VMEM((latents, CHANNELS), bf16),
            pltpu.VMEM((8, latents), f32),
            pltpu.VMEM((count, tall, rows), bf16),
            pltpu.VMEM((count, 8, rows), f32),
            pltpu.VMEM((kinds, 2, xs.shape[1], rows), bf16),
            pltpu.VMEM((number, 2, rows, width // 2), bf16),
            pltpu.VMEM((number, xs.shape[1], width // 2), bf16),
            pltpu.VMEM((number, 2, count // 2) + chunk, bf16),
            pltpu.VMEM((teams, number) + chunk, bf16),
            pltpu.VMEM((number, depth, width // 2), f32),
            DMA((2, number)),
            DMA((2, number)),
            DMA((2, number)),
            DMA((count // 2, 2, number)),
            DMA((count // 2, 2, number)),
            DMA((teams - 1, number)),
            DMA((teams - 1, number)),
            DMA((number,)),
            DMA((number,)),
            DMA((number,)),
            DMA((2, count)),
            DMA((2, count)),
            DMA((2, count)),
            DMA((2, count // 2, number)),
            DMA((teams, 2, count // 2, number)),
            DMA((2, count - 1)),
            DMA((2, count - 1)),
            DMA((2, 2 * teams - 1)),
            DMA((2, 2 * teams - 1)),
            DMA((2, count - 1)),
            DMA((2, count - 1)),
            DMA((count - 1,)),
            DMA((count - 1,)),
            DMA,
            DMA,
        ],
        compiler_params=pltpu.CompilerParams(
            collective_id=collective_id, has_side_effects=True, vmem_limit_bytes=60 * 2**20
        ),
    )(values, hot_codes(tile), table, gained, at, a, back, rows_in, gains, xs, gs)


def peers(count):
    group, me = lax.axis_index("img"), lax.axis_index("pix")
    return [(group, lax.rem(me + d, count)) for d in range(1, count)]


def plane(count):
    group, me = lax.axis_index("img"), lax.axis_index("pix")
    other = group + 1 - 2 * lax.rem(group, 2)
    return peers(count) + [(other, lax.rem(me + d, count)) for d in range(count)]


class Owners:
    def __init__(self, count, images):
        self.group, self.me = lax.axis_index("img"), lax.axis_index("pix")
        self.core = lax.rem(self.group, 2)
        self.base = self.group - self.core
        self.images = images
        self.chips = count // (2 * images)
        self.sharers = 2 * self.chips
        self.slot = lax.rem(self.me, self.chips) * 2 + self.core
        image = self.me // self.chips
        self.image = lax.rem(image, images)
        self.home = self.base + image // images

    def device(self, group, image, slot):
        core = lax.rem(group, 2)
        chip = (core * self.images + image) * self.chips + slot // 2
        return self.base + lax.rem(slot, 2), chip

    def is_me(self, device):
        return (device[0] == self.group) & (device[1] == self.me)


def share_rows(channels, count):
    channels = -(-channels // 16) * 16
    return -(-(-(-channels // count)) // 8) * 8


def gelu_parts(z):
    slope = (2.0 / jnp.pi) ** 0.5
    square = z * z
    bend = jnp.tanh(slope * z * (1.0 + 0.044715 * square))
    half = 0.5 * (1.0 + bend)
    return z * half, half + 0.5 * z * (1.0 - bend * bend) * slope * (1.0 + 0.134145 * square)


def latent_kernel(
    count,
    images,
    part_ref,
    stat_ref,
    own_ref,
    cot_ref,
    mix_ref,
    gain_ref,
    in_gain_ref,
    w_ref,
    late_up,
    late_down,
    out_ref,
    xs_ref,
    gs_ref,
    back_ref,
    row_ref,
    gain_out,
    wv,
    one,
    two,
    three,
    pre,
    grad,
    flow,
    low,
    heads_q,
    kv,
    probs,
    kv_out,
    kv_in,
    cot,
    final,
    mean,
    own_v,
    own_sem,
    w_sem,
    ring_own,
    ring_send,
    ring_recv,
    hand_send,
    hand_recv,
    kv_send,
    kv_recv,
    gkv_send,
    gkv_recv,
    cot_own,
    cot_send,
    cot_recv,
    out_own,
    out_send,
    out_recv,
):
    rows, width = one.shape
    depth = width // count
    owners = Owners(count, images)
    sharers = owners.sharers
    latents = rows * sharers
    per = count // sharers
    rows_here = latents // count
    spare = depth - rows_here
    group, me = lax.axis_index("img"), lax.axis_index("pix")
    slot, image, home = owners.slot, owners.image, owners.home
    block = 256
    blocks = width // block
    row_block = min(rows, 64)
    up_one, down_one, m_query, m_key, m_value, m_out, up_two, down_two = range(8)
    scale = HEAD_DIM ** (-0.5)

    def load(k):
        return pltpu.make_async_copy(w_ref.at[k], wv.at[k], w_sem.at[k])

    early, late_refs = w_ref.shape[0], (late_up, late_down)
    late = len(late_refs)
    own_copy = pltpu.make_async_copy(
        own_ref.at[pl.ds(pl.multiple_of(slot * rows, 16), rows)], own_v, own_sem
    )
    own_copy.start()
    for k in range(early):
        load(k).start()
    greet(plane(count))

    core = lax.rem(group, 2)
    ring = ring_place(count)
    sides = ((group, ring_device(ring + 1, count)), (group, ring_device(ring - 1, count)))
    other = (group + 1 - 2 * core, me)

    reach = count // 2

    def spot(k, stage, way, last, source=False):
        begin = (core * 2 + way) * (width // 4) if last else core * (width // 2)
        some = pl.ds(pl.multiple_of(begin, 128), width // 4 if last else width // 2)
        if source:
            return late_refs[k].at[:, some]
        origin = ring_device(ring - stage if way == 0 else ring + stage, count)
        here = pl.ds(pl.multiple_of(origin * depth, depth), depth)
        return wv.at[early + k, here, some]

    def hop(k, stage, way, start=False, last=False):
        return pltpu.make_async_remote_copy(
            spot(k, stage, way, last, start),
            spot(k, stage, way, last),
            ring_send.at[stage, way, k],
            ring_recv.at[stage, way, k],
            device_id=sides[way],
            device_id_type=MESH,
        )

    def hand(k, stage, way, last=False):
        return pltpu.make_async_remote_copy(
            spot(k, stage, way, last),
            spot(k, stage, way, last),
            hand_send.at[stage - 1, way, k],
            hand_recv.at[stage - 1, way, k],
            device_id=other,
            device_id_type=MESH,
        )

    def ring_keep(k):
        here = pl.ds(pl.multiple_of(me * depth, depth), depth)
        return pltpu.make_async_copy(late_refs[k], wv.at[early + k, here], ring_own.at[k])

    for k in range(late):
        for way in range(2):
            hop(k, 0, way, True, reach == 1).start()
        ring_keep(k).start()

    def relays(first, end):
        for stage in range(first, min(end, reach + 1)):
            for k in range(late):
                for way in range(2):
                    last = stage == reach
                    hop(k, stage - 1, way, last=last).wait_recv()
                    if stage < reach:
                        hop(k, stage, way, last=stage == reach - 1).start()
                    hand(k, stage, way, last).start()

    def arrived(k):
        ring_keep(k).wait()
        for stage in range(1, reach + 1):
            for way in range(2):
                hand(k, stage, way, stage == reach).wait_recv()

    def cot_push(i):
        to = owners.device(group, i, me // per)
        return to, pltpu.make_async_remote_copy(
            cot_ref.at[i],
            cot.at[lax.rem(me, per)],
            cot_send.at[i],
            cot_recv.at[lax.rem(me, per)],
            device_id=to,
            device_id_type=MESH,
        )

    def cot_keep():
        return pltpu.make_async_copy(cot_ref.at[image], cot.at[lax.rem(me, per)], cot_own)

    for i in range(images):
        to, copy = cot_push(i)

        @pl.when(jnp.logical_not(owners.is_me(to)))
        def _():
            copy.start()

        @pl.when(owners.is_me(to))
        def _():
            cot_keep().start()

    def columns(j, wide=block):
        return pl.ds(pl.multiple_of(j * wide, wide), wide)

    def over_columns(body, times=blocks):
        pl.loop(0, times)(body)

    def over_rows(body):
        @pl.loop(0, rows // row_block)
        def _(r):
            body(pl.ds(pl.multiple_of(r * row_block, 16), row_block))

    def put_x(j, c, value):
        xs_ref[j, columns(c), :] = value.T

    def centre(rows_f32):
        average = jnp.mean(rows_f32, axis=1, keepdims=True)
        centred = rows_f32 - average
        spread = jnp.mean(centred * centred, axis=1, keepdims=True)
        scale_rows = lax.rsqrt(spread + eps)
        return centred * scale_rows, scale_rows

    def norm(source, k, target):
        def body(r):
            target[r] = (centre(source[r])[0] * gain_ref[k : k + 1, :]).astype(bf16)

        over_rows(body)

    def norm_grad(source, k):
        def body(r):
            hat, scale_rows = centre(source[r])
            given = flow[r]
            gain_out[k : k + 1, :] += jnp.sum(given * hat, axis=0, keepdims=True)
            given = given * gain_ref[k : k + 1, :]
            along = jnp.mean(given * hat, axis=1, keepdims=True)
            grad[r] += scale_rows * (given - jnp.mean(given, axis=1, keepdims=True) - hat * along)

        over_rows(body)

    gain_out[...] = jnp.zeros_like(gain_out)

    top = jnp.max(stat_ref[:, 0:1, :], axis=0)
    total = jnp.zeros_like(top)
    for d in range(count):
        total = total + jnp.exp2(stat_ref[d, 0:1, :] - top) * stat_ref[d, 1:2, :]
    raw = jnp.zeros(part_ref.shape[1:], f32)
    for d in range(count):
        raw = raw + part_ref[d].astype(f32) * (jnp.exp2(stat_ref[d, 0:1, :] - top) / total)
    mean[0] = raw
    mean[1] = raw * in_gain_ref[...]
    row_ref[...] = jnp.zeros_like(row_ref)
    row_ref[0:1, :] = top + jnp.log(total) * LOG2E

    tall = count * spare
    mean_tall = mean[1]
    if tall > mean_tall.shape[0]:
        mean_tall = jnp.concatenate(
            [mean_tall, jnp.zeros((tall - mean_tall.shape[0], rows), f32)], axis=0
        )
    share = share_rows(mean.shape[1], count)
    place = lax.broadcasted_iota(jnp.int32, (rows_here, rows), 0)
    source_row = lax.broadcasted_iota(jnp.int32, (rows_here, rows), 1) + slot * rows
    for o in range(count):
        picks = jnp.where(place + o * rows_here == source_row, 1.0, 0.0)
        piece = [picks, mean_tall[o * share : (o + 1) * share]]
        if spare > share:
            piece.append(jnp.zeros((spare - share, rows), f32))
        xs_ref[6, o * depth : (o + 1) * depth, :] = jnp.concatenate(piece, axis=0).astype(bf16)

    mean_low = mean[1].astype(bf16)

    def make_one(j):
        one[:, columns(j)] = own_v[:, columns(j)].astype(f32) + mm_tn(
            mean_low,
            mix_ref[j // (blocks // 2), : mean.shape[1], columns(lax.rem(j, blocks // 2))],
        )

    own_copy.wait()
    over_columns(make_one)

    def ready(k):
        if k < early:
            load(k).wait()
        else:
            arrived(k - early)

    def feed(source, target, k, up, down, normed, x_hidden, keep):
        norm(source, k, normed)
        ready(up)

        def make_hidden(j):
            value = mm_nt(normed[...], wv[up, columns(j), :])
            pre[keep, :, columns(j)] = value
            hidden = gelu_parts(value)[0].astype(bf16)
            low[:, columns(j)] = hidden
            put_x(x_hidden, j, hidden)

        over_columns(make_hidden)
        ready(down)

        def make_branch(j):
            value = source[:, columns(j)] + mm(low[...], wv[down, :, columns(j)])
            target[:, columns(j)] = value.astype(target.dtype)

        over_columns(make_branch)

    def feed_back(source, k, up, down, branch, x_pre, keep):
        @over_columns
        def _(j):
            value = mm_nt(branch[...], wv[down, columns(j), :])
            value = (value * gelu_parts(pre[keep, :, columns(j)])[1]).astype(bf16)
            low[:, columns(j)] = value
            put_x(x_pre, j, value)

        @over_columns
        def _(j):
            flow[:, columns(j)] = mm(low[...], wv[up, :, columns(j)])

        norm_grad(source, k)

    feed(one, two, 0, up_one, down_one, gs_ref.at[4], 3, 0)
    relays(1, 2)

    norm(two, 1, low)

    load(m_key).wait()
    load(m_value).wait()

    def make_kv(j):
        put_x(0, j, low[:, columns(j)])
        kv[0, slot, :, columns(j)] = mm(low[...], wv[m_key, :, columns(j)]).astype(bf16)
        kv[1, slot, :, columns(j)] = mm(low[...], wv[m_value, :, columns(j)]).astype(bf16)

    over_columns(make_kv)

    def sharer(d):
        return owners.device(home, image, lax.rem(slot + d, sharers))

    def kv_push(d):
        return pltpu.make_async_remote_copy(
            kv.at[:, slot],
            kv.at[:, slot],
            kv_send.at[d - 1],
            kv_recv.at[d - 1],
            device_id=sharer(d),
            device_id_type=MESH,
        )

    for d in range(1, sharers):
        kv_push(d).start()
    load(m_query).wait()

    @over_columns
    def _(j):
        heads_q[:, columns(j)] = mm(low[...], wv[m_query, :, columns(j)]).astype(bf16)

    for d in range(1, sharers):
        kv_push(d).wait_recv()

    def attend(h):
        c = columns(h, HEAD_DIM)
        k_all = kv[0, :, :, c].reshape(latents, HEAD_DIM)
        v_all = kv[1, :, :, c].reshape(latents, HEAD_DIM)
        scores = mm_nt(heads_q[:, c], k_all) * scale
        shifted = jnp.exp(scores - jnp.max(scores, axis=1, keepdims=True))
        p = shifted / jnp.sum(shifted, axis=1, keepdims=True)
        probs[h] = p
        low[:, c] = mm(p.astype(bf16), v_all).astype(bf16)

    pl.loop(0, HEADS // 2)(attend)
    relays(2, 3)
    pl.loop(HEADS // 2, HEADS)(attend)
    relays(3, 4)

    @over_columns
    def _(j):
        put_x(1, j, low[:, columns(j)])

    ready(m_out)

    @over_columns
    def _(j):
        three[:, columns(j)] = two[:, columns(j)] + mm(low[...], wv[m_out, :, columns(j)])

    relays(4, reach + 1)
    feed(three, final, 2, up_two, down_two, gs_ref.at[6], 5, 1)

    def out_push(b):
        to = (home, slot * per + b)
        return to, pltpu.make_async_remote_copy(
            final.at[pl.ds(b * rows_here, rows_here)],
            out_ref.at[image],
            out_send.at[b],
            out_recv.at[image],
            device_id=to,
            device_id_type=MESH,
        )

    def out_keep():
        mine = pl.ds(pl.multiple_of(lax.rem(me, per) * rows_here, 16), rows_here)
        return pltpu.make_async_copy(final.at[mine], out_ref.at[image], out_own)

    for b in range(per):
        to, copy = out_push(b)

        @pl.when(jnp.logical_not(owners.is_me(to)))
        def _():
            copy.start()

        @pl.when(owners.is_me(to))
        def _():
            out_keep().start()

    def cot_from(b):
        return pltpu.make_async_remote_copy(
            cot_ref.at[0],
            cot.at[b],
            cot_send.at[0],
            cot_recv.at[b],
            device_id=(group, me),
            device_id_type=MESH,
        )

    for b in range(per):

        local = owners.is_me((home, slot * per + b))

        @pl.when(jnp.logical_not(local))
        def _():
            cot_from(b).wait_recv()

        @pl.when(local)
        def _():
            cot_keep().wait()

    given = cot[...].reshape(rows, width)
    gs_ref[7] = given
    grad[...] = given.astype(f32)
    feed_back(three, 2, up_two, down_two, gs_ref.at[7], 4, 1)

    gs_ref[3] = grad[...].astype(bf16)

    @over_columns
    def _(j):
        low[:, columns(j)] = mm_nt(gs_ref[3], wv[m_out, columns(j), :]).astype(bf16)

    @pl.loop(0, HEADS)
    def _(h):
        c = columns(h, HEAD_DIM)
        k_all = kv[0, :, :, c].reshape(latents, HEAD_DIM)
        v_all = kv[1, :, :, c].reshape(latents, HEAD_DIM)
        p = probs[h]
        g_mixed = low[:, c]
        g_p = mm_nt(g_mixed, v_all)
        g_v = mm_tn(p.astype(bf16), g_mixed)
        delta = jnp.sum(p * g_p, axis=1, keepdims=True)
        g_s = (p * (g_p - delta)).astype(bf16)
        gs_ref[0, :, c] = (mm(g_s, k_all) * scale).astype(bf16)
        g_k = mm_tn(g_s, heads_q[:, c]) * scale
        kv_out[:, 0, :, c] = g_k.reshape(sharers, rows, HEAD_DIM).astype(bf16)
        kv_out[:, 1, :, c] = g_v.reshape(sharers, rows, HEAD_DIM).astype(bf16)

    def gkv_push(d):
        to = lax.rem(slot + d, sharers)
        return pltpu.make_async_remote_copy(
            kv_out.at[to],
            kv_in.at[d - 1],
            gkv_send.at[d - 1],
            gkv_recv.at[d - 1],
            device_id=sharer(d),
            device_id_type=MESH,
        )

    for d in range(1, sharers):
        gkv_push(d).start()

    @over_columns
    def _(j):
        flow[:, columns(j)] = mm_nt(gs_ref[0], wv[m_query, columns(j), :])

    for d in range(1, sharers):
        gkv_push(d).wait_recv()
    for which in range(2):

        @over_columns
        def _(j):
            value = kv_out[slot, which, :, columns(j)].astype(f32)
            for d in range(1, sharers):
                value = value + kv_in[d - 1, which, :, columns(j)].astype(f32)
            gs_ref[1 + which, :, columns(j)] = value.astype(bf16)

    @over_columns
    def _(j):
        flow[:, columns(j)] += mm_nt(gs_ref[1], wv[m_key, columns(j), :]) + mm_nt(
            gs_ref[2], wv[m_value, columns(j), :]
        )

    norm_grad(two, 1)
    gs_ref[5] = grad[...].astype(bf16)
    feed_back(one, 0, up_one, down_one, gs_ref.at[5], 2, 0)
    gs_ref[8] = grad[...].astype(bf16)
    half = width // 2
    back = mm_nt(mix_ref[0, : mean.shape[1], :], gs_ref[8, :, :half])
    back = back + mm_nt(mix_ref[1, : mean.shape[1], :], gs_ref[8, :, half:])
    back_ref[...] = back.astype(bf16)
    row_ref[1:2, :] = jnp.sum(back * mean[1], axis=0, keepdims=True)
    in_gain = jnp.broadcast_to(
        jnp.sum(back * mean[0], axis=1, keepdims=True), (back.shape[0], 128)
    )
    gain_out[3:4, : back.shape[0]] = in_gain.T[0:1, :]

    for i in range(images):
        to, copy = cot_push(i)

        @pl.when(jnp.logical_not(owners.is_me(to)))
        def _():
            copy.wait_send()

    for d in range(1, sharers):
        kv_push(d).wait_send()
        gkv_push(d).wait_send()
    for k in range(late):
        for stage in range(reach):
            for way in range(2):
                last = stage == reach - 1
                hop(k, stage, way, stage == 0, last).wait_send()
                hand(k, stage + 1, way, last).wait_send()

    def out_from(i):
        return pltpu.make_async_remote_copy(
            final.at[pl.ds(0, rows_here)],
            out_ref.at[i],
            out_send.at[0],
            out_recv.at[i],
            device_id=(group, me),
            device_id_type=MESH,
        )

    for b in range(per):
        to, copy = out_push(b)

        @pl.when(jnp.logical_not(owners.is_me(to)))
        def _():
            copy.wait_send()

    for i in range(images):
        local = owners.is_me(owners.device(group, i, me // per))

        @pl.when(jnp.logical_not(local))
        def _():
            out_from(i).wait_recv()

        @pl.when(local)
        def _():
            out_keep().wait()


def latent_pass(parts, stats, own, cotangent, mix, gains, in_gain, whole, late, rows, collective_id):
    count = lax.axis_size("pix")
    images, rows_here, width = cotangent.shape
    channels = parts.shape[1]
    sharers = count // images
    per = count // sharers
    inside = pl.BlockSpec(memory_space=pltpu.VMEM)
    anywhere = pl.BlockSpec(memory_space=pl.ANY)
    whole_f32 = pltpu.VMEM((rows, width), f32)
    whole_low = pltpu.VMEM((rows, width), bf16)
    ring = DMA((count // 2, 2, len(late)))
    shape = jax.ShapeDtypeStruct
    return pl.pallas_call(
        functools.partial(latent_kernel, count, images),
        out_shape=[
            shape((images, rows_here, width), bf16),
            shape((7, width, rows), bf16),
            shape((9, rows, width), bf16),
            shape((channels, rows), bf16),
            shape((8, rows), f32),
            shape((8, width), f32),
        ],
        in_specs=[inside] * 2 + [anywhere] * 2 + [inside] * 3 + [anywhere] * 3,
        out_specs=[anywhere] + [inside] * 5,
        scratch_shapes=[
            pltpu.VMEM((8, width, width), bf16),
            whole_f32,
            whole_f32,
            whole_f32,
            pltpu.VMEM((2, rows, width), f32),
            whole_f32,
            whole_f32,
            whole_low,
            whole_low,
            pltpu.VMEM((2, sharers, rows, width), bf16),
            pltpu.VMEM((HEADS, rows, rows * sharers), f32),
            pltpu.VMEM((sharers, 2, rows, width), bf16),
            pltpu.VMEM((max(sharers - 1, 1), 2, rows, width), bf16),
            pltpu.VMEM((per, rows_here, width), bf16),
            whole_low,
            pltpu.VMEM((2, channels, rows), f32),
            whole_low,
            DMA,
            DMA((whole.shape[0],)),
            DMA((len(late),)),
            ring,
            ring,
            ring,
            ring,
            DMA((sharers,)),
            DMA((sharers,)),
            DMA((sharers,)),
            DMA((sharers,)),
            DMA,
            DMA((images,)),
            DMA((per,)),
            DMA,
            DMA((per,)),
            DMA((images,)),
        ],
        compiler_params=pltpu.CompilerParams(
            collective_id=collective_id, has_side_effects=True, vmem_limit_bytes=60 * 2**20
        ),
    )(parts, stats, own, cotangent, mix, gains, in_gain, whole, *late)


def tail_kernel(
    count,
    channels,
    t_ref,
    g_ref,
    z_ref,
    a_ref,
    lat_ref,
    qcols_ref,
    ncols_ref,
    wq_ref,
    wk_ref,
    wv_ref,
    wco_ref,
    gain_ref,
    lat_gain_ref,
    sum_ref,
    lat_out,
    lat_gain_out,
    gains_out,
    wq_out,
    wk_out,
    wv_out,
    wco_out,
    up_one_out,
    up_two_out,
    down_one_out,
    down_two_out,
    sq_out,
    sk_out,
    sv_out,
    so_out,
    z_v,
    query_grad,
    flow,
):
    me = lax.axis_index("pix")
    width = wq_ref.shape[0]
    depth = wco_ref.shape[0]
    rows_here = lat_out.shape[0]
    latents = lat_ref.shape[0]
    across = t_ref.shape[1]
    for k, to in (
        (0, sq_out),
        (1, sk_out),
        (2, sv_out),
        (3, so_out),
        (5, down_one_out),
        (7, down_two_out),
    ):
        to[...] = sum_ref[k]
    t = t_ref[...].astype(f32)
    tx = (t * (gain_ref[...] * width ** (-0.5))).astype(bf16)
    for o in range(count):
        gains_out[:, o * depth : (o + 1) * depth] = g_ref[o]
    row = jnp.sum(a_ref[:, :across] * t, axis=0, keepdims=True)
    gains_out[3:4, :across] += row
    wk_out[...] = mm_tn(tx, qcols_ref[...])[:channels]

    @pl.loop(0, width // 256)
    def _(j):
        columns = pl.ds(pl.multiple_of(j * 256, 256), 256)
        query_grad[:, columns] = mm_nt(tx, wk_ref[columns, :across]).astype(bf16)

    @pl.loop(0, width // 256)
    def _(j):
        columns = pl.ds(pl.multiple_of(j * 256, 256), 256)
        wq_out[:, columns] = mm_tn(ncols_ref[...], query_grad[:, columns])
        flow[:, columns] = mm_nt(query_grad[...], wq_ref[columns, :])

    share = share_rows(channels, count)
    half = width // 2
    for o in range(count):
        for h in range(2):
            z_v[o * share : (o + 1) * share, h * half : (h + 1) * half] = z_ref[h, o, :share].astype(f32)
    cross = z_v[...].astype(bf16)
    wv_out[...] = mm_nt(cross, wco_ref[...])[:channels]
    wco_out[...] = mm_tn(wv_ref[...], cross)

    up_one_out[...] = sum_ref[4].T
    up_two_out[...] = sum_ref[6].T
    lat_gain_out[...] = jnp.zeros_like(lat_gain_out)

    @pl.loop(0, count)
    def _(o):
        here = pl.ds(pl.multiple_of(o * rows_here, rows_here), rows_here)
        rows = lat_ref[here, :].astype(f32)
        average = jnp.mean(rows, axis=1, keepdims=True)
        centred = rows - average
        scale = lax.rsqrt(jnp.mean(centred * centred, axis=1, keepdims=True) + eps)
        hat = centred * scale
        given = flow[here, :]
        lat_gain_out[...] += jnp.sum(given * hat, axis=0, keepdims=True)

        @pl.when(o == me)
        def _():
            gained = given * lat_gain_ref[...]
            along = jnp.mean(gained * hat, axis=1, keepdims=True)
            moved = scale * (gained - jnp.mean(gained, axis=1, keepdims=True) - hat * along)
            lat_out[...] = moved + sum_ref[8, :rows_here, :]


def tail_pass(t, g, z, a, lat, qcols, ncols, wq, wk, wv, wco, gain, lat_gain, summed, channels):
    count = z.shape[1]
    _, depth, width = summed.shape
    latents = lat.shape[0]
    share = share_rows(channels, count)
    inside = pl.BlockSpec(memory_space=pltpu.VMEM)
    anywhere = pl.BlockSpec(memory_space=pl.ANY)
    shape = lambda *dims: jax.ShapeDtypeStruct(dims, f32)
    plain = shape(depth, width)
    return pl.pallas_call(
        functools.partial(tail_kernel, count, channels),
        out_shape=[
            shape(latents // count, width),
            shape(1, width),
            shape(8, width),
            plain,
            shape(channels, depth),
            shape(channels, depth),
            plain,
            shape(width, depth),
            shape(width, depth),
        ]
        + [plain] * 6,
        in_specs=[inside] * 14,
        out_specs=[inside] * 15,
        scratch_shapes=[
            pltpu.VMEM((count * share, width), f32),
            pltpu.VMEM((latents, width), bf16),
            pltpu.VMEM((latents, width), f32),
        ],
        compiler_params=pltpu.CompilerParams(vmem_limit_bytes=48 * 2**20),
    )(t, g, z, a, lat, qcols, ncols, wq, wk, wv, wco, gain, lat_gain, summed)


def local(
    rgb_pixels,
    keep_mask,
    latent_array,
    gain_input,
    gain_latent,
    w_query,
    w_key,
    w_value,
    w_cross_out,
    gain_mlp_one,
    w_up_one,
    w_down_one,
    gain_self,
    w_self_query,
    w_self_key,
    w_self_value,
    w_self_out,
    gain_mlp_two,
    w_up_two,
    w_down_two,
    cotangent,
):
    images, _, pixels = rgb_pixels.shape
    rows_here, width = latent_array.shape
    count = lax.axis_size("pix")
    me = lax.axis_index("pix")
    latents = rows_here * count
    sharers = count // images
    rows_own = latents // sharers
    depth = w_query.shape[0]
    channels = gain_input.shape[0]
    tall = -(-channels // 16) * 16

    side = -(-channels // 512) * 512
    key_t = jnp.pad(w_key.T, ((0, 0), (0, side - channels)))
    blocks = -(-tall // (16 * count)) * 16 * count
    value_pad = jnp.pad(w_value, ((0, blocks - channels), (0, 0)))
    shards = [w_up_one.T, w_down_one, w_self_query, w_self_key, w_self_value, w_self_out]
    late = [w_up_two.T, w_down_two]

    lines = pixels // SIDE
    u, sin_u, cos_u = angles(me * lines + lax.iota(jnp.int32, lines))
    w, sin_w, cos_w = angles(lax.iota(jnp.int32, SIDE))

    def zeros(rows, columns):
        return jnp.zeros((rows, columns), f32)

    pad = CHANNELS - 4 - SIDE - lines
    table = jnp.concatenate(
        [
            jnp.concatenate(
                [zeros(SIDE, 4), w, zeros(SIDE, BANDS), sin_w, zeros(SIDE, BANDS), cos_w], axis=1
            ),
            jnp.concatenate(
                [zeros(lines, 3), u, zeros(lines, 1), sin_u, zeros(lines, BANDS), cos_u, zeros(lines, BANDS)],
                axis=1,
            ),
            zeros(pad, channels),
            jnp.eye(3, channels, dtype=f32),
            jnp.ones((1, channels), f32),
        ],
        axis=0,
    )
    row_sum = u[:, 0] + jnp.sum(sin_u + cos_u, axis=1)
    col_sum = w[:, 0] + jnp.sum(sin_w + cos_w, axis=1)
    row_square = u[:, 0] ** 2 + jnp.sum(sin_u**2 + cos_u**2, axis=1)
    col_square = w[:, 0] ** 2 + jnp.sum(sin_w**2 + cos_w**2, axis=1)
    feature_sum = (row_sum[:, None] + col_sum[None, :]).reshape(1, pixels)
    feature_square = (row_square[:, None] + col_square[None, :]).reshape(1, pixels)
    colours = rgb_pixels.astype(f32)
    average = (jnp.sum(colours, axis=1) + feature_sum) / channels
    spread = (jnp.sum(colours**2, axis=1) + feature_square) / channels - average**2
    scale = lax.rsqrt(spread + eps)
    keep = keep_mask.astype(f32)

    own_values = jnp.concatenate([colours, -average[:, None, :]], axis=1) * scale[:, None, :]
    values = jnp.concatenate(
        [scale[:, None], keep[:, None], jnp.zeros((images, 2, pixels), f32), own_values], axis=1
    )
    table = jnp.pad(table, ((0, 0), (0, side - channels)))
    gained = table * jnp.pad(gain_input, (0, side - channels))[None, :]
    (
        latent_full,
        query_mat,
        key_full,
        whole,
        latent_normed,
        queries,
        score_mat,
        at,
        a_low,
        value_out,
        raw_parts,
        stat_parts,
    ) = forward_pass(
        values,
        table,
        gained,
        gain_latent,
        latent_array,
        w_query,
        key_t,
        value_pad,
        w_cross_out,
        shards,
        tall,
        0,
    )
    latent_full = latent_full.reshape(latents, width)
    whole = whole.reshape(-1, width, width)

    latent_out, xs, gs, back_t, row_stats, gain_grads = latent_pass(
        raw_parts,
        stat_parts,
        latent_full,
        cotangent,
        value_out.reshape(2, blocks, width // 2),
        jnp.stack([gain_mlp_one, gain_self, gain_mlp_two]),
        jnp.pad(gain_input, (0, tall - channels))[:, None],
        whole,
        late,
        rows_own,
        4,
    )
    across = -(-channels // 128) * 128
    grad_raw, gain_sums, cross_sum, grad_pixels, summed = backward_pass(
        values,
        table,
        gained,
        at,
        a_low,
        back_t,
        row_stats,
        gain_grads,
        xs,
        gs,
        channels,
        2,
    )

    share = share_rows(channels, count)
    (
        grad_latent_array,
        gain_latent_sum,
        gain_sums,
        grad_w_query,
        grad_w_key,
        grad_w_value,
        grad_w_cross_out,
        g_up_one,
        g_up_two,
        g_down_one,
        g_down_two,
        g_sq,
        g_sk,
        g_sv,
        g_so,
    ) = tail_pass(
        grad_raw.reshape(latents, across),
        gain_sums,
        cross_sum,
        score_mat,
        latent_full,
        lax.dynamic_slice_in_dim(queries, me * depth, depth, 1),
        lax.dynamic_slice_in_dim(latent_normed, me * depth, depth, 1),
        query_mat.reshape(width, width),
        key_full.reshape(width, side),
        jnp.pad(w_value, ((0, share * count - channels), (0, 0))),
        w_cross_out,
        jnp.pad(gain_input, (0, across - channels))[None],
        gain_latent[None],
        summed,
        channels,
    )
    gain_one, gain_attn, gain_two = gain_sums[0], gain_sums[1], gain_sums[2]
    gain_in = gain_sums[3, :channels]
    grad_gain_latent = gain_latent_sum[0]
    return (
        latent_out,
        grad_pixels,
        grad_latent_array,
        gain_in,
        grad_gain_latent,
        grad_w_query,
        grad_w_key,
        grad_w_value,
        grad_w_cross_out,
        gain_one,
        g_up_one,
        g_down_one,
        gain_attn,
        g_sq,
        g_sk,
        g_sv,
        g_so,
        gain_two,
        g_up_two,
        g_down_two,
    )


def solution(mesh):
    rows, columns, copied = P("pix", None), P(None, "pix"), P()
    return jax.shard_map(
        local,
        mesh=mesh,
        in_specs=(
            P("img", None, "pix"),
            P("img", "pix"),
            rows,
            copied,
            copied,
            rows,
            columns,
            columns,
            rows,
            copied,
            columns,
            rows,
            copied,
            rows,
            rows,
            rows,
            rows,
            copied,
            columns,
            rows,
            P("img", "pix", None),
        ),
        out_specs=(
            P("img", "pix", None),
            P("img", None, "pix"),
            rows,
            copied,
            copied,
            rows,
            columns,
            columns,
            rows,
            copied,
            columns,
            rows,
            copied,
            rows,
            rows,
            rows,
            rows,
            copied,
            columns,
            rows,
        ),
        check_vma=False,
    )
```

```python
import functools

import jax
import jax.numpy as jnp
from jax import lax
from jax.experimental import pallas as pl
from jax.experimental.pallas import tpu as pltpu
from jax.sharding import PartitionSpec as P

HEADS = 8
HEAD_DIM = 128
BANDS = 64
SIDE = 224
CHANNELS = 256
LOG2E = 1.4426950408889634

eps = 1e-05
f32 = jnp.float32
bf16 = jnp.bfloat16


def exact(left, right):
    return jnp.dot(left, right, precision=lax.Precision.HIGHEST, preferred_element_type=f32)


def mm(left, right):
    return jnp.dot(left, right, preferred_element_type=f32)


def mm_nt(left, right):
    return lax.dot_general(left, right, (((1,), (1,)), ((), ())), preferred_element_type=f32)


def mm_tn(left, right):
    return lax.dot_general(left, right, (((0,), (0,)), ((), ())), preferred_element_type=f32)


def angles(index):
    place = index.astype(f32) * (2.0 / (SIDE - 1)) - 1.0
    steps = lax.iota(jnp.int32, BANDS).astype(f32)
    frequency = 1.0 + steps * ((SIDE / 2.0 - 1.0) / (BANDS - 1))
    angle = jnp.pi * place[:, None] * frequency[None, :]
    return place[:, None], jnp.sin(angle), jnp.cos(angle)


def pixel_tile(pixels):
    return 896 if pixels % 896 == 0 else pixels


MESH = pl.DeviceIdType.MESH
DMA = pltpu.SemaphoreType.DMA


def ring_place(count):
    me = lax.axis_index("pix")
    return jnp.where(me % 2 == 0, me // 2, count - 1 - me // 2)


def ring_device(place, count):
    place = lax.rem(place + 2 * count, count)
    return jnp.where(place < count // 2, 2 * place, 2 * (count - 1 - place) + 1)


def greet(devices):
    barrier = pltpu.get_barrier_semaphore()
    for device in devices:
        pl.semaphore_signal(barrier, inc=1, device_id=device, device_id_type=MESH)
    pl.semaphore_wait(barrier, len(devices))


def hot_codes(tile):
    pixel = lax.broadcasted_iota(jnp.int32, (CHANNELS, tile), 1)
    channel = lax.broadcasted_iota(jnp.int32, (CHANNELS, tile), 0)
    start = channel - SIDE - pixel // SIDE
    code = jnp.where((start >= 0) & (channel < CHANNELS - 4), start, -2)
    return jnp.where(channel < SIDE, jnp.where(channel == pixel % SIDE, -1, -2), code)


def build_xt(values, base, code_ref):
    code = code_ref[...]
    hot = jnp.where((code == -1) | (code == base), values[0:1, :], 0.0)
    last = hot[CHANNELS - 8 :, :]
    k = lax.broadcasted_iota(jnp.int32, last.shape, 0)
    last = jnp.where(k >= 4, values, last)
    return jnp.concatenate([hot[: CHANNELS - 8, :], last], axis=0)


def build_both(values, base, code_ref):
    keep = values[1:2, :]
    xt = build_xt(values, base, code_ref).astype(bf16)
    k = lax.broadcasted_iota(jnp.int32, (16, values.shape[1]), 0)
    ones = jnp.where(k == 0, keep, 0.0).astype(bf16)
    return xt.T, jnp.concatenate([xt * keep.astype(bf16), ones], axis=0)


def forward_kernel(
    count,
    teams,
    images,
    tile,
    mats,
    v_ref,
    code_ref,
    table_ref,
    gained_ref,
    gain_ref,
    lat_ref,
    wq_ref,
    wk_ref,
    wv_ref,
    wco_ref,
    *refs,
):
    shards = refs[:mats]
    forward_body(
        count,
        teams,
        images,
        tile,
        v_ref,
        code_ref,
        table_ref,
        gained_ref,
        gain_ref,
        lat_ref,
        wq_ref,
        wk_ref,
        wv_ref,
        wco_ref,
        shards,
        *refs[mats:],
    )


def forward_body(
    count,
    teams,
    images,
    tile,
    v_ref,
    code_ref,
    table_ref,
    gained_ref,
    gain_ref,
    lat_ref,
    wq_ref,
    wk_ref,
    wv_ref,
    wco_ref,
    shards,
    lat_full,
    wq_full,
    wk_full,
    w_full,
    normed_ref,
    query_ref,
    a_ref,
    at_ref,
    alow_ref,
    mix_ref,
    part_ref,
    stat_ref,
    mix_raw,
    mix_in,
    acc,
    top,
    u_send,
    s_send,
    own_sem,
    send_sem,
    recv_sem,
    hand_send,
    hand_recv,
    mix_send,
    mix_recv,
    mix_hand,
    x_send,
    x_recv,
    u_own,
    u_out,
    u_in,
):
    pixels = v_ref.shape[2]
    steps = pixels // tile
    lines = tile // SIDE
    owners = Owners(count, images)
    sharers = owners.sharers
    rows = part_ref.shape[2]
    width = wq_ref.shape[1]
    latents = normed_ref.shape[0]
    group, me = lax.axis_index("img"), lax.axis_index("pix")
    core = lax.rem(group, 2)
    place = ring_place(count)
    sides = ((group, ring_device(place + 1, count)), (group, ring_device(place - 1, count)))
    other = (group + 1 - 2 * core, me)
    team = group // 2
    partners = [(lax.rem(team + d, teams) * 2 + core, me) for d in range(1, teams)]
    greet(plane(count) + partners)
    sources = (lat_ref, wq_ref, wk_ref)
    fulls = (lat_full, wq_full, wk_full, w_full)
    mats = len(shards)

    reach = count // 2

    def spot(a, k, stage, way, last, source=False):
        wide = fulls[a].shape[3] // 4
        begin = (core * 2 + way) * wide if last else core * 2 * wide
        columns = pl.ds(pl.multiple_of(begin, 128), wide if last else 2 * wide)
        if source:
            return (sources[a] if a < 3 else shards[k]).at[:, columns]
        origin = ring_device(place - stage if way == 0 else place + stage, count)
        return fulls[a].at[k, origin, :, columns]

    def hop(a, k, stage, way, first=False, last=False):
        return pltpu.make_async_remote_copy(
            spot(a, k, stage, way, last, first),
            spot(a, k, stage, way, last),
            send_sem.at[stage, way, a + k],
            recv_sem.at[stage, way, a + k],
            device_id=sides[way],
            device_id_type=MESH,
        )

    def hand(a, k, stage, way, last=False):
        part = spot(a, k, stage, way, last)
        return pltpu.make_async_remote_copy(
            part,
            part,
            hand_send.at[stage - 1, way, a + k],
            hand_recv.at[stage - 1, way, a + k],
            device_id=other,
            device_id_type=MESH,
        )

    def relay(a, k, stage):
        for way in range(2):
            hop(a, k, stage - 1, way).wait_recv()

            @pl.when(stage == reach - 1)
            def _():
                hop(a, k, stage, way, last=True).start()

            @pl.when(stage != reach - 1)
            def _():
                hop(a, k, stage, way).start()

            hand(a, k, stage, way).start()

    def relay_end(a, k):
        for way in range(2):
            hop(a, k, reach - 1, way, last=True).wait_recv()
            hand(a, k, reach, way, last=True).start()

    def start_ring(a, k):
        for way in range(2):
            hop(a, k, 0, way, True, reach == 1).start()

    alone = 1

    def at_home(k):
        return (k < alone) | (lax.rem(jnp.int32(k), teams) == team)

    def over_x(k, stage, way, d, last=False):
        part = spot(3, k, stage, way, last)
        return pltpu.make_async_remote_copy(
            part,
            part,
            x_send.at[d, stage - 1, way, k],
            x_recv.at[stage - 1, way, k],
            device_id=partners[d],
            device_id_type=MESH,
        )

    def pass_x(k, stage, last=False):
        @pl.when(k >= alone)
        def _():
            for way in range(2):
                for d in range(teams - 1):
                    over_x(k, stage, way, d, last).start()

    def take_x(k, stage, last=False):
        for way in range(2):
            over_x(k, stage, way, 0, last).wait_recv()
            hand(3, k, stage, way, last).start()

    def relay_weight(k, stage):
        home = at_home(k)

        @pl.when(home)
        def _():
            relay(3, k, stage)
            pass_x(k, stage)

        @pl.when(jnp.logical_not(home) & (stage > 1))
        def _():
            take_x(k, stage - 1)

    def relay_weight_end(k):
        home = at_home(k)

        @pl.when(home)
        def _():
            relay_end(3, k)
            pass_x(k, reach, True)

        @pl.when(jnp.logical_not(home))
        def _():
            take_x(k, reach - 1)

    def sent(a, k):
        for way in range(2):
            for stage in range(reach):
                last = stage == reach - 1
                hop(a, k, stage, way, stage == 0, last).wait_send()
                hand(a, k, stage + 1, way, last).wait_send()

    def handed(a, k):
        for way in range(2):
            for stage in range(1, reach + 1):
                hand(a, k, stage, way, stage == reach).wait_recv()

    own = [
        pltpu.make_async_copy(shards[k], fulls[3].at[k, me], own_sem.at[k]) for k in range(mats)
    ]
    for a in range(3):
        start_ring(a, 0)
    others = peers(count)
    used = -(-part_ref.shape[1] // mix_raw.shape[1])

    def mix_copy(source, target, stage, index, device):
        return pltpu.make_async_remote_copy(
            source,
            target,
            mix_send.at[stage, index],
            mix_recv.at[stage, index],
            device_id=device,
            device_id_type=MESH,
        )

    def mix_scatter(d):
        return mix_copy(mix_raw.at[others[d][1]], mix_in.at[d], 0, d, others[d])

    def mix_gather(d):
        return mix_copy(mix_ref.at[core, me], mix_ref.at[core, me], 1, d, others[d])

    def mix_from(d):
        source = lax.rem(me + count - 1 - d, count)
        return source, mix_copy(mix_ref.at[core, source], mix_ref.at[core, source], 1, d, others[d])

    def mix_pass():
        return pltpu.make_async_remote_copy(
            mix_ref.at[core],
            mix_ref.at[core],
            mix_hand.at[0],
            mix_hand.at[1],
            device_id=other,
            device_id_type=MESH,
        )

    half = width // 2
    columns = pl.ds(pl.multiple_of(core * half, 128), half)
    mix_raw[...] = mm(wv_ref[...], wco_ref[:, columns]).astype(bf16).reshape(mix_raw.shape)
    for a in range(3):
        fulls[a][0, me] = sources[a][...]
    for copy in own:
        copy.start()
    each = -(-mats // reach)
    for stage in range(1, reach + 1):
        for a in range(3):
            if stage < reach:
                relay(a, 0, jnp.int32(stage))
            else:
                relay_end(a, 0)
        for k in range((stage - 1) * each, min(stage * each, mats)):

            @pl.when(at_home(k))
            def _():
                start_ring(3, k)


    for d in range(count - 1):

        @pl.when(others[d][1] < used)
        def _():
            mix_scatter(d).start()

    for a in range(3):
        handed(a, 0)

    rows_here = lat_ref.shape[0]
    relays = (reach - 1) * mats
    early = min(relays, width // 256)

    def relay_number(e):
        relay_weight(lax.rem(e, mats), 1 + e // mats)

    @pl.loop(0, count)
    def _(o):
        block = lat_full[0, o].astype(f32)
        average = jnp.mean(block, axis=1, keepdims=True)
        centred = block - average
        spread = jnp.mean(centred * centred, axis=1, keepdims=True)
        normed = (centred * lax.rsqrt(spread + eps) * gain_ref[...]).astype(bf16)
        normed_ref[pl.ds(pl.multiple_of(o * rows_here, rows_here), rows_here), :] = normed

    @pl.loop(0, width // 256)
    def _(j):
        @pl.when(j < early)
        def _():
            relay_number(j)

        columns = pl.ds(pl.multiple_of(j * 256, 256), 256)
        weight = wq_full[0, :, :, columns].reshape(width, 256)
        query_ref[:, columns] = mm(normed_ref[...], weight).astype(bf16)

    a_ref[...] = mm(query_ref[...], wk_full[0].reshape(width, wk_ref.shape[1])) * (width ** (-0.5))

    def exact_nt(left, right):
        return lax.dot_general(
            left,
            right,
            (((1,), (1,)), ((), ())),
            precision=lax.Precision.HIGHEST,
            preferred_element_type=f32,
        )

    at_ref[...] = (exact_nt(gained_ref[...], a_ref[...]) * LOG2E).astype(bf16)
    alow_ref[...] = exact_nt(a_ref[...], gained_ref[...]).astype(bf16)

    table_t = table_ref[...].T[: part_ref.shape[1], :]

    @pl.when(me < used)
    def _():
        total = mix_raw[me].astype(f32)
        for d in range(count - 1):
            mix_scatter(d).wait_recv()
            total = total + mix_in[d].astype(f32)
        mix_ref[core, me] = total.astype(bf16)
        for d in range(count - 1):
            mix_gather(d).start()

    def u_push(i, h):
        to = owners.device(group, i, jnp.int32(h))
        sems = lambda which: dict(
            send_sem=u_out.at[which, i * sharers + h],
            recv_sem=u_in.at[which, me],
            device_id=to,
            device_id_type=MESH,
        )
        return to, (
            pltpu.make_async_remote_copy(u_send.at[i, h], part_ref.at[me], **sems(0)),
            pltpu.make_async_remote_copy(s_send.at[i, h], stat_ref.at[me], **sems(1)),
        )

    def u_keep():
        i, h = owners.image, owners.slot
        return (
            pltpu.make_async_copy(u_send.at[i, h], part_ref.at[me], u_own.at[0]),
            pltpu.make_async_copy(s_send.at[i, h], stat_ref.at[me], u_own.at[1]),
        )

    @pl.loop(0, images * steps)
    def _(t):
        i, step = t // steps, lax.rem(t, steps)

        @pl.when(t + early < relays)
        def _():
            relay_number(t + early)

        @pl.when(step == 0)
        def _():
            acc[...] = jnp.zeros_like(acc)
            top[...] = jnp.full_like(top, -jnp.inf)

        values = v_ref[i, :, pl.ds(pl.multiple_of(step * tile, 128), tile)]
        base = step * lines
        x, xt = build_both(values, base, code_ref)
        first, second = slice(0, tile // 2), slice(tile // 2, tile)
        scores = [mm(x[half], at_ref[...]) for half in (first, second)]
        old, total = top[0:1, :], acc[...]
        for half, score in zip((first, second), scores):
            new = jnp.maximum(old, jnp.max(score, axis=0, keepdims=True))
            weights = jnp.exp2(score - new).astype(bf16)
            total = total * jnp.exp2(old - new) + mm(xt[:, half], weights)
            old = new
        acc[...] = total
        top[...] = jnp.broadcast_to(old, top.shape)

        @pl.when(step == steps - 1)
        def _():
            raw = jnp.dot(
                table_t,
                acc[:CHANNELS, :],
                precision=lax.Precision.HIGHEST,
                preferred_element_type=f32,
            ).astype(bf16)
            stats = jnp.concatenate([top[0:1, :], acc[CHANNELS : CHANNELS + 1, :], top[0:6, :]], axis=0)
            for h in range(sharers):
                u_send[i, h] = raw[:, h * rows : (h + 1) * rows]
                s_send[i, h] = stats[:, h * rows : (h + 1) * rows]
            for h in range(sharers):
                to, copies = u_push(i, h)

                @pl.when(jnp.logical_not(owners.is_me(to)))
                def _():
                    for copy in copies:
                        copy.start()

                @pl.when(owners.is_me(to))
                def _():
                    for copy in u_keep():
                        copy.start()

    if images * steps + early < relays:

        @pl.loop(images * steps + early, relays)
        def _(e):
            relay_number(e)

    for d in range(count - 1):
        source, copy = mix_from(d)

        @pl.when(source < used)
        def _():
            copy.wait_recv()

    for o in range(used, count):
        mix_ref[core, o] = jnp.zeros_like(mix_raw[0])
    mix_pass().start()

    pl.loop(0, mats)(relay_weight_end)

    @pl.loop(alone, mats)
    def _(k):
        @pl.when(jnp.logical_not(at_home(k)))
        def _():
            take_x(k, reach, True)

    for copy in own:
        copy.wait()
    mix_pass().wait()
    for d in range(count - 1):

        @pl.when(others[d][1] < used)
        def _():
            mix_scatter(d).wait_send()

        @pl.when(me < used)
        def _():
            mix_gather(d).wait_send()

    for a in range(3):
        sent(a, 0)

    for k in range(mats):
        home = at_home(k)

        @pl.when(home)
        def _():
            sent(3, k)
            if k >= alone:
                for stage in range(1, reach + 1):
                    for way in range(2):
                        for d in range(teams - 1):
                            over_x(k, stage, way, d, stage == reach).wait_send()

        @pl.when(jnp.logical_not(home))
        def _():
            for way in range(2):
                for stage in range(1, reach + 1):
                    hand(3, k, stage, way, stage == reach).wait_send()

        handed(3, k)

    def u_from(source):
        sems = lambda which: dict(
            send_sem=u_out.at[which, 0],
            recv_sem=u_in.at[which, source],
            device_id=(owners.home, source),
            device_id_type=MESH,
        )
        return (
            pltpu.make_async_remote_copy(u_send.at[0, 0], part_ref.at[source], **sems(0)),
            pltpu.make_async_remote_copy(s_send.at[0, 0], stat_ref.at[source], **sems(1)),
        )

    for i in range(images):
        for h in range(sharers):
            to, copies = u_push(i, h)

            @pl.when(jnp.logical_not(owners.is_me(to)))
            def _():
                for copy in copies:
                    copy.wait_send()

    for source in range(count):
        local = owners.is_me((owners.home, source))

        @pl.when(local)
        def _():
            for copy in u_keep():
                copy.wait()

        @pl.when(jnp.logical_not(local))
        def _():
            for copy in u_from(source):
                copy.wait_recv()


def forward_pass(
    values, table, gained, gain_latent, lat, wq, wk, wv, wco, shards, tall, collective_id
):
    count = lax.axis_size("pix")
    images, _, pixels = values.shape
    tile = pixel_tile(pixels)
    rows_here, width = lat.shape
    latents = rows_here * count
    sharers = count // images
    rows = latents // sharers
    mats = len(shards)
    inside = pl.BlockSpec(memory_space=pltpu.VMEM)
    anywhere = pl.BlockSpec(memory_space=pl.ANY)
    shape = jax.ShapeDtypeStruct

    def full(array, number=1):
        return shape((number, count) + array.shape, array.dtype)

    ring = DMA((count // 2, 2, 3 + mats))
    return pl.pallas_call(
        functools.partial(forward_kernel, count, lax.axis_size("img") // 2, images, tile, mats),
        out_shape=[full(lat), full(wq), full(wk), full(shards[0], mats)]
        + [
            shape((latents, width), bf16),
            shape((latents, width), bf16),
            shape((latents, wk.shape[1]), f32),
            shape((CHANNELS, latents), bf16),
            shape((latents, CHANNELS), bf16),
            shape((2, count, wv.shape[0] // count, width // 2), bf16),
            shape((count, tall, rows), bf16),
            shape((count, 8, rows), f32),
        ],
        in_specs=[inside] * (10 + mats),
        out_specs=[inside] * 3 + [anywhere] + [inside] * 6 + [anywhere] * 2,
        scratch_shapes=[
            pltpu.VMEM((count, wv.shape[0] // count, width // 2), bf16),
            pltpu.VMEM((count - 1, wv.shape[0] // count, width // 2), bf16),
            pltpu.VMEM((CHANNELS + 16, latents), f32),
            pltpu.VMEM((8, latents), f32),
            pltpu.VMEM((images, sharers, tall, rows), bf16),
            pltpu.VMEM((images, sharers, 8, rows), f32),
            DMA((mats,)),
            ring,
            ring,
            ring,
            ring,
            DMA((2, count - 1)),
            DMA((2, count - 1)),
            DMA((2,)),
            DMA((max(lax.axis_size("img") // 2 - 1, 1), count // 2, 2, mats)),
            DMA((count // 2, 2, mats)),
            DMA((2,)),
            DMA((2, count)),
            DMA((2, count)),
        ],
        compiler_params=pltpu.CompilerParams(
            collective_id=collective_id, has_side_effects=True, vmem_limit_bytes=48 * 2**20
        ),
    )(values, hot_codes(tile), table, gained, gain_latent[None], lat, wq, wk, wv, wco, *shards)


def backward_kernel(
    count,
    teams,
    images,
    tile,
    channels,
    v_ref,
    code_ref,
    table_ref,
    gained_ref,
    at_ref,
    a_ref,
    back_ref,
    row_ref,
    gain_ref,
    xs_ref,
    gs_ref,
    t_out,
    g_out,
    z_out,
    pixel_ref,
    out_ref,
    t_raw,
    t_in,
    t_img,
    g_raw,
    g_in,
    g_img,
    z_own,
    t_acc,
    bt,
    b_low,
    stat,
    back_all,
    row_all,
    xv,
    gv,
    terms,
    held,
    across,
    done,
    load_sem,
    pair_send,
    pair_recv,
    send_sem,
    recv_sem,
    cross_send,
    cross_recv,
    out_sem,
    hand_send,
    hand_recv,
    back_send,
    back_recv,
    pass_send,
    foreign_send,
    foreign_recv,
    sum_send,
    sum_recv,
    img_send,
    img_recv,
    last_send,
    last_recv,
    z_send,
    z_recv,
    z_hand_send,
    z_hand_recv,
):
    number, rows, width = gs_ref.shape
    kinds = xs_ref.shape[0]
    owners = Owners(count, images)
    sharers = owners.sharers
    steps = v_ref.shape[2] // tile
    lines = tile // SIDE
    depth = xs_ref.shape[1] // count
    half, wide = width // 2, width // 4
    group, me = lax.axis_index("img"), lax.axis_index("pix")
    core, team = lax.rem(group, 2), group // 2
    place = ring_place(count)
    sides = ((group, ring_device(place + 1, count)), (group, ring_device(place - 1, count)))
    other = (group + 1 - 2 * core, me)
    partners = [(lax.rem(team + d, teams) * 2 + core, me) for d in range(1, teams)]
    crowd = 2 * teams
    others = peers(count)
    same_place = [(lax.rem(group + d, crowd), me) for d in range(1, crowd)]
    far = [
        (lax.rem(team + d, teams) * 2 + c, me) for d in range(1, teams) for c in range(2)
    ]
    greet(plane(count) + far)

    def send(source, target, sems, index, device):
        return pltpu.make_async_remote_copy(
            source,
            target,
            sems[0].at[index],
            sems[1].at[index],
            device_id=device,
            device_id_type=MESH,
        )

    def scatter(d):
        to, sems = others[d][1], (sum_send, sum_recv)
        return (
            send(t_raw.at[to], t_in.at[d], sems, (0, d), others[d]),
            send(g_raw.at[to], g_in.at[d], sems, (1, d), others[d]),
        )

    def over(d):
        sems = (img_send, img_recv)
        return (
            send(t_img.at[group], t_img.at[group], sems, (0, d), same_place[d]),
            send(g_img.at[group], g_img.at[group], sems, (1, d), same_place[d]),
        )

    def gather(d):
        sems = (last_send, last_recv)
        return (
            send(t_out.at[me], t_out.at[me], sems, (0, d), others[d]),
            send(g_out.at[me], g_out.at[me], sems, (1, d), others[d]),
        )

    def z_push(d):
        return send(z_own, z_out.at[core, me], (z_send, z_recv), d, others[d])

    def z_hand():
        return pltpu.make_async_remote_copy(
            z_out.at[core],
            z_out.at[core],
            z_hand_send,
            z_hand_recv,
            device_id=other,
            device_id_type=MESH,
        )

    for o in range(count):
        g_raw[o] = gain_ref[:, o * depth : (o + 1) * depth]

    own_index = owners.image * sharers + owners.slot

    def back_push(d):
        to = (owners.home, lax.rem(me + 2 * d, count))
        sems = lambda which: dict(
            send_sem=back_send.at[which, d],
            recv_sem=back_recv.at[which, own_index],
            device_id=to,
            device_id_type=MESH,
        )
        return to, (
            pltpu.make_async_remote_copy(back_ref, back_all.at[own_index], **sems(0)),
            pltpu.make_async_remote_copy(row_ref, row_all.at[own_index], **sems(1)),
        )

    def back_from(source):
        sems = lambda which: dict(
            send_sem=back_send.at[which, 0],
            recv_sem=back_recv.at[which, source],
            device_id=(group, me),
            device_id_type=MESH,
        )
        return (
            pltpu.make_async_remote_copy(back_ref, back_all.at[source], **sems(0)),
            pltpu.make_async_remote_copy(row_ref, row_all.at[source], **sems(1)),
        )

    def back_hand(block):
        to = (group, me + 1 - 2 * lax.rem(me, 2))
        sems = lambda which: dict(
            send_sem=pass_send.at[which, block],
            recv_sem=back_recv.at[which, block],
            device_id=to,
            device_id_type=MESH,
        )
        return (
            pltpu.make_async_remote_copy(back_all.at[block], back_all.at[block], **sems(0)),
            pltpu.make_async_remote_copy(row_all.at[block], row_all.at[block], **sems(1)),
        )

    def back_owner(image, slot):
        sender = owners.device(group, image, slot)
        return sender, lax.rem(sender[1], 2) == lax.rem(me, 2)

    for d in range(count // 2):
        to, copies = back_push(d)

        @pl.when(jnp.logical_not(owners.is_me(to)))
        def _():
            for copy in copies:
                copy.start()

        @pl.when(owners.is_me(to))
        def _():
            back_all[own_index] = back_ref[...]
            row_all[own_index] = row_ref[...]

    def load_x(j):
        return pltpu.make_async_copy(xs_ref.at[j], xv.at[j, core], load_sem.at[0, j])

    def load_g(k):
        part = gs_ref.at[k, :, pl.ds(pl.multiple_of(core * half, 128), half)]
        return pltpu.make_async_copy(part, gv.at[k, core], load_sem.at[1, k])

    def pair_x(j):
        return pltpu.make_async_remote_copy(
            xs_ref.at[j],
            xv.at[j, core],
            pair_send.at[0, j],
            pair_recv.at[0, j],
            device_id=other,
            device_id_type=MESH,
        )

    def pair_g(k):
        part = gs_ref.at[k, :, pl.ds(pl.multiple_of((1 - core) * half, 128), half)]
        return pltpu.make_async_remote_copy(
            part,
            gv.at[k, core],
            pair_send.at[1, k],
            pair_recv.at[1, k],
            device_id=other,
            device_id_type=MESH,
        )

    low, high = (4, 8) if number == 9 and count > 4 and 4 % teams == 0 else (0, 0)
    if teams == 1:
        low, high = 0, 0
    reach = count // 2

    def alone(k):
        return (k >= low) & (k < high)

    def at_home(k):
        return jnp.logical_not(alone(k)) | (lax.rem(k, teams) == team)

    def foreign(k, sender, way, stage):
        slot = (k // teams) * teams + sender
        rows_in = pl.ds((way * reach + stage) * depth, depth)
        return pltpu.make_async_remote_copy(
            terms.at[k, rows_in],
            held.at[slot, way, stage],
            foreign_send.at[way, stage, k],
            foreign_recv.at[sender, way, stage, k],
            device_id=(lax.rem(k, teams) * 2 + core, me),
            device_id_type=MESH,
        )

    pieces = [(way, stage) for way in range(2) for stage in range(reach)]
    order = [(i + low) % number for i in range(number)] if high else list(range(number))
    for k in order:
        j = max(k - (number - kinds), 0)
        if k == 0 or k > number - kinds:
            load_x(j).start()
            pair_x(j).start()
        load_g(k).start()
        pair_g(k).start()

    def turn(k):
        return lax.rem(k + number - 1, number)

    def owner_at(stage, way):
        ahead = reach - stage
        return ring_device(place + ahead if way == 0 else place - ahead, count)

    def rows_of(owner):
        return pl.ds(pl.multiple_of(owner * depth, depth), depth)

    def quarter(q):
        return slice(q * wide, (q + 1) * wide)

    def hop(k, stage, way, start=False):
        if start:
            source = terms.at[k, rows_of(owner_at(0, way)), quarter(way)]
            target = held.at[k, way, 0, :, quarter(way)]
        else:
            source = held.at[k, way, stage - 1]
            target = held.at[k, way, stage]
        return pltpu.make_async_remote_copy(
            source,
            target,
            send_sem.at[stage, way, k],
            recv_sem.at[stage, way, k],
            device_id=sides[way],
            device_id_type=MESH,
        )

    def cross(k, d):
        return pltpu.make_async_remote_copy(
            across.at[team, k],
            across.at[team, k],
            cross_send.at[d, k],
            cross_recv.at[d, k],
            device_id=partners[d],
            device_id_type=MESH,
        )

    @pl.loop(0, number)
    def _(i):
        k = lax.rem(i + low, number)
        j = jnp.maximum(k - (number - kinds), 0)

        @pl.when((k == 0) | (k > number - kinds))
        def _():
            load_x(j).wait()
            pair_x(j).wait_recv()

        load_g(k).wait()
        pair_g(k).wait_recv()
        for r in range(0, width, 256):
            piece = slice(r, r + 256)
            terms[k, piece, :] = (
                mm(xv[j, 0, piece, :], gv[k, 0]) + mm(xv[j, 1, piece, :], gv[k, 1])
            ).astype(bf16)

        @pl.when(jnp.logical_not(alone(k)))
        def _():
            for way in range(2):
                hop(k, 0, way, True).start()

        @pl.when(jnp.logical_not(at_home(k)))
        def _():
            for way, stage in pieces:
                foreign(k, team, way, stage).start()

    def launch(k):
        @pl.when(at_home(k))
        def _():
            for way, stage in pieces:
                here = pl.ds((way * reach + stage) * depth, depth)
                total = terms[k, here, :].astype(f32)
                for d in range(1, teams):
                    sender = lax.rem(team + d, teams)
                    foreign(k, sender, way, stage).wait_recv()
                    slot = (k // teams) * teams + sender
                    total = total + held[slot, way, stage].astype(f32)
                terms[k, here, :] = total.astype(bf16)
            for way in range(2):
                hop(k, 0, way, True).start()

    for block in range(count):
        sender, direct = back_owner(block // sharers, jnp.int32(block % sharers))

        @pl.when(direct)
        def _():
            @pl.when(jnp.logical_not(owners.is_me(sender)))
            def _():
                for copy in back_from(block):
                    copy.wait_recv()

            for copy in back_hand(block):
                copy.start()

    def relay(k, stage):
        for way in range(2):
            here = rows_of(owner_at(stage, way))

            @pl.when(stage == 1)
            def _():
                hop(k, 0, way, True).wait_recv()
                both = terms[k, here, quarter(way)].astype(f32)
                both = both + held[k, way, 0, :, quarter(way)].astype(f32)
                held[k, way, 0, :, quarter(way)] = both.astype(bf16)
                held[k, way, 0, :, quarter(1 - way)] = terms[k, here, quarter(1 - way)]

            @pl.when(stage > 1)
            def _():
                hop(k, stage - 1, way).wait_recv()
                both = terms[k, here, :].astype(f32) + held[k, way, stage - 1].astype(f32)
                held[k, way, stage - 1] = both.astype(bf16)

            hop(k, stage, way).start()

    def finish(k):
        columns = pl.ds(pl.multiple_of(core * half, 128), half)
        return pltpu.make_async_copy(done.at[k], out_ref.at[k, :, columns], out_sem.at[k])

    def hand(k):
        columns = pl.ds(pl.multiple_of(core * half, 128), half)
        return pltpu.make_async_remote_copy(
            done.at[k],
            out_ref.at[k, :, columns],
            hand_send.at[k],
            hand_recv.at[k],
            device_id=other,
            device_id_type=MESH,
        )

    def settle(k):
        for way in range(2):
            hop(k, reach - 1, way, reach == 1).wait_recv()
        total = terms[k, rows_of(me), :].astype(f32)
        for way in range(2):
            total = total + held[k, way, reach - 1].astype(f32)
        across[team, k] = total.astype(bf16)
        for d in range(teams - 1):
            cross(k, d).start()

    span_k = 3 if number % 3 == 0 else number
    groups = number // span_k
    events = reach * number

    def cross_from(k, d):
        return pltpu.make_async_remote_copy(
            across.at[team, k],
            across.at[team, k],
            cross_send.at[0, k],
            cross_recv.at[d, k],
            device_id=partners[0] if teams > 1 else other,
            device_id_type=MESH,
        )

    def complete(k):
        @pl.when(jnp.logical_not(alone(k)))
        def _():
            for d in range(teams - 1):
                cross(k, d).wait_recv()
            total = across[0, k].astype(f32)
            for t in range(1, teams):
                total = total + across[t, k].astype(f32)
            done[k] = total

        @pl.when(alone(k))
        def _():
            home = lax.rem(k, teams)

            @pl.when(home != team)
            def _():
                cross_from(k, lax.rem(team + 2 * teams - home - 1, teams)).wait_recv()

            done[k] = across[home, k].astype(f32)

        finish(k).start()
        hand(k).start()

        @pl.when(k == number - 1)
        def _():
            rows_here = t_raw.shape[1]
            mine = done[number - 1, rows_here : rows_here + z_own.shape[0], :].astype(bf16)
            z_own[...] = mine
            z_out[core, me] = mine
            for d in range(count - 1):
                z_push(d).start()

    def event(e):
        block, k = e // span_k, lax.rem(e, span_k)
        block = jnp.where(block == 0, 0, block + 1)
        g, slot = block // reach, lax.rem(block, reach)
        settles = (slot == 1) | (g == groups)

        @pl.when(settles)
        def _():
            one = turn((g - 1) * span_k + k)

            @pl.when(at_home(one))
            def _():
                settle(one)

            @pl.when(g > 1)
            def _():
                complete(turn((g - 2) * span_k + k))

        @pl.when(jnp.logical_not(settles))
        def _():
            one = turn(g * span_k + k)

            @pl.when(at_home(one))
            def _():
                relay(one, jnp.maximum(slot, 1))

            if high:

                @pl.when((g == 0) & (slot == reach - 1) & (k == span_k - 1))
                def _():
                    launch(jnp.int32(low))

                @pl.when((g == 1) & (slot == 2))
                def _():
                    launch(low + 1 + k)

    tiles = images * steps
    paced = tiles
    middle = (paced + events) // 2
    t_acc[...] = jnp.zeros_like(t_acc)

    @pl.loop(0, tiles)
    def _(t):
        image = lax.rem(t // steps + owners.image, images)
        step = lax.rem(t, steps)
        e = t

        @pl.when(t + 1 > e)
        def _():
            event(e)

        @pl.when(step == 0)
        def _():
            for h in range(sharers):
                source = image * sharers + h

                _, direct = back_owner(image, jnp.int32(h))

                @pl.when(jnp.logical_not(direct))
                def _():
                    for copy in back_from(source):
                        copy.wait_recv()

                here = slice(h * rows, (h + 1) * rows)
                wide = jnp.dot(
                    gained_ref[:, : back_ref.shape[0]],
                    back_all[source].astype(f32),
                    precision=lax.Precision.HIGHEST,
                    preferred_element_type=f32,
                )
                bt[:, here] = wide.astype(bf16)
                b_low[here, :] = wide.T.astype(bf16)
                stat[:, here] = row_all[source]

        span = pl.ds(pl.multiple_of(step * tile, 128), tile)
        values = v_ref[image, :, span]
        x, xt = build_both(values, step * lines, code_ref)
        halves = (slice(0, tile // 2), slice(tile // 2, tile))
        products = [(mm(x[half], at_ref[...]), mm(x[half], bt[...])) for half in halves]
        kept, ends = [], []
        for half, (scores, grad_p) in zip(halves, products):
            probs = jnp.exp2(scores - stat[0:1, :])
            grad_s = (probs * (grad_p - stat[1:2, :])).astype(bf16)
            kept.append(grad_s)
            back = mm(grad_s, a_ref[...]) + mm(probs.astype(bf16), b_low[...])
            along = jnp.sum(back * x[half].astype(f32), axis=1, keepdims=True)
            end = back[:, CHANNELS - 128 :]
            lane = lax.broadcasted_iota(jnp.int32, end.shape, 1)
            ends.append(jnp.where(lane == 120, along, end))
        t_acc[...] += mm(xt, jnp.concatenate(kept, axis=0))
        ends = jnp.concatenate(ends, axis=0).T[120:128, :] * (values[0:1, :] * values[1:2, :])
        hat = values[4:7, :] + values[7:8, :]
        mean_part = ends[7:8, :] + hat * ends[0:1, :]
        pixel_ref[image, :, span] = ends[4:7, :] - mean_part * (1.0 / channels)

    t_sum = lax.dot_general(
        t_acc[:CHANNELS, :],
        table_ref[:, : t_raw.shape[2]],
        (((0,), (0,)), ((), ())),
        precision=lax.Precision.HIGHEST,
        preferred_element_type=f32,
    )
    t_raw[...] = t_sum.astype(bf16).reshape(t_raw.shape)
    for d in range(count - 1):
        for copy in scatter(d):
            copy.start()

    pl.loop(paced, middle)(event)
    t_sum, g_sum = t_raw[me].astype(f32), g_raw[me]
    for d in range(count - 1):
        for copy in scatter(d):
            copy.wait_recv()
        t_sum = t_sum + t_in[d].astype(f32)
        g_sum = g_sum + g_in[d]
    t_img[group] = t_sum.astype(bf16)
    g_img[group] = g_sum
    for d in range(crowd - 1):
        for copy in over(d):
            copy.start()

    pl.loop(middle, events)(event)

    @pl.loop((groups - 1) * span_k, number)
    def _(k):
        complete(turn(k))

    for d in range(crowd - 1):
        for copy in over(d):
            copy.wait_recv()
    t_sum, g_sum = t_img[0].astype(f32), g_img[0]
    for i in range(1, crowd):
        t_sum = t_sum + t_img[i].astype(f32)
        g_sum = g_sum + g_img[i]
    t_out[me] = t_sum.astype(bf16)
    g_out[me] = g_sum
    for d in range(count - 1):
        for copy in gather(d):
            copy.start()
    for d in range(count - 1):
        z_push(d).wait()
    z_hand().start()
    for d in range(count - 1):
        for copy in gather(d):
            copy.wait()
        for copy in scatter(d):
            copy.wait_send()
    for d in range(crowd - 1):
        for copy in over(d):
            copy.wait_send()
    z_hand().wait()

    @pl.loop(0, number)
    def _(k):
        finish(k).wait()
        hand(k).wait()
        pair_g(k).wait_send()

        @pl.when(at_home(k))
        def _():
            for way in range(2):
                for stage in range(reach):
                    hop(k, stage, way, stage == 0).wait_send()
            for d in range(teams - 1):
                cross(k, d).wait_send()

        @pl.when(jnp.logical_not(at_home(k)))
        def _():
            for way, stage in pieces:
                foreign(k, team, way, stage).wait_send()

    @pl.loop(0, kinds)
    def _(j):
        pair_x(j).wait_send()

    for d in range(count // 2):
        to, copies = back_push(d)

        @pl.when(jnp.logical_not(owners.is_me(to)))
        def _():
            for copy in copies:
                copy.wait_send()

    for block in range(count):
        _, direct = back_owner(block // sharers, jnp.int32(block % sharers))

        @pl.when(direct)
        def _():
            for copy in back_hand(block):
                copy.wait_send()


def backward_pass(
    values, table, gained, at, a, back, rows_in, gains, xs, gs, channels, collective_id
):
    count = lax.axis_size("pix")
    teams = lax.axis_size("img") // 2
    kinds, _, rows = xs.shape
    number, _, width = gs.shape
    depth = xs.shape[1] // count
    anywhere = pl.BlockSpec(memory_space=pl.ANY)
    inside = pl.BlockSpec(memory_space=pltpu.VMEM)
    chunk = (depth, width // 2)
    images, _, pixels = values.shape
    tile = pixel_tile(pixels)
    latents = at.shape[1]
    tall = back.shape[0]
    shape = jax.ShapeDtypeStruct
    rows_here = latents // count
    t_shape = shape((count, rows_here, -(-channels // 128) * 128), bf16)
    g_shape = shape((count, 8, depth), f32)
    spare = min(-(-share_rows(channels, count) // 16) * 16, depth - rows_here)
    return pl.pallas_call(
        functools.partial(backward_kernel, count, teams, images, tile, channels),
        out_shape=[
            t_shape,
            g_shape,
            shape((2, count, spare, width // 2), bf16),
            shape((images, 3, pixels), f32),
            shape((number, depth, width), f32),
        ],
        in_specs=[inside] * 9 + [anywhere] * 2,
        out_specs=[inside] * 4 + [anywhere],
        scratch_shapes=[
            pltpu.VMEM(t_shape.shape, bf16),
            pltpu.VMEM((count - 1,) + t_shape.shape[1:], bf16),
            pltpu.VMEM((2 * teams,) + t_shape.shape[1:], bf16),
            pltpu.VMEM(g_shape.shape, f32),
            pltpu.VMEM((count - 1,) + g_shape.shape[1:], f32),
            pltpu.VMEM((2 * teams,) + g_shape.shape[1:], f32),
            pltpu.VMEM((spare, width // 2), bf16),
            pltpu.VMEM((CHANNELS + 16, latents), f32),
            pltpu.VMEM((CHANNELS, latents), bf16),
            pltpu.VMEM((latents, CHANNELS), bf16),
            pltpu.VMEM((8, latents), f32),
            pltpu.VMEM((count, tall, rows), bf16),
            pltpu.VMEM((count, 8, rows), f32),
            pltpu.VMEM((kinds, 2, xs.shape[1], rows), bf16),
            pltpu.VMEM((number, 2, rows, width // 2), bf16),
            pltpu.VMEM((number, xs.shape[1], width // 2), bf16),
            pltpu.VMEM((number, 2, count // 2) + chunk, bf16),
            pltpu.VMEM((teams, number) + chunk, bf16),
            pltpu.VMEM((number, depth, width // 2), f32),
            DMA((2, number)),
            DMA((2, number)),
            DMA((2, number)),
            DMA((count // 2, 2, number)),
            DMA((count // 2, 2, number)),
            DMA((teams - 1, number)),
            DMA((teams - 1, number)),
            DMA((number,)),
            DMA((number,)),
            DMA((number,)),
            DMA((2, count)),
            DMA((2, count)),
            DMA((2, count)),
            DMA((2, count // 2, number)),
            DMA((teams, 2, count // 2, number)),
            DMA((2, count - 1)),
            DMA((2, count - 1)),
            DMA((2, 2 * teams - 1)),
            DMA((2, 2 * teams - 1)),
            DMA((2, count - 1)),
            DMA((2, count - 1)),
            DMA((count - 1,)),
            DMA((count - 1,)),
            DMA,
            DMA,
        ],
        compiler_params=pltpu.CompilerParams(
            collective_id=collective_id, has_side_effects=True, vmem_limit_bytes=60 * 2**20
        ),
    )(values, hot_codes(tile), table, gained, at, a, back, rows_in, gains, xs, gs)


def peers(count):
    group, me = lax.axis_index("img"), lax.axis_index("pix")
    return [(group, lax.rem(me + d, count)) for d in range(1, count)]


def plane(count):
    group, me = lax.axis_index("img"), lax.axis_index("pix")
    other = group + 1 - 2 * lax.rem(group, 2)
    return peers(count) + [(other, lax.rem(me + d, count)) for d in range(count)]


class Owners:
    def __init__(self, count, images):
        self.group, self.me = lax.axis_index("img"), lax.axis_index("pix")
        self.core = lax.rem(self.group, 2)
        self.base = self.group - self.core
        self.images = images
        self.chips = count // (2 * images)
        self.sharers = 2 * self.chips
        self.slot = lax.rem(self.me, self.chips) * 2 + self.core
        image = self.me // self.chips
        self.image = lax.rem(image, images)
        self.home = self.base + image // images

    def device(self, group, image, slot):
        core = lax.rem(group, 2)
        chip = (core * self.images + image) * self.chips + slot // 2
        return self.base + lax.rem(slot, 2), chip

    def is_me(self, device):
        return (device[0] == self.group) & (device[1] == self.me)


def share_rows(channels, count):
    channels = -(-channels // 16) * 16
    return -(-(-(-channels // count)) // 8) * 8


def gelu_parts(z):
    slope = (2.0 / jnp.pi) ** 0.5
    square = z * z
    bend = jnp.tanh(slope * z * (1.0 + 0.044715 * square))
    half = 0.5 * (1.0 + bend)
    return z * half, half + 0.5 * z * (1.0 - bend * bend) * slope * (1.0 + 0.134145 * square)


def latent_kernel(
    count,
    images,
    part_ref,
    stat_ref,
    own_ref,
    cot_ref,
    mix_ref,
    gain_ref,
    in_gain_ref,
    w_ref,
    late_down,
    out_ref,
    xs_ref,
    gs_ref,
    back_ref,
    row_ref,
    gain_out,
    wv,
    one,
    two,
    three,
    pre,
    grad,
    flow,
    low,
    heads_q,
    kv,
    probs,
    kv_out,
    kv_in,
    cot,
    final,
    mean,
    own_v,
    own_sem,
    w_sem,
    ring_own,
    ring_send,
    ring_recv,
    hand_send,
    hand_recv,
    kv_send,
    kv_recv,
    gkv_send,
    gkv_recv,
    cot_own,
    cot_send,
    cot_recv,
    out_own,
    out_send,
    out_recv,
):
    rows, width = one.shape
    depth = width // count
    owners = Owners(count, images)
    sharers = owners.sharers
    latents = rows * sharers
    per = count // sharers
    rows_here = latents // count
    spare = depth - rows_here
    group, me = lax.axis_index("img"), lax.axis_index("pix")
    slot, image, home = owners.slot, owners.image, owners.home
    block = 256
    blocks = width // block
    row_block = min(rows, 64)
    up_one, down_one, m_query, m_key, m_value, m_out, up_two, down_two = range(8)
    scale = HEAD_DIM ** (-0.5)

    def load(k):
        return pltpu.make_async_copy(w_ref.at[k], wv.at[k], w_sem.at[k])

    early, late_refs = w_ref.shape[0], (late_down,)
    late = len(late_refs)
    own_copy = pltpu.make_async_copy(
        own_ref.at[pl.ds(pl.multiple_of(slot * rows, 16), rows)], own_v, own_sem
    )
    own_copy.start()
    for k in range(early):
        load(k).start()
    greet(plane(count))

    core = lax.rem(group, 2)
    ring = ring_place(count)
    sides = ((group, ring_device(ring + 1, count)), (group, ring_device(ring - 1, count)))
    other = (group + 1 - 2 * core, me)

    reach = count // 2

    def spot(k, stage, way, last, source=False):
        begin = (core * 2 + way) * (width // 4) if last else core * (width // 2)
        some = pl.ds(pl.multiple_of(begin, 128), width // 4 if last else width // 2)
        if source:
            return late_refs[k].at[:, some]
        origin = ring_device(ring - stage if way == 0 else ring + stage, count)
        here = pl.ds(pl.multiple_of(origin * depth, depth), depth)
        return wv.at[early + k, here, some]

    def hop(k, stage, way, start=False, last=False):
        return pltpu.make_async_remote_copy(
            spot(k, stage, way, last, start),
            spot(k, stage, way, last),
            ring_send.at[stage, way, k],
            ring_recv.at[stage, way, k],
            device_id=sides[way],
            device_id_type=MESH,
        )

    def hand(k, stage, way, last=False):
        return pltpu.make_async_remote_copy(
            spot(k, stage, way, last),
            spot(k, stage, way, last),
            hand_send.at[stage - 1, way, k],
            hand_recv.at[stage - 1, way, k],
            device_id=other,
            device_id_type=MESH,
        )

    def ring_keep(k):
        here = pl.ds(pl.multiple_of(me * depth, depth), depth)
        return pltpu.make_async_copy(late_refs[k], wv.at[early + k, here], ring_own.at[k])

    for k in range(late):
        for way in range(2):
            hop(k, 0, way, True, reach == 1).start()
        ring_keep(k).start()

    def relays(first, end):
        for stage in range(first, min(end, reach + 1)):
            for k in range(late):
                for way in range(2):
                    last = stage == reach
                    hop(k, stage - 1, way, last=last).wait_recv()
                    if stage < reach:
                        hop(k, stage, way, last=stage == reach - 1).start()
                    hand(k, stage, way, last).start()

    def arrived(k):
        ring_keep(k).wait()
        for stage in range(1, reach + 1):
            for way in range(2):
                hand(k, stage, way, stage == reach).wait_recv()

    def cot_push(i):
        to = owners.device(group, i, me // per)
        return to, pltpu.make_async_remote_copy(
            cot_ref.at[i],
            cot.at[lax.rem(me, per)],
            cot_send.at[i],
            cot_recv.at[lax.rem(me, per)],
            device_id=to,
            device_id_type=MESH,
        )

    def cot_keep():
        return pltpu.make_async_copy(cot_ref.at[image], cot.at[lax.rem(me, per)], cot_own)

    for i in range(images):
        to, copy = cot_push(i)

        @pl.when(jnp.logical_not(owners.is_me(to)))
        def _():
            copy.start()

        @pl.when(owners.is_me(to))
        def _():
            cot_keep().start()

    def columns(j, wide=block):
        return pl.ds(pl.multiple_of(j * wide, wide), wide)

    def over_columns(body, times=blocks):
        pl.loop(0, times)(body)

    def over_rows(body):
        @pl.loop(0, rows // row_block)
        def _(r):
            body(pl.ds(pl.multiple_of(r * row_block, 16), row_block))

    def put_x(j, c, value):
        xs_ref[j, columns(c), :] = value.T

    def centre(rows_f32):
        average = jnp.mean(rows_f32, axis=1, keepdims=True)
        centred = rows_f32 - average
        spread = jnp.mean(centred * centred, axis=1, keepdims=True)
        scale_rows = lax.rsqrt(spread + eps)
        return centred * scale_rows, scale_rows

    def norm(source, k, target):
        def body(r):
            target[r] = (centre(source[r])[0] * gain_ref[k : k + 1, :]).astype(bf16)

        over_rows(body)

    def norm_grad(source, k):
        def body(r):
            hat, scale_rows = centre(source[r])
            given = flow[r]
            gain_out[k : k + 1, :] += jnp.sum(given * hat, axis=0, keepdims=True)
            given = given * gain_ref[k : k + 1, :]
            along = jnp.mean(given * hat, axis=1, keepdims=True)
            grad[r] += scale_rows * (given - jnp.mean(given, axis=1, keepdims=True) - hat * along)

        over_rows(body)

    gain_out[...] = jnp.zeros_like(gain_out)

    top = jnp.max(stat_ref[:, 0:1, :], axis=0)
    total = jnp.zeros_like(top)
    for d in range(count):
        total = total + jnp.exp2(stat_ref[d, 0:1, :] - top) * stat_ref[d, 1:2, :]
    raw = jnp.zeros(part_ref.shape[1:], f32)
    for d in range(count):
        raw = raw + part_ref[d].astype(f32) * (jnp.exp2(stat_ref[d, 0:1, :] - top) / total)
    mean[0] = raw
    mean[1] = raw * in_gain_ref[...]
    row_ref[...] = jnp.zeros_like(row_ref)
    row_ref[0:1, :] = top + jnp.log(total) * LOG2E

    tall = count * spare
    mean_tall = mean[1]
    if tall > mean_tall.shape[0]:
        mean_tall = jnp.concatenate(
            [mean_tall, jnp.zeros((tall - mean_tall.shape[0], rows), f32)], axis=0
        )
    share = share_rows(mean.shape[1], count)
    place = lax.broadcasted_iota(jnp.int32, (rows_here, rows), 0)
    source_row = lax.broadcasted_iota(jnp.int32, (rows_here, rows), 1) + slot * rows
    for o in range(count):
        picks = jnp.where(place + o * rows_here == source_row, 1.0, 0.0)
        piece = [picks, mean_tall[o * share : (o + 1) * share]]
        if spare > share:
            piece.append(jnp.zeros((spare - share, rows), f32))
        xs_ref[6, o * depth : (o + 1) * depth, :] = jnp.concatenate(piece, axis=0).astype(bf16)

    mean_low = mean[1].astype(bf16)

    def make_one(j):
        one[:, columns(j)] = own_v[:, columns(j)].astype(f32) + mm_tn(
            mean_low,
            mix_ref[j // (blocks // 2), : mean.shape[1], columns(lax.rem(j, blocks // 2))],
        )

    own_copy.wait()
    over_columns(make_one)

    def ready(k):
        if k < early:
            load(k).wait()
        else:
            arrived(k - early)

    def feed(source, target, k, up, down, normed, x_hidden, keep):
        norm(source, k, normed)
        ready(up)

        def make_hidden(j):
            value = mm_nt(normed[...], wv[up, columns(j), :])
            pre[keep, :, columns(j)] = value
            hidden = gelu_parts(value)[0].astype(bf16)
            low[:, columns(j)] = hidden
            put_x(x_hidden, j, hidden)

        over_columns(make_hidden)
        if down >= early:
            relays(4, reach + 1)
        ready(down)

        def make_branch(j):
            value = source[:, columns(j)] + mm(low[...], wv[down, :, columns(j)])
            target[:, columns(j)] = value.astype(target.dtype)

        over_columns(make_branch)

    def feed_back(source, k, up, down, branch, x_pre, keep):
        @over_columns
        def _(j):
            value = mm_nt(branch[...], wv[down, columns(j), :])
            value = (value * gelu_parts(pre[keep, :, columns(j)])[1]).astype(bf16)
            low[:, columns(j)] = value
            put_x(x_pre, j, value)

        @over_columns
        def _(j):
            flow[:, columns(j)] = mm(low[...], wv[up, :, columns(j)])

        norm_grad(source, k)

    feed(one, two, 0, up_one, down_one, gs_ref.at[4], 3, 0)
    relays(1, 2)

    norm(two, 1, low)

    load(m_key).wait()
    load(m_value).wait()

    def make_kv(j):
        put_x(0, j, low[:, columns(j)])
        kv[0, slot, :, columns(j)] = mm(low[...], wv[m_key, :, columns(j)]).astype(bf16)
        kv[1, slot, :, columns(j)] = mm(low[...], wv[m_value, :, columns(j)]).astype(bf16)

    over_columns(make_kv)

    def sharer(d):
        return owners.device(home, image, lax.rem(slot + d, sharers))

    def kv_push(d):
        return pltpu.make_async_remote_copy(
            kv.at[:, slot],
            kv.at[:, slot],
            kv_send.at[d - 1],
            kv_recv.at[d - 1],
            device_id=sharer(d),
            device_id_type=MESH,
        )

    for d in range(1, sharers):
        kv_push(d).start()
    load(m_query).wait()

    @over_columns
    def _(j):
        heads_q[:, columns(j)] = mm(low[...], wv[m_query, :, columns(j)]).astype(bf16)

    for d in range(1, sharers):
        kv_push(d).wait_recv()

    def attend(h):
        c = columns(h, HEAD_DIM)
        k_all = kv[0, :, :, c].reshape(latents, HEAD_DIM)
        v_all = kv[1, :, :, c].reshape(latents, HEAD_DIM)
        scores = mm_nt(heads_q[:, c], k_all) * scale
        shifted = jnp.exp(scores - jnp.max(scores, axis=1, keepdims=True))
        p = shifted / jnp.sum(shifted, axis=1, keepdims=True)
        probs[h] = p
        low[:, c] = mm(p.astype(bf16), v_all).astype(bf16)

    pl.loop(0, HEADS // 2)(attend)
    relays(2, 3)
    pl.loop(HEADS // 2, HEADS)(attend)
    relays(3, 4)

    @over_columns
    def _(j):
        put_x(1, j, low[:, columns(j)])

    ready(m_out)

    @over_columns
    def _(j):
        three[:, columns(j)] = two[:, columns(j)] + mm(low[...], wv[m_out, :, columns(j)])

    feed(three, final, 2, up_two, down_two, gs_ref.at[6], 5, 1)

    def out_push(b):
        to = (home, slot * per + b)
        return to, pltpu.make_async_remote_copy(
            final.at[pl.ds(b * rows_here, rows_here)],
            out_ref.at[image],
            out_send.at[b],
            out_recv.at[image],
            device_id=to,
            device_id_type=MESH,
        )

    def out_keep():
        mine = pl.ds(pl.multiple_of(lax.rem(me, per) * rows_here, 16), rows_here)
        return pltpu.make_async_copy(final.at[mine], out_ref.at[image], out_own)

    for b in range(per):
        to, copy = out_push(b)

        @pl.when(jnp.logical_not(owners.is_me(to)))
        def _():
            copy.start()

        @pl.when(owners.is_me(to))
        def _():
            out_keep().start()

    def cot_from(b):
        return pltpu.make_async_remote_copy(
            cot_ref.at[0],
            cot.at[b],
            cot_send.at[0],
            cot_recv.at[b],
            device_id=(group, me),
            device_id_type=MESH,
        )

    for b in range(per):

        local = owners.is_me((home, slot * per + b))

        @pl.when(jnp.logical_not(local))
        def _():
            cot_from(b).wait_recv()

        @pl.when(local)
        def _():
            cot_keep().wait()

    given = cot[...].reshape(rows, width)
    gs_ref[7] = given
    grad[...] = given.astype(f32)
    feed_back(three, 2, up_two, down_two, gs_ref.at[7], 4, 1)

    gs_ref[3] = grad[...].astype(bf16)

    @over_columns
    def _(j):
        low[:, columns(j)] = mm_nt(gs_ref[3], wv[m_out, columns(j), :]).astype(bf16)

    @pl.loop(0, HEADS)
    def _(h):
        c = columns(h, HEAD_DIM)
        k_all = kv[0, :, :, c].reshape(latents, HEAD_DIM)
        v_all = kv[1, :, :, c].reshape(latents, HEAD_DIM)
        p = probs[h]
        g_mixed = low[:, c]
        g_p = mm_nt(g_mixed, v_all)
        g_v = mm_tn(p.astype(bf16), g_mixed)
        delta = jnp.sum(p * g_p, axis=1, keepdims=True)
        g_s = (p * (g_p - delta)).astype(bf16)
        gs_ref[0, :, c] = (mm(g_s, k_all) * scale).astype(bf16)
        g_k = mm_tn(g_s, heads_q[:, c]) * scale
        kv_out[:, 0, :, c] = g_k.reshape(sharers, rows, HEAD_DIM).astype(bf16)
        kv_out[:, 1, :, c] = g_v.reshape(sharers, rows, HEAD_DIM).astype(bf16)

    def gkv_push(d):
        to = lax.rem(slot + d, sharers)
        return pltpu.make_async_remote_copy(
            kv_out.at[to],
            kv_in.at[d - 1],
            gkv_send.at[d - 1],
            gkv_recv.at[d - 1],
            device_id=sharer(d),
            device_id_type=MESH,
        )

    for d in range(1, sharers):
        gkv_push(d).start()

    @over_columns
    def _(j):
        flow[:, columns(j)] = mm_nt(gs_ref[0], wv[m_query, columns(j), :])

    for d in range(1, sharers):
        gkv_push(d).wait_recv()
    for which in range(2):

        @over_columns
        def _(j):
            value = kv_out[slot, which, :, columns(j)].astype(f32)
            for d in range(1, sharers):
                value = value + kv_in[d - 1, which, :, columns(j)].astype(f32)
            gs_ref[1 + which, :, columns(j)] = value.astype(bf16)

    @over_columns
    def _(j):
        flow[:, columns(j)] += mm_nt(gs_ref[1], wv[m_key, columns(j), :]) + mm_nt(
            gs_ref[2], wv[m_value, columns(j), :]
        )

    norm_grad(two, 1)
    gs_ref[5] = grad[...].astype(bf16)
    feed_back(one, 0, up_one, down_one, gs_ref.at[5], 2, 0)
    gs_ref[8] = grad[...].astype(bf16)
    half = width // 2
    back = mm_nt(mix_ref[0, : mean.shape[1], :], gs_ref[8, :, :half])
    back = back + mm_nt(mix_ref[1, : mean.shape[1], :], gs_ref[8, :, half:])
    back_ref[...] = back.astype(bf16)
    row_ref[1:2, :] = jnp.sum(back * mean[1], axis=0, keepdims=True)
    in_gain = jnp.broadcast_to(
        jnp.sum(back * mean[0], axis=1, keepdims=True), (back.shape[0], 128)
    )
    gain_out[3:4, : back.shape[0]] = in_gain.T[0:1, :]

    for i in range(images):
        to, copy = cot_push(i)

        @pl.when(jnp.logical_not(owners.is_me(to)))
        def _():
            copy.wait_send()

    for d in range(1, sharers):
        kv_push(d).wait_send()
        gkv_push(d).wait_send()
    for k in range(late):
        for stage in range(reach):
            for way in range(2):
                last = stage == reach - 1
                hop(k, stage, way, stage == 0, last).wait_send()
                hand(k, stage + 1, way, last).wait_send()

    def out_from(i):
        return pltpu.make_async_remote_copy(
            final.at[pl.ds(0, rows_here)],
            out_ref.at[i],
            out_send.at[0],
            out_recv.at[i],
            device_id=(group, me),
            device_id_type=MESH,
        )

    for b in range(per):
        to, copy = out_push(b)

        @pl.when(jnp.logical_not(owners.is_me(to)))
        def _():
            copy.wait_send()

    for i in range(images):
        local = owners.is_me(owners.device(group, i, me // per))

        @pl.when(jnp.logical_not(local))
        def _():
            out_from(i).wait_recv()

        @pl.when(local)
        def _():
            out_keep().wait()


def latent_pass(parts, stats, own, cotangent, mix, gains, in_gain, whole, late, rows, collective_id):
    count = lax.axis_size("pix")
    images, rows_here, width = cotangent.shape
    channels = parts.shape[1]
    sharers = count // images
    per = count // sharers
    inside = pl.BlockSpec(memory_space=pltpu.VMEM)
    anywhere = pl.BlockSpec(memory_space=pl.ANY)
    whole_f32 = pltpu.VMEM((rows, width), f32)
    whole_low = pltpu.VMEM((rows, width), bf16)
    ring = DMA((count // 2, 2, len(late)))
    shape = jax.ShapeDtypeStruct
    return pl.pallas_call(
        functools.partial(latent_kernel, count, images),
        out_shape=[
            shape((images, rows_here, width), bf16),
            shape((7, width, rows), bf16),
            shape((9, rows, width), bf16),
            shape((channels, rows), bf16),
            shape((8, rows), f32),
            shape((8, width), f32),
        ],
        in_specs=[inside] * 2 + [anywhere] * 2 + [inside] * 3 + [anywhere] * 2,
        out_specs=[anywhere] + [inside] * 5,
        scratch_shapes=[
            pltpu.VMEM((8, width, width), bf16),
            whole_f32,
            whole_f32,
            whole_f32,
            pltpu.VMEM((2, rows, width), f32),
            whole_f32,
            whole_f32,
            whole_low,
            whole_low,
            pltpu.VMEM((2, sharers, rows, width), bf16),
            pltpu.VMEM((HEADS, rows, rows * sharers), f32),
            pltpu.VMEM((sharers, 2, rows, width), bf16),
            pltpu.VMEM((max(sharers - 1, 1), 2, rows, width), bf16),
            pltpu.VMEM((per, rows_here, width), bf16),
            whole_low,
            pltpu.VMEM((2, channels, rows), f32),
            whole_low,
            DMA,
            DMA((whole.shape[0],)),
            DMA((len(late),)),
            ring,
            ring,
            ring,
            ring,
            DMA((sharers,)),
            DMA((sharers,)),
            DMA((sharers,)),
            DMA((sharers,)),
            DMA,
            DMA((images,)),
            DMA((per,)),
            DMA,
            DMA((per,)),
            DMA((images,)),
        ],
        compiler_params=pltpu.CompilerParams(
            collective_id=collective_id, has_side_effects=True, vmem_limit_bytes=60 * 2**20
        ),
    )(parts, stats, own, cotangent, mix, gains, in_gain, whole, *late)


def tail_kernel(
    count,
    channels,
    t_ref,
    g_ref,
    z_ref,
    a_ref,
    lat_ref,
    qcols_ref,
    ncols_ref,
    wq_ref,
    wk_ref,
    wv_ref,
    wco_ref,
    gain_ref,
    lat_gain_ref,
    sum_ref,
    lat_out,
    lat_gain_out,
    gains_out,
    wq_out,
    wk_out,
    wv_out,
    wco_out,
    up_one_out,
    up_two_out,
    down_one_out,
    down_two_out,
    sq_out,
    sk_out,
    sv_out,
    so_out,
    z_v,
    query_grad,
    flow,
):
    me = lax.axis_index("pix")
    width = wq_ref.shape[0]
    depth = wco_ref.shape[0]
    rows_here = lat_out.shape[0]
    latents = lat_ref.shape[0]
    across = t_ref.shape[1]
    for k, to in (
        (0, sq_out),
        (1, sk_out),
        (2, sv_out),
        (3, so_out),
        (5, down_one_out),
        (7, down_two_out),
    ):
        to[...] = sum_ref[k]
    t = t_ref[...].astype(f32)
    tx = (t * (gain_ref[...] * width ** (-0.5))).astype(bf16)
    for o in range(count):
        gains_out[:, o * depth : (o + 1) * depth] = g_ref[o]
    row = jnp.sum(a_ref[:, :across] * t, axis=0, keepdims=True)
    gains_out[3:4, :across] += row
    wk_out[...] = mm_tn(tx, qcols_ref[...])[:channels]

    @pl.loop(0, width // 256)
    def _(j):
        columns = pl.ds(pl.multiple_of(j * 256, 256), 256)
        query_grad[:, columns] = mm_nt(tx, wk_ref[columns, :across]).astype(bf16)

    @pl.loop(0, width // 256)
    def _(j):
        columns = pl.ds(pl.multiple_of(j * 256, 256), 256)
        wq_out[:, columns] = mm_tn(ncols_ref[...], query_grad[:, columns])
        flow[:, columns] = mm_nt(query_grad[...], wq_ref[columns, :])

    share = share_rows(channels, count)
    half = width // 2
    for o in range(count):
        for h in range(2):
            z_v[o * share : (o + 1) * share, h * half : (h + 1) * half] = z_ref[h, o, :share].astype(f32)
    cross = z_v[...].astype(bf16)
    wv_out[...] = mm_nt(cross, wco_ref[...])[:channels]
    wco_out[...] = mm_tn(wv_ref[...], cross)

    up_one_out[...] = sum_ref[4].T
    up_two_out[...] = sum_ref[6].T
    lat_gain_out[...] = jnp.zeros_like(lat_gain_out)

    @pl.loop(0, count)
    def _(o):
        here = pl.ds(pl.multiple_of(o * rows_here, rows_here), rows_here)
        rows = lat_ref[here, :].astype(f32)
        average = jnp.mean(rows, axis=1, keepdims=True)
        centred = rows - average
        scale = lax.rsqrt(jnp.mean(centred * centred, axis=1, keepdims=True) + eps)
        hat = centred * scale
        given = flow[here, :]
        lat_gain_out[...] += jnp.sum(given * hat, axis=0, keepdims=True)

        @pl.when(o == me)
        def _():
            gained = given * lat_gain_ref[...]
            along = jnp.mean(gained * hat, axis=1, keepdims=True)
            moved = scale * (gained - jnp.mean(gained, axis=1, keepdims=True) - hat * along)
            lat_out[...] = moved + sum_ref[8, :rows_here, :]


def tail_pass(t, g, z, a, lat, qcols, ncols, wq, wk, wv, wco, gain, lat_gain, summed, channels):
    count = z.shape[1]
    _, depth, width = summed.shape
    latents = lat.shape[0]
    share = share_rows(channels, count)
    inside = pl.BlockSpec(memory_space=pltpu.VMEM)
    anywhere = pl.BlockSpec(memory_space=pl.ANY)
    shape = lambda *dims: jax.ShapeDtypeStruct(dims, f32)
    plain = shape(depth, width)
    return pl.pallas_call(
        functools.partial(tail_kernel, count, channels),
        out_shape=[
            shape(latents // count, width),
            shape(1, width),
            shape(8, width),
            plain,
            shape(channels, depth),
            shape(channels, depth),
            plain,
            shape(width, depth),
            shape(width, depth),
        ]
        + [plain] * 6,
        in_specs=[inside] * 14,
        out_specs=[inside] * 15,
        scratch_shapes=[
            pltpu.VMEM((count * share, width), f32),
            pltpu.VMEM((latents, width), bf16),
            pltpu.VMEM((latents, width), f32),
        ],
        compiler_params=pltpu.CompilerParams(vmem_limit_bytes=48 * 2**20),
    )(t, g, z, a, lat, qcols, ncols, wq, wk, wv, wco, gain, lat_gain, summed)


def local(
    rgb_pixels,
    keep_mask,
    latent_array,
    gain_input,
    gain_latent,
    w_query,
    w_key,
    w_value,
    w_cross_out,
    gain_mlp_one,
    w_up_one,
    w_down_one,
    gain_self,
    w_self_query,
    w_self_key,
    w_self_value,
    w_self_out,
    gain_mlp_two,
    w_up_two,
    w_down_two,
    cotangent,
):
    images, _, pixels = rgb_pixels.shape
    rows_here, width = latent_array.shape
    count = lax.axis_size("pix")
    me = lax.axis_index("pix")
    latents = rows_here * count
    sharers = count // images
    rows_own = latents // sharers
    depth = w_query.shape[0]
    channels = gain_input.shape[0]
    tall = -(-channels // 16) * 16

    side = -(-channels // 512) * 512
    key_t = jnp.pad(w_key.T, ((0, 0), (0, side - channels)))
    blocks = -(-tall // (16 * count)) * 16 * count
    value_pad = jnp.pad(w_value, ((0, blocks - channels), (0, 0)))
    shards = [
        w_up_one.T,
        w_down_one,
        w_self_query,
        w_self_key,
        w_self_value,
        w_self_out,
        w_up_two.T,
    ]
    late = [w_down_two]

    lines = pixels // SIDE
    u, sin_u, cos_u = angles(me * lines + lax.iota(jnp.int32, lines))
    w, sin_w, cos_w = angles(lax.iota(jnp.int32, SIDE))

    def zeros(rows, columns):
        return jnp.zeros((rows, columns), f32)

    pad = CHANNELS - 4 - SIDE - lines
    table = jnp.concatenate(
        [
            jnp.concatenate(
                [zeros(SIDE, 4), w, zeros(SIDE, BANDS), sin_w, zeros(SIDE, BANDS), cos_w], axis=1
            ),
            jnp.concatenate(
                [zeros(lines, 3), u, zeros(lines, 1), sin_u, zeros(lines, BANDS), cos_u, zeros(lines, BANDS)],
                axis=1,
            ),
            zeros(pad, channels),
            jnp.eye(3, channels, dtype=f32),
            jnp.ones((1, channels), f32),
        ],
        axis=0,
    )
    row_sum = u[:, 0] + jnp.sum(sin_u + cos_u, axis=1)
    col_sum = w[:, 0] + jnp.sum(sin_w + cos_w, axis=1)
    row_square = u[:, 0] ** 2 + jnp.sum(sin_u**2 + cos_u**2, axis=1)
    col_square = w[:, 0] ** 2 + jnp.sum(sin_w**2 + cos_w**2, axis=1)
    feature_sum = (row_sum[:, None] + col_sum[None, :]).reshape(1, pixels)
    feature_square = (row_square[:, None] + col_square[None, :]).reshape(1, pixels)
    colours = rgb_pixels.astype(f32)
    average = (jnp.sum(colours, axis=1) + feature_sum) / channels
    spread = (jnp.sum(colours**2, axis=1) + feature_square) / channels - average**2
    scale = lax.rsqrt(spread + eps)
    keep = keep_mask.astype(f32)

    own_values = jnp.concatenate([colours, -average[:, None, :]], axis=1) * scale[:, None, :]
    values = jnp.concatenate(
        [scale[:, None], keep[:, None], jnp.zeros((images, 2, pixels), f32), own_values], axis=1
    )
    table = jnp.pad(table, ((0, 0), (0, side - channels)))
    gained = table * jnp.pad(gain_input, (0, side - channels))[None, :]
    (
        latent_full,
        query_mat,
        key_full,
        whole,
        latent_normed,
        queries,
        score_mat,
        at,
        a_low,
        value_out,
        raw_parts,
        stat_parts,
    ) = forward_pass(
        values,
        table,
        gained,
        gain_latent,
        latent_array,
        w_query,
        key_t,
        value_pad,
        w_cross_out,
        shards,
        tall,
        0,
    )
    latent_full = latent_full.reshape(latents, width)
    whole = whole.reshape(-1, width, width)

    latent_out, xs, gs, back_t, row_stats, gain_grads = latent_pass(
        raw_parts,
        stat_parts,
        latent_full,
        cotangent,
        value_out.reshape(2, blocks, width // 2),
        jnp.stack([gain_mlp_one, gain_self, gain_mlp_two]),
        jnp.pad(gain_input, (0, tall - channels))[:, None],
        whole,
        late,
        rows_own,
        4,
    )
    across = -(-channels // 128) * 128
    grad_raw, gain_sums, cross_sum, grad_pixels, summed = backward_pass(
        values,
        table,
        gained,
        at,
        a_low,
        back_t,
        row_stats,
        gain_grads,
        xs,
        gs,
        channels,
        2,
    )

    share = share_rows(channels, count)
    (
        grad_latent_array,
        gain_latent_sum,
        gain_sums,
        grad_w_query,
        grad_w_key,
        grad_w_value,
        grad_w_cross_out,
        g_up_one,
        g_up_two,
        g_down_one,
        g_down_two,
        g_sq,
        g_sk,
        g_sv,
        g_so,
    ) = tail_pass(
        grad_raw.reshape(latents, across),
        gain_sums,
        cross_sum,
        score_mat,
        latent_full,
        lax.dynamic_slice_in_dim(queries, me * depth, depth, 1),
        lax.dynamic_slice_in_dim(latent_normed, me * depth, depth, 1),
        query_mat.reshape(width, width),
        key_full.reshape(width, side),
        jnp.pad(w_value, ((0, share * count - channels), (0, 0))),
        w_cross_out,
        jnp.pad(gain_input, (0, across - channels))[None],
        gain_latent[None],
        summed,
        channels,
    )
    gain_one, gain_attn, gain_two = gain_sums[0], gain_sums[1], gain_sums[2]
    gain_in = gain_sums[3, :channels]
    grad_gain_latent = gain_latent_sum[0]
    return (
        latent_out,
        grad_pixels,
        grad_latent_array,
        gain_in,
        grad_gain_latent,
        grad_w_query,
        grad_w_key,
        grad_w_value,
        grad_w_cross_out,
        gain_one,
        g_up_one,
        g_down_one,
        gain_attn,
        g_sq,
        g_sk,
        g_sv,
        g_so,
        gain_two,
        g_up_two,
        g_down_two,
    )


def solution(mesh):
    rows, columns, copied = P("pix", None), P(None, "pix"), P()
    return jax.shard_map(
        local,
        mesh=mesh,
        in_specs=(
            P("img", None, "pix"),
            P("img", "pix"),
            rows,
            copied,
            copied,
            rows,
            columns,
            columns,
            rows,
            copied,
            columns,
            rows,
            copied,
            rows,
            rows,
            rows,
            rows,
            copied,
            columns,
            rows,
            P("img", "pix", None),
        ),
        out_specs=(
            P("img", "pix", None),
            P("img", None, "pix"),
            rows,
            copied,
            copied,
            rows,
            columns,
            columns,
            rows,
            copied,
            columns,
            rows,
            copied,
            rows,
            rows,
            rows,
            rows,
            copied,
            columns,
            rows,
        ),
        check_vma=False,
    )
```

```python
import functools

import jax
import jax.numpy as jnp
from jax import lax
from jax.experimental import pallas as pl
from jax.experimental.pallas import tpu as pltpu
from jax.sharding import PartitionSpec as P

HEADS = 8
HEAD_DIM = 128
BANDS = 64
SIDE = 224
CHANNELS = 256
LOG2E = 1.4426950408889634

eps = 1e-05
f32 = jnp.float32
bf16 = jnp.bfloat16


def exact(left, right):
    return jnp.dot(left, right, precision=lax.Precision.HIGHEST, preferred_element_type=f32)


def mm(left, right):
    return jnp.dot(left, right, preferred_element_type=f32)


def mm_nt(left, right):
    return lax.dot_general(left, right, (((1,), (1,)), ((), ())), preferred_element_type=f32)


def mm_tn(left, right):
    return lax.dot_general(left, right, (((0,), (0,)), ((), ())), preferred_element_type=f32)


def angles(index):
    place = index.astype(f32) * (2.0 / (SIDE - 1)) - 1.0
    steps = lax.iota(jnp.int32, BANDS).astype(f32)
    frequency = 1.0 + steps * ((SIDE / 2.0 - 1.0) / (BANDS - 1))
    angle = jnp.pi * place[:, None] * frequency[None, :]
    return place[:, None], jnp.sin(angle), jnp.cos(angle)


def pixel_tile(pixels):
    return 896 if pixels % 896 == 0 else pixels


MESH = pl.DeviceIdType.MESH
DMA = pltpu.SemaphoreType.DMA


def ring_place(count):
    me = lax.axis_index("pix")
    return jnp.where(me % 2 == 0, me // 2, count - 1 - me // 2)


def ring_device(place, count):
    place = lax.rem(place + 2 * count, count)
    return jnp.where(place < count // 2, 2 * place, 2 * (count - 1 - place) + 1)


def greet(devices):
    barrier = pltpu.get_barrier_semaphore()
    for device in devices:
        pl.semaphore_signal(barrier, inc=1, device_id=device, device_id_type=MESH)
    pl.semaphore_wait(barrier, len(devices))


def hot_codes(tile):
    pixel = lax.broadcasted_iota(jnp.int32, (CHANNELS, tile), 1)
    channel = lax.broadcasted_iota(jnp.int32, (CHANNELS, tile), 0)
    start = channel - SIDE - pixel // SIDE
    code = jnp.where((start >= 0) & (channel < CHANNELS - 4), start, -2)
    return jnp.where(channel < SIDE, jnp.where(channel == pixel % SIDE, -1, -2), code)


def build_xt(values, base, code_ref):
    code = code_ref[...]
    hot = jnp.where((code == -1) | (code == base), values[0:1, :], 0.0)
    last = hot[CHANNELS - 8 :, :]
    k = lax.broadcasted_iota(jnp.int32, last.shape, 0)
    last = jnp.where(k >= 4, values, last)
    return jnp.concatenate([hot[: CHANNELS - 8, :], last], axis=0)


def build_both(values, base, code_ref):
    keep = values[1:2, :]
    xt = build_xt(values, base, code_ref).astype(bf16)
    k = lax.broadcasted_iota(jnp.int32, (16, values.shape[1]), 0)
    ones = jnp.where(k == 0, keep, 0.0).astype(bf16)
    return xt.T, jnp.concatenate([xt * keep.astype(bf16), ones], axis=0)


def forward_kernel(
    count,
    teams,
    images,
    tile,
    mats,
    v_ref,
    code_ref,
    table_ref,
    gained_ref,
    gain_ref,
    lat_ref,
    wq_ref,
    wk_ref,
    wv_ref,
    wco_ref,
    *refs,
):
    shards = refs[:mats]
    forward_body(
        count,
        teams,
        images,
        tile,
        v_ref,
        code_ref,
        table_ref,
        gained_ref,
        gain_ref,
        lat_ref,
        wq_ref,
        wk_ref,
        wv_ref,
        wco_ref,
        shards,
        *refs[mats:],
    )


def forward_body(
    count,
    teams,
    images,
    tile,
    v_ref,
    code_ref,
    table_ref,
    gained_ref,
    gain_ref,
    lat_ref,
    wq_ref,
    wk_ref,
    wv_ref,
    wco_ref,
    shards,
    lat_full,
    wq_full,
    wk_full,
    w_full,
    normed_ref,
    query_ref,
    a_ref,
    at_ref,
    alow_ref,
    mix_ref,
    part_ref,
    stat_ref,
    mix_raw,
    mix_in,
    acc,
    top,
    u_send,
    s_send,
    own_sem,
    send_sem,
    recv_sem,
    hand_send,
    hand_recv,
    mix_send,
    mix_recv,
    mix_hand,
    x_send,
    x_recv,
    u_own,
    u_out,
    u_in,
):
    pixels = v_ref.shape[2]
    steps = pixels // tile
    lines = tile // SIDE
    owners = Owners(count, images)
    sharers = owners.sharers
    rows = part_ref.shape[2]
    width = wq_ref.shape[1]
    latents = normed_ref.shape[0]
    group, me = lax.axis_index("img"), lax.axis_index("pix")
    core = lax.rem(group, 2)
    place = ring_place(count)
    sides = ((group, ring_device(place + 1, count)), (group, ring_device(place - 1, count)))
    other = (group + 1 - 2 * core, me)
    team = group // 2
    partners = [(lax.rem(team + d, teams) * 2 + core, me) for d in range(1, teams)]
    greet(plane(count) + partners)
    sources = (lat_ref, wq_ref, wk_ref)
    fulls = (lat_full, wq_full, wk_full, w_full)
    mats = len(shards)

    reach = count // 2

    def spot(a, k, stage, way, last, source=False):
        wide = fulls[a].shape[3] // 4
        begin = (core * 2 + way) * wide if last else core * 2 * wide
        columns = pl.ds(pl.multiple_of(begin, 128), wide if last else 2 * wide)
        if source:
            return (sources[a] if a < 3 else shards[k]).at[:, columns]
        origin = ring_device(place - stage if way == 0 else place + stage, count)
        return fulls[a].at[k, origin, :, columns]

    def hop(a, k, stage, way, first=False, last=False):
        return pltpu.make_async_remote_copy(
            spot(a, k, stage, way, last, first),
            spot(a, k, stage, way, last),
            send_sem.at[stage, way, a + k],
            recv_sem.at[stage, way, a + k],
            device_id=sides[way],
            device_id_type=MESH,
        )

    def hand(a, k, stage, way, last=False):
        part = spot(a, k, stage, way, last)
        return pltpu.make_async_remote_copy(
            part,
            part,
            hand_send.at[stage - 1, way, a + k],
            hand_recv.at[stage - 1, way, a + k],
            device_id=other,
            device_id_type=MESH,
        )

    def relay(a, k, stage):
        for way in range(2):
            hop(a, k, stage - 1, way).wait_recv()

            @pl.when(stage == reach - 1)
            def _():
                hop(a, k, stage, way, last=True).start()

            @pl.when(stage != reach - 1)
            def _():
                hop(a, k, stage, way).start()

            hand(a, k, stage, way).start()

    def relay_end(a, k):
        for way in range(2):
            hop(a, k, reach - 1, way, last=True).wait_recv()
            hand(a, k, reach, way, last=True).start()

    def start_ring(a, k):
        for way in range(2):
            hop(a, k, 0, way, True, reach == 1).start()

    alone = 1

    def at_home(k):
        return (k < alone) | (lax.rem(jnp.int32(k), teams) == team)

    def over_x(k, stage, way, d, last=False):
        part = spot(3, k, stage, way, last)
        return pltpu.make_async_remote_copy(
            part,
            part,
            x_send.at[d, stage - 1, way, k],
            x_recv.at[stage - 1, way, k],
            device_id=partners[d],
            device_id_type=MESH,
        )

    def pass_x(k, stage, last=False):
        @pl.when(k >= alone)
        def _():
            for way in range(2):
                for d in range(teams - 1):
                    over_x(k, stage, way, d, last).start()

    def take_x(k, stage, last=False):
        for way in range(2):
            over_x(k, stage, way, 0, last).wait_recv()
            hand(3, k, stage, way, last).start()

    def relay_weight(k, stage):
        home = at_home(k)

        @pl.when(home)
        def _():
            relay(3, k, stage)
            pass_x(k, stage)

        @pl.when(jnp.logical_not(home) & (stage > 1))
        def _():
            take_x(k, stage - 1)

    def relay_weight_end(k):
        home = at_home(k)

        @pl.when(home)
        def _():
            relay_end(3, k)
            pass_x(k, reach, True)

        @pl.when(jnp.logical_not(home))
        def _():
            take_x(k, reach - 1)

    def sent(a, k):
        for way in range(2):
            for stage in range(reach):
                last = stage == reach - 1
                hop(a, k, stage, way, stage == 0, last).wait_send()
                hand(a, k, stage + 1, way, last).wait_send()

    def handed(a, k):
        for way in range(2):
            for stage in range(1, reach + 1):
                hand(a, k, stage, way, stage == reach).wait_recv()

    own = [
        pltpu.make_async_copy(shards[k], fulls[3].at[k, me], own_sem.at[k]) for k in range(mats)
    ]
    for a in range(3):
        start_ring(a, 0)
    others = peers(count)
    used = -(-part_ref.shape[1] // mix_raw.shape[1])

    def mix_copy(source, target, stage, index, device):
        return pltpu.make_async_remote_copy(
            source,
            target,
            mix_send.at[stage, index],
            mix_recv.at[stage, index],
            device_id=device,
            device_id_type=MESH,
        )

    def mix_scatter(d):
        return mix_copy(mix_raw.at[others[d][1]], mix_in.at[d], 0, d, others[d])

    def mix_gather(d):
        return mix_copy(mix_ref.at[core, me], mix_ref.at[core, me], 1, d, others[d])

    def mix_from(d):
        source = lax.rem(me + count - 1 - d, count)
        return source, mix_copy(mix_ref.at[core, source], mix_ref.at[core, source], 1, d, others[d])

    def mix_pass():
        return pltpu.make_async_remote_copy(
            mix_ref.at[core],
            mix_ref.at[core],
            mix_hand.at[0],
            mix_hand.at[1],
            device_id=other,
            device_id_type=MESH,
        )

    half = width // 2
    columns = pl.ds(pl.multiple_of(core * half, 128), half)
    mix_raw[...] = mm(wv_ref[...], wco_ref[:, columns]).astype(bf16).reshape(mix_raw.shape)
    for a in range(3):
        fulls[a][0, me] = sources[a][...]
    for copy in own:
        copy.start()
    each = -(-mats // reach)
    for stage in range(1, reach + 1):
        for a in range(3):
            if stage < reach:
                relay(a, 0, jnp.int32(stage))
            else:
                relay_end(a, 0)
        for k in range((stage - 1) * each, min(stage * each, mats)):

            @pl.when(at_home(k))
            def _():
                start_ring(3, k)


    for d in range(count - 1):

        @pl.when(others[d][1] < used)
        def _():
            mix_scatter(d).start()

    for a in range(3):
        handed(a, 0)

    rows_here = lat_ref.shape[0]
    relays = (reach - 1) * mats
    early = min(relays, width // 256 + 3)

    def relay_number(e):
        relay_weight(lax.rem(e, mats), 1 + e // mats)

    @pl.loop(0, count)
    def _(o):
        block = lat_full[0, o].astype(f32)
        average = jnp.mean(block, axis=1, keepdims=True)
        centred = block - average
        spread = jnp.mean(centred * centred, axis=1, keepdims=True)
        normed = (centred * lax.rsqrt(spread + eps) * gain_ref[...]).astype(bf16)
        normed_ref[pl.ds(pl.multiple_of(o * rows_here, rows_here), rows_here), :] = normed

    pl.loop(0, min(early, 3))(relay_number)

    @pl.loop(0, width // 256)
    def _(j):
        @pl.when(j + 3 < early)
        def _():
            relay_number(j + 3)

        columns = pl.ds(pl.multiple_of(j * 256, 256), 256)
        weight = wq_full[0, :, :, columns].reshape(width, 256)
        query_ref[:, columns] = mm(normed_ref[...], weight).astype(bf16)

    a_ref[...] = mm(query_ref[...], wk_full[0].reshape(width, wk_ref.shape[1])) * (width ** (-0.5))

    def exact_nt(left, right):
        return lax.dot_general(
            left,
            right,
            (((1,), (1,)), ((), ())),
            precision=lax.Precision.HIGHEST,
            preferred_element_type=f32,
        )

    at_ref[...] = (exact_nt(gained_ref[...], a_ref[...]) * LOG2E).astype(bf16)
    alow_ref[...] = exact_nt(a_ref[...], gained_ref[...]).astype(bf16)

    table_t = table_ref[...].T[: part_ref.shape[1], :]

    @pl.when(me < used)
    def _():
        total = mix_raw[me].astype(f32)
        for d in range(count - 1):
            mix_scatter(d).wait_recv()
            total = total + mix_in[d].astype(f32)
        mix_ref[core, me] = total.astype(bf16)
        for d in range(count - 1):
            mix_gather(d).start()

    def u_push(i, h):
        to = owners.device(group, i, jnp.int32(h))
        sems = lambda which: dict(
            send_sem=u_out.at[which, i * sharers + h],
            recv_sem=u_in.at[which, me],
            device_id=to,
            device_id_type=MESH,
        )
        return to, (
            pltpu.make_async_remote_copy(u_send.at[i, h], part_ref.at[me], **sems(0)),
            pltpu.make_async_remote_copy(s_send.at[i, h], stat_ref.at[me], **sems(1)),
        )

    def u_keep():
        i, h = owners.image, owners.slot
        return (
            pltpu.make_async_copy(u_send.at[i, h], part_ref.at[me], u_own.at[0]),
            pltpu.make_async_copy(s_send.at[i, h], stat_ref.at[me], u_own.at[1]),
        )

    @pl.loop(0, images * steps)
    def _(t):
        i, step = t // steps, lax.rem(t, steps)

        @pl.when(t + early < relays)
        def _():
            relay_number(t + early)

        @pl.when(step == 0)
        def _():
            acc[...] = jnp.zeros_like(acc)
            top[...] = jnp.full_like(top, -jnp.inf)

        values = v_ref[i, :, pl.ds(pl.multiple_of(step * tile, 128), tile)]
        base = step * lines
        x, xt = build_both(values, base, code_ref)
        first, second = slice(0, tile // 2), slice(tile // 2, tile)
        scores = [mm(x[half], at_ref[...]) for half in (first, second)]
        old, total = top[0:1, :], acc[...]
        for half, score in zip((first, second), scores):
            new = jnp.maximum(old, jnp.max(score, axis=0, keepdims=True))
            weights = jnp.exp2(score - new).astype(bf16)
            total = total * jnp.exp2(old - new) + mm(xt[:, half], weights)
            old = new
        acc[...] = total
        top[...] = jnp.broadcast_to(old, top.shape)

        @pl.when(step == steps - 1)
        def _():
            raw = jnp.dot(
                table_t,
                acc[:CHANNELS, :],
                precision=lax.Precision.HIGHEST,
                preferred_element_type=f32,
            ).astype(bf16)
            stats = jnp.concatenate([top[0:1, :], acc[CHANNELS : CHANNELS + 1, :], top[0:6, :]], axis=0)
            for h in range(sharers):
                u_send[i, h] = raw[:, h * rows : (h + 1) * rows]
                s_send[i, h] = stats[:, h * rows : (h + 1) * rows]
            for h in range(sharers):
                to, copies = u_push(i, h)

                @pl.when(jnp.logical_not(owners.is_me(to)))
                def _():
                    for copy in copies:
                        copy.start()

                @pl.when(owners.is_me(to))
                def _():
                    for copy in u_keep():
                        copy.start()

    if images * steps + early < relays:

        @pl.loop(images * steps + early, relays)
        def _(e):
            relay_number(e)

    for d in range(count - 1):
        source, copy = mix_from(d)

        @pl.when(source < used)
        def _():
            copy.wait_recv()

    for o in range(used, count):
        mix_ref[core, o] = jnp.zeros_like(mix_raw[0])
    mix_pass().start()

    pl.loop(0, mats)(relay_weight_end)

    @pl.loop(alone, mats)
    def _(k):
        @pl.when(jnp.logical_not(at_home(k)))
        def _():
            take_x(k, reach, True)

    for copy in own:
        copy.wait()
    mix_pass().wait()
    for d in range(count - 1):

        @pl.when(others[d][1] < used)
        def _():
            mix_scatter(d).wait_send()

        @pl.when(me < used)
        def _():
            mix_gather(d).wait_send()

    for a in range(3):
        sent(a, 0)

    for k in range(mats):
        home = at_home(k)

        @pl.when(home)
        def _():
            sent(3, k)
            if k >= alone:
                for stage in range(1, reach + 1):
                    for way in range(2):
                        for d in range(teams - 1):
                            over_x(k, stage, way, d, stage == reach).wait_send()

        @pl.when(jnp.logical_not(home))
        def _():
            for way in range(2):
                for stage in range(1, reach + 1):
                    hand(3, k, stage, way, stage == reach).wait_send()

        handed(3, k)

    def u_from(source):
        sems = lambda which: dict(
            send_sem=u_out.at[which, 0],
            recv_sem=u_in.at[which, source],
            device_id=(owners.home, source),
            device_id_type=MESH,
        )
        return (
            pltpu.make_async_remote_copy(u_send.at[0, 0], part_ref.at[source], **sems(0)),
            pltpu.make_async_remote_copy(s_send.at[0, 0], stat_ref.at[source], **sems(1)),
        )

    for i in range(images):
        for h in range(sharers):
            to, copies = u_push(i, h)

            @pl.when(jnp.logical_not(owners.is_me(to)))
            def _():
                for copy in copies:
                    copy.wait_send()

    for source in range(count):
        local = owners.is_me((owners.home, source))

        @pl.when(local)
        def _():
            for copy in u_keep():
                copy.wait()

        @pl.when(jnp.logical_not(local))
        def _():
            for copy in u_from(source):
                copy.wait_recv()


def forward_pass(
    values, table, gained, gain_latent, lat, wq, wk, wv, wco, shards, tall, collective_id
):
    count = lax.axis_size("pix")
    images, _, pixels = values.shape
    tile = pixel_tile(pixels)
    rows_here, width = lat.shape
    latents = rows_here * count
    sharers = count // images
    rows = latents // sharers
    mats = len(shards)
    inside = pl.BlockSpec(memory_space=pltpu.VMEM)
    anywhere = pl.BlockSpec(memory_space=pl.ANY)
    shape = jax.ShapeDtypeStruct

    def full(array, number=1):
        return shape((number, count) + array.shape, array.dtype)

    ring = DMA((count // 2, 2, 3 + mats))
    return pl.pallas_call(
        functools.partial(forward_kernel, count, lax.axis_size("img") // 2, images, tile, mats),
        out_shape=[full(lat), full(wq), full(wk), full(shards[0], mats)]
        + [
            shape((latents, width), bf16),
            shape((latents, width), bf16),
            shape((latents, wk.shape[1]), f32),
            shape((CHANNELS, latents), bf16),
            shape((latents, CHANNELS), bf16),
            shape((2, count, wv.shape[0] // count, width // 2), bf16),
            shape((count, tall, rows), bf16),
            shape((count, 8, rows), f32),
        ],
        in_specs=[inside] * (10 + mats),
        out_specs=[inside] * 3 + [anywhere] + [inside] * 6 + [anywhere] * 2,
        scratch_shapes=[
            pltpu.VMEM((count, wv.shape[0] // count, width // 2), bf16),
            pltpu.VMEM((count - 1, wv.shape[0] // count, width // 2), bf16),
            pltpu.VMEM((CHANNELS + 16, latents), f32),
            pltpu.VMEM((8, latents), f32),
            pltpu.VMEM((images, sharers, tall, rows), bf16),
            pltpu.VMEM((images, sharers, 8, rows), f32),
            DMA((mats,)),
            ring,
            ring,
            ring,
            ring,
            DMA((2, count - 1)),
            DMA((2, count - 1)),
            DMA((2,)),
            DMA((max(lax.axis_size("img") // 2 - 1, 1), count // 2, 2, mats)),
            DMA((count // 2, 2, mats)),
            DMA((2,)),
            DMA((2, count)),
            DMA((2, count)),
        ],
        compiler_params=pltpu.CompilerParams(
            collective_id=collective_id, has_side_effects=True, vmem_limit_bytes=48 * 2**20
        ),
    )(values, hot_codes(tile), table, gained, gain_latent[None], lat, wq, wk, wv, wco, *shards)


def backward_kernel(
    count,
    teams,
    images,
    tile,
    channels,
    v_ref,
    code_ref,
    table_ref,
    gained_ref,
    at_ref,
    a_ref,
    back_ref,
    row_ref,
    gain_ref,
    xs_ref,
    gs_ref,
    t_out,
    g_out,
    z_out,
    pixel_ref,
    out_ref,
    t_raw,
    t_in,
    t_img,
    g_raw,
    g_in,
    g_img,
    z_own,
    t_acc,
    bt,
    b_low,
    stat,
    back_all,
    row_all,
    xv,
    gv,
    terms,
    held,
    across,
    done,
    load_sem,
    pair_send,
    pair_recv,
    send_sem,
    recv_sem,
    cross_send,
    cross_recv,
    out_sem,
    hand_send,
    hand_recv,
    back_send,
    back_recv,
    pass_send,
    foreign_send,
    foreign_recv,
    sum_send,
    sum_recv,
    img_send,
    img_recv,
    last_send,
    last_recv,
    z_send,
    z_recv,
    z_hand_send,
    z_hand_recv,
):
    number, rows, width = gs_ref.shape
    kinds = xs_ref.shape[0]
    owners = Owners(count, images)
    sharers = owners.sharers
    steps = v_ref.shape[2] // tile
    lines = tile // SIDE
    depth = xs_ref.shape[1] // count
    half, wide = width // 2, width // 4
    group, me = lax.axis_index("img"), lax.axis_index("pix")
    core, team = lax.rem(group, 2), group // 2
    place = ring_place(count)
    sides = ((group, ring_device(place + 1, count)), (group, ring_device(place - 1, count)))
    other = (group + 1 - 2 * core, me)
    partners = [(lax.rem(team + d, teams) * 2 + core, me) for d in range(1, teams)]
    crowd = 2 * teams
    others = peers(count)
    same_place = [(lax.rem(group + d, crowd), me) for d in range(1, crowd)]
    far = [
        (lax.rem(team + d, teams) * 2 + c, me) for d in range(1, teams) for c in range(2)
    ]
    greet(plane(count) + far)

    def send(source, target, sems, index, device):
        return pltpu.make_async_remote_copy(
            source,
            target,
            sems[0].at[index],
            sems[1].at[index],
            device_id=device,
            device_id_type=MESH,
        )

    def scatter(d):
        to, sems = others[d][1], (sum_send, sum_recv)
        return (
            send(t_raw.at[to], t_in.at[d], sems, (0, d), others[d]),
            send(g_raw.at[to], g_in.at[d], sems, (1, d), others[d]),
        )

    def over(d):
        sems = (img_send, img_recv)
        return (
            send(t_img.at[group], t_img.at[group], sems, (0, d), same_place[d]),
            send(g_img.at[group], g_img.at[group], sems, (1, d), same_place[d]),
        )

    def gather(d):
        sems = (last_send, last_recv)
        return (
            send(t_out.at[me], t_out.at[me], sems, (0, d), others[d]),
            send(g_out.at[me], g_out.at[me], sems, (1, d), others[d]),
        )

    def z_push(d):
        return send(z_own, z_out.at[core, me], (z_send, z_recv), d, others[d])

    def z_hand():
        return pltpu.make_async_remote_copy(
            z_out.at[core],
            z_out.at[core],
            z_hand_send,
            z_hand_recv,
            device_id=other,
            device_id_type=MESH,
        )

    for o in range(count):
        g_raw[o] = gain_ref[:, o * depth : (o + 1) * depth]

    own_index = owners.image * sharers + owners.slot

    def back_push(d):
        to = (owners.home, lax.rem(me + 2 * d, count))
        sems = lambda which: dict(
            send_sem=back_send.at[which, d],
            recv_sem=back_recv.at[which, own_index],
            device_id=to,
            device_id_type=MESH,
        )
        return to, (
            pltpu.make_async_remote_copy(back_ref, back_all.at[own_index], **sems(0)),
            pltpu.make_async_remote_copy(row_ref, row_all.at[own_index], **sems(1)),
        )

    def back_from(source):
        sems = lambda which: dict(
            send_sem=back_send.at[which, 0],
            recv_sem=back_recv.at[which, source],
            device_id=(group, me),
            device_id_type=MESH,
        )
        return (
            pltpu.make_async_remote_copy(back_ref, back_all.at[source], **sems(0)),
            pltpu.make_async_remote_copy(row_ref, row_all.at[source], **sems(1)),
        )

    def back_hand(block):
        to = (group, me + 1 - 2 * lax.rem(me, 2))
        sems = lambda which: dict(
            send_sem=pass_send.at[which, block],
            recv_sem=back_recv.at[which, block],
            device_id=to,
            device_id_type=MESH,
        )
        return (
            pltpu.make_async_remote_copy(back_all.at[block], back_all.at[block], **sems(0)),
            pltpu.make_async_remote_copy(row_all.at[block], row_all.at[block], **sems(1)),
        )

    def back_owner(image, slot):
        sender = owners.device(group, image, slot)
        return sender, lax.rem(sender[1], 2) == lax.rem(me, 2)

    for d in range(count // 2):
        to, copies = back_push(d)

        @pl.when(jnp.logical_not(owners.is_me(to)))
        def _():
            for copy in copies:
                copy.start()

        @pl.when(owners.is_me(to))
        def _():
            back_all[own_index] = back_ref[...]
            row_all[own_index] = row_ref[...]

    def load_x(j):
        return pltpu.make_async_copy(xs_ref.at[j], xv.at[j, core], load_sem.at[0, j])

    def load_g(k):
        part = gs_ref.at[k, :, pl.ds(pl.multiple_of(core * half, 128), half)]
        return pltpu.make_async_copy(part, gv.at[k, core], load_sem.at[1, k])

    def pair_x(j):
        return pltpu.make_async_remote_copy(
            xs_ref.at[j],
            xv.at[j, core],
            pair_send.at[0, j],
            pair_recv.at[0, j],
            device_id=other,
            device_id_type=MESH,
        )

    def pair_g(k):
        part = gs_ref.at[k, :, pl.ds(pl.multiple_of((1 - core) * half, 128), half)]
        return pltpu.make_async_remote_copy(
            part,
            gv.at[k, core],
            pair_send.at[1, k],
            pair_recv.at[1, k],
            device_id=other,
            device_id_type=MESH,
        )

    low, high = (4, 8) if number == 9 and count > 4 and 4 % teams == 0 else (0, 0)
    if teams == 1:
        low, high = 0, 0
    reach = count // 2

    def alone(k):
        return (k >= low) & (k < high)

    def at_home(k):
        return jnp.logical_not(alone(k)) | (lax.rem(k, teams) == team)

    def foreign(k, sender, way, stage):
        slot = (k // teams) * teams + sender
        rows_in = pl.ds((way * reach + stage) * depth, depth)
        return pltpu.make_async_remote_copy(
            terms.at[k, rows_in],
            held.at[slot, way, stage],
            foreign_send.at[way, stage, k],
            foreign_recv.at[sender, way, stage, k],
            device_id=(lax.rem(k, teams) * 2 + core, me),
            device_id_type=MESH,
        )

    pieces = [(way, stage) for way in range(2) for stage in range(reach)]
    order = [(i + low) % number for i in range(number)] if high else list(range(number))
    for k in order:
        j = max(k - (number - kinds), 0)
        if k == 0 or k > number - kinds:
            load_x(j).start()
            pair_x(j).start()
        load_g(k).start()
        pair_g(k).start()

    def turn(k):
        return lax.rem(k + number - 1, number)

    def owner_at(stage, way):
        ahead = reach - stage
        return ring_device(place + ahead if way == 0 else place - ahead, count)

    def rows_of(owner):
        return pl.ds(pl.multiple_of(owner * depth, depth), depth)

    def quarter(q):
        return slice(q * wide, (q + 1) * wide)

    def hop(k, stage, way, start=False):
        if start:
            source = terms.at[k, rows_of(owner_at(0, way)), quarter(way)]
            target = held.at[k, way, 0, :, quarter(way)]
        else:
            source = held.at[k, way, stage - 1]
            target = held.at[k, way, stage]
        return pltpu.make_async_remote_copy(
            source,
            target,
            send_sem.at[stage, way, k],
            recv_sem.at[stage, way, k],
            device_id=sides[way],
            device_id_type=MESH,
        )

    def cross(k, d):
        return pltpu.make_async_remote_copy(
            across.at[team, k],
            across.at[team, k],
            cross_send.at[d, k],
            cross_recv.at[d, k],
            device_id=partners[d],
            device_id_type=MESH,
        )

    @pl.loop(0, number)
    def _(i):
        k = lax.rem(i + low, number)
        j = jnp.maximum(k - (number - kinds), 0)

        @pl.when((k == 0) | (k > number - kinds))
        def _():
            load_x(j).wait()
            pair_x(j).wait_recv()

        load_g(k).wait()
        pair_g(k).wait_recv()
        for r in range(0, width, 256):
            piece = slice(r, r + 256)
            terms[k, piece, :] = (
                mm(xv[j, 0, piece, :], gv[k, 0]) + mm(xv[j, 1, piece, :], gv[k, 1])
            ).astype(bf16)

        @pl.when(jnp.logical_not(alone(k)))
        def _():
            for way in range(2):
                hop(k, 0, way, True).start()

        @pl.when(jnp.logical_not(at_home(k)))
        def _():
            for way, stage in pieces:
                foreign(k, team, way, stage).start()

    def launch(k):
        @pl.when(at_home(k))
        def _():
            for way, stage in pieces:
                here = pl.ds((way * reach + stage) * depth, depth)
                total = terms[k, here, :].astype(f32)
                for d in range(1, teams):
                    sender = lax.rem(team + d, teams)
                    foreign(k, sender, way, stage).wait_recv()
                    slot = (k // teams) * teams + sender
                    total = total + held[slot, way, stage].astype(f32)
                terms[k, here, :] = total.astype(bf16)
            for way in range(2):
                hop(k, 0, way, True).start()

    for block in range(count):
        sender, direct = back_owner(block // sharers, jnp.int32(block % sharers))

        @pl.when(direct)
        def _():
            @pl.when(jnp.logical_not(owners.is_me(sender)))
            def _():
                for copy in back_from(block):
                    copy.wait_recv()

            for copy in back_hand(block):
                copy.start()

    def relay(k, stage):
        for way in range(2):
            here = rows_of(owner_at(stage, way))

            @pl.when(stage == 1)
            def _():
                hop(k, 0, way, True).wait_recv()
                both = terms[k, here, quarter(way)].astype(f32)
                both = both + held[k, way, 0, :, quarter(way)].astype(f32)
                held[k, way, 0, :, quarter(way)] = both.astype(bf16)
                held[k, way, 0, :, quarter(1 - way)] = terms[k, here, quarter(1 - way)]

            @pl.when(stage > 1)
            def _():
                hop(k, stage - 1, way).wait_recv()
                both = terms[k, here, :].astype(f32) + held[k, way, stage - 1].astype(f32)
                held[k, way, stage - 1] = both.astype(bf16)

            hop(k, stage, way).start()

    def finish(k):
        columns = pl.ds(pl.multiple_of(core * half, 128), half)
        return pltpu.make_async_copy(done.at[k], out_ref.at[k, :, columns], out_sem.at[k])

    def hand(k):
        columns = pl.ds(pl.multiple_of(core * half, 128), half)
        return pltpu.make_async_remote_copy(
            done.at[k],
            out_ref.at[k, :, columns],
            hand_send.at[k],
            hand_recv.at[k],
            device_id=other,
            device_id_type=MESH,
        )

    def settle(k):
        for way in range(2):
            hop(k, reach - 1, way, reach == 1).wait_recv()
        total = terms[k, rows_of(me), :].astype(f32)
        for way in range(2):
            total = total + held[k, way, reach - 1].astype(f32)
        across[team, k] = total.astype(bf16)
        for d in range(teams - 1):
            cross(k, d).start()

    span_k = 3 if number % 3 == 0 else number
    groups = number // span_k
    events = reach * number

    def cross_from(k, d):
        return pltpu.make_async_remote_copy(
            across.at[team, k],
            across.at[team, k],
            cross_send.at[0, k],
            cross_recv.at[d, k],
            device_id=partners[0] if teams > 1 else other,
            device_id_type=MESH,
        )

    def complete(k):
        @pl.when(jnp.logical_not(alone(k)))
        def _():
            for d in range(teams - 1):
                cross(k, d).wait_recv()
            total = across[0, k].astype(f32)
            for t in range(1, teams):
                total = total + across[t, k].astype(f32)
            done[k] = total

        @pl.when(alone(k))
        def _():
            home = lax.rem(k, teams)

            @pl.when(home != team)
            def _():
                cross_from(k, lax.rem(team + 2 * teams - home - 1, teams)).wait_recv()

            done[k] = across[home, k].astype(f32)

        finish(k).start()
        hand(k).start()

        @pl.when(k == number - 1)
        def _():
            rows_here = t_raw.shape[1]
            mine = done[number - 1, rows_here : rows_here + z_own.shape[0], :].astype(bf16)
            z_own[...] = mine
            z_out[core, me] = mine
            for d in range(count - 1):
                z_push(d).start()

    def event(e):
        block, k = e // span_k, lax.rem(e, span_k)
        block = jnp.where(block == 0, 0, block + 1)
        g, slot = block // reach, lax.rem(block, reach)
        settles = (slot == 1) | (g == groups)

        @pl.when(settles)
        def _():
            one = turn((g - 1) * span_k + k)

            @pl.when(at_home(one))
            def _():
                settle(one)

            @pl.when(g > 1)
            def _():
                complete(turn((g - 2) * span_k + k))

        @pl.when(jnp.logical_not(settles))
        def _():
            one = turn(g * span_k + k)

            @pl.when(at_home(one))
            def _():
                relay(one, jnp.maximum(slot, 1))

            if high:

                @pl.when((g == 0) & (slot == reach - 1) & (k == span_k - 1))
                def _():
                    launch(jnp.int32(low))

                @pl.when((g == 1) & (slot == 2))
                def _():
                    launch(low + 1 + k)

    tiles = images * steps
    paced = tiles
    middle = (paced + events) // 2
    t_acc[...] = jnp.zeros_like(t_acc)

    @pl.loop(0, tiles)
    def _(t):
        image = lax.rem(t // steps + owners.image, images)
        step = lax.rem(t, steps)
        e = t

        @pl.when(t + 1 > e)
        def _():
            event(e)

        @pl.when(step == 0)
        def _():
            for h in range(sharers):
                source = image * sharers + h

                _, direct = back_owner(image, jnp.int32(h))

                @pl.when(jnp.logical_not(direct))
                def _():
                    for copy in back_from(source):
                        copy.wait_recv()

                here = slice(h * rows, (h + 1) * rows)
                wide = jnp.dot(
                    gained_ref[:, : back_ref.shape[0]],
                    back_all[source].astype(f32),
                    precision=lax.Precision.HIGHEST,
                    preferred_element_type=f32,
                )
                bt[:, here] = wide.astype(bf16)
                b_low[here, :] = wide.T.astype(bf16)
                stat[:, here] = row_all[source]

        span = pl.ds(pl.multiple_of(step * tile, 128), tile)
        values = v_ref[image, :, span]
        x, xt = build_both(values, step * lines, code_ref)
        halves = (slice(0, tile // 2), slice(tile // 2, tile))
        products = [(mm(x[half], at_ref[...]), mm(x[half], bt[...])) for half in halves]
        kept, ends = [], []
        for half, (scores, grad_p) in zip(halves, products):
            probs = jnp.exp2(scores - stat[0:1, :])
            grad_s = (probs * (grad_p - stat[1:2, :])).astype(bf16)
            kept.append(grad_s)
            back = mm(grad_s, a_ref[...]) + mm(probs.astype(bf16), b_low[...])
            along = jnp.sum(back * x[half].astype(f32), axis=1, keepdims=True)
            end = back[:, CHANNELS - 128 :]
            lane = lax.broadcasted_iota(jnp.int32, end.shape, 1)
            ends.append(jnp.where(lane == 120, along, end))
        t_acc[...] += mm(xt, jnp.concatenate(kept, axis=0))
        ends = jnp.concatenate(ends, axis=0).T[120:128, :] * (values[0:1, :] * values[1:2, :])
        hat = values[4:7, :] + values[7:8, :]
        mean_part = ends[7:8, :] + hat * ends[0:1, :]
        pixel_ref[image, :, span] = ends[4:7, :] - mean_part * (1.0 / channels)

    t_sum = lax.dot_general(
        t_acc[:CHANNELS, :],
        table_ref[:, : t_raw.shape[2]],
        (((0,), (0,)), ((), ())),
        precision=lax.Precision.HIGHEST,
        preferred_element_type=f32,
    )
    t_raw[...] = t_sum.astype(bf16).reshape(t_raw.shape)
    for d in range(count - 1):
        for copy in scatter(d):
            copy.start()

    pl.loop(paced, middle)(event)
    t_sum, g_sum = t_raw[me].astype(f32), g_raw[me]
    for d in range(count - 1):
        for copy in scatter(d):
            copy.wait_recv()
        t_sum = t_sum + t_in[d].astype(f32)
        g_sum = g_sum + g_in[d]
    t_img[group] = t_sum.astype(bf16)
    g_img[group] = g_sum
    for d in range(crowd - 1):
        for copy in over(d):
            copy.start()

    pl.loop(middle, events)(event)

    @pl.loop((groups - 1) * span_k, number)
    def _(k):
        complete(turn(k))

    for d in range(crowd - 1):
        for copy in over(d):
            copy.wait_recv()
    t_sum, g_sum = t_img[0].astype(f32), g_img[0]
    for i in range(1, crowd):
        t_sum = t_sum + t_img[i].astype(f32)
        g_sum = g_sum + g_img[i]
    t_out[me] = t_sum.astype(bf16)
    g_out[me] = g_sum
    for d in range(count - 1):
        for copy in gather(d):
            copy.start()
    for d in range(count - 1):
        z_push(d).wait()
    z_hand().start()
    for d in range(count - 1):
        for copy in gather(d):
            copy.wait()
        for copy in scatter(d):
            copy.wait_send()
    for d in range(crowd - 1):
        for copy in over(d):
            copy.wait_send()
    z_hand().wait()

    @pl.loop(0, number)
    def _(k):
        finish(k).wait()
        hand(k).wait()
        pair_g(k).wait_send()

        @pl.when(at_home(k))
        def _():
            for way in range(2):
                for stage in range(reach):
                    hop(k, stage, way, stage == 0).wait_send()
            for d in range(teams - 1):
                cross(k, d).wait_send()

        @pl.when(jnp.logical_not(at_home(k)))
        def _():
            for way, stage in pieces:
                foreign(k, team, way, stage).wait_send()

    @pl.loop(0, kinds)
    def _(j):
        pair_x(j).wait_send()

    for d in range(count // 2):
        to, copies = back_push(d)

        @pl.when(jnp.logical_not(owners.is_me(to)))
        def _():
            for copy in copies:
                copy.wait_send()

    for block in range(count):
        _, direct = back_owner(block // sharers, jnp.int32(block % sharers))

        @pl.when(direct)
        def _():
            for copy in back_hand(block):
                copy.wait_send()


def backward_pass(
    values, table, gained, at, a, back, rows_in, gains, xs, gs, channels, collective_id
):
    count = lax.axis_size("pix")
    teams = lax.axis_size("img") // 2
    kinds, _, rows = xs.shape
    number, _, width = gs.shape
    depth = xs.shape[1] // count
    anywhere = pl.BlockSpec(memory_space=pl.ANY)
    inside = pl.BlockSpec(memory_space=pltpu.VMEM)
    chunk = (depth, width // 2)
    images, _, pixels = values.shape
    tile = pixel_tile(pixels)
    latents = at.shape[1]
    tall = back.shape[0]
    shape = jax.ShapeDtypeStruct
    rows_here = latents // count
    t_shape = shape((count, rows_here, -(-channels // 128) * 128), bf16)
    g_shape = shape((count, 8, depth), f32)
    spare = min(-(-share_rows(channels, count) // 16) * 16, depth - rows_here)
    return pl.pallas_call(
        functools.partial(backward_kernel, count, teams, images, tile, channels),
        out_shape=[
            t_shape,
            g_shape,
            shape((2, count, spare, width // 2), bf16),
            shape((images, 3, pixels), f32),
            shape((number, depth, width), f32),
        ],
        in_specs=[inside] * 9 + [anywhere] * 2,
        out_specs=[inside] * 4 + [anywhere],
        scratch_shapes=[
            pltpu.VMEM(t_shape.shape, bf16),
            pltpu.VMEM((count - 1,) + t_shape.shape[1:], bf16),
            pltpu.VMEM((2 * teams,) + t_shape.shape[1:], bf16),
            pltpu.VMEM(g_shape.shape, f32),
            pltpu.VMEM((count - 1,) + g_shape.shape[1:], f32),
            pltpu.VMEM((2 * teams,) + g_shape.shape[1:], f32),
            pltpu.VMEM((spare, width // 2), bf16),
            pltpu.VMEM((CHANNELS + 16, latents), f32),
            pltpu.VMEM((CHANNELS, latents), bf16),
            pltpu.VMEM((latents, CHANNELS), bf16),
            pltpu.VMEM((8, latents), f32),
            pltpu.VMEM((count, tall, rows), bf16),
            pltpu.VMEM((count, 8, rows), f32),
            pltpu.VMEM((kinds, 2, xs.shape[1], rows), bf16),
            pltpu.VMEM((number, 2, rows, width // 2), bf16),
            pltpu.VMEM((number, xs.shape[1], width // 2), bf16),
            pltpu.VMEM((number, 2, count // 2) + chunk, bf16),
            pltpu.VMEM((teams, number) + chunk, bf16),
            pltpu.VMEM((number, depth, width // 2), f32),
            DMA((2, number)),
            DMA((2, number)),
            DMA((2, number)),
            DMA((count // 2, 2, number)),
            DMA((count // 2, 2, number)),
            DMA((teams - 1, number)),
            DMA((teams - 1, number)),
            DMA((number,)),
            DMA((number,)),
            DMA((number,)),
            DMA((2, count)),
            DMA((2, count)),
            DMA((2, count)),
            DMA((2, count // 2, number)),
            DMA((teams, 2, count // 2, number)),
            DMA((2, count - 1)),
            DMA((2, count - 1)),
            DMA((2, 2 * teams - 1)),
            DMA((2, 2 * teams - 1)),
            DMA((2, count - 1)),
            DMA((2, count - 1)),
            DMA((count - 1,)),
            DMA((count - 1,)),
            DMA,
            DMA,
        ],
        compiler_params=pltpu.CompilerParams(
            collective_id=collective_id, has_side_effects=True, vmem_limit_bytes=60 * 2**20
        ),
    )(values, hot_codes(tile), table, gained, at, a, back, rows_in, gains, xs, gs)


def peers(count):
    group, me = lax.axis_index("img"), lax.axis_index("pix")
    return [(group, lax.rem(me + d, count)) for d in range(1, count)]


def plane(count):
    group, me = lax.axis_index("img"), lax.axis_index("pix")
    other = group + 1 - 2 * lax.rem(group, 2)
    return peers(count) + [(other, lax.rem(me + d, count)) for d in range(count)]


class Owners:
    def __init__(self, count, images):
        self.group, self.me = lax.axis_index("img"), lax.axis_index("pix")
        self.core = lax.rem(self.group, 2)
        self.base = self.group - self.core
        self.images = images
        self.chips = count // (2 * images)
        self.sharers = 2 * self.chips
        self.slot = lax.rem(self.me, self.chips) * 2 + self.core
        image = self.me // self.chips
        self.image = lax.rem(image, images)
        self.home = self.base + image // images

    def device(self, group, image, slot):
        core = lax.rem(group, 2)
        chip = (core * self.images + image) * self.chips + slot // 2
        return self.base + lax.rem(slot, 2), chip

    def is_me(self, device):
        return (device[0] == self.group) & (device[1] == self.me)


def share_rows(channels, count):
    channels = -(-channels // 16) * 16
    return -(-(-(-channels // count)) // 8) * 8


def gelu_parts(z):
    slope = (2.0 / jnp.pi) ** 0.5
    square = z * z
    bend = jnp.tanh(slope * z * (1.0 + 0.044715 * square))
    half = 0.5 * (1.0 + bend)
    return z * half, half + 0.5 * z * (1.0 - bend * bend) * slope * (1.0 + 0.134145 * square)


def latent_kernel(
    count,
    images,
    part_ref,
    stat_ref,
    own_ref,
    cot_ref,
    mix_ref,
    gain_ref,
    in_gain_ref,
    w_ref,
    late_down,
    out_ref,
    xs_ref,
    gs_ref,
    back_ref,
    row_ref,
    gain_out,
    wv,
    one,
    two,
    three,
    pre,
    grad,
    flow,
    low,
    heads_q,
    kv,
    probs,
    kv_out,
    kv_in,
    cot,
    final,
    mean,
    own_v,
    own_sem,
    w_sem,
    ring_own,
    ring_send,
    ring_recv,
    hand_send,
    hand_recv,
    kv_send,
    kv_recv,
    gkv_send,
    gkv_recv,
    cot_own,
    cot_send,
    cot_recv,
    out_own,
    out_send,
    out_recv,
):
    rows, width = one.shape
    depth = width // count
    owners = Owners(count, images)
    sharers = owners.sharers
    latents = rows * sharers
    per = count // sharers
    rows_here = latents // count
    spare = depth - rows_here
    group, me = lax.axis_index("img"), lax.axis_index("pix")
    slot, image, home = owners.slot, owners.image, owners.home
    block = 256
    blocks = width // block
    row_block = min(rows, 64)
    up_one, down_one, m_query, m_key, m_value, m_out, up_two, down_two = range(8)
    scale = HEAD_DIM ** (-0.5)

    def load(k):
        return pltpu.make_async_copy(w_ref.at[k], wv.at[k], w_sem.at[k])

    early, late_refs = w_ref.shape[0], (late_down,)
    late = len(late_refs)
    own_copy = pltpu.make_async_copy(
        own_ref.at[pl.ds(pl.multiple_of(slot * rows, 16), rows)], own_v, own_sem
    )
    own_copy.start()
    for k in range(early):
        load(k).start()
    greet(plane(count))

    core = lax.rem(group, 2)
    ring = ring_place(count)
    sides = ((group, ring_device(ring + 1, count)), (group, ring_device(ring - 1, count)))
    other = (group + 1 - 2 * core, me)

    reach = count // 2

    def spot(k, stage, way, last, source=False):
        begin = (core * 2 + way) * (width // 4) if last else core * (width // 2)
        some = pl.ds(pl.multiple_of(begin, 128), width // 4 if last else width // 2)
        if source:
            return late_refs[k].at[:, some]
        origin = ring_device(ring - stage if way == 0 else ring + stage, count)
        here = pl.ds(pl.multiple_of(origin * depth, depth), depth)
        return wv.at[early + k, here, some]

    def hop(k, stage, way, start=False, last=False):
        return pltpu.make_async_remote_copy(
            spot(k, stage, way, last, start),
            spot(k, stage, way, last),
            ring_send.at[stage, way, k],
            ring_recv.at[stage, way, k],
            device_id=sides[way],
            device_id_type=MESH,
        )

    def hand(k, stage, way, last=False):
        return pltpu.make_async_remote_copy(
            spot(k, stage, way, last),
            spot(k, stage, way, last),
            hand_send.at[stage - 1, way, k],
            hand_recv.at[stage - 1, way, k],
            device_id=other,
            device_id_type=MESH,
        )

    def ring_keep(k):
        here = pl.ds(pl.multiple_of(me * depth, depth), depth)
        return pltpu.make_async_copy(late_refs[k], wv.at[early + k, here], ring_own.at[k])

    for k in range(late):
        for way in range(2):
            hop(k, 0, way, True, reach == 1).start()
        ring_keep(k).start()

    def relays(first, end):
        for stage in range(first, min(end, reach + 1)):
            for k in range(late):
                for way in range(2):
                    last = stage == reach
                    hop(k, stage - 1, way, last=last).wait_recv()
                    if stage < reach:
                        hop(k, stage, way, last=stage == reach - 1).start()
                    hand(k, stage, way, last).start()

    def arrived(k):
        ring_keep(k).wait()
        for stage in range(1, reach + 1):
            for way in range(2):
                hand(k, stage, way, stage == reach).wait_recv()

    def cot_push(i):
        to = owners.device(group, i, me // per)
        return to, pltpu.make_async_remote_copy(
            cot_ref.at[i],
            cot.at[lax.rem(me, per)],
            cot_send.at[i],
            cot_recv.at[lax.rem(me, per)],
            device_id=to,
            device_id_type=MESH,
        )

    def cot_keep():
        return pltpu.make_async_copy(cot_ref.at[image], cot.at[lax.rem(me, per)], cot_own)

    for i in range(images):
        to, copy = cot_push(i)

        @pl.when(jnp.logical_not(owners.is_me(to)))
        def _():
            copy.start()

        @pl.when(owners.is_me(to))
        def _():
            cot_keep().start()

    def columns(j, wide=block):
        return pl.ds(pl.multiple_of(j * wide, wide), wide)

    def over_columns(body, times=blocks):
        pl.loop(0, times)(body)

    def over_rows(body):
        @pl.loop(0, rows // row_block)
        def _(r):
            body(pl.ds(pl.multiple_of(r * row_block, 16), row_block))

    def put_x(j, c, value):
        xs_ref[j, columns(c), :] = value.T

    def centre(rows_f32):
        average = jnp.mean(rows_f32, axis=1, keepdims=True)
        centred = rows_f32 - average
        spread = jnp.mean(centred * centred, axis=1, keepdims=True)
        scale_rows = lax.rsqrt(spread + eps)
        return centred * scale_rows, scale_rows

    def norm(source, k, target):
        def body(r):
            target[r] = (centre(source[r])[0] * gain_ref[k : k + 1, :]).astype(bf16)

        over_rows(body)

    def norm_grad(source, k):
        def body(r):
            hat, scale_rows = centre(source[r])
            given = flow[r]
            gain_out[k : k + 1, :] += jnp.sum(given * hat, axis=0, keepdims=True)
            given = given * gain_ref[k : k + 1, :]
            along = jnp.mean(given * hat, axis=1, keepdims=True)
            grad[r] += scale_rows * (given - jnp.mean(given, axis=1, keepdims=True) - hat * along)

        over_rows(body)

    gain_out[...] = jnp.zeros_like(gain_out)

    top = jnp.max(stat_ref[:, 0:1, :], axis=0)
    total = jnp.zeros_like(top)
    for d in range(count):
        total = total + jnp.exp2(stat_ref[d, 0:1, :] - top) * stat_ref[d, 1:2, :]
    raw = jnp.zeros(part_ref.shape[1:], f32)
    for d in range(count):
        raw = raw + part_ref[d].astype(f32) * (jnp.exp2(stat_ref[d, 0:1, :] - top) / total)
    mean[0] = raw
    mean[1] = raw * in_gain_ref[...]
    row_ref[...] = jnp.zeros_like(row_ref)
    row_ref[0:1, :] = top + jnp.log(total) * LOG2E

    tall = count * spare
    mean_tall = mean[1]
    if tall > mean_tall.shape[0]:
        mean_tall = jnp.concatenate(
            [mean_tall, jnp.zeros((tall - mean_tall.shape[0], rows), f32)], axis=0
        )
    share = share_rows(mean.shape[1], count)
    place = lax.broadcasted_iota(jnp.int32, (rows_here, rows), 0)
    source_row = lax.broadcasted_iota(jnp.int32, (rows_here, rows), 1) + slot * rows
    for o in range(count):
        picks = jnp.where(place + o * rows_here == source_row, 1.0, 0.0)
        piece = [picks, mean_tall[o * share : (o + 1) * share]]
        if spare > share:
            piece.append(jnp.zeros((spare - share, rows), f32))
        xs_ref[6, o * depth : (o + 1) * depth, :] = jnp.concatenate(piece, axis=0).astype(bf16)

    mean_low = mean[1].astype(bf16)

    def make_one(j):
        one[:, columns(j)] = own_v[:, columns(j)].astype(f32) + mm_tn(
            mean_low,
            mix_ref[j // (blocks // 2), : mean.shape[1], columns(lax.rem(j, blocks // 2))],
        )

    own_copy.wait()
    over_columns(make_one)

    def ready(k):
        if k < early:
            load(k).wait()
        else:
            arrived(k - early)

    def feed(source, target, k, up, down, normed, x_hidden, keep):
        norm(source, k, normed)
        ready(up)

        def make_hidden(j):
            value = mm_nt(normed[...], wv[up, columns(j), :])
            pre[keep, :, columns(j)] = value
            hidden = gelu_parts(value)[0].astype(bf16)
            low[:, columns(j)] = hidden
            put_x(x_hidden, j, hidden)

        over_columns(make_hidden)
        if down >= early:
            relays(4, reach + 1)
        ready(down)

        def make_branch(j):
            value = source[:, columns(j)] + mm(low[...], wv[down, :, columns(j)])
            target[:, columns(j)] = value.astype(target.dtype)

        over_columns(make_branch)

    def feed_back(source, k, up, down, branch, x_pre, keep):
        @over_columns
        def _(j):
            value = mm_nt(branch[...], wv[down, columns(j), :])
            value = (value * gelu_parts(pre[keep, :, columns(j)])[1]).astype(bf16)
            low[:, columns(j)] = value
            put_x(x_pre, j, value)

        @over_columns
        def _(j):
            flow[:, columns(j)] = mm(low[...], wv[up, :, columns(j)])

        norm_grad(source, k)

    feed(one, two, 0, up_one, down_one, gs_ref.at[4], 3, 0)
    relays(1, 2)

    norm(two, 1, low)

    load(m_key).wait()
    load(m_value).wait()

    def make_kv(j):
        put_x(0, j, low[:, columns(j)])
        kv[0, slot, :, columns(j)] = mm(low[...], wv[m_key, :, columns(j)]).astype(bf16)
        kv[1, slot, :, columns(j)] = mm(low[...], wv[m_value, :, columns(j)]).astype(bf16)

    over_columns(make_kv)

    def sharer(d):
        return owners.device(home, image, lax.rem(slot + d, sharers))

    def kv_push(d):
        return pltpu.make_async_remote_copy(
            kv.at[:, slot],
            kv.at[:, slot],
            kv_send.at[d - 1],
            kv_recv.at[d - 1],
            device_id=sharer(d),
            device_id_type=MESH,
        )

    for d in range(1, sharers):
        kv_push(d).start()
    load(m_query).wait()

    @over_columns
    def _(j):
        heads_q[:, columns(j)] = mm(low[...], wv[m_query, :, columns(j)]).astype(bf16)

    for d in range(1, sharers):
        kv_push(d).wait_recv()

    def attend(h):
        c = columns(h, HEAD_DIM)
        k_all = kv[0, :, :, c].reshape(latents, HEAD_DIM)
        v_all = kv[1, :, :, c].reshape(latents, HEAD_DIM)
        scores = mm_nt(heads_q[:, c], k_all) * scale
        shifted = jnp.exp(scores - jnp.max(scores, axis=1, keepdims=True))
        p = shifted / jnp.sum(shifted, axis=1, keepdims=True)
        probs[h] = p
        low[:, c] = mm(p.astype(bf16), v_all).astype(bf16)

    pl.loop(0, HEADS // 2)(attend)
    relays(2, 3)
    pl.loop(HEADS // 2, HEADS)(attend)
    relays(3, 4)

    @over_columns
    def _(j):
        put_x(1, j, low[:, columns(j)])

    ready(m_out)

    @over_columns
    def _(j):
        three[:, columns(j)] = two[:, columns(j)] + mm(low[...], wv[m_out, :, columns(j)])

    feed(three, final, 2, up_two, down_two, gs_ref.at[6], 5, 1)

    def out_push(b):
        to = (home, slot * per + b)
        return to, pltpu.make_async_remote_copy(
            final.at[pl.ds(b * rows_here, rows_here)],
            out_ref.at[image],
            out_send.at[b],
            out_recv.at[image],
            device_id=to,
            device_id_type=MESH,
        )

    def out_keep():
        mine = pl.ds(pl.multiple_of(lax.rem(me, per) * rows_here, 16), rows_here)
        return pltpu.make_async_copy(final.at[mine], out_ref.at[image], out_own)

    for b in range(per):
        to, copy = out_push(b)

        @pl.when(jnp.logical_not(owners.is_me(to)))
        def _():
            copy.start()

        @pl.when(owners.is_me(to))
        def _():
            out_keep().start()

    def cot_from(b):
        return pltpu.make_async_remote_copy(
            cot_ref.at[0],
            cot.at[b],
            cot_send.at[0],
            cot_recv.at[b],
            device_id=(group, me),
            device_id_type=MESH,
        )

    for b in range(per):

        local = owners.is_me((home, slot * per + b))

        @pl.when(jnp.logical_not(local))
        def _():
            cot_from(b).wait_recv()

        @pl.when(local)
        def _():
            cot_keep().wait()

    given = cot[...].reshape(rows, width)
    gs_ref[7] = given
    grad[...] = given.astype(f32)
    feed_back(three, 2, up_two, down_two, gs_ref.at[7], 4, 1)

    gs_ref[3] = grad[...].astype(bf16)

    @over_columns
    def _(j):
        low[:, columns(j)] = mm_nt(gs_ref[3], wv[m_out, columns(j), :]).astype(bf16)

    @pl.loop(0, HEADS)
    def _(h):
        c = columns(h, HEAD_DIM)
        k_all = kv[0, :, :, c].reshape(latents, HEAD_DIM)
        v_all = kv[1, :, :, c].reshape(latents, HEAD_DIM)
        p = probs[h]
        g_mixed = low[:, c]
        g_p = mm_nt(g_mixed, v_all)
        g_v = mm_tn(p.astype(bf16), g_mixed)
        delta = jnp.sum(p * g_p, axis=1, keepdims=True)
        g_s = (p * (g_p - delta)).astype(bf16)
        gs_ref[0, :, c] = (mm(g_s, k_all) * scale).astype(bf16)
        g_k = mm_tn(g_s, heads_q[:, c]) * scale
        kv_out[:, 0, :, c] = g_k.reshape(sharers, rows, HEAD_DIM).astype(bf16)
        kv_out[:, 1, :, c] = g_v.reshape(sharers, rows, HEAD_DIM).astype(bf16)

    def gkv_push(d):
        to = lax.rem(slot + d, sharers)
        return pltpu.make_async_remote_copy(
            kv_out.at[to],
            kv_in.at[d - 1],
            gkv_send.at[d - 1],
            gkv_recv.at[d - 1],
            device_id=sharer(d),
            device_id_type=MESH,
        )

    for d in range(1, sharers):
        gkv_push(d).start()

    @over_columns
    def _(j):
        flow[:, columns(j)] = mm_nt(gs_ref[0], wv[m_query, columns(j), :])

    for d in range(1, sharers):
        gkv_push(d).wait_recv()
    for which in range(2):

        @over_columns
        def _(j):
            value = kv_out[slot, which, :, columns(j)].astype(f32)
            for d in range(1, sharers):
                value = value + kv_in[d - 1, which, :, columns(j)].astype(f32)
            gs_ref[1 + which, :, columns(j)] = value.astype(bf16)

    @over_columns
    def _(j):
        flow[:, columns(j)] += mm_nt(gs_ref[1], wv[m_key, columns(j), :]) + mm_nt(
            gs_ref[2], wv[m_value, columns(j), :]
        )

    norm_grad(two, 1)
    gs_ref[5] = grad[...].astype(bf16)
    feed_back(one, 0, up_one, down_one, gs_ref.at[5], 2, 0)
    gs_ref[8] = grad[...].astype(bf16)
    half = width // 2
    back = mm_nt(mix_ref[0, : mean.shape[1], :], gs_ref[8, :, :half])
    back = back + mm_nt(mix_ref[1, : mean.shape[1], :], gs_ref[8, :, half:])
    back_ref[...] = back.astype(bf16)
    row_ref[1:2, :] = jnp.sum(back * mean[1], axis=0, keepdims=True)
    in_gain = jnp.broadcast_to(
        jnp.sum(back * mean[0], axis=1, keepdims=True), (back.shape[0], 128)
    )
    gain_out[3:4, : back.shape[0]] = in_gain.T[0:1, :]

    for i in range(images):
        to, copy = cot_push(i)

        @pl.when(jnp.logical_not(owners.is_me(to)))
        def _():
            copy.wait_send()

    for d in range(1, sharers):
        kv_push(d).wait_send()
        gkv_push(d).wait_send()
    for k in range(late):
        for stage in range(reach):
            for way in range(2):
                last = stage == reach - 1
                hop(k, stage, way, stage == 0, last).wait_send()
                hand(k, stage + 1, way, last).wait_send()

    def out_from(i):
        return pltpu.make_async_remote_copy(
            final.at[pl.ds(0, rows_here)],
            out_ref.at[i],
            out_send.at[0],
            out_recv.at[i],
            device_id=(group, me),
            device_id_type=MESH,
        )

    for b in range(per):
        to, copy = out_push(b)

        @pl.when(jnp.logical_not(owners.is_me(to)))
        def _():
            copy.wait_send()

    for i in range(images):
        local = owners.is_me(owners.device(group, i, me // per))

        @pl.when(jnp.logical_not(local))
        def _():
            out_from(i).wait_recv()

        @pl.when(local)
        def _():
            out_keep().wait()


def latent_pass(parts, stats, own, cotangent, mix, gains, in_gain, whole, late, rows, collective_id):
    count = lax.axis_size("pix")
    images, rows_here, width = cotangent.shape
    channels = parts.shape[1]
    sharers = count // images
    per = count // sharers
    inside = pl.BlockSpec(memory_space=pltpu.VMEM)
    anywhere = pl.BlockSpec(memory_space=pl.ANY)
    whole_f32 = pltpu.VMEM((rows, width), f32)
    whole_low = pltpu.VMEM((rows, width), bf16)
    ring = DMA((count // 2, 2, len(late)))
    shape = jax.ShapeDtypeStruct
    return pl.pallas_call(
        functools.partial(latent_kernel, count, images),
        out_shape=[
            shape((images, rows_here, width), bf16),
            shape((7, width, rows), bf16),
            shape((9, rows, width), bf16),
            shape((channels, rows), bf16),
            shape((8, rows), f32),
            shape((8, width), f32),
        ],
        in_specs=[inside] * 2 + [anywhere] * 2 + [inside] * 3 + [anywhere] * 2,
        out_specs=[anywhere] + [inside] * 5,
        scratch_shapes=[
            pltpu.VMEM((8, width, width), bf16),
            whole_f32,
            whole_f32,
            whole_f32,
            pltpu.VMEM((2, rows, width), f32),
            whole_f32,
            whole_f32,
            whole_low,
            whole_low,
            pltpu.VMEM((2, sharers, rows, width), bf16),
            pltpu.VMEM((HEADS, rows, rows * sharers), f32),
            pltpu.VMEM((sharers, 2, rows, width), bf16),
            pltpu.VMEM((max(sharers - 1, 1), 2, rows, width), bf16),
            pltpu.VMEM((per, rows_here, width), bf16),
            whole_low,
            pltpu.VMEM((2, channels, rows), f32),
            whole_low,
            DMA,
            DMA((whole.shape[0],)),
            DMA((len(late),)),
            ring,
            ring,
            ring,
            ring,
            DMA((sharers,)),
            DMA((sharers,)),
            DMA((sharers,)),
            DMA((sharers,)),
            DMA,
            DMA((images,)),
            DMA((per,)),
            DMA,
            DMA((per,)),
            DMA((images,)),
        ],
        compiler_params=pltpu.CompilerParams(
            collective_id=collective_id, has_side_effects=True, vmem_limit_bytes=60 * 2**20
        ),
    )(parts, stats, own, cotangent, mix, gains, in_gain, whole, *late)


def tail_kernel(
    count,
    channels,
    t_ref,
    g_ref,
    z_ref,
    a_ref,
    lat_ref,
    qcols_ref,
    ncols_ref,
    wq_ref,
    wk_ref,
    wv_ref,
    wco_ref,
    gain_ref,
    lat_gain_ref,
    sum_ref,
    lat_out,
    lat_gain_out,
    gains_out,
    wq_out,
    wk_out,
    wv_out,
    wco_out,
    up_one_out,
    up_two_out,
    down_one_out,
    down_two_out,
    sq_out,
    sk_out,
    sv_out,
    so_out,
    z_v,
    query_grad,
    flow,
):
    me = lax.axis_index("pix")
    width = wq_ref.shape[0]
    depth = wco_ref.shape[0]
    rows_here = lat_out.shape[0]
    latents = lat_ref.shape[0]
    across = t_ref.shape[1]
    for k, to in (
        (0, sq_out),
        (1, sk_out),
        (2, sv_out),
        (3, so_out),
        (5, down_one_out),
        (7, down_two_out),
    ):
        to[...] = sum_ref[k]
    t = t_ref[...].astype(f32)
    tx = (t * (gain_ref[...] * width ** (-0.5))).astype(bf16)
    for o in range(count):
        gains_out[:, o * depth : (o + 1) * depth] = g_ref[o]
    row = jnp.sum(a_ref[:, :across] * t, axis=0, keepdims=True)
    gains_out[3:4, :across] += row
    wk_out[...] = mm_tn(tx, qcols_ref[...])[:channels]

    @pl.loop(0, width // 256)
    def _(j):
        columns = pl.ds(pl.multiple_of(j * 256, 256), 256)
        query_grad[:, columns] = mm_nt(tx, wk_ref[columns, :across]).astype(bf16)

    @pl.loop(0, width // 256)
    def _(j):
        columns = pl.ds(pl.multiple_of(j * 256, 256), 256)
        wq_out[:, columns] = mm_tn(ncols_ref[...], query_grad[:, columns])
        flow[:, columns] = mm_nt(query_grad[...], wq_ref[columns, :])

    share = share_rows(channels, count)
    half = width // 2
    for o in range(count):
        for h in range(2):
            z_v[o * share : (o + 1) * share, h * half : (h + 1) * half] = z_ref[h, o, :share].astype(f32)
    cross = z_v[...].astype(bf16)
    wv_out[...] = mm_nt(cross, wco_ref[...])[:channels]
    wco_out[...] = mm_tn(wv_ref[...], cross)

    up_one_out[...] = sum_ref[4].T
    up_two_out[...] = sum_ref[6].T
    lat_gain_out[...] = jnp.zeros_like(lat_gain_out)

    @pl.loop(0, count)
    def _(o):
        here = pl.ds(pl.multiple_of(o * rows_here, rows_here), rows_here)
        rows = lat_ref[here, :].astype(f32)
        average = jnp.mean(rows, axis=1, keepdims=True)
        centred = rows - average
        scale = lax.rsqrt(jnp.mean(centred * centred, axis=1, keepdims=True) + eps)
        hat = centred * scale
        given = flow[here, :]
        lat_gain_out[...] += jnp.sum(given * hat, axis=0, keepdims=True)

        @pl.when(o == me)
        def _():
            gained = given * lat_gain_ref[...]
            along = jnp.mean(gained * hat, axis=1, keepdims=True)
            moved = scale * (gained - jnp.mean(gained, axis=1, keepdims=True) - hat * along)
            lat_out[...] = moved + sum_ref[8, :rows_here, :]


def tail_pass(t, g, z, a, lat, qcols, ncols, wq, wk, wv, wco, gain, lat_gain, summed, channels):
    count = z.shape[1]
    _, depth, width = summed.shape
    latents = lat.shape[0]
    share = share_rows(channels, count)
    inside = pl.BlockSpec(memory_space=pltpu.VMEM)
    anywhere = pl.BlockSpec(memory_space=pl.ANY)
    shape = lambda *dims: jax.ShapeDtypeStruct(dims, f32)
    plain = shape(depth, width)
    return pl.pallas_call(
        functools.partial(tail_kernel, count, channels),
        out_shape=[
            shape(latents // count, width),
            shape(1, width),
            shape(8, width),
            plain,
            shape(channels, depth),
            shape(channels, depth),
            plain,
            shape(width, depth),
            shape(width, depth),
        ]
        + [plain] * 6,
        in_specs=[inside] * 14,
        out_specs=[inside] * 15,
        scratch_shapes=[
            pltpu.VMEM((count * share, width), f32),
            pltpu.VMEM((latents, width), bf16),
            pltpu.VMEM((latents, width), f32),
        ],
        compiler_params=pltpu.CompilerParams(vmem_limit_bytes=48 * 2**20),
    )(t, g, z, a, lat, qcols, ncols, wq, wk, wv, wco, gain, lat_gain, summed)


def local(
    rgb_pixels,
    keep_mask,
    latent_array,
    gain_input,
    gain_latent,
    w_query,
    w_key,
    w_value,
    w_cross_out,
    gain_mlp_one,
    w_up_one,
    w_down_one,
    gain_self,
    w_self_query,
    w_self_key,
    w_self_value,
    w_self_out,
    gain_mlp_two,
    w_up_two,
    w_down_two,
    cotangent,
):
    images, _, pixels = rgb_pixels.shape
    rows_here, width = latent_array.shape
    count = lax.axis_size("pix")
    me = lax.axis_index("pix")
    latents = rows_here * count
    sharers = count // images
    rows_own = latents // sharers
    depth = w_query.shape[0]
    channels = gain_input.shape[0]
    tall = -(-channels // 16) * 16

    side = -(-channels // 512) * 512
    key_t = jnp.pad(w_key.T, ((0, 0), (0, side - channels)))
    blocks = -(-tall // (16 * count)) * 16 * count
    value_pad = jnp.pad(w_value, ((0, blocks - channels), (0, 0)))
    shards = [
        w_up_one.T,
        w_down_one,
        w_self_query,
        w_self_key,
        w_self_value,
        w_self_out,
        w_up_two.T,
    ]
    late = [w_down_two]

    lines = pixels // SIDE
    u, sin_u, cos_u = angles(me * lines + lax.iota(jnp.int32, lines))
    w, sin_w, cos_w = angles(lax.iota(jnp.int32, SIDE))

    def zeros(rows, columns):
        return jnp.zeros((rows, columns), f32)

    pad = CHANNELS - 4 - SIDE - lines
    table = jnp.concatenate(
        [
            jnp.concatenate(
                [zeros(SIDE, 4), w, zeros(SIDE, BANDS), sin_w, zeros(SIDE, BANDS), cos_w], axis=1
            ),
            jnp.concatenate(
                [zeros(lines, 3), u, zeros(lines, 1), sin_u, zeros(lines, BANDS), cos_u, zeros(lines, BANDS)],
                axis=1,
            ),
            zeros(pad, channels),
            jnp.eye(3, channels, dtype=f32),
            jnp.ones((1, channels), f32),
        ],
        axis=0,
    )
    row_sum = u[:, 0] + jnp.sum(sin_u + cos_u, axis=1)
    col_sum = w[:, 0] + jnp.sum(sin_w + cos_w, axis=1)
    row_square = u[:, 0] ** 2 + jnp.sum(sin_u**2 + cos_u**2, axis=1)
    col_square = w[:, 0] ** 2 + jnp.sum(sin_w**2 + cos_w**2, axis=1)
    feature_sum = (row_sum[:, None] + col_sum[None, :]).reshape(1, pixels)
    feature_square = (row_square[:, None] + col_square[None, :]).reshape(1, pixels)
    colours = rgb_pixels.astype(f32)
    average = (jnp.sum(colours, axis=1) + feature_sum) / channels
    spread = (jnp.sum(colours**2, axis=1) + feature_square) / channels - average**2
    scale = lax.rsqrt(spread + eps)
    keep = keep_mask.astype(f32)

    own_values = jnp.concatenate([colours, -average[:, None, :]], axis=1) * scale[:, None, :]
    values = jnp.concatenate(
        [scale[:, None], keep[:, None], jnp.zeros((images, 2, pixels), f32), own_values], axis=1
    )
    table = jnp.pad(table, ((0, 0), (0, side - channels)))
    gained = table * jnp.pad(gain_input, (0, side - channels))[None, :]
    (
        latent_full,
        query_mat,
        key_full,
        whole,
        latent_normed,
        queries,
        score_mat,
        at,
        a_low,
        value_out,
        raw_parts,
        stat_parts,
    ) = forward_pass(
        values,
        table,
        gained,
        gain_latent,
        latent_array,
        w_query,
        key_t,
        value_pad,
        w_cross_out,
        shards,
        tall,
        0,
    )
    latent_full = latent_full.reshape(latents, width)
    whole = whole.reshape(-1, width, width)

    latent_out, xs, gs, back_t, row_stats, gain_grads = latent_pass(
        raw_parts,
        stat_parts,
        latent_full,
        cotangent,
        value_out.reshape(2, blocks, width // 2),
        jnp.stack([gain_mlp_one, gain_self, gain_mlp_two]),
        jnp.pad(gain_input, (0, tall - channels))[:, None],
        whole,
        late,
        rows_own,
        4,
    )
    across = -(-channels // 128) * 128
    grad_raw, gain_sums, cross_sum, grad_pixels, summed = backward_pass(
        values,
        table,
        gained,
        at,
        a_low,
        back_t,
        row_stats,
        gain_grads,
        xs,
        gs,
        channels,
        2,
    )

    share = share_rows(channels, count)
    (
        grad_latent_array,
        gain_latent_sum,
        gain_sums,
        grad_w_query,
        grad_w_key,
        grad_w_value,
        grad_w_cross_out,
        g_up_one,
        g_up_two,
        g_down_one,
        g_down_two,
        g_sq,
        g_sk,
        g_sv,
        g_so,
    ) = tail_pass(
        grad_raw.reshape(latents, across),
        gain_sums,
        cross_sum,
        score_mat,
        latent_full,
        lax.dynamic_slice_in_dim(queries, me * depth, depth, 1),
        lax.dynamic_slice_in_dim(latent_normed, me * depth, depth, 1),
        query_mat.reshape(width, width),
        key_full.reshape(width, side),
        jnp.pad(w_value, ((0, share * count - channels), (0, 0))),
        w_cross_out,
        jnp.pad(gain_input, (0, across - channels))[None],
        gain_latent[None],
        summed,
        channels,
    )
    gain_one, gain_attn, gain_two = gain_sums[0], gain_sums[1], gain_sums[2]
    gain_in = gain_sums[3, :channels]
    grad_gain_latent = gain_latent_sum[0]
    return (
        latent_out,
        grad_pixels,
        grad_latent_array,
        gain_in,
        grad_gain_latent,
        grad_w_query,
        grad_w_key,
        grad_w_value,
        grad_w_cross_out,
        gain_one,
        g_up_one,
        g_down_one,
        gain_attn,
        g_sq,
        g_sk,
        g_sv,
        g_so,
        gain_two,
        g_up_two,
        g_down_two,
    )


def solution(mesh):
    rows, columns, copied = P("pix", None), P(None, "pix"), P()
    return jax.shard_map(
        local,
        mesh=mesh,
        in_specs=(
            P("img", None, "pix"),
            P("img", "pix"),
            rows,
            copied,
            copied,
            rows,
            columns,
            columns,
            rows,
            copied,
            columns,
            rows,
            copied,
            rows,
            rows,
            rows,
            rows,
            copied,
            columns,
            rows,
            P("img", "pix", None),
        ),
        out_specs=(
            P("img", "pix", None),
            P("img", None, "pix"),
            rows,
            copied,
            copied,
            rows,
            columns,
            columns,
            rows,
            copied,
            columns,
            rows,
            copied,
            rows,
            rows,
            rows,
            rows,
            copied,
            columns,
            rows,
        ),
        check_vma=False,
    )
```
